32 devices in a mesh: dp: 4 (over y, x), blk: 2 (over core), sp: 4 (over z).
Axes of the slice: x: 2, y: 2, z: 4, core: 2. Of those that a mesh axis runs over, the one named last changes fastest.
Arguments:
- tokens: bfloat16 [4096, 2048], P(('dp', 'blk', 'sp')), may hold values from -24 to 24
- query_weight: bfloat16 [2048, 2048], P(('dp', 'blk', 'sp')), may hold values from -1 to 1
- key_weight: bfloat16 [2048, 2048], P(('dp', 'blk', 'sp')), may hold values from -1 to 1
- value_weight: bfloat16 [2048, 2048], P(('dp', 'blk', 'sp')), may hold values from -0.125 to 0.125
- output_weight: bfloat16 [2048, 2048], P(('dp', 'blk', 'sp')), may hold values from -0.5 to 0.5
- router_weight: bfloat16 [2048, 64], P(('dp', 'blk', 'sp')), may hold values from -16 to 16
- attention_gain: bfloat16 [2048], P(('dp', 'blk', 'sp')), may hold values from 0.099609375 to 1.8984375
- query_gain: bfloat16 [2048], P(('dp', 'blk', 'sp')), may hold values from 0.6 to 1.4
- key_gain: bfloat16 [2048], P(('dp', 'blk', 'sp')), may hold values from 0.6 to 1.4
- feature_gain: bfloat16 [2048], P(('dp', 'blk', 'sp')), may hold values from 0.099609375 to 1.8984375
- gate_weight: bfloat16 [64, 2048, 1024], P(('dp', 'sp'), None, 'blk'), may hold values from -0.125 to 0.125
- up_weight: bfloat16 [64, 2048, 1024], P(('dp', 'sp'), None, 'blk'), may hold values from -0.125 to 0.125
- down_weight: bfloat16 [64, 1024, 2048], P(('dp', 'sp'), 'blk'), may hold values from -6 to 6
- routes: int32 [4096, 8], P(('dp', 'blk', 'sp')), may hold values from 0 to 63, all different within a row; in each aligned block of 128 rows (0 to 127, 128 to 255, ...) at most 24 rows name the same one
- cotangent: bfloat16 [4096, 2048], P(('dp', 'blk', 'sp')), may hold values from -6 to 6
Outputs:
- block_output: bfloat16 [4096, 2048], P(('dp', 'blk', 'sp'))
- input_gradient: float32 [4096, 2048], P(('dp', 'blk', 'sp'))
- query_gradient: float32 [2048, 2048], P(('dp', 'blk', 'sp'))
- key_gradient: float32 [2048, 2048], P(('dp', 'blk', 'sp'))
- value_gradient: float32 [2048, 2048], P(('dp', 'blk', 'sp'))
- output_gradient: float32 [2048, 2048], P(('dp', 'blk', 'sp'))
- router_gradient: float32 [2048, 64], P(('dp', 'blk', 'sp'))
- gradient_attention: float32 [2048], P(('dp', 'blk', 'sp'))
- gradient_queries: float32 [2048], P(('dp', 'blk', 'sp'))
- gradient_keys: float32 [2048], P(('dp', 'blk', 'sp'))
- gradient_features: float32 [2048], P(('dp', 'blk', 'sp'))
- gate_gradient: float32 [64, 2048, 1024], P(('dp', 'sp'), None, 'blk')
- up_gradient: float32 [64, 2048, 1024], P(('dp', 'sp'), None, 'blk')
- down_gradient: float32 [64, 1024, 2048], P(('dp', 'sp'), 'blk')
The draws below stay inside these ranges and needn't reach their ends.
Inputs may be any that keep to these rules, and one draw needn't show every extreme that they name: `routes`: each row names 8 different experts. In the rows of one device no expert is named more than 24 times, a bound that some block reaches.
All inputs are finite; a program needn't handle non-finite values.
Results may differ from the reference program's by a relative error of at most 0.02.
Values may be sent and summed in bfloat16 or wider, within the bound.
A program may use at most 384 MiB of HBM per device.

```python
import math
import jax
import jax.numpy as jnp
import numpy as np
from jax import lax

D = 2048
HEADS = 16
HEAD_DIM = 128
FF = 1024
EXPERTS = 64
TOPK = 8
TOK_DEV = 128
SEQ = 1024
TOKENS = 4096
CAP = 24
N_DP = 4
N_BLK = 2
DEVICES = 32


def projection(key, salt_value):
    base_draw = jnp.clip(jax.random.normal(jax.random.fold_in(key, salt_value), (D, D), jnp.float32), -6.0, 6.0)
    return base_draw * D ** (-0.5)


def draw_tokens(key, part):
    first_key = jax.random.fold_in(key, 1)
    second_key = jax.random.fold_in(key, 2)
    base_draw = jnp.clip(jax.random.normal(first_key, (TOKENS, D), jnp.float32), -6.0, 6.0)
    row_scale = jnp.exp(jax.random.uniform(second_key, (TOKENS, 1), jnp.float32, math.log(0.3), math.log(3.0)))
    return jnp.clip(base_draw * row_scale, -24.0, 24.0).astype(jnp.bfloat16)


def draw_query_weight(key, part):
    return projection(key, 21).astype(jnp.bfloat16)


def draw_key_weight(key, part):
    return projection(key, 22).astype(jnp.bfloat16)


def draw_router_weight(key, part):
    base_draw = jnp.clip(jax.random.normal(jax.random.fold_in(key, 51), (D, EXPERTS), jnp.float32), -6.0, 6.0) * (0.45 * D ** (-0.5))
    column_scale = jnp.exp(jax.random.uniform(jax.random.fold_in(key, 52), (1, EXPERTS), jnp.float32, 0.0, math.log(1.5)))
    return jnp.clip(base_draw * column_scale, -16.0, 16.0).astype(jnp.bfloat16)


def draw_query_gain(key, part):
    return jax.random.uniform(jax.random.fold_in(key, 41), (D,), jnp.float32, 0.6, 1.4).astype(jnp.bfloat16)


def draw_key_gain(key, part):
    return jax.random.uniform(jax.random.fold_in(key, 42), (D,), jnp.float32, 0.6, 1.4).astype(jnp.bfloat16)


def levels(rng, dims, pieces, least, largest):
    factor_of = 1.0
    for position, parts in pieces:
        draws = jax.random.uniform(jax.random.fold_in(jax.random.fold_in(rng, 6), position), (parts,), jnp.float32, least / len(pieces), largest / len(pieces))
        factor_of = factor_of * jnp.repeat(jnp.exp(draws), dims[position] // parts).reshape((-1,) + (1,) * (len(dims) - 1 - position))
    return factor_of


def shared_out(rng, own, number, rows, number_of, top, reach, lean):
    order = jax.random.permutation(rng, number_of)
    crowded, ordinary = portions_of(number_of, rows * top, reach, lean, True), portions_of(number_of, rows * top, reach, lean, False)
    places = jnp.arange(number_of)

    def named(sizes, offset_by):
        used = int((sizes > 0).sum())
        fixed = max(1, used // 4)
        moved = fixed + (places - fixed + offset_by * (used - fixed)) % max(1, number_of - fixed)
        return jnp.zeros((number_of,), jnp.int32).at[order[jnp.where(places < fixed, places, moved)]].set(jnp.asarray(sizes, jnp.int32))

    sizes = jnp.where(number % 4 == 0, named(crowded, number // 4), named(ordinary, number - number // 4 - 1))
    mixed = jax.random.permutation(jax.random.fold_in(own, 3), number_of)
    giver, sink = mixed[0:number_of // 2 * 2:2], mixed[1:number_of // 2 * 2:2]
    room = jnp.minimum(sizes[giver] - 1, reach - sizes[sink]) // 2
    room = jnp.where((giver == order[0]) | (sink == order[0]) | (sizes[sink] == 0), 0, jnp.maximum(room, 0))
    moved = jax.random.randint(jax.random.fold_in(own, 4), (number_of // 2,), 0, 1 << 20) % (room + 1)
    sizes = sizes.at[giver].add(-moved).at[sink].add(moved)
    labels = jnp.searchsorted(jnp.cumsum(sizes), jnp.arange(rows * top), side="right").astype(jnp.int32)
    grid = labels.reshape(top, rows).T
    grid = grid[jax.random.permutation(jax.random.fold_in(own, 1), rows)]
    offset_by = jax.random.randint(jax.random.fold_in(own, 2), (rows, 1), 0, top)
    return jnp.take_along_axis(grid, (jnp.arange(top)[None, :] + offset_by) % top, axis=1)


def portions_of(amount, total, most, lean, full):
    loads = [(1 << 20) // math.isqrt(grade ** lean) + 1 for grade in range(1, amount + 1)]
    largest = most if full else min(most, max(-(-total // amount), total * loads[0] // sum(loads)))
    least = 1 if total - largest >= amount - 1 else 0
    counts, spare = [largest] + [least] * (amount - 1), total - largest - least * (amount - 1)
    while spare > 0:
        candidates = [i for i in range(1, amount) if counts[i] < largest] or [i for i in range(1, amount) if counts[i] < most]
        mass, remaining = sum([loads[i] for i in candidates]), spare
        for i in candidates:
            more = min(most - counts[i], max(1, remaining * loads[i] // mass), spare)
            counts[i] = counts[i] + more
            spare = spare - more
    return np.array(counts)


def gaussian(key, shape, scale, limit, shards=(), kind=jnp.bfloat16):
    factor_of = levels(key, shape, shards, -0.22, 0.18) if shards else 1.0
    result = jax.random.normal(key, shape, jnp.float32) * scale * factor_of
    return jnp.minimum(jnp.maximum(result, -limit), limit).astype(kind)


def setup_inputs(seed: int = 0) -> dict:
    key_of = jax.random.split(jax.random.key(seed), 16)
    tokens = draw_tokens(jax.random.fold_in(key_of[15], 71), 0)
    query_weight = draw_query_weight(jax.random.fold_in(key_of[15], 71), 0)
    key_weight = draw_key_weight(jax.random.fold_in(key_of[15], 71), 0)
    value_weight = gaussian(key_of[3], (D, D), D ** -0.5, 0.125, ((0, 32),))
    output_weight = gaussian(key_of[4], (D, D), (D // 16) ** -0.5, 0.5, ((0, 32),))
    router_weight = draw_router_weight(jax.random.fold_in(key_of[15], 71), 0)
    attention_gain = jnp.clip(1.0 + 0.18 * jax.random.normal(key_of[6], (D,), jnp.float32), 0.099609375, 1.8984375).astype(jnp.bfloat16)
    query_gain = draw_query_gain(jax.random.fold_in(key_of[15], 71), 0)
    key_gain = draw_key_gain(jax.random.fold_in(key_of[15], 71), 0)
    feature_gain = jnp.clip(1.0 + 0.18 * jax.random.normal(key_of[9], (D,), jnp.float32), 0.099609375, 1.8984375).astype(jnp.bfloat16)
    gate_weight = gaussian(key_of[10], (EXPERTS, D, FF), D ** -0.5, 0.125, ((0, 16), (2, 2)))
    up_weight = gaussian(key_of[11], (EXPERTS, D, FF), D ** -0.5, 0.125, ((0, 16), (2, 2)))
    down_weight = gaussian(key_of[12], (EXPERTS, FF, D), (max(FF // 1024, 1)) ** -0.5, 6.0, ((0, 16), (1, 2)))
    routes_keys = jax.random.split(jax.random.fold_in(key_of[13], 1), TOKENS // TOK_DEV)
    routes_turns = jax.random.permutation(jax.random.fold_in(key_of[13], 3), TOKENS // TOK_DEV)
    routes = jax.vmap(lambda own, number: shared_out(jax.random.fold_in(key_of[13], 2), own, number, TOK_DEV, EXPERTS, TOPK, CAP, 1))(routes_keys, routes_turns).reshape((TOKENS, TOPK))
    cotangent = gaussian(key_of[14], (TOKENS, D), 1.0, 6.0, ((0, 32),))
    return {"tokens": tokens, "query_weight": query_weight, "key_weight": key_weight, "value_weight": value_weight, "output_weight": output_weight, "router_weight": router_weight, "attention_gain": attention_gain, "query_gain": query_gain, "key_gain": key_gain, "feature_gain": feature_gain, "gate_weight": gate_weight, "up_weight": up_weight, "down_weight": down_weight, "routes": routes, "cotangent": cotangent}


@jax.custom_vjp
def low(v):
    return lax.optimization_barrier(v.astype(jnp.bfloat16)).astype(jnp.float32)

@jax.custom_vjp
def low_back(v):
    return v

def low_keep(v):
    return (low(v), None)

def low_pass(kept, grad):
    return (grad,)

def back_keep(v):
    return (v, None)

def back_low(kept, grad):
    return (low(grad),)
low.defvjp(low_keep, low_pass)
low_back.defvjp(back_keep, back_low)
NORM_EPSILON = 1e-05
ROPE_BASE = 10000.0
MASKED = -1e+30
HIGHEST_PRECISION = lax.Precision.HIGHEST

def matmul(left, right):
    return jnp.dot(left, right, precision=HIGHEST_PRECISION, preferred_element_type=jnp.float32)

def norm_apply(values, norm_gain):
    return values * lax.rsqrt(lax.optimization_barrier(jnp.mean(values * values, axis=-1, keepdims=True)) + NORM_EPSILON) * norm_gain

def rope_tables(positions, head_size):
    half_size = head_size // 2
    frequencies = jnp.exp(-math.log(ROPE_BASE) * 2.0 * jnp.arange(half_size, dtype=jnp.float32) / head_size)
    angles = positions.astype(jnp.float32)[:, None] * frequencies[None, :]
    return (jnp.cos(angles), jnp.sin(angles))

def rotate(values, cosine, sine):
    half_size = values.shape[-1] // 2
    first_half = values[..., :half_size]
    second_half = values[..., half_size:]
    cosine_row = cosine[:, None, :]
    sine_row = sine[:, None, :]
    return jnp.concatenate([first_half * cosine_row - second_half * sine_row, second_half * cosine_row + first_half * sine_row], axis=-1)

def rank_slots(route_rows):
    flat_experts = route_rows.reshape(-1)
    onehot = (flat_experts[:, None] == jnp.arange(EXPERTS, dtype=jnp.int32)[None, :]).astype(jnp.int32)
    return lax.optimization_barrier(jnp.sum(jnp.cumsum(onehot, axis=0) * onehot, axis=1)) - 1

def head_major(values):
    grouped = values.reshape(N_DP, SEQ, HEADS, HEAD_DIM).transpose(0, 2, 1, 3)
    return grouped.reshape(N_DP * HEADS, SEQ, HEAD_DIM)

def attend(inputs):
    query_head, key_head, value_head = inputs
    scores = low_back(matmul(query_head, key_head.T) * (1.0 / math.sqrt(HEAD_DIM)))
    causal = jnp.arange(SEQ)[:, None] >= jnp.arange(SEQ)[None, :]
    scores = jnp.where(causal, scores, MASKED)
    attn_weights = jax.nn.softmax(scores, axis=-1)
    return matmul(low(attn_weights), value_head)

def reference(tokens, query_weight, key_weight, value_weight, output_weight, router_weight, attention_gain, query_gain, key_gain, feature_gain, gate_weight, up_weight, down_weight, routes, cotangent):
    device_routes = routes.reshape(DEVICES, TOK_DEV * TOPK)
    slot_rank = jax.vmap(rank_slots)(device_routes)
    device_ids = jnp.arange(DEVICES, dtype=jnp.int32)[:, None]
    slot_index = (device_routes * DEVICES + device_ids) * CAP + slot_rank
    token_index = device_ids * TOK_DEV + jnp.arange(TOK_DEV * TOPK, dtype=jnp.int32)[None, :] // TOPK
    slot_token = jnp.zeros((EXPERTS * DEVICES * CAP,), jnp.int32).at[slot_index.reshape(-1)].set(token_index.reshape(-1))
    slot_valid = jnp.zeros((EXPERTS * DEVICES * CAP,), jnp.float32).at[slot_index.reshape(-1)].set(1.0)
    slot_token = slot_token.reshape(EXPERTS, DEVICES * CAP)
    slot_valid = slot_valid.reshape(EXPERTS, DEVICES * CAP)
    route_slot = slot_index.reshape(TOKENS, TOPK)
    positions = jnp.arange(TOKENS, dtype=jnp.int32) % SEQ
    cosine, sine = rope_tables(positions, HEAD_DIM)
    part_width = FF // N_BLK

    def layer_forward(tokens_f, query_w, key_w, value_w, output_w, router_w, attention_g, query_g, key_g, feature_g, gate_w, up_w, down_w):
        normed = low(norm_apply(tokens_f, attention_g))
        query_lin = low_back(matmul(normed, query_w))
        key_lin = low_back(matmul(normed, key_w))
        value_rows = low_back(low(matmul(normed, value_w)))
        query_rot = rotate(norm_apply(query_lin, query_g).reshape(TOKENS, HEADS, HEAD_DIM), cosine, sine)
        key_rot = rotate(norm_apply(key_lin, key_g).reshape(TOKENS, HEADS, HEAD_DIM), cosine, sine)
        query_rot = low_back(low(query_rot))
        key_rot = low_back(low(key_rot))
        context = lax.map(jax.checkpoint(attend), (head_major(query_rot), head_major(key_rot), head_major(value_rows.reshape(TOKENS, HEADS, HEAD_DIM))))
        context = context.reshape(N_DP, HEADS, SEQ, HEAD_DIM).transpose(0, 2, 1, 3).reshape(TOKENS, D)
        context = low_back(low(context))
        attended = low_back(matmul(context, output_w))
        residual = tokens_f + attended
        features = low(norm_apply(residual, feature_g))
        logits = low_back(matmul(features, router_w))
        router_probs = jax.nn.softmax(logits, axis=-1)

        def run_expert(inputs):
            gate_expert, up_expert, down_expert, token_rows, valid_rows = inputs
            slot_rows = features[token_rows] * valid_rows[:, None]
            expert_total = jnp.zeros((DEVICES * CAP, D), jnp.float32)
            for half_index in range(N_BLK):
                low_col = half_index * part_width
                copy_rows = low_back(slot_rows)
                gate_values = low_back(matmul(copy_rows, gate_expert[:, low_col:low_col + part_width]))
                up_values = low_back(matmul(copy_rows, up_expert[:, low_col:low_col + part_width]))
                hidden = low_back(low(jax.nn.silu(gate_values) * up_values))
                expert_total = expert_total + low(matmul(hidden, down_expert[low_col:low_col + part_width, :]))
            return low_back(expert_total)
        expert_rows = lax.map(jax.checkpoint(run_expert), (gate_w, up_w, down_w, slot_token, slot_valid))
        flat_rows = expert_rows.reshape(EXPERTS * DEVICES * CAP, D)
        picked = flat_rows[route_slot]
        route_probs = jnp.take_along_axis(router_probs, routes, axis=1)
        mixture = lax.optimization_barrier(jnp.sum(route_probs[:, :, None] * picked, axis=1))
        return residual + mixture
    primals = (tokens.astype(jnp.float32), query_weight.astype(jnp.float32), key_weight.astype(jnp.float32), value_weight.astype(jnp.float32), output_weight.astype(jnp.float32), router_weight.astype(jnp.float32), attention_gain.astype(jnp.float32), query_gain.astype(jnp.float32), key_gain.astype(jnp.float32), feature_gain.astype(jnp.float32), gate_weight.astype(jnp.float32), up_weight.astype(jnp.float32), down_weight.astype(jnp.float32))
    output, pullback = jax.vjp(layer_forward, *primals)
    grads_all = pullback(cotangent.astype(jnp.float32))
    return (output.astype(jnp.bfloat16), grads_all[0], grads_all[1], grads_all[2], grads_all[3], grads_all[4], grads_all[5], grads_all[6], grads_all[7], grads_all[8], grads_all[9], grads_all[10], grads_all[11], grads_all[12])
```

```python
import functools
import math

import jax
import jax.numpy as jnp
from jax import lax
from jax.experimental import pallas as pl
from jax.experimental.pallas import tpu as pltpu
from jax.sharding import PartitionSpec as P

DP, BLK, SP = AXES = ("dp", "blk", "sp")

HEADS = 16
HEAD_DIM = 128
EXPERTS = 64
TOPK = 8
CAP = 24


NORM_EPSILON = 1e-05
ROPE_BASE = 10000.0
MASKED = -1e30


def norm_apply(values, norm_gain):
    return (
        values
        * lax.rsqrt(jnp.mean(values * values, axis=-1, keepdims=True) + NORM_EPSILON)
        * norm_gain
    )


def rope_tables(positions, head_size):
    half_size = head_size // 2
    frequencies = jnp.exp(
        -math.log(ROPE_BASE) * 2.0 * jnp.arange(half_size, dtype=jnp.float32) / head_size
    )
    angles = positions.astype(jnp.float32)[:, None] * frequencies[None, :]
    return (jnp.cos(angles), jnp.sin(angles))


def rotate(values, cosine, sine):
    half_size = values.shape[-1] // 2
    first_half = values[..., :half_size]
    second_half = values[..., half_size:]
    cosine_row = cosine[:, None, :]
    sine_row = sine[:, None, :]
    return jnp.concatenate(
        [
            first_half * cosine_row - second_half * sine_row,
            second_half * cosine_row + first_half * sine_row,
        ],
        axis=-1,
    )


def rank_slots(route_rows):
    flat_experts = route_rows.reshape(-1)
    onehot = (flat_experts[:, None] == jnp.arange(EXPERTS, dtype=jnp.int32)[None, :]).astype(
        jnp.int32
    )
    return (flat_experts, jnp.sum(jnp.cumsum(onehot, axis=0) * onehot, axis=1) - 1)


MESH_ID = pl.DeviceIdType.MESH
VMEM_BYTES = 56 * 1024 * 1024


class Place:
    def __init__(self):
        self.dp = lax.axis_index(DP)
        self.blk = lax.axis_index(BLK)
        self.z = lax.axis_index(SP)
        self.x = self.dp % 2
        self.y = self.dp // 2
        self.col = self.blk * 4 + self.z

    def column(self, k):
        if k == 0:
            return self.dp
        if k == 1:
            return self.dp + 1 - 2 * self.x
        if k == 2:
            return self.dp + 2 - 4 * self.y
        return 3 - self.dp

    def at(self, k=0, blk=None, z=None):
        return (self.column(k), self.blk if blk is None else blk, self.z if z is None else z)


def entry_barrier(place, reach):
    barrier = pltpu.get_barrier_semaphore()

    def tell(target):
        pl.semaphore_signal(barrier, inc=1, device_id=target, device_id_type=MESH_ID)

    if reach == "all":
        me = (place.dp * 2 + place.blk) * 4 + place.z

        @pl.loop(1, 32)
        def _(step):
            other = (me + step) % 32
            tell((other // 8, (other // 4) % 2, other % 4))

        pl.semaphore_wait(barrier, 31)
    elif reach == "column":

        @pl.loop(1, 8)
        def _(step):
            other = (place.col + step) % 8
            tell((place.dp, other // 4, other % 4))

        pl.semaphore_wait(barrier, 7)
    else:
        planes = reach == "planes"
        tell(place.at(0, 1 - place.blk))
        if planes:
            tell(place.at(1))
            tell(place.at(2))

        @pl.when(place.z > 0)
        def _():
            tell(place.at(z=place.z - 1))

        @pl.when(place.z < 3)
        def _():
            tell(place.at(z=place.z + 1))

        ends = (3 - place.z) // 3 + place.z // 3
        pl.semaphore_wait(barrier, 3 + (2 if planes else 0) - ends)


def remote(src, dst, send_sem, recv_sem, target):
    return pltpu.make_async_remote_copy(
        src_ref=src,
        dst_ref=dst,
        send_sem=send_sem,
        recv_sem=recv_sem,
        device_id=target,
        device_id_type=MESH_ID,
    )


class GatherFlow:
    SENDS = 40
    RECVS = 37

    def __init__(self, place, src, out, send, recv, full, direct=False):
        self.p, self.src, self.out, self.send, self.recv, self.full = place, src, out, send, recv, full
        self.direct = direct
        self.half = src.shape[0] // 2

    def slot(self, k, blk, s):
        if self.full:
            return (self.p.column(k) * 2 + blk) * 4 + s
        return blk * 4 + s

    def block(self, k, s, blk=None):
        return self.out.at[self.slot(k, self.p.blk if blk is None else blk, s)]

    def copies(self, k, s, own=False):
        src = self.src if own else self.block(k, s)
        return src, self.block(k, s)

    def up(self, s, own=False):
        src, dst = self.copies(0, s, own)
        return remote(src, dst, self.send.at[s], self.recv.at[s], self.p.at(z=jnp.minimum(self.p.z + 1, 3)))

    def down(self, s, own=False):
        src, dst = self.copies(0, s, own)
        return remote(src, dst, self.send.at[4 + s], self.recv.at[s], self.p.at(z=jnp.maximum(self.p.z - 1, 0)))

    def across_x(self, s, own=False):
        src, dst = self.copies(0, s, own)
        return remote(src, dst, self.send.at[8 + s], self.recv.at[4 + s], self.p.at(1))

    def across_y(self, s, own=False):
        src, dst = self.copies(0, s, own)
        return remote(src, dst, self.send.at[12 + s], self.recv.at[8 + s], self.p.at(2))

    def turn_y(self, s):
        ref = self.block(1, s).at[pl.ds(0, self.half)]
        return remote(ref, ref, self.send.at[16 + s], self.recv.at[12 + s], self.p.at(2))

    def turn_x(self, s):
        ref = self.block(2, s).at[pl.ds(self.half, self.half)]
        return remote(ref, ref, self.send.at[20 + s], self.recv.at[16 + s], self.p.at(1))

    def core(self, k, s, own=False):
        src, dst = self.copies(k, s, own)
        return remote(
            src, dst, self.send.at[24 + 4 * k + s], self.recv.at[20 + 4 * k + s], self.p.at(0, 1 - self.p.blk)
        )

    def got(self, sem, ref):
        remote(ref, ref, self.send.at[0], self.recv.at[sem], self.p.at(0, 1 - self.p.blk)).wait_recv()

    def own_copy(self):
        return pltpu.make_async_copy(self.src, self.block(0, self.p.z), self.recv.at[36])

    def spread(self, s, own=False):
        if self.full:
            self.across_x(s, own).start()
            self.across_y(s, own).start()
        self.core(0, s, own).start()

    def straight(self, step):
        z = self.p.z
        return remote(
            self.src, self.block(0, z), self.send.at[step - 1], self.recv.at[z], self.p.at(z=(z + step) % 4)
        )

    def begin(self):
        z = self.p.z
        if self.direct:
            for step in (1, 2, 3):
                self.straight(step).start()
            self.spread(z, True)
            self.own_copy().start()
            return

        @pl.when(z < 3)
        def _():
            self.up(z, True).start()

        @pl.when(z > 0)
        def _():
            self.down(z, True).start()

        self.spread(z, True)
        self.own_copy().start()

    def along(self, d):
        z = self.p.z

        @pl.when(z >= d)
        def _():
            s = z - d
            self.got(s, self.block(0, s))

            if not self.direct:

                @pl.when(z < 3)
                def _():
                    self.up(s).start()

            self.spread(s)

        @pl.when(z + d <= 3)
        def _():
            s = z + d
            self.got(s, self.block(0, s))

            if not self.direct:

                @pl.when(z > 0)
                def _():
                    self.down(s).start()

            self.spread(s)

    def each(self, d, act):
        z = self.p.z
        if d == 0:
            act(z)
            return

        @pl.when(z >= d)
        def _():
            act(z - d)

        @pl.when(z + d <= 3)
        def _():
            act(z + d)

    def turn(self, d):
        if not self.full:
            return

        def act(s):
            self.got(4 + s, self.block(1, s))
            self.turn_y(s).start()
            self.core(1, s).start()
            self.got(8 + s, self.block(2, s))
            self.turn_x(s).start()
            self.core(2, s).start()

        self.each(d, act)

    def corner(self, d):
        if not self.full:
            return

        def act(s):
            self.got(12 + s, self.block(3, s).at[pl.ds(0, self.half)])
            self.got(16 + s, self.block(3, s).at[pl.ds(self.half, self.half)])
            self.core(3, s).start()

        self.each(d, act)

    def settle_plane(self, s):
        for k in range(4 if self.full else 1):
            self.got(20 + 4 * k + s, self.block(k, s, 1 - self.p.blk))
            self.core(k, s).wait_send()
        if self.full:
            self.across_x(s).wait_send()
            self.across_y(s).wait_send()
            self.turn_x(s).wait_send()
            self.turn_y(s).wait_send()

    def finish(self):
        z = self.p.z

        @pl.loop(0, 4)
        def _(s):
            self.settle_plane(s)
            if not self.direct:

                @pl.when((s <= z) & (z < 3))
                def _():
                    self.up(s).wait_send()

                @pl.when((s >= z) & (z > 0))
                def _():
                    self.down(s).wait_send()

        if self.direct:
            for step in (1, 2, 3):
                self.straight(step).wait_send()
        self.own_copy().wait()

    def steps(self):
        return [
            self.begin,
            lambda: self.along(1),
            lambda: self.turn(0),
            lambda: self.along(2),
            lambda: self.turn(1),
            lambda: self.along(3),
            lambda: self.corner(0),
            lambda: self.turn(2),
            lambda: self.corner(1),
            lambda: self.turn(3),
            lambda: self.corner(2),
            lambda: self.corner(3),
            self.finish,
        ]


class PlaneFlow(GatherFlow):
    def __init__(self, place, blocks, out, send, recv, local):
        super().__init__(place, blocks[0][1], out, send, recv, True)
        self.blocks, self.local = blocks, local

    def begin(self):
        for i, (s, src) in enumerate(self.blocks):
            self.src = src
            self.spread(s, True)
            pltpu.make_async_copy(src, self.block(0, s), self.local.at[i]).start()

    def turns(self):
        for s, _ in self.blocks:
            self.got(4 + s, self.block(1, s))
            self.turn_y(s).start()
            self.core(1, s).start()
            self.got(8 + s, self.block(2, s))
            self.turn_x(s).start()
            self.core(2, s).start()

    def corners(self):
        for s, _ in self.blocks:
            self.got(12 + s, self.block(3, s).at[pl.ds(0, self.half)])
            self.got(16 + s, self.block(3, s).at[pl.ds(self.half, self.half)])
            self.core(3, s).start()

    def finish(self):
        for i, (s, src) in enumerate(self.blocks):
            self.settle_plane(s)
            pltpu.make_async_copy(src, self.block(0, s), self.local.at[i]).wait()


def run_flows(flows):
    lists = [flow.steps() for flow in flows]
    for position in range(max(len(steps) for steps in lists)):
        for steps in lists:
            if position < len(steps):
                steps[position]()


def gather_call(arrays, fulls, name, collective_id):
    count = len(arrays)

    def kernel(*refs):
        srcs, outs = refs[:count], refs[count : 2 * count]
        sems = refs[2 * count :]
        place = Place()
        entry_barrier(place, "planes" if any(fulls) else "line")
        run_flows(
            [
                GatherFlow(place, srcs[i], outs[i], sems[2 * i], sems[2 * i + 1], fulls[i])
                for i in range(count)
            ]
        )

    scratch = []
    for _ in arrays:
        scratch += [pltpu.SemaphoreType.DMA((GatherFlow.SENDS,)), pltpu.SemaphoreType.DMA((GatherFlow.RECVS,))]
    return pl.pallas_call(
        kernel,
        out_shape=[
            jax.ShapeDtypeStruct((32 if full else 8,) + a.shape, a.dtype) for a, full in zip(arrays, fulls)
        ],
        in_specs=[pl.BlockSpec(memory_space=pl.ANY)] * count,
        out_specs=[pl.BlockSpec(memory_space=pl.ANY)] * count,
        scratch_shapes=scratch,
        compiler_params=pltpu.CompilerParams(collective_id=collective_id, has_side_effects=True),
        name=name,
    )(*arrays)


def add_rows(dst, terms, rows):
    @pl.loop(0, rows // 16)
    def _(i):
        at = pl.ds(pl.multiple_of(i * 16, 16), 16)
        total = terms[0][at, :].astype(jnp.float32)
        for term in terms[1:]:
            total = total + term[at, :].astype(jnp.float32)
        dst[at, :] = total.astype(dst.dtype)


class ScatterFlow:
    SENDS = 16 + 8 + 8 + 4 + 4
    RECVS = 16 + 8 + 8 + 4 + 4
    LOCALS = 20

    def __init__(self, place, part, out, scratch, full, plane_only=False):
        self.p, self.part, self.out, self.full, self.plane_only = place, part, out, full, plane_only
        if full:
            (self.acc, self.near, self.half_in, self.side_in, self.line_in, self.sum, self.send, self.recv, self.local) = scratch
        else:
            (self.acc, self.near, self.line_in, self.sum, self.send, self.recv, self.local) = scratch
        self.columns = 4 if full else 1
        self.rows = part.shape[1]
        self.half = self.rows // 2

    @staticmethod
    def scratch(rows, width, dtype, full):
        columns = 4 if full else 1
        shapes = [
            pltpu.VMEM((columns, 4, rows, width), dtype),
            pltpu.VMEM((columns, 4, rows, width), dtype),
        ]
        if full:
            shapes += [pltpu.VMEM((2, 4, rows // 2, width), dtype), pltpu.VMEM((2, 4, rows, width), dtype)]
        return shapes + [
            pltpu.VMEM((2, 4, rows, width), dtype),
            pltpu.VMEM((rows, width), jnp.float32),
            pltpu.SemaphoreType.DMA((ScatterFlow.SENDS,)),
            pltpu.SemaphoreType.DMA((ScatterFlow.RECVS,)),
            pltpu.SemaphoreType.DMA((ScatterFlow.LOCALS,)),
        ]

    def slot(self, k, blk, s):
        if self.full:
            return (self.p.column(k) * 2 + blk) * 4 + s
        return blk * 4 + s

    def order(self, i):
        z = self.p.z
        return [3 * (1 - z // 2), (2 + 3 * z) % 5, 1 + z % 2, z][i]

    def load(self, k, s):
        return pltpu.make_async_copy(
            self.part.at[self.slot(k, self.p.blk, s)], self.acc.at[k, s], self.local.at[4 * k + s]
        )

    def core(self, k, s):
        return remote(
            self.part.at[self.slot(k, 1 - self.p.blk, s)],
            self.near.at[k, s],
            self.send.at[4 * k + s],
            self.recv.at[4 * k + s],
            self.p.at(0, 1 - self.p.blk),
        )

    def half_x(self, s):
        return remote(
            self.acc.at[3, s, pl.ds(0, self.half)],
            self.half_in.at[0, s],
            self.send.at[16 + s],
            self.recv.at[16 + s],
            self.p.at(1),
        )

    def half_y(self, s):
        return remote(
            self.acc.at[3, s, pl.ds(self.half, self.half)],
            self.half_in.at[1, s],
            self.send.at[20 + s],
            self.recv.at[20 + s],
            self.p.at(2),
        )

    def side_x(self, s):
        return remote(
            self.acc.at[1, s], self.side_in.at[0, s], self.send.at[24 + s], self.recv.at[24 + s], self.p.at(1)
        )

    def side_y(self, s):
        return remote(
            self.acc.at[2, s], self.side_in.at[1, s], self.send.at[28 + s], self.recv.at[28 + s], self.p.at(2)
        )

    def line_up(self, s):
        return remote(
            self.acc.at[0, s],
            self.line_in.at[0, s],
            self.send.at[32 + s],
            self.recv.at[32 + s],
            self.p.at(z=jnp.minimum(self.p.z + 1, 3)),
        )

    def line_down(self, s):
        return remote(
            self.acc.at[0, s],
            self.line_in.at[1, s],
            self.send.at[36 + s],
            self.recv.at[36 + s],
            self.p.at(z=jnp.maximum(self.p.z - 1, 0)),
        )

    def begin(self):
        for i in range(4):
            s = self.order(i)
            for k in reversed(range(self.columns)):
                self.core(k, s).start()
                self.load(k, s).start()

    def arrive(self, k, s):
        self.load(k, s).wait()
        self.core(k, s).wait_recv()
        return [self.acc.at[k, s], self.near.at[k, s]]

    def stage1(self, i):
        if not self.full:
            return
        s = self.order(i)
        add_rows(self.acc.at[3, s], self.arrive(3, s), self.rows)
        self.half_x(s).start()
        self.half_y(s).start()

    def stage2(self, i):
        if not self.full:
            return
        s = self.order(i)
        first, second = pl.ds(0, self.half), pl.ds(self.half, self.half)
        terms = self.arrive(2, s)
        late = [term.at[first] for term in terms] + [self.half_in.at[0, s]]
        rest = [term.at[second] for term in terms]
        add_rows(rest[0], rest, self.half)
        self.half_x(s).wait_recv()
        add_rows(late[0], late, self.half)
        self.side_y(s).start()
        terms = self.arrive(1, s)
        late = [term.at[second] for term in terms] + [self.half_in.at[1, s]]
        rest = [term.at[first] for term in terms]
        add_rows(rest[0], rest, self.half)
        self.half_y(s).wait_recv()
        add_rows(late[0], late, self.half)
        self.side_x(s).start()

    def stage3(self, i):
        s = self.order(i)
        z = self.p.z
        terms = self.arrive(0, s)
        if self.full:
            self.side_x(s).wait_recv()
            self.side_y(s).wait_recv()
            terms = terms + [self.side_in.at[0, s], self.side_in.at[1, s]]
        add_rows(self.acc.at[0, s], terms, self.rows)
        if self.plane_only:
            self.keep_plane(i).start()
        elif i < 3:

            @pl.when(z == 0)
            def _():
                self.line_up(s).start()

            @pl.when(z == 3)
            def _():
                self.line_down(s).start()

    def chain(self, i):
        s = self.order(i)
        z = self.p.z

        @pl.when((z > 0) & (z < s) & (z < 3))
        def _():
            self.line_up(s).wait_recv()
            add_rows(self.acc.at[0, s], [self.acc.at[0, s], self.line_in.at[0, s]], self.rows)
            self.line_up(s).start()

        @pl.when((z < 3) & (z > s) & (z > 0))
        def _():
            self.line_down(s).wait_recv()
            add_rows(self.acc.at[0, s], [self.acc.at[0, s], self.line_in.at[1, s]], self.rows)
            self.line_down(s).start()

    def final(self):
        z = self.p.z
        mine, above, below = self.acc.at[0, z], self.line_in.at[0, z], self.line_in.at[1, z]

        @pl.when(z > 0)
        def _():
            self.line_up(z).wait_recv()

        @pl.when(z < 3)
        def _():
            self.line_down(z).wait_recv()

        @pl.when(z == 0)
        def _():
            add_rows(self.sum, [mine, below], self.rows)

        @pl.when(z == 3)
        def _():
            add_rows(self.sum, [mine, above], self.rows)

        @pl.when((z > 0) & (z < 3))
        def _():
            add_rows(self.sum, [mine, above, below], self.rows)

        done = pltpu.make_async_copy(self.sum, self.out, self.local.at[0])
        done.start()

        @pl.loop(0, 4)
        def _(s):
            for k in range(self.columns):
                self.core(k, s).wait_send()
            if self.full:
                self.half_x(s).wait_send()
                self.half_y(s).wait_send()
                self.side_x(s).wait_send()
                self.side_y(s).wait_send()

            @pl.when(s > z)
            def _():
                self.line_up(s).wait_send()

            @pl.when(s < z)
            def _():
                self.line_down(s).wait_send()

        done.wait()

    def keep_plane(self, i):
        s = self.order(i)
        return pltpu.make_async_copy(self.acc.at[0, s], self.out.at[s], self.local.at[16 + i])

    def settle_plane(self):
        for i in range(4):
            s = self.order(i)
            self.keep_plane(i).wait()
            for k in range(4):
                self.core(k, s).wait_send()
            self.half_x(s).wait_send()
            self.half_y(s).wait_send()
            self.side_x(s).wait_send()
            self.side_y(s).wait_send()

    def steps(self):
        plan = [
            (self.stage1, 0),
            (self.stage1, 1),
            (self.stage2, 0),
            (self.stage1, 2),
            (self.stage2, 1),
            (self.stage3, 0),
            (self.stage1, 3),
            (self.stage2, 2),
            (self.stage3, 1),
            (self.chain, 0),
            (self.stage2, 3),
            (self.stage3, 2),
            (self.chain, 1),
            (self.chain, 2),
            (self.stage3, 3),
        ]
        return [self.begin] + [functools.partial(act, i) for act, i in plan] + [self.final]


def local_params():
    return pltpu.CompilerParams(vmem_limit_bytes=VMEM_BYTES)


def inner(left, right, left_dim=1, right_dim=0):
    return lax.dot_general(
        left, right, (((left_dim,), (right_dim,)), ((), ())), preferred_element_type=jnp.float32
    )


def pick_rows(picks, features, grads, experts):
    pairs, picked, pair_rows = picks.shape
    width = features.shape[-1]
    per = picked // experts

    def kernel(pick_ref, feature_ref, grad_ref, row_ref, grad_row_ref):
        for src, dst in ((feature_ref, row_ref), (grad_ref, grad_row_ref)):
            rows = inner(pick_ref[0], src[0]).astype(dst.dtype)
            for e in range(experts):
                dst[e] = rows[e * per : (e + 1) * per]

    shape = jax.ShapeDtypeStruct((experts, pairs * per, width), features.dtype)
    source = pl.BlockSpec((1, pair_rows, width), lambda p: (p, 0, 0))
    target = pl.BlockSpec((experts, per, width), lambda p: (0, p, 0))
    return pl.pallas_call(
        kernel,
        out_shape=[shape, shape],
        grid=(pairs,),
        in_specs=[pl.BlockSpec((1, picked, pair_rows), lambda p: (p, 0, 0)), source, source],
        out_specs=[target, target],
        compiler_params=local_params(),
        name="pick_rows",
    )(picks, features, grads)


def put_rows_back(places, out_rows, input_rows):
    pairs, pair_rows, picked = places.shape
    experts, _, width = out_rows.shape
    per = picked // experts

    def kernel(place_ref, out_ref, input_ref, out_sum, input_sum):
        for src, dst in ((out_ref, out_sum), (input_ref, input_sum)):
            rows = jnp.concatenate([src[e] for e in range(experts)], axis=0)
            dst[0] = inner(place_ref[0], rows).astype(dst.dtype)

    shape = jax.ShapeDtypeStruct((pairs, pair_rows, width), out_rows.dtype)
    source = pl.BlockSpec((experts, per, width), lambda p: (0, p, 0))
    target = pl.BlockSpec((1, pair_rows, width), lambda p: (p, 0, 0))
    return pl.pallas_call(
        kernel,
        out_shape=[shape, shape],
        grid=(pairs,),
        in_specs=[pl.BlockSpec((1, pair_rows, picked), lambda p: (p, 0, 0)), source, source],
        out_specs=[target, target],
        compiler_params=local_params(),
        name="put_rows_back",
    )(places, out_rows, input_rows)


def run_experts(rows, grads, probs, gate_weight, up_weight, down_weight):
    experts, slots, width = rows.shape
    hidden = gate_weight.shape[2]
    parts = 2
    part = slots // parts

    def kernel(x, c, p, wg, wu, wd, weighted, gate_back, up_back, out, back, prob_back):
        gate = inner(x[0], wg[0])
        up = inner(x[0], wu[0])
        plain = inner(c[0], wd[0], 1, 1)
        prob = p[0]
        sig = jax.nn.sigmoid(gate)
        act = gate * sig
        hid = act * up
        prob_back[0] = jnp.sum(hid * plain, axis=1, keepdims=True)
        low = (hid * prob).astype(jnp.bfloat16)
        weighted[0] = low
        grad = plain * prob
        gate_low = (grad * up * sig * (1.0 + gate * (1.0 - sig))).astype(jnp.bfloat16)
        up_low = (grad * act).astype(jnp.bfloat16)
        gate_back[0] = gate_low
        up_back[0] = up_low
        out[0] = inner(low, wd[0]).astype(jnp.bfloat16)
        back[0] = (inner(gate_low, wg[0], 1, 1) + inner(up_low, wu[0], 1, 1)).astype(jnp.bfloat16)

    def block(size):
        return pl.BlockSpec((1, part, size), lambda e, i: (e, i, 0))

    def whole(shape):
        return pl.BlockSpec((1,) + shape[1:], lambda e, i: (e, 0, 0))

    narrow = jax.ShapeDtypeStruct((experts, slots, hidden), rows.dtype)
    wide = jax.ShapeDtypeStruct(rows.shape, rows.dtype)
    column = jax.ShapeDtypeStruct((experts, slots, 1), jnp.float32)
    return pl.pallas_call(
        kernel,
        out_shape=[narrow, narrow, narrow, wide, wide, column],
        grid=(experts, parts),
        in_specs=[
            block(width),
            block(width),
            block(1),
            whole(gate_weight.shape),
            whole(up_weight.shape),
            whole(down_weight.shape),
        ],
        out_specs=[block(hidden)] * 3 + [block(width)] * 2 + [block(1)],
        compiler_params=local_params(),
        name="run_experts",
    )(rows, grads, probs, gate_weight, up_weight, down_weight)


class ColumnsFlow:
    SENDS = 24 + 1 + 8
    RECVS = 8 + 1 + 8
    LOCALS = 4

    def __init__(self, place, sources, rows_in, wide, tall, send, recv, local):
        self.p, self.sources, self.rows_in, self.wide, self.tall = place, sources, rows_in, wide, tall
        self.send, self.recv, self.local = send, recv, local
        self.rows = rows_in.shape[0]
        self.share = wide.shape[1] // len(sources)

    def wide_rows(self, col):
        return pl.ds(pl.multiple_of((self.p.dp * 8 + col) * self.rows, self.rows), self.rows)

    def piece(self, i, to, start):
        share = self.share
        src = self.sources[i].at[:, pl.ds(pl.multiple_of(to * share, share), share)]
        dst = self.wide.at[self.wide_rows(self.p.col), pl.ds(i * share, share)]
        return src, dst

    def scatter(self, step, i):
        to = (self.p.col + step) % 8
        src, dst = self.piece(i, to, step)
        return remote(
            src, dst, self.send.at[3 * step + i], self.recv.at[self.p.col], (self.p.dp, to // 4, to % 4)
        )

    def keep(self, i):
        src, dst = self.piece(i, self.p.col, 0)
        return pltpu.make_async_copy(src, dst, self.local.at[i])

    def tall_rows(self, k):
        return self.tall.at[pl.ds(pl.multiple_of(self.p.column(k) * self.rows, self.rows), self.rows)]

    def swap(self):
        group = self.p.dp * 2 + self.p.blk
        dst = self.tall.at[pl.ds(pl.multiple_of(self.p.z * self.rows, self.rows), self.rows)]
        return remote(
            self.rows_in, dst, self.send.at[24], self.recv.at[8], (self.p.z, group // 4, group % 4)
        )

    def stay(self):
        return pltpu.make_async_copy(self.rows_in, self.tall_rows(0), self.local.at[3])

    def at_home(self):
        group = self.p.dp * 2 + self.p.blk
        return (self.p.z == self.p.dp) & (group == self.p.col)

    def band(self, which, k):
        if which == 0:
            height = 8 * self.rows
            return self.wide.at[pl.ds(pl.multiple_of(self.p.column(k) * height, height), height)]
        return self.tall_rows(k)

    def across(self, which, k):
        ref = self.band(which, 0)
        slot = 4 * which + k - 1
        return remote(ref, ref, self.send.at[25 + slot], self.recv.at[9 + slot], self.p.at(k))

    def part(self, which, k, first):
        ref = self.band(which, k)
        half = ref.shape[0] // 2
        return ref.at[pl.ds(0 if first else half, half)]

    def turn(self, which, k):
        ref = self.part(which, k, k == 1)
        slot = 4 * which + 1 + k
        return remote(ref, ref, self.send.at[25 + slot], self.recv.at[9 + slot], self.p.at(3 - k))

    def got(self, sem, ref):
        remote(ref, ref, self.send.at[0], self.recv.at[sem], self.p.at(0, 1 - self.p.blk)).wait_recv()

    def begin(self):
        home = self.at_home()

        @pl.when(home)
        def _():
            self.stay().start()

        @pl.when(jnp.logical_not(home))
        def _():
            self.swap().start()

        @pl.loop(1, 8)
        def _(step):
            for i in range(3):
                self.scatter(step, i).start()

        for i in range(3):
            self.keep(i).start()

    def settle(self):
        home = self.at_home()

        @pl.when(home)
        def _():
            self.stay().wait()

        @pl.when(jnp.logical_not(home))
        def _():
            self.got(8, self.tall_rows(0))

        self.across(1, 1).start()
        self.across(1, 2).start()
        for i in range(3):
            self.keep(i).wait()

        @pl.loop(1, 8)
        def _(step):
            col = (self.p.col + step) % 8
            self.got(col, self.wide.at[self.wide_rows(col)])

        self.across(0, 1).start()
        self.across(0, 2).start()

    def turns(self):
        for which in (1, 0):
            for k in (1, 2):
                self.got(9 + 4 * which + k - 1, self.band(which, k))
                self.turn(which, k).start()

    def finish(self):
        for which in (1, 0):
            for k in (1, 2):
                self.got(9 + 4 * which + 1 + k, self.part(which, 3, k == 1))
                self.turn(which, k).wait_send()
                self.across(which, k).wait_send()

        @pl.when(jnp.logical_not(self.at_home()))
        def _():
            self.swap().wait_send()

        @pl.loop(1, 8)
        def _(step):
            for i in range(3):
                self.scatter(step, i).wait_send()


class SumsFlow:
    SENDS = 8 + 8 + 1
    RECVS = 8 + 8 + 1
    LOCALS = 10

    def __init__(self, place, wide, tall, wide_out, tall_out, scratch):
        self.p = place
        self.parts = (wide, tall)
        self.outs = (wide_out, tall_out)
        self.acc, self.half_in, self.side_in = scratch[0:2], scratch[2:4], scratch[4:6]
        self.send, self.recv, self.local = scratch[6:9]
        self.rows = tall_out.shape[0]

    @staticmethod
    def scratch(wide, tall):
        shapes = []
        for kind in ((4, 1), (2, 2), (2, 1)):
            for part in (wide, tall):
                shapes.append(pltpu.VMEM((kind[0], part.shape[1] // kind[1], part.shape[2]), part.dtype))
        return shapes + [
            pltpu.SemaphoreType.DMA((SumsFlow.SENDS,)),
            pltpu.SemaphoreType.DMA((SumsFlow.RECVS,)),
            pltpu.SemaphoreType.DMA((SumsFlow.LOCALS,)),
        ]

    def load(self, which, k):
        return pltpu.make_async_copy(
            self.parts[which].at[self.p.column(k)], self.acc[which].at[k], self.local.at[4 * which + k]
        )

    def halves(self, ref):
        half = ref.shape[0] // 2
        return ref.at[pl.ds(0, half)], ref.at[pl.ds(half, half)]

    def corner(self, which, k):
        src = self.halves(self.acc[which].at[3])[k - 1]
        slot = 4 * which + k - 1
        return remote(src, self.half_in[which].at[k - 1], self.send.at[slot], self.recv.at[slot], self.p.at(k))

    def side(self, which, k):
        slot = 4 * which + 1 + k
        return remote(
            self.acc[which].at[k], self.side_in[which].at[k - 1], self.send.at[slot], self.recv.at[slot], self.p.at(k)
        )

    def deal(self, step):
        to = (self.p.col + step) % 8
        src = self.acc[0].at[0, pl.ds(pl.multiple_of(to * self.rows, self.rows), self.rows)]
        return remote(
            src, self.outs[0].at[self.p.col], self.send.at[8 + step], self.recv.at[8 + self.p.col], (self.p.dp, to // 4, to % 4)
        )

    def keep(self):
        src = self.acc[0].at[0, pl.ds(pl.multiple_of(self.p.col * self.rows, self.rows), self.rows)]
        return pltpu.make_async_copy(src, self.outs[0].at[self.p.col], self.local.at[8])

    def swap(self):
        return remote(
            self.acc[1].at[0], self.outs[1], self.send.at[16], self.recv.at[16], (self.p.col // 2, self.p.col % 2, self.p.dp)
        )

    def stay(self):
        return pltpu.make_async_copy(self.acc[1].at[0], self.outs[1], self.local.at[9])

    def at_home(self):
        return (self.p.col // 2 == self.p.dp) & (self.p.col % 2 == self.p.blk) & (self.p.z == self.p.dp)

    def begin(self):
        for which in (1, 0):
            for k in (3, 2, 1, 0):
                self.load(which, k).start()
        for which in (1, 0):
            self.load(which, 3).wait()
            self.corner(which, 1).start()
            self.corner(which, 2).start()

    def sides(self):
        for which in (1, 0):
            for k, other in ((2, 1), (1, 2)):
                self.load(which, k).wait()
                self.corner(which, other).wait_recv()
                target = self.halves(self.acc[which].at[k])[other - 1]
                add_rows(target, [target, self.half_in[which].at[other - 1]], target.shape[0])
                self.side(which, k).start()

    def total(self):
        for which in (1, 0):
            self.load(which, 0).wait()
            self.side(which, 1).wait_recv()
            self.side(which, 2).wait_recv()
            mine = self.acc[which].at[0]
            add_rows(mine, [mine, self.side_in[which].at[0], self.side_in[which].at[1]], mine.shape[0])
            if which == 1:
                home = self.at_home()

                @pl.when(home)
                def _():
                    self.stay().start()

                @pl.when(jnp.logical_not(home))
                def _():
                    self.swap().start()

        @pl.loop(1, 8)
        def _(step):
            self.deal(step).start()

        self.keep().start()

    def finish(self):
        home = self.at_home()

        @pl.when(home)
        def _():
            self.stay().wait()

        @pl.when(jnp.logical_not(home))
        def _():
            self.swap().wait()

        self.keep().wait()

        @pl.loop(1, 8)
        def _(step):
            col = (self.p.col + step) % 8
            landed = self.outs[0].at[col]
            remote(
                landed, landed, self.send.at[0], self.recv.at[8 + col], self.p.at(0, 1 - self.p.blk)
            ).wait_recv()
            self.deal(step).wait_send()

        for which in (1, 0):
            for k in (1, 2):
                self.corner(which, k).wait_send()
                self.side(which, k).wait_send()

    def steps(self):
        idle = lambda: None
        return [self.begin, self.sides, idle, idle, self.total, idle, idle, idle, idle, idle, idle, idle, idle, idle, idle, idle, self.finish]


class DealFlow:
    def __init__(self, place, src, out, send, recv, local):
        self.p, self.src, self.out, self.send, self.recv, self.local = place, src, out, send, recv, local
        self.me = (place.dp * 2 + place.blk) * 4 + place.z

    def copy(self, step):
        to = (self.me + step) % 32
        return remote(
            self.src.at[to], self.out.at[self.me], self.send.at[step], self.recv.at[self.me], (to // 8, (to // 4) % 2, to % 4)
        )

    def keep(self):
        return pltpu.make_async_copy(self.src.at[self.me], self.out.at[self.me], self.local.at[0])

    def begin(self):
        self.keep().start()

        @pl.loop(1, 32)
        def _(step):
            self.copy(step).start()

    def finish(self):
        self.keep().wait()

        @pl.loop(1, 32)
        def _(step):
            landed = self.out.at[(self.me + step) % 32]
            remote(
                landed,
                landed,
                self.send.at[0],
                self.recv.at[(self.me + step) % 32],
                self.p.at(0, 1 - self.p.blk),
            ).wait_recv()
            self.copy(step).wait_send()

    @staticmethod
    def scratch():
        return [pltpu.SemaphoreType.DMA((32,)), pltpu.SemaphoreType.DMA((32,)), pltpu.SemaphoreType.DMA((1,))]

    def steps(self, length=18):
        return [self.begin] + [lambda: None] * (length - 2) + [self.finish]


def hbm_call(kernel, shapes, scratch, name, collective_id, args, aliases=None):
    return pl.pallas_call(
        kernel,
        out_shape=shapes,
        in_specs=[pl.BlockSpec(memory_space=pl.ANY)] * len(args),
        out_specs=[pl.BlockSpec(memory_space=pl.ANY)] * len(shapes),
        scratch_shapes=scratch,
        input_output_aliases=aliases or {},
        compiler_params=pltpu.CompilerParams(
            collective_id=collective_id, has_side_effects=True, vmem_limit_bytes=VMEM_BYTES
        ),
        name=name,
    )(*args)


def gather_sems():
    return [pltpu.SemaphoreType.DMA((GatherFlow.SENDS,)), pltpu.SemaphoreType.DMA((GatherFlow.RECVS,))]


def plane_sems(count):
    return gather_sems() + [pltpu.SemaphoreType.DMA((count,))]


def opening_call(tokens, small, cotangent, query_weight, key_weight, value_weight, output_weight):
    width = tokens.shape[1]
    rows = query_weight.shape[0]

    def kernel(tok, sml, cot, wq, wk, wv, wo, tok_out, sml_out, cot_out, wide, tall, *sems):
        place = Place()
        entry_barrier(place, "all")
        weights = ColumnsFlow(place, (wq, wk, wv), wo, wide, tall, *sems[7:10])
        line = GatherFlow(place, tok, tok_out, sems[0], sems[1], False)
        params = GatherFlow(place, sml, sml_out, sems[2], sems[3], True, True)
        plane = PlaneFlow(place, [(place.z, cot)], cot_out, *sems[4:7])
        params.begin()
        weights.begin()
        for d in range(1, 4):
            params.along(d)
        plane.begin()
        for d in range(4):
            params.turn(d)
        plane.turns()
        weights.settle()
        line.begin()
        for d in range(4):
            params.corner(d)
        plane.corners()
        line.along(1)
        params.finish()
        line.along(2)
        weights.turns()
        line.along(3)
        plane.finish()
        line.finish()
        weights.finish()

    shapes = [
        jax.ShapeDtypeStruct((8,) + tokens.shape, tokens.dtype),
        jax.ShapeDtypeStruct((32,) + small.shape, small.dtype),
        jax.ShapeDtypeStruct((32,) + cotangent.shape, cotangent.dtype),
        jax.ShapeDtypeStruct((32 * rows, 3 * width // 8), tokens.dtype),
        jax.ShapeDtypeStruct((4 * rows, width), tokens.dtype),
    ]
    scratch = gather_sems() * 2 + plane_sems(1)
    scratch += [
        pltpu.SemaphoreType.DMA((ColumnsFlow.SENDS,)),
        pltpu.SemaphoreType.DMA((ColumnsFlow.RECVS,)),
        pltpu.SemaphoreType.DMA((ColumnsFlow.LOCALS,)),
    ]
    return hbm_call(
        kernel,
        shapes,
        scratch,
        "opening",
        1,
        (tokens, small, cotangent, query_weight, key_weight, value_weight, output_weight),
    )


def attended_call(part, others, gathered):
    line = ScatterFlow.scratch(part.shape[1], part.shape[2], part.dtype, False)

    def kernel(part_ref, first, second, third, _, out, gathered_out, *scratch):
        place = Place()
        entry_barrier(place, "planes")
        flow = ScatterFlow(place, part_ref, out, scratch[: len(line)], False)
        blocks = [((place.z + 4 - j) % 4, src) for j, src in ((1, first), (2, second), (3, third))]
        plane = PlaneFlow(place, blocks, gathered_out, *scratch[len(line) :])
        flow.begin()
        plane.begin()
        flow.stage3(0)
        flow.stage3(1)
        flow.chain(0)
        plane.turns()
        flow.stage3(2)
        flow.chain(1)
        flow.chain(2)
        flow.stage3(3)
        flow.final()
        plane.corners()
        plane.finish()

    shapes = [
        jax.ShapeDtypeStruct(part.shape[1:], jnp.float32),
        jax.ShapeDtypeStruct(gathered.shape, gathered.dtype),
    ]
    return hbm_call(
        kernel, shapes, line + plane_sems(3), "attended", 5, (part,) + tuple(others) + (gathered,), {4: 1}
    )


def closing_call(normed_part, wide, tall):
    line = ScatterFlow.scratch(normed_part.shape[1], normed_part.shape[2], normed_part.dtype, False)
    sums = SumsFlow.scratch(wide, tall)
    rows = tall.shape[1]

    def kernel(part, wide_in, tall_in, out, wide_out, tall_out, *scratch):
        place = Place()
        entry_barrier(place, "all")
        weights = SumsFlow(place, wide_in, tall_in, wide_out, tall_out, scratch[len(line) :])
        flow = ScatterFlow(place, part, out, scratch[: len(line)], False)
        weights.begin()
        flow.begin()
        flow.stage3(0)
        flow.stage3(1)
        weights.sides()
        flow.chain(0)
        flow.stage3(2)
        flow.chain(1)
        flow.chain(2)
        flow.stage3(3)
        weights.total()
        flow.final()
        weights.finish()

    shapes = [
        jax.ShapeDtypeStruct(normed_part.shape[1:], jnp.float32),
        jax.ShapeDtypeStruct((8, rows, wide.shape[2]), wide.dtype),
        jax.ShapeDtypeStruct((rows, tall.shape[2]), tall.dtype),
    ]
    return hbm_call(kernel, shapes, line + sums, "closing", 2, (normed_part, wide, tall))


def residual_grad_call(grad, logit_grad, out_part):
    sums = ScatterFlow.scratch(out_part.shape[1], out_part.shape[2], out_part.dtype, True)

    def kernel(grad_ref, logit_ref, part_ref, grad_out, logit_out, out, *scratch):
        place = Place()
        entry_barrier(place, "planes")
        line = GatherFlow(place, grad_ref, grad_out, scratch[0], scratch[1], False)
        logits = GatherFlow(place, logit_ref, logit_out, scratch[2], scratch[3], True)
        flow = ScatterFlow(place, part_ref, out, scratch[4:], True, True)
        line.begin()
        logits.begin()
        flow.begin()
        flow.stage1(0)
        flow.stage1(1)
        line.along(1)
        logits.along(1)
        logits.turn(0)
        flow.stage2(0)
        flow.stage1(2)
        line.along(2)
        logits.along(2)
        logits.turn(1)
        flow.stage1(3)
        flow.stage2(1)
        flow.stage3(0)
        line.along(3)
        logits.along(3)
        logits.turn(2)
        logits.turn(3)
        flow.stage2(2)
        flow.stage3(1)
        for d in range(4):
            logits.corner(d)
        flow.stage2(3)
        flow.stage3(2)
        line.finish()
        logits.finish()
        flow.stage3(3)
        flow.settle_plane()

    shapes = [
        jax.ShapeDtypeStruct((8,) + grad.shape, grad.dtype),
        jax.ShapeDtypeStruct((32,) + logit_grad.shape, logit_grad.dtype),
        jax.ShapeDtypeStruct((4,) + out_part.shape[1:], out_part.dtype),
    ]
    return hbm_call(kernel, shapes, gather_sems() * 2 + sums, "residual_grad", 7, (grad, logit_grad, out_part))


class WeightGrads:
    PARTS = 4

    @staticmethod
    def scratch(rows, hidden):
        slots, part = rows.shape[1], rows.shape[2] // WeightGrads.PARTS
        return [
            pltpu.VMEM((2, 2, slots, part), rows.dtype),
            pltpu.VMEM((2, 3, slots, hidden), rows.dtype),
            pltpu.VMEM((2, 2, part, hidden), jnp.float32),
            pltpu.VMEM((2, hidden, part), jnp.float32),
            pltpu.SemaphoreType.DMA((2, 5)),
            pltpu.SemaphoreType.DMA((2, 3)),
        ]

    def __init__(self, ins, outs, scratch):
        self.ins, self.outs = ins, outs
        self.wide, self.narrow, self.tall, self.flat, self.in_sems, self.out_sems = scratch
        self.part = self.wide.shape[3]
        self.units = ins[0].shape[0] * self.PARTS

    def columns(self, unit):
        return pl.ds(pl.multiple_of((unit % self.PARTS) * self.part, self.part), self.part)

    def loads(self, unit, slot):
        e = unit // self.PARTS
        copies = []
        for i in range(2):
            copies.append((self.ins[i].at[e, :, self.columns(unit)], self.wide.at[slot, i]))
        for i in range(3):
            copies.append((self.ins[2 + i].at[e], self.narrow.at[slot, i]))
        return [pltpu.make_async_copy(s, d, self.in_sems.at[slot, n]) for n, (s, d) in enumerate(copies)]

    def stores(self, unit, slot):
        e, columns = unit // self.PARTS, self.columns(unit)
        copies = [
            (self.tall.at[slot, 0], self.outs[0].at[e, columns]),
            (self.tall.at[slot, 1], self.outs[1].at[e, columns]),
            (self.flat.at[slot], self.outs[2].at[e, :, columns]),
        ]
        return [pltpu.make_async_copy(s, d, self.out_sems.at[slot, n]) for n, (s, d) in enumerate(copies)]

    def begin(self):
        for copy in self.loads(0, 0):
            copy.start()

    def run(self, unit):
        slot = unit % 2

        @pl.when(unit + 1 < self.units)
        def _():
            for copy in self.loads(unit + 1, 1 - slot):
                copy.start()

        for copy in self.loads(unit, slot):
            copy.wait()

        @pl.when(unit >= 2)
        def _():
            for copy in self.stores(unit - 2, slot):
                copy.wait()

        rows, grads = self.wide[slot, 0], self.wide[slot, 1]
        self.tall[slot, 0] = inner(rows, self.narrow[slot, 1], 0, 0)
        self.tall[slot, 1] = inner(rows, self.narrow[slot, 2], 0, 0)
        self.flat[slot] = inner(self.narrow[slot, 0], grads, 0, 0)
        for copy in self.stores(unit, slot):
            copy.start()

    def finish(self):
        for unit in (self.units - 2, self.units - 1):
            for copy in self.stores(unit, unit % 2):
                copy.wait()


def experts_back_call(part, dealt, rows, grads, weighted, gate_back, up_back):
    sums = ScatterFlow.scratch(part.shape[1], part.shape[2], part.dtype, True)
    experts, _, width = rows.shape
    hidden = weighted.shape[2]

    def kernel(part_ref, dealt_ref, *refs):
        ins, (out, dealt_out), outs, scratch = refs[:5], refs[5:7], refs[7:10], refs[10:]
        place = Place()
        entry_barrier(place, "all")
        deal = DealFlow(place, dealt_ref, dealt_out, *scratch[:3])
        flow = ScatterFlow(place, part_ref, out, scratch[3 : 3 + len(sums)], True)
        grads_here = WeightGrads(ins, outs, scratch[3 + len(sums) :])
        deal.begin()
        steps = flow.steps()
        steps[0]()
        grads_here.begin()

        @pl.loop(0, grads_here.units)
        def _(unit):
            for i, step in enumerate(steps[1:-1]):
                pl.when(unit == i)(step)
            grads_here.run(unit)

        steps[-1]()
        grads_here.finish()
        deal.finish()

    shapes = [
        jax.ShapeDtypeStruct(part.shape[1:], jnp.float32),
        jax.ShapeDtypeStruct(dealt.shape, dealt.dtype),
        jax.ShapeDtypeStruct((experts, width, hidden), jnp.float32),
        jax.ShapeDtypeStruct((experts, width, hidden), jnp.float32),
        jax.ShapeDtypeStruct((experts, hidden, width), jnp.float32),
    ]
    scratch = DealFlow.scratch() + sums + WeightGrads.scratch(rows, hidden)
    return hbm_call(
        kernel, shapes, scratch, "experts_back", 3, (part, dealt, rows, grads, weighted, gate_back, up_back)
    )


def column_sum(values, name, collective_id):
    def kernel(src, out, landed, send, recv):
        place = Place()
        entry_barrier(place, "column")

        def copy(step):
            to = (place.col + step) % 8
            return remote(
                src, landed.at[place.col], send.at[step], recv.at[place.col], (place.dp, to // 4, to % 4)
            )

        @pl.loop(1, 8)
        def _(step):
            copy(step).start()

        landed[place.col] = src[...]

        @pl.loop(1, 8)
        def _(step):
            col = (place.col + step) % 8
            remote(src, landed.at[col], send.at[0], recv.at[col], place.at(0, 1 - place.blk)).wait_recv()
            copy(step).wait_send()

        total = landed[0]
        for col in range(1, 8):
            total = total + landed[col]
        out[...] = total

    return pl.pallas_call(
        kernel,
        out_shape=jax.ShapeDtypeStruct(values.shape, values.dtype),
        in_specs=[pl.BlockSpec(memory_space=pltpu.VMEM)],
        out_specs=pl.BlockSpec(memory_space=pltpu.VMEM),
        scratch_shapes=[
            pltpu.VMEM((8,) + values.shape, values.dtype),
            pltpu.SemaphoreType.DMA((8,)),
            pltpu.SemaphoreType.DMA((8,)),
        ],
        compiler_params=pltpu.CompilerParams(collective_id=collective_id, has_side_effects=True),
        name=name,
    )(values)


def deal_sum(values, collective_id):
    def kernel(src, out, landed, send, recv, local):
        place = Place()
        entry_barrier(place, "all")
        flow = DealFlow(place, src, landed, send, recv, local)
        flow.begin()
        flow.finish()
        total = landed[0]
        for index in range(1, 32):
            total = total + landed[index]
        out[...] = total

    return pl.pallas_call(
        kernel,
        out_shape=jax.ShapeDtypeStruct(values.shape[1:], values.dtype),
        in_specs=[pl.BlockSpec(memory_space=pltpu.VMEM)],
        out_specs=pl.BlockSpec(memory_space=pltpu.VMEM),
        scratch_shapes=[pltpu.VMEM(values.shape, values.dtype)] + DealFlow.scratch(),
        compiler_params=pltpu.CompilerParams(collective_id=collective_id, has_side_effects=True),
        name="gain_gradients",
    )(values)


def product(left, right, sums, batches=((), ()), out=jnp.float32):
    return lax.dot_general(left, right, (sums, batches), preferred_element_type=out)


def shift_line(rows, step):
    size = lax.axis_size(SP)
    return lax.ppermute(rows, SP, [(i, (i + step) % size) for i in range(size)])


HEAD_BATCH = ((1,), (1,))
BATCH = ((0,), (0,))


def rotate_heads(values, cosine, sine):
    rows, width = values.shape
    heads = values.reshape(rows, width // HEAD_DIM, HEAD_DIM)
    return rotate(heads, cosine, sine).reshape(rows, width)


def body_fast(
    tokens,
    query_weight,
    key_weight,
    value_weight,
    output_weight,
    router_weight,
    attention_gain,
    query_gain,
    key_gain,
    feature_gain,
    gate_weight,
    up_weight,
    down_weight,
    routes,
    cotangent,
):
    tok_rows, model_width = tokens.shape
    column_size = 8
    devices = 32
    share = model_width // column_size
    heads_here = share // HEAD_DIM
    seq_rows = tok_rows * column_size
    experts_here = gate_weight.shape[0]
    own_rows = query_weight.shape[0]
    score_scale = 1.0 / math.sqrt(HEAD_DIM)
    column = lax.axis_index(BLK) * 4 + lax.axis_index(SP)
    f32, bf16 = jnp.float32, jnp.bfloat16

    gains = jnp.stack([attention_gain, query_gain, key_gain, feature_gain], axis=1)
    named_here = routes.astype(bf16).reshape(own_rows, tok_rows * TOPK // own_rows)
    filled = EXPERTS + 4 + named_here.shape[1]
    small = jnp.concatenate(
        [router_weight, gains, named_here, jnp.zeros((own_rows, 128 - filled), bf16)], axis=1
    )
    tokens_all, small_all, cotangent_all, wide_weight, tall_weight = opening_call(
        tokens, small, cotangent, query_weight, key_weight, value_weight, output_weight
    )
    routes_all = small_all[:, :, EXPERTS + 4 : filled].astype(jnp.int32).reshape(devices, tok_rows, TOPK)
    small_all = small_all.reshape(model_width, 128)
    router_full = small_all[:, :EXPERTS]
    gain_all = small_all[:, EXPERTS : EXPERTS + 4].astype(f32)
    gain_attention, gain_feature = gain_all[:, 0], gain_all[:, 3]
    gain_share = lax.dynamic_slice_in_dim(gain_all, column * share, share, axis=0)
    gain_query, gain_key = gain_share[:, 1], gain_share[:, 2]

    sequence = tokens_all.reshape(seq_rows, model_width).astype(f32)
    normed_all = norm_apply(sequence, gain_attention).astype(bf16)
    linear = jnp.dot(normed_all, wide_weight, preferred_element_type=f32)
    query_lin, key_lin = linear[:, :share], linear[:, share : 2 * share]
    values = linear[:, 2 * share :].astype(bf16)
    squares = jnp.stack([jnp.sum(query_lin * query_lin, axis=1), jnp.sum(key_lin * key_lin, axis=1)])
    squares = column_sum(squares.reshape(16, seq_rows // 8), "square_sums", 4).reshape(2, seq_rows)
    own_cotangent, squares = lax.optimization_barrier((cotangent, squares))
    cotangent_others = [shift_line(own_cotangent, j) for j in (1, 2, 3)]
    scales = lax.rsqrt(squares / model_width + NORM_EPSILON)
    query_r, key_r = scales[0][:, None], scales[1][:, None]
    cosine, sine = rope_tables(jnp.arange(seq_rows, dtype=jnp.int32), HEAD_DIM)
    query_u, key_u = query_lin * query_r, key_lin * key_r
    queries = rotate_heads(query_u * gain_query, cosine, sine).astype(bf16)
    keys = rotate_heads(key_u * gain_key, cosine, sine).astype(bf16)

    def split(rows):
        return rows.reshape(seq_rows, heads_here, HEAD_DIM)

    scores = product(split(queries), split(keys), ((2,), (2,)), HEAD_BATCH)
    places = jnp.arange(seq_rows, dtype=jnp.int32)
    causal = places[None, :] <= places[:, None]
    scores = jnp.where(causal[None], scores * score_scale, MASKED)
    attn_weights = jax.nn.softmax(scores, axis=-1)
    attn_low = attn_weights.astype(bf16)
    context = product(attn_low, split(values), ((2,), (0,)), ((0,), (1,))).transpose(1, 0, 2)
    context = context.astype(bf16).reshape(seq_rows, share)
    attended_part = jnp.dot(context, tall_weight, preferred_element_type=f32).astype(bf16)
    attended, cotangent_all = attended_call(
        attended_part.reshape(column_size, tok_rows, model_width), cotangent_others, cotangent_all
    )

    tokens_f = tokens.astype(f32)
    residual = tokens_f + attended
    features_f, feature_pull = jax.vjp(norm_apply, residual, gain_feature)
    features = features_f.astype(bf16)
    logits = jnp.dot(features, router_full, preferred_element_type=f32)
    router_probs = jax.nn.softmax(logits, axis=-1)
    features_all, probs_all = gather_call(
        [features, router_probs.reshape(tok_rows // 2, 2 * EXPERTS)], [True, True], "features_gather", 6
    )

    first_expert = (lax.axis_index(DP) * 4 + lax.axis_index(SP)) * experts_here
    expert_ids = first_expert + jnp.arange(experts_here, dtype=jnp.int32)
    named = jnp.any(routes_all[:, None] == expert_ids[None, :, None, None], axis=3)
    named_low = named.astype(bf16)
    earlier = (jnp.arange(tok_rows)[:, None] < jnp.arange(tok_rows)[None, :]).astype(bf16)
    rank = product(named_low, earlier, ((2,), (0,))).astype(jnp.int32)
    slot = jnp.arange(CAP, dtype=jnp.int32)
    hot = (named[:, :, None, :] & (rank[:, :, None, :] == slot[None, None, :, None])).astype(bf16)
    pairs = devices // 2
    hot = hot.reshape(pairs, 2, experts_here, CAP, tok_rows)
    zero = jnp.zeros_like(hot[:, 0])
    picks = jnp.concatenate(
        [jnp.concatenate([hot[:, 0], zero], axis=3), jnp.concatenate([zero, hot[:, 1]], axis=3)], axis=2
    )
    pair_rows = 2 * tok_rows
    slots = devices * CAP
    pick_matrix = picks.reshape(pairs, experts_here * 2 * CAP, pair_rows)
    features_all = features_all.reshape(pairs, pair_rows, model_width)
    cotangent_all = cotangent_all.reshape(pairs, pair_rows, model_width)
    expert_rows, grad_rows = pick_rows(pick_matrix, features_all, cotangent_all, experts_here)
    probs_all = probs_all.reshape(pairs, pair_rows, EXPERTS)
    probs_here = lax.dynamic_slice_in_dim(probs_all, first_expert, experts_here, axis=2)
    slot_probs = jnp.sum(picks.astype(f32) * probs_here.transpose(0, 2, 1)[:, :, None, :], axis=3)
    slot_probs = slot_probs.transpose(1, 0, 2).reshape(experts_here, slots)[:, :, None]
    weighted_hidden, gate_grad, up_grad, out_rows, input_rows, slot_grad = run_experts(
        expert_rows, grad_rows, slot_probs, gate_weight, up_weight, down_weight
    )
    token_grad = jnp.sum(
        picks.astype(f32) * slot_grad.reshape(experts_here, pairs, 2 * CAP).transpose(1, 0, 2)[:, :, :, None],
        axis=2,
    )
    token_grad = token_grad.reshape(pairs, experts_here, 2, tok_rows).transpose(0, 2, 1, 3)
    token_grad = token_grad.reshape(devices, experts_here, tok_rows)
    token_grad = jnp.pad(token_grad, ((0, 0), (0, 8 - experts_here), (0, 0)))
    out_part, input_part = put_rows_back(pick_matrix.transpose(0, 2, 1), out_rows, input_rows)
    out_part = out_part.reshape(devices, tok_rows, model_width)
    input_part = input_part.reshape(devices, tok_rows, model_width)
    input_grad, prob_parts, gate_grad_local, up_grad_local, down_grad_local = experts_back_call(
        input_part, token_grad, expert_rows, grad_rows, weighted_hidden, gate_grad, up_grad
    )

    prob_parts = prob_parts.reshape(4, 2, 4, 8, tok_rows)[:, :, :, :experts_here]
    prob_grad = jnp.sum(prob_parts, axis=1).reshape(EXPERTS, tok_rows).T
    logit_grad = (
        router_probs * (prob_grad - jnp.sum(prob_grad * router_probs, axis=-1, keepdims=True))
    ).astype(bf16)
    feature_grad = jnp.dot(logit_grad, router_full.T, preferred_element_type=f32) + input_grad
    residual_part, feature_gain_grad = feature_pull(feature_grad)
    residual_grad = cotangent.astype(f32) + residual_part
    attended_grad = residual_grad.astype(bf16)
    grads_all, logit_all, out_sums = residual_grad_call(
        attended_grad, logit_grad.reshape(tok_rows // 2, 2 * EXPERTS), out_part
    )
    mixture = jnp.zeros((tok_rows, model_width), f32)
    for j in range(4):
        there = (lax.axis_index(SP) + j) % 4
        block = lax.dynamic_index_in_dim(out_sums, there, axis=0, keepdims=False)
        mixture = mixture + (block if j == 0 else shift_line(block, j)).astype(f32)
    block_output = (residual + mixture).astype(bf16)
    own_index = (lax.axis_index(DP) * 2 + lax.axis_index(BLK)) * 4 + lax.axis_index(SP)
    own_features = lax.dynamic_slice_in_dim(
        features_all.reshape(devices * tok_rows, model_width), own_index * own_rows, own_rows, axis=1
    )
    router_grad = product(own_features, logit_all.reshape(devices * tok_rows, EXPERTS), ((0,), (0,)))

    grads_all = grads_all.reshape(seq_rows, model_width)
    tall_grad = product(context, grads_all, ((0,), (0,))).astype(bf16)
    context_grad = product(grads_all, tall_weight, ((1,), (1,))).astype(bf16)
    prob_dots = product(split(context_grad), split(values), ((2,), (2,)), HEAD_BATCH)
    row_delta = jnp.sum(attn_weights * prob_dots, axis=-1, keepdims=True)
    score_grad = (attn_weights * (prob_dots - row_delta)).astype(bf16)
    query_back = product(score_grad, split(keys), ((2,), (0,)), ((0,), (1,))).transpose(1, 0, 2) * score_scale
    key_back = product(score_grad, split(queries), ((1,), (0,)), ((0,), (1,))).transpose(1, 0, 2) * score_scale
    value_low = product(attn_low, split(context_grad), ((1,), (0,)), ((0,), (1,))).transpose(1, 0, 2)
    value_low = value_low.astype(bf16).reshape(seq_rows, share)

    def unrotate(grad):
        grad = grad.astype(bf16).astype(f32).reshape(seq_rows, share)
        return rotate_heads(grad, cosine, -sine)

    query_back, key_back = unrotate(query_back), unrotate(key_back)
    query_gain_grad = jnp.sum(query_back * query_u, axis=0)
    key_gain_grad = jnp.sum(key_back * key_u, axis=0)
    query_w, key_w = query_back * gain_query, key_back * gain_key
    dots = jnp.stack([jnp.sum(query_w * query_u, axis=1), jnp.sum(key_w * key_u, axis=1)])
    dots = column_sum(dots.reshape(16, seq_rows // 8), "dot_sums", 8).reshape(2, seq_rows) / model_width
    query_low = (query_r * (query_w - query_u * dots[0][:, None])).astype(bf16)
    key_low = (key_r * (key_w - key_u * dots[1][:, None])).astype(bf16)
    linear_grad = jnp.concatenate([query_low, key_low, value_low], axis=1)
    wide_grad = product(normed_all, linear_grad, ((0,), (0,))).astype(bf16)
    normed_part = product(linear_grad, wide_weight, ((1,), (1,))).astype(bf16)
    normed_part, mixture = lax.optimization_barrier((normed_part, mixture))
    normed_grad, wide_back, tall_back = closing_call(
        normed_part.reshape(column_size, tok_rows, model_width),
        wide_grad.reshape(4, model_width // 4, 3 * share),
        tall_grad.reshape(4, share // 4, model_width),
    )
    _, attention_pull = jax.vjp(norm_apply, tokens_f, gain_attention)
    tokens_part, attention_gain_grad = attention_pull(normed_grad)
    input_gradient = residual_grad + tokens_part
    wide_back = wide_back.reshape(column_size, own_rows, 3, share).transpose(2, 1, 0, 3)
    wide_back = wide_back.reshape(3, own_rows, model_width).astype(f32)

    def spread(share_grad):
        placed = jnp.zeros((model_width,), f32)
        return lax.dynamic_update_slice(placed, share_grad, (column * share,))

    gain_grads = jnp.stack(
        [attention_gain_grad, spread(query_gain_grad), spread(key_gain_grad), feature_gain_grad]
    )
    gain_grads = gain_grads.reshape(4, devices, own_rows).transpose(1, 0, 2)
    gain_grads = jnp.pad(gain_grads, ((0, 0), (0, 4), (0, 128 - own_rows)))
    gain_sums = deal_sum(gain_grads, 9)
    return (
        block_output,
        input_gradient,
        wide_back[0],
        wide_back[1],
        wide_back[2],
        tall_back.astype(f32),
        router_grad,
        gain_sums[0, :own_rows],
        gain_sums[1, :own_rows],
        gain_sums[2, :own_rows],
        gain_sums[3, :own_rows],
        gate_grad_local,
        up_grad_local,
        down_grad_local,
    )


def body(
    tokens,
    query_weight,
    key_weight,
    value_weight,
    output_weight,
    router_weight,
    attention_gain,
    query_gain,
    key_gain,
    feature_gain,
    gate_weight,
    up_weight,
    down_weight,
    routes,
    cotangent,
):
    sp_size = lax.axis_size(SP)
    blk_size = lax.axis_size(BLK)
    dp_size = lax.axis_size(DP)
    tok_rows = tokens.shape[0]
    model_width = tokens.shape[1]
    heads_here = HEADS // sp_size
    head_width = heads_here * HEAD_DIM
    experts_here = gate_weight.shape[0]
    capacity = CAP
    score_scale = 1.0 / math.sqrt(HEAD_DIM)
    (
        query_full,
        key_full,
        value_full,
        output_full,
        router_full,
        gain_attention,
        gain_query,
        gain_key,
        gain_feature,
    ) = (
        lax.all_gather(query_weight, AXES, axis=0, tiled=True),
        lax.all_gather(key_weight, AXES, axis=0, tiled=True),
        lax.all_gather(value_weight, AXES, axis=0, tiled=True),
        lax.all_gather(output_weight, AXES, axis=0, tiled=True),
        lax.all_gather(router_weight, AXES, axis=0, tiled=True),
        lax.all_gather(attention_gain, AXES, axis=0, tiled=True),
        lax.all_gather(query_gain, AXES, axis=0, tiled=True),
        lax.all_gather(key_gain, AXES, axis=0, tiled=True),
        lax.all_gather(feature_gain, AXES, axis=0, tiled=True),
    )
    gain_attention = gain_attention.astype(jnp.float32)
    gain_query = gain_query.astype(jnp.float32)
    gain_key = gain_key.astype(jnp.float32)
    gain_feature = gain_feature.astype(jnp.float32)
    tokens_f = tokens.astype(jnp.float32)
    normed_f, attention_pull = jax.vjp(norm_apply, tokens_f, gain_attention)
    normed = normed_f.astype(jnp.bfloat16)
    query_lin = jnp.dot(normed, query_full, preferred_element_type=jnp.float32)
    key_lin = jnp.dot(normed, key_full, preferred_element_type=jnp.float32)
    value_rows = jnp.dot(normed, value_full, preferred_element_type=jnp.float32).astype(
        jnp.bfloat16
    )
    seq_start = (lax.axis_index(BLK) * sp_size + lax.axis_index(SP)) * tok_rows
    cosine, sine = rope_tables(seq_start + jnp.arange(tok_rows, dtype=jnp.int32), HEAD_DIM)

    def rotated(linear, norm_gain):
        normalized = norm_apply(linear, norm_gain).reshape(
            tok_rows, model_width // HEAD_DIM, HEAD_DIM
        )
        return rotate(normalized, cosine, sine).reshape(tok_rows, model_width)

    query_rot, query_pull = jax.vjp(rotated, query_lin, gain_query)
    key_rot, key_pull = jax.vjp(rotated, key_lin, gain_key)
    query_heads, key_heads, value_heads = (
        lax.all_to_all(
            query_rot.astype(jnp.bfloat16).reshape(tok_rows, sp_size, head_width),
            SP,
            split_axis=1,
            concat_axis=0,
            tiled=True,
        ),
        lax.all_to_all(
            key_rot.astype(jnp.bfloat16).reshape(tok_rows, sp_size, head_width),
            SP,
            split_axis=1,
            concat_axis=0,
            tiled=True,
        ),
        lax.all_to_all(
            value_rows.reshape(tok_rows, sp_size, head_width),
            SP,
            split_axis=1,
            concat_axis=0,
            tiled=True,
        ),
    )
    head_rows = sp_size * tok_rows
    keys_all, values_all = (
        lax.all_gather(key_heads, BLK, axis=0, tiled=True),
        lax.all_gather(value_heads, BLK, axis=0, tiled=True),
    )
    key_rows = keys_all.shape[0]
    keys_all = keys_all.reshape(key_rows, heads_here, HEAD_DIM)
    values_all = values_all.reshape(key_rows, heads_here, HEAD_DIM)
    block_rows = math.gcd(512, head_rows)
    blocks = head_rows // block_rows
    query_base = lax.axis_index(BLK) * head_rows
    key_places = jnp.arange(key_rows, dtype=jnp.int32)
    query_blocks = query_heads.reshape(blocks, block_rows, heads_here, HEAD_DIM)
    block_starts = jnp.arange(blocks, dtype=jnp.int32) * block_rows

    def masked_scores(block_queries, block_start):
        scores = (
            jnp.einsum("qhd,khd->hqk", block_queries, keys_all, preferred_element_type=jnp.float32)
            * score_scale
        )
        query_places = query_base + block_start + jnp.arange(block_rows, dtype=jnp.int32)
        causal = key_places[None, :] <= query_places[:, None]
        return jnp.where(causal[None], scores, MASKED)

    def attend_block(block_input):
        block_queries, block_start = block_input
        scores = masked_scores(block_queries, block_start)
        row_peak = jnp.max(scores, axis=-1, keepdims=True)
        exponent = jnp.exp(scores - row_peak)
        row_total = jnp.sum(exponent, axis=-1, keepdims=True)
        attn_weights = (exponent / row_total).astype(jnp.bfloat16)
        context = jnp.einsum(
            "hqk,khd->qhd", attn_weights, values_all, preferred_element_type=jnp.float32
        )
        return (context.astype(jnp.bfloat16), (row_peak + jnp.log(row_total))[..., 0])

    context_blocks, logsum = lax.map(attend_block, (query_blocks, block_starts))
    context_rows = lax.all_to_all(
        context_blocks.reshape(head_rows, 1, head_width),
        SP,
        split_axis=0,
        concat_axis=1,
        tiled=True,
    ).reshape(tok_rows, model_width)
    attended = jnp.dot(context_rows, output_full, preferred_element_type=jnp.float32)
    residual = tokens_f + attended
    features_f, feature_pull = jax.vjp(norm_apply, residual, gain_feature)
    features = features_f.astype(jnp.bfloat16)
    logits = jnp.dot(features, router_full, preferred_element_type=jnp.float32)
    router_probs = jax.nn.softmax(logits, axis=-1)
    flat_experts, slot_rank = rank_slots(routes)
    slot_index = flat_experts * capacity + slot_rank
    token_of = jnp.arange(tok_rows * TOPK, dtype=jnp.int32) // TOPK
    slot_token = jnp.zeros((EXPERTS * capacity,), jnp.int32).at[slot_index].set(token_of)
    slot_used = jnp.zeros((EXPERTS * capacity,), jnp.bool_).at[slot_index].set(True)
    slot_rows = jnp.where(slot_used[:, None], features[slot_token], jnp.zeros((), jnp.bfloat16))

    def spread_halves(per_slot):
        grouped = per_slot.reshape(dp_size, 1, sp_size, experts_here, capacity, model_width)
        grouped = jnp.broadcast_to(
            grouped, (dp_size, blk_size, sp_size, experts_here, capacity, model_width)
        )
        return grouped.reshape(dp_size * blk_size * sp_size, experts_here, capacity, model_width)

    def join_halves(returned):
        grouped = returned.reshape(
            dp_size, blk_size, sp_size, experts_here, capacity, model_width
        ).astype(jnp.float32)
        return jnp.sum(grouped, axis=1).reshape(EXPERTS * capacity, model_width)

    send_rows = spread_halves(slot_rows)
    arrived = lax.all_to_all(
        send_rows, AXES, split_axis=0, concat_axis=0, tiled=True
    )
    gate_values = jnp.einsum(
        "secd,edf->secf", arrived, gate_weight, preferred_element_type=jnp.float32
    )
    up_values = jnp.einsum("secd,edf->secf", arrived, up_weight, preferred_element_type=jnp.float32)
    hidden = (jax.nn.silu(gate_values) * up_values).astype(jnp.bfloat16)
    part_out = jnp.einsum(
        "secf,efd->secd", hidden, down_weight, preferred_element_type=jnp.float32
    ).astype(jnp.bfloat16)
    returned = lax.all_to_all(
        part_out, AXES, split_axis=0, concat_axis=0, tiled=True
    )
    expert_out = join_halves(returned)
    route_rows = expert_out[slot_index].reshape(tok_rows, TOPK, model_width)
    route_probs = jnp.take_along_axis(router_probs, routes, axis=1)
    block_output = (residual + jnp.sum(route_probs[:, :, None] * route_rows, axis=1)).astype(
        jnp.bfloat16
    )
    out_grad = cotangent.astype(jnp.float32)
    route_grad = (
        (route_probs[:, :, None] * out_grad[:, None, :])
        .astype(jnp.bfloat16)
        .reshape(tok_rows * TOPK, model_width)
    )
    prob_route = jnp.sum(out_grad[:, None, :] * route_rows, axis=-1)
    expert_ids = jnp.arange(EXPERTS, dtype=jnp.int32)
    prob_grad = jnp.sum(
        jnp.where(routes[:, :, None] == expert_ids[None, None, :], prob_route[:, :, None], 0.0),
        axis=1,
    )
    logit_grad = (
        router_probs * (prob_grad - jnp.sum(prob_grad * router_probs, axis=-1, keepdims=True))
    ).astype(jnp.bfloat16)
    router_grad_full = jnp.dot(features.T, logit_grad, preferred_element_type=jnp.float32)
    gradient_slots = (
        jnp.zeros((EXPERTS * capacity, model_width), jnp.bfloat16).at[slot_index].set(route_grad)
    )
    gradient_send = spread_halves(gradient_slots)
    gradient_arrived, rows_arrived = (
        lax.all_to_all(gradient_send, AXES, split_axis=0, concat_axis=0, tiled=True),
        lax.all_to_all(send_rows, AXES, split_axis=0, concat_axis=0, tiled=True),
    )
    gate_values = jnp.einsum(
        "secd,edf->secf", rows_arrived, gate_weight, preferred_element_type=jnp.float32
    )
    up_values = jnp.einsum(
        "secd,edf->secf", rows_arrived, up_weight, preferred_element_type=jnp.float32
    )
    sigmoid_values = jax.nn.sigmoid(gate_values)
    silu_values = gate_values * sigmoid_values
    hidden = (silu_values * up_values).astype(jnp.bfloat16)
    hidden_grad = jnp.einsum(
        "secd,efd->secf", gradient_arrived, down_weight, preferred_element_type=jnp.float32
    ).astype(jnp.bfloat16)
    down_grad_local = jnp.einsum(
        "secf,secd->efd", hidden, gradient_arrived, preferred_element_type=jnp.float32
    )
    hidden_wide = hidden_grad.astype(jnp.float32)
    gate_grad = (
        hidden_wide * up_values * sigmoid_values * (1.0 + gate_values * (1.0 - sigmoid_values))
    ).astype(jnp.bfloat16)
    up_grad = (hidden_wide * silu_values).astype(jnp.bfloat16)
    gate_grad_local = jnp.einsum(
        "secd,secf->edf", rows_arrived, gate_grad, preferred_element_type=jnp.float32
    )
    up_grad_local = jnp.einsum(
        "secd,secf->edf", rows_arrived, up_grad, preferred_element_type=jnp.float32
    )
    input_parts = (
        jnp.einsum("secf,edf->secd", gate_grad, gate_weight, preferred_element_type=jnp.float32)
        + jnp.einsum("secf,edf->secd", up_grad, up_weight, preferred_element_type=jnp.float32)
    ).astype(jnp.bfloat16)
    returned_grads = lax.all_to_all(
        input_parts, AXES, split_axis=0, concat_axis=0, tiled=True
    )
    slot_input_grad = join_halves(returned_grads)
    expert_input_grad = slot_input_grad[slot_index].reshape(tok_rows, TOPK, model_width)
    feature_grad = jnp.dot(logit_grad, router_full.T, preferred_element_type=jnp.float32) + jnp.sum(
        expert_input_grad, axis=1
    )
    residual_part, feature_gain_grad = feature_pull(feature_grad)
    residual_grad = out_grad + residual_part
    attended_grad = residual_grad.astype(jnp.bfloat16)
    output_grad_full = jnp.dot(context_rows.T, attended_grad, preferred_element_type=jnp.float32)
    context_grad = jnp.dot(attended_grad, output_full.T, preferred_element_type=jnp.float32).astype(
        jnp.bfloat16
    )
    context_heads_grad = lax.all_to_all(
        context_grad.reshape(tok_rows, sp_size, head_width),
        SP,
        split_axis=1,
        concat_axis=0,
        tiled=True,
    )
    context_heads_grad = context_heads_grad.reshape(blocks, block_rows, heads_here, HEAD_DIM)

    def backward_block(carry, block_input):
        key_total, value_total = carry
        block_queries, block_grads, block_logsum, block_start = block_input
        scores = masked_scores(block_queries, block_start)
        attn_weights = jnp.exp(scores - block_logsum[..., None])
        prob_dots = jnp.einsum(
            "qhd,khd->hqk", block_grads, values_all, preferred_element_type=jnp.float32
        )
        row_delta = jnp.sum(attn_weights * prob_dots, axis=-1, keepdims=True)
        score_grad = (attn_weights * (prob_dots - row_delta)).astype(jnp.bfloat16)
        query_grad = (
            jnp.einsum("hqk,khd->qhd", score_grad, keys_all, preferred_element_type=jnp.float32)
            * score_scale
        )
        key_total = (
            key_total
            + jnp.einsum(
                "hqk,qhd->khd", score_grad, block_queries, preferred_element_type=jnp.float32
            )
            * score_scale
        )
        value_total = value_total + jnp.einsum(
            "hqk,qhd->khd",
            attn_weights.astype(jnp.bfloat16),
            block_grads,
            preferred_element_type=jnp.float32,
        )
        return ((key_total, value_total), query_grad.astype(jnp.bfloat16))

    zero_keys = jnp.zeros((key_rows, heads_here, HEAD_DIM), jnp.float32)
    (key_total, value_total), query_grads = lax.scan(
        backward_block,
        (zero_keys, zero_keys),
        (query_blocks, context_heads_grad, logsum, block_starts),
    )
    key_mine, value_mine = (
        lax.psum_scatter(key_total, BLK, scatter_dimension=0, tiled=True),
        lax.psum_scatter(value_total, BLK, scatter_dimension=0, tiled=True),
    )
    query_back, key_back, value_back = (
        lax.all_to_all(
            query_grads.reshape(head_rows, 1, head_width),
            SP,
            split_axis=0,
            concat_axis=1,
            tiled=True,
        ),
        lax.all_to_all(
            key_mine.astype(jnp.bfloat16).reshape(head_rows, 1, head_width),
            SP,
            split_axis=0,
            concat_axis=1,
            tiled=True,
        ),
        lax.all_to_all(
            value_mine.astype(jnp.bfloat16).reshape(head_rows, 1, head_width),
            SP,
            split_axis=0,
            concat_axis=1,
            tiled=True,
        ),
    )
    query_lin_grad, query_gain_grad = query_pull(
        query_back.reshape(tok_rows, model_width).astype(jnp.float32)
    )
    key_lin_grad, key_gain_grad = key_pull(
        key_back.reshape(tok_rows, model_width).astype(jnp.float32)
    )
    query_lin_low = query_lin_grad.astype(jnp.bfloat16)
    key_lin_low = key_lin_grad.astype(jnp.bfloat16)
    value_low = value_back.reshape(tok_rows, model_width)
    query_grad_full = jnp.dot(normed.T, query_lin_low, preferred_element_type=jnp.float32)
    key_grad_full = jnp.dot(normed.T, key_lin_low, preferred_element_type=jnp.float32)
    value_grad_full = jnp.dot(normed.T, value_low, preferred_element_type=jnp.float32)
    normed_grad = jnp.dot(query_lin_low, query_full.T, preferred_element_type=jnp.float32)
    normed_grad = normed_grad + jnp.dot(key_lin_low, key_full.T, preferred_element_type=jnp.float32)
    normed_grad = normed_grad + jnp.dot(value_low, value_full.T, preferred_element_type=jnp.float32)
    tokens_part, attention_gain_grad = attention_pull(normed_grad)
    input_gradient = residual_grad + tokens_part
    summed = (
        lax.psum_scatter(query_grad_full, AXES, scatter_dimension=0, tiled=True),
        lax.psum_scatter(key_grad_full, AXES, scatter_dimension=0, tiled=True),
        lax.psum_scatter(value_grad_full, AXES, scatter_dimension=0, tiled=True),
        lax.psum_scatter(output_grad_full, AXES, scatter_dimension=0, tiled=True),
        lax.psum_scatter(router_grad_full, AXES, scatter_dimension=0, tiled=True),
        lax.psum_scatter(attention_gain_grad, AXES, scatter_dimension=0, tiled=True),
        lax.psum_scatter(query_gain_grad, AXES, scatter_dimension=0, tiled=True),
        lax.psum_scatter(key_gain_grad, AXES, scatter_dimension=0, tiled=True),
        lax.psum_scatter(feature_gain_grad, AXES, scatter_dimension=0, tiled=True),
    )
    return (
        block_output,
        input_gradient,
        summed[0],
        summed[1],
        summed[2],
        summed[3],
        summed[4],
        summed[5],
        summed[6],
        summed[7],
        summed[8],
        gate_grad_local,
        up_grad_local,
        down_grad_local,
    )


def solution(mesh):
    in_specs = (
        P(AXES, None),
        P(AXES, None),
        P(AXES, None),
        P(AXES, None),
        P(AXES, None),
        P(AXES, None),
        P(AXES),
        P(AXES),
        P(AXES),
        P(AXES),
        P((DP, SP), None, BLK),
        P((DP, SP), None, BLK),
        P((DP, SP), BLK, None),
        P(AXES, None),
        P(AXES, None),
    )
    out_specs = (
        P(AXES, None),
        P(AXES, None),
        P(AXES, None),
        P(AXES, None),
        P(AXES, None),
        P(AXES, None),
        P(AXES, None),
        P(AXES),
        P(AXES),
        P(AXES),
        P(AXES),
        P((DP, SP), None, BLK),
        P((DP, SP), None, BLK),
        P((DP, SP), BLK, None),
    )
    fast = dict(mesh.shape) == {DP: 4, BLK: 2, SP: 4}
    return jax.shard_map(body_fast if fast else body, mesh=mesh, in_specs=in_specs, out_specs=out_specs, check_vma=False)
```

```python
import functools
import math

import jax
import jax.numpy as jnp
from jax import lax
from jax.experimental import pallas as pl
from jax.experimental.pallas import tpu as pltpu
from jax.sharding import PartitionSpec as P

DP, BLK, SP = AXES = ("dp", "blk", "sp")

HEADS = 16
HEAD_DIM = 128
EXPERTS = 64
TOPK = 8
CAP = 24


NORM_EPSILON = 1e-05
ROPE_BASE = 10000.0
MASKED = -1e30


def norm_apply(values, norm_gain):
    return (
        values
        * lax.rsqrt(jnp.mean(values * values, axis=-1, keepdims=True) + NORM_EPSILON)
        * norm_gain
    )


def rope_tables(positions, head_size):
    half_size = head_size // 2
    frequencies = jnp.exp(
        -math.log(ROPE_BASE) * 2.0 * jnp.arange(half_size, dtype=jnp.float32) / head_size
    )
    angles = positions.astype(jnp.float32)[:, None] * frequencies[None, :]
    return (jnp.cos(angles), jnp.sin(angles))


def rotate(values, cosine, sine):
    half_size = values.shape[-1] // 2
    first_half = values[..., :half_size]
    second_half = values[..., half_size:]
    cosine_row = cosine[:, None, :]
    sine_row = sine[:, None, :]
    return jnp.concatenate(
        [
            first_half * cosine_row - second_half * sine_row,
            second_half * cosine_row + first_half * sine_row,
        ],
        axis=-1,
    )


def rank_slots(route_rows):
    flat_experts = route_rows.reshape(-1)
    onehot = (flat_experts[:, None] == jnp.arange(EXPERTS, dtype=jnp.int32)[None, :]).astype(
        jnp.int32
    )
    return (flat_experts, jnp.sum(jnp.cumsum(onehot, axis=0) * onehot, axis=1) - 1)


MESH_ID = pl.DeviceIdType.MESH
VMEM_BYTES = 56 * 1024 * 1024


class Place:
    def __init__(self):
        self.dp = lax.axis_index(DP)
        self.blk = lax.axis_index(BLK)
        self.z = lax.axis_index(SP)
        self.x = self.dp % 2
        self.y = self.dp // 2
        self.col = self.blk * 4 + self.z

    def column(self, k):
        if k == 0:
            return self.dp
        if k == 1:
            return self.dp + 1 - 2 * self.x
        if k == 2:
            return self.dp + 2 - 4 * self.y
        return 3 - self.dp

    def at(self, k=0, blk=None, z=None):
        return (self.column(k), self.blk if blk is None else blk, self.z if z is None else z)


def entry_barrier(place, reach):
    barrier = pltpu.get_barrier_semaphore()

    def tell(target):
        pl.semaphore_signal(barrier, inc=1, device_id=target, device_id_type=MESH_ID)

    if reach == "all":
        me = (place.dp * 2 + place.blk) * 4 + place.z

        @pl.loop(1, 32)
        def _(step):
            other = (me + step) % 32
            tell((other // 8, (other // 4) % 2, other % 4))

        pl.semaphore_wait(barrier, 31)
    elif reach == "column":

        @pl.loop(1, 8)
        def _(step):
            other = (place.col + step) % 8
            tell((place.dp, other // 4, other % 4))

        pl.semaphore_wait(barrier, 7)
    else:
        planes = reach == "planes"
        tell(place.at(0, 1 - place.blk))
        if planes:
            tell(place.at(1))
            tell(place.at(2))

        @pl.when(place.z > 0)
        def _():
            tell(place.at(z=place.z - 1))

        @pl.when(place.z < 3)
        def _():
            tell(place.at(z=place.z + 1))

        ends = (3 - place.z) // 3 + place.z // 3
        pl.semaphore_wait(barrier, 3 + (2 if planes else 0) - ends)


def remote(src, dst, send_sem, recv_sem, target):
    return pltpu.make_async_remote_copy(
        src_ref=src,
        dst_ref=dst,
        send_sem=send_sem,
        recv_sem=recv_sem,
        device_id=target,
        device_id_type=MESH_ID,
    )


class GatherFlow:
    SENDS = 40
    RECVS = 37

    def __init__(self, place, src, out, send, recv, full, direct=False, others=False):
        self.p, self.src, self.out, self.send, self.recv, self.full = place, src, out, send, recv, full
        self.direct, self.others = direct, others
        self.half = src.shape[0] // 2

    def slot(self, k, blk, s):
        if self.full:
            return (self.p.column(k) * 2 + blk) * 4 + s
        return blk * 4 + s

    def block(self, k, s, blk=None):
        return self.out.at[self.slot(k, self.p.blk if blk is None else blk, s)]

    def copies(self, k, s, own=False):
        src = self.src if own else self.block(k, s)
        return src, self.block(k, s)

    def up(self, s, own=False):
        src, dst = self.copies(0, s, own)
        return remote(src, dst, self.send.at[s], self.recv.at[s], self.p.at(z=jnp.minimum(self.p.z + 1, 3)))

    def down(self, s, own=False):
        src, dst = self.copies(0, s, own)
        return remote(src, dst, self.send.at[4 + s], self.recv.at[s], self.p.at(z=jnp.maximum(self.p.z - 1, 0)))

    def across_x(self, s, own=False):
        src, dst = self.copies(0, s, own)
        return remote(src, dst, self.send.at[8 + s], self.recv.at[4 + s], self.p.at(1))

    def across_y(self, s, own=False):
        src, dst = self.copies(0, s, own)
        return remote(src, dst, self.send.at[12 + s], self.recv.at[8 + s], self.p.at(2))

    def turn_y(self, s):
        ref = self.block(1, s).at[pl.ds(0, self.half)]
        return remote(ref, ref, self.send.at[16 + s], self.recv.at[12 + s], self.p.at(2))

    def turn_x(self, s):
        ref = self.block(2, s).at[pl.ds(self.half, self.half)]
        return remote(ref, ref, self.send.at[20 + s], self.recv.at[16 + s], self.p.at(1))

    def core(self, k, s, own=False):
        src, dst = self.copies(k, s, own)
        return remote(
            src, dst, self.send.at[24 + 4 * k + s], self.recv.at[20 + 4 * k + s], self.p.at(0, 1 - self.p.blk)
        )

    def got(self, sem, ref):
        remote(ref, ref, self.send.at[0], self.recv.at[sem], self.p.at(0, 1 - self.p.blk)).wait_recv()

    def own_copy(self):
        return pltpu.make_async_copy(self.src, self.block(0, self.p.z), self.recv.at[36])

    def spread(self, s, own=False):
        if self.full:
            self.across_x(s, own).start()
            self.across_y(s, own).start()
        self.core(0, s, own).start()

    def straight(self, step):
        z = self.p.z
        return remote(
            self.src, self.block(0, z), self.send.at[step - 1], self.recv.at[z], self.p.at(z=(z + step) % 4)
        )

    def begin(self):
        z = self.p.z
        if self.direct:
            for step in (1, 2, 3):
                self.straight(step).start()
            self.spread(z, True)
            self.own_copy().start()
            return

        @pl.when(z < 3)
        def _():
            self.up(z, True).start()

        @pl.when(z > 0)
        def _():
            self.down(z, True).start()

        if not self.others:
            self.spread(z, True)
            self.own_copy().start()

    def along(self, d):
        z = self.p.z

        @pl.when(z >= d)
        def _():
            s = z - d
            self.got(s, self.block(0, s))

            if not self.direct:

                @pl.when(z < 3)
                def _():
                    self.up(s).start()

            self.spread(s)

        @pl.when(z + d <= 3)
        def _():
            s = z + d
            self.got(s, self.block(0, s))

            if not self.direct:

                @pl.when(z > 0)
                def _():
                    self.down(s).start()

            self.spread(s)

    def each(self, d, act):
        z = self.p.z
        if d == 0:
            if not self.others:
                act(z)
            return

        @pl.when(z >= d)
        def _():
            act(z - d)

        @pl.when(z + d <= 3)
        def _():
            act(z + d)

    def turn(self, d):
        if not self.full:
            return

        def act(s):
            self.got(4 + s, self.block(1, s))
            self.turn_y(s).start()
            self.core(1, s).start()
            self.got(8 + s, self.block(2, s))
            self.turn_x(s).start()
            self.core(2, s).start()

        self.each(d, act)

    def corner(self, d):
        if not self.full:
            return

        def act(s):
            self.got(12 + s, self.block(3, s).at[pl.ds(0, self.half)])
            self.got(16 + s, self.block(3, s).at[pl.ds(self.half, self.half)])
            self.core(3, s).start()

        self.each(d, act)

    def settle_plane(self, s):
        for k in range(4 if self.full else 1):
            self.got(20 + 4 * k + s, self.block(k, s, 1 - self.p.blk))
            self.core(k, s).wait_send()
        if self.full:
            self.across_x(s).wait_send()
            self.across_y(s).wait_send()
            self.turn_x(s).wait_send()
            self.turn_y(s).wait_send()

    def finish(self):
        z = self.p.z

        @pl.loop(0, 4)
        def _(s):
            pl.when((s != z) | (not self.others))(lambda: self.settle_plane(s))
            if not self.direct:

                @pl.when((s <= z) & (z < 3))
                def _():
                    self.up(s).wait_send()

                @pl.when((s >= z) & (z > 0))
                def _():
                    self.down(s).wait_send()

        if self.direct:
            for step in (1, 2, 3):
                self.straight(step).wait_send()
        if not self.others:
            self.own_copy().wait()

    def steps(self):
        return [
            self.begin,
            lambda: self.along(1),
            lambda: self.turn(0),
            lambda: self.along(2),
            lambda: self.turn(1),
            lambda: self.along(3),
            lambda: self.corner(0),
            lambda: self.turn(2),
            lambda: self.corner(1),
            lambda: self.turn(3),
            lambda: self.corner(2),
            lambda: self.corner(3),
            self.finish,
        ]


class PlaneFlow(GatherFlow):
    def __init__(self, place, blocks, out, send, recv, local):
        super().__init__(place, blocks[0][1], out, send, recv, True)
        self.blocks, self.local = blocks, local

    def begin(self):
        for i, (s, src) in enumerate(self.blocks):
            self.src = src
            self.spread(s, True)
            pltpu.make_async_copy(src, self.block(0, s), self.local.at[i]).start()

    def turns(self):
        for s, _ in self.blocks:
            self.got(4 + s, self.block(1, s))
            self.turn_y(s).start()
            self.core(1, s).start()
            self.got(8 + s, self.block(2, s))
            self.turn_x(s).start()
            self.core(2, s).start()

    def corners(self):
        for s, _ in self.blocks:
            self.got(12 + s, self.block(3, s).at[pl.ds(0, self.half)])
            self.got(16 + s, self.block(3, s).at[pl.ds(self.half, self.half)])
            self.core(3, s).start()

    def finish(self):
        for i, (s, src) in enumerate(self.blocks):
            self.settle_plane(s)
            pltpu.make_async_copy(src, self.block(0, s), self.local.at[i]).wait()


class PlaneFlow(GatherFlow):
    def __init__(self, place, blocks, out, send, recv, local):
        super().__init__(place, blocks[0][1], out, send, recv, True)
        self.blocks, self.local = blocks, local

    def begin(self):
        for i, (s, src) in enumerate(self.blocks):
            self.src = src
            self.spread(s, True)
            pltpu.make_async_copy(src, self.block(0, s), self.local.at[i]).start()

    def turns(self):
        for s, _ in self.blocks:
            self.got(4 + s, self.block(1, s))
            self.turn_y(s).start()
            self.core(1, s).start()
            self.got(8 + s, self.block(2, s))
            self.turn_x(s).start()
            self.core(2, s).start()

    def corners(self):
        for s, _ in self.blocks:
            self.got(12 + s, self.block(3, s).at[pl.ds(0, self.half)])
            self.got(16 + s, self.block(3, s).at[pl.ds(self.half, self.half)])
            self.core(3, s).start()

    def finish(self):
        for i, (s, src) in enumerate(self.blocks):
            self.settle_plane(s)
            pltpu.make_async_copy(src, self.block(0, s), self.local.at[i]).wait()


def run_flows(flows):
    lists = [flow.steps() for flow in flows]
    for position in range(max(len(steps) for steps in lists)):
        for steps in lists:
            if position < len(steps):
                steps[position]()


def add_rows(dst, terms, rows):
    @pl.loop(0, rows // 16)
    def _(i):
        at = pl.ds(pl.multiple_of(i * 16, 16), 16)
        total = terms[0][at, :].astype(jnp.float32)
        for term in terms[1:]:
            total = total + term[at, :].astype(jnp.float32)
        dst[at, :] = total.astype(dst.dtype)


class ScatterFlow:
    SENDS = 16 + 8 + 8 + 4 + 4
    RECVS = 16 + 8 + 8 + 4 + 4
    LOCALS = 20

    def __init__(self, place, part, out, scratch, full, band=None):
        self.p, self.part, self.out, self.full, self.plane_only = place, part, out, full, band is not None
        if full:
            (self.acc, self.near, self.half_in, self.side_in, self.line_in, self.sum, self.send, self.recv, self.local) = scratch
        else:
            (self.acc, self.near, self.line_in, self.sum, self.send, self.recv, self.local) = scratch
        self.columns = 4 if full else 1
        first, self.rows = band or (0, part.shape[1])
        self.band = pl.ds(first, self.rows)
        self.half = self.rows // 2

    @staticmethod
    def scratch(rows, width, dtype, full):
        columns = 4 if full else 1
        shapes = [
            pltpu.VMEM((columns, 4, rows, width), dtype),
            pltpu.VMEM((columns, 4, rows, width), dtype),
        ]
        if full:
            shapes += [pltpu.VMEM((2, 4, rows // 2, width), dtype), pltpu.VMEM((2, 4, rows, width), dtype)]
        return shapes + [
            pltpu.VMEM((2, 4, rows, width), dtype),
            pltpu.VMEM((rows, width), jnp.float32),
            pltpu.SemaphoreType.DMA((ScatterFlow.SENDS,)),
            pltpu.SemaphoreType.DMA((ScatterFlow.RECVS,)),
            pltpu.SemaphoreType.DMA((ScatterFlow.LOCALS,)),
        ]

    def slot(self, k, blk, s):
        if self.full:
            return (self.p.column(k) * 2 + blk) * 4 + s
        return blk * 4 + s

    def order(self, i):
        z = self.p.z
        return [3 * (1 - z // 2), (2 + 3 * z) % 5, 1 + z % 2, z][i]

    def load(self, k, s):
        return pltpu.make_async_copy(
            self.part.at[self.slot(k, self.p.blk, s), self.band], self.acc.at[k, s], self.local.at[4 * k + s]
        )

    def core(self, k, s):
        return remote(
            self.part.at[self.slot(k, 1 - self.p.blk, s), self.band],
            self.near.at[k, s],
            self.send.at[4 * k + s],
            self.recv.at[4 * k + s],
            self.p.at(0, 1 - self.p.blk),
        )

    def half_x(self, s):
        return remote(
            self.acc.at[3, s, pl.ds(0, self.half)],
            self.half_in.at[0, s],
            self.send.at[16 + s],
            self.recv.at[16 + s],
            self.p.at(1),
        )

    def half_y(self, s):
        return remote(
            self.acc.at[3, s, pl.ds(self.half, self.half)],
            self.half_in.at[1, s],
            self.send.at[20 + s],
            self.recv.at[20 + s],
            self.p.at(2),
        )

    def side_x(self, s):
        return remote(
            self.acc.at[1, s], self.side_in.at[0, s], self.send.at[24 + s], self.recv.at[24 + s], self.p.at(1)
        )

    def side_y(self, s):
        return remote(
            self.acc.at[2, s], self.side_in.at[1, s], self.send.at[28 + s], self.recv.at[28 + s], self.p.at(2)
        )

    def line_up(self, s):
        return remote(
            self.acc.at[0, s],
            self.line_in.at[0, s],
            self.send.at[32 + s],
            self.recv.at[32 + s],
            self.p.at(z=jnp.minimum(self.p.z + 1, 3)),
        )

    def line_down(self, s):
        return remote(
            self.acc.at[0, s],
            self.line_in.at[1, s],
            self.send.at[36 + s],
            self.recv.at[36 + s],
            self.p.at(z=jnp.maximum(self.p.z - 1, 0)),
        )

    def begin(self):
        for i in range(4):
            s = self.order(i)
            for k in reversed(range(self.columns)):
                self.core(k, s).start()
                self.load(k, s).start()

    def arrive(self, k, s):
        self.load(k, s).wait()
        self.core(k, s).wait_recv()
        return [self.acc.at[k, s], self.near.at[k, s]]

    def stage1(self, i):
        if not self.full:
            return
        s = self.order(i)
        add_rows(self.acc.at[3, s], self.arrive(3, s), self.rows)
        self.half_x(s).start()
        self.half_y(s).start()

    def stage2(self, i):
        if not self.full:
            return
        s = self.order(i)
        first, second = pl.ds(0, self.half), pl.ds(self.half, self.half)
        terms = self.arrive(2, s)
        late = [term.at[first] for term in terms] + [self.half_in.at[0, s]]
        rest = [term.at[second] for term in terms]
        add_rows(rest[0], rest, self.half)
        self.half_x(s).wait_recv()
        add_rows(late[0], late, self.half)
        self.side_y(s).start()
        terms = self.arrive(1, s)
        late = [term.at[second] for term in terms] + [self.half_in.at[1, s]]
        rest = [term.at[first] for term in terms]
        add_rows(rest[0], rest, self.half)
        self.half_y(s).wait_recv()
        add_rows(late[0], late, self.half)
        self.side_x(s).start()

    def stage3(self, i):
        s = self.order(i)
        z = self.p.z
        terms = self.arrive(0, s)
        if self.full:
            self.side_x(s).wait_recv()
            self.side_y(s).wait_recv()
            terms = terms + [self.side_in.at[0, s], self.side_in.at[1, s]]
        add_rows(self.acc.at[0, s], terms, self.rows)
        if self.plane_only:
            self.keep_plane(i).start()
        elif i < 3:

            @pl.when(z == 0)
            def _():
                self.line_up(s).start()

            @pl.when(z == 3)
            def _():
                self.line_down(s).start()

    def chain(self, i):
        s = self.order(i)
        z = self.p.z

        @pl.when((z > 0) & (z < s) & (z < 3))
        def _():
            self.line_up(s).wait_recv()
            add_rows(self.acc.at[0, s], [self.acc.at[0, s], self.line_in.at[0, s]], self.rows)
            self.line_up(s).start()

        @pl.when((z < 3) & (z > s) & (z > 0))
        def _():
            self.line_down(s).wait_recv()
            add_rows(self.acc.at[0, s], [self.acc.at[0, s], self.line_in.at[1, s]], self.rows)
            self.line_down(s).start()

    def final(self):
        z = self.p.z
        mine, above, below = self.acc.at[0, z], self.line_in.at[0, z], self.line_in.at[1, z]

        @pl.when(z > 0)
        def _():
            self.line_up(z).wait_recv()

        @pl.when(z < 3)
        def _():
            self.line_down(z).wait_recv()

        @pl.when(z == 0)
        def _():
            add_rows(self.sum, [mine, below], self.rows)

        @pl.when(z == 3)
        def _():
            add_rows(self.sum, [mine, above], self.rows)

        @pl.when((z > 0) & (z < 3))
        def _():
            add_rows(self.sum, [mine, above, below], self.rows)

        done = pltpu.make_async_copy(self.sum, self.out, self.local.at[0])
        done.start()

        @pl.loop(0, 4)
        def _(s):
            for k in range(self.columns):
                self.core(k, s).wait_send()
            if self.full:
                self.half_x(s).wait_send()
                self.half_y(s).wait_send()
                self.side_x(s).wait_send()
                self.side_y(s).wait_send()

            @pl.when(s > z)
            def _():
                self.line_up(s).wait_send()

            @pl.when(s < z)
            def _():
                self.line_down(s).wait_send()

        done.wait()

    def keep_plane(self, i):
        s = self.order(i)
        return pltpu.make_async_copy(self.acc.at[0, s], self.out.at[s], self.local.at[16 + i])

    def settle_plane(self):
        for i in range(4):
            s = self.order(i)
            self.keep_plane(i).wait()
            for k in range(4):
                self.core(k, s).wait_send()
            self.half_x(s).wait_send()
            self.half_y(s).wait_send()
            self.side_x(s).wait_send()
            self.side_y(s).wait_send()

    def steps(self):
        plan = [
            (self.stage1, 0),
            (self.stage1, 1),
            (self.stage2, 0),
            (self.stage1, 2),
            (self.stage2, 1),
            (self.stage3, 0),
            (self.stage1, 3),
            (self.stage2, 2),
            (self.stage3, 1),
            (self.chain, 0),
            (self.stage2, 3),
            (self.stage3, 2),
            (self.chain, 1),
            (self.chain, 2),
            (self.stage3, 3),
        ]
        return [self.begin] + [functools.partial(act, i) for act, i in plan] + [self.final]


def local_params():
    return pltpu.CompilerParams(vmem_limit_bytes=VMEM_BYTES)


def inner(left, right, left_dim=1, right_dim=0):
    return lax.dot_general(
        left, right, (((left_dim,), (right_dim,)), ((), ())), preferred_element_type=jnp.float32
    )


def is_place(places, per):
    return lax.broadcasted_iota(jnp.int32, (per, places.shape[1]), 0) == places


def one_hot(places, per):
    experts = places.shape[0]
    hot = [is_place(places[e : e + 1], per).astype(jnp.float32) for e in range(experts)]
    return jnp.concatenate(hot, axis=0).astype(jnp.bfloat16)


def pick_rows(places, probs, features, per):
    pairs, experts, pair_rows = places.shape
    width = features.shape[-1]
    step = 2

    def kernel(place_ref, prob_ref, feature_ref, row_ref, row_prob_ref):
        for i in range(step):
            rows = inner(one_hot(place_ref[i], per), feature_ref[i]).astype(row_ref.dtype)
            for e in range(experts):
                at = pl.ds(i * per, per)
                row_ref[e, at] = rows[e * per : (e + 1) * per]
                hot = is_place(place_ref[i, e : e + 1], per)
                row_prob_ref[e, at] = jnp.sum(
                    jnp.where(hot, prob_ref[i, e : e + 1], 0.0), axis=1, keepdims=True
                )

    small = pl.BlockSpec((step, experts, pair_rows), lambda p: (p, 0, 0))
    return pl.pallas_call(
        kernel,
        out_shape=[
            jax.ShapeDtypeStruct((experts, pairs * per, width), features.dtype),
            jax.ShapeDtypeStruct((experts, pairs * per, 1), jnp.float32),
        ],
        grid=(pairs // step,),
        in_specs=[small, small, pl.BlockSpec((step, pair_rows, width), lambda p: (p, 0, 0))],
        out_specs=[
            pl.BlockSpec((experts, step * per, width), lambda p: (0, p, 0)),
            pl.BlockSpec((experts, step * per, 1), lambda p: (0, p, 0)),
        ],
        compiler_params=local_params(),
        name="pick_rows",
    )(places, probs, features)


def put_rows_back(places, rows, row_grads):
    pairs, experts, pair_rows = places.shape
    _, slots, width = rows.shape
    per = slots // pairs
    step = 2
    half = pair_rows // 2

    def kernel(place_ref, row_ref, grad_ref, sum_ref, prob_ref):
        for i in range(step):
            at = pl.ds(i * per, per)
            gathered = jnp.concatenate([row_ref[e, at] for e in range(experts)], axis=0)
            sum_ref[i] = inner(one_hot(place_ref[i], per), gathered, 0, 0).astype(sum_ref.dtype)
            prob_ref[2 * i : 2 * i + 2] = jnp.zeros((2, 8, half), jnp.float32)
            for e in range(experts):
                hot = is_place(place_ref[i, e : e + 1], per)
                line = jnp.sum(jnp.where(hot, grad_ref[e, at], 0.0), axis=0, keepdims=True)
                prob_ref[2 * i, e : e + 1] = line[:, :half]
                prob_ref[2 * i + 1, e : e + 1] = line[:, half:]

    return pl.pallas_call(
        kernel,
        out_shape=[
            jax.ShapeDtypeStruct((pairs, pair_rows, width), rows.dtype),
            jax.ShapeDtypeStruct((2 * pairs, 8, half), jnp.float32),
        ],
        grid=(pairs // step,),
        in_specs=[
            pl.BlockSpec((step, experts, pair_rows), lambda p: (p, 0, 0)),
            pl.BlockSpec((experts, step * per, width), lambda p: (0, p, 0)),
            pl.BlockSpec((experts, step * per, 1), lambda p: (0, p, 0)),
        ],
        out_specs=[
            pl.BlockSpec((step, pair_rows, width), lambda p: (p, 0, 0)),
            pl.BlockSpec((2 * step, 8, half), lambda p: (p, 0, 0)),
        ],
        compiler_params=local_params(),
        name="put_rows_back",
    )(places, rows, row_grads)


def run_experts(rows, plain_grads, probs, gate_weight, up_weight):
    experts, slots, width = rows.shape
    hidden = gate_weight.shape[2]
    parts = 2
    part = slots // parts

    def kernel(x, plain_ref, p, wg, wu, weighted, gate_back, up_back, back, prob_back):
        gate = inner(x[0], wg[0])
        up = inner(x[0], wu[0])
        plain = plain_ref[0]
        prob = p[0]
        sig = jax.nn.sigmoid(gate)
        act = gate * sig
        hid = act * up
        prob_back[0] = jnp.sum(hid * plain, axis=1, keepdims=True)
        weighted[0] = (hid * prob).astype(jnp.bfloat16)
        grad = plain * prob
        gate_low = (grad * up * sig * (1.0 + gate * (1.0 - sig))).astype(jnp.bfloat16)
        up_low = (grad * act).astype(jnp.bfloat16)
        gate_back[0] = gate_low
        up_back[0] = up_low
        back[0] = (inner(gate_low, wg[0], 1, 1) + inner(up_low, wu[0], 1, 1)).astype(jnp.bfloat16)

    def block(size):
        return pl.BlockSpec((1, part, size), lambda e, i: (e, i, 0))

    weight = pl.BlockSpec((1, width, hidden), lambda e, i: (e, 0, 0))
    narrow = jax.ShapeDtypeStruct((experts, slots, hidden), rows.dtype)
    return pl.pallas_call(
        kernel,
        out_shape=[
            narrow,
            narrow,
            narrow,
            jax.ShapeDtypeStruct(rows.shape, rows.dtype),
            jax.ShapeDtypeStruct((experts, slots, 1), jnp.float32),
        ],
        grid=(experts, parts),
        in_specs=[block(width), block(hidden), block(1), weight, weight],
        out_specs=[block(hidden)] * 3 + [block(width), block(1)],
        compiler_params=local_params(),
        name="run_experts",
    )(rows, plain_grads, probs, gate_weight, up_weight)


class PickWork:
    GROUP = 4

    def __init__(self, places, source, weight, rows_out, plain_out, scratch):
        self.places, self.source, self.weight = places, source, weight
        self.rows_out, self.plain_out = rows_out, plain_out
        self.block, self.rows, self.plain, self.held, self.in_sems, self.out_sems, self.held_sem = scratch
        self.pairs = source.shape[0]
        self.units = self.pairs + self.GROUP
        self.experts = weight.shape[0]
        self.per = self.rows.shape[2] // self.GROUP

    @staticmethod
    def scratch(source, weight, per):
        experts, hidden, width = weight.shape
        group = PickWork.GROUP * per
        return [
            pltpu.VMEM((2,) + source.shape[1:], source.dtype),
            pltpu.VMEM((2, experts, group, width), source.dtype),
            pltpu.VMEM((2, experts, group, hidden), jnp.float32),
            pltpu.VMEM(weight.shape, weight.dtype),
            pltpu.SemaphoreType.DMA((2,)),
            pltpu.SemaphoreType.DMA((2, 2)),
            pltpu.SemaphoreType.DMA((1,)),
        ]

    def load(self, unit, slot):
        return pltpu.make_async_copy(self.source.at[unit], self.block.at[slot], self.in_sems.at[slot])

    def hold(self):
        return pltpu.make_async_copy(self.weight, self.held, self.held_sem.at[0])

    def stores(self, group, slot):
        height = self.GROUP * self.per
        at = pl.ds(pl.multiple_of(group * height, height), height)
        return [
            pltpu.make_async_copy(self.rows.at[slot], self.rows_out.at[:, at], self.out_sems.at[slot, 0]),
            pltpu.make_async_copy(self.plain.at[slot], self.plain_out.at[:, at], self.out_sems.at[slot, 1]),
        ]

    def begin(self):
        self.hold().start()
        self.load(0, 0).start()

    def pick(self, unit):
        slot, group, turn = unit % 2, unit // self.GROUP, unit % self.GROUP
        side = group % 2

        @pl.when(unit + 1 < self.pairs)
        def _():
            self.load(unit + 1, 1 - slot).start()

        @pl.when((turn == 0) & (group >= 2))
        def _():
            for copy in self.stores(group - 2, side):
                copy.wait()

        self.load(unit, slot).wait()
        rows = inner(one_hot(self.places[unit], self.per), self.block[slot]).astype(self.rows.dtype)
        for e in range(self.experts):
            at = pl.ds(pl.multiple_of(turn * self.per, self.per), self.per)
            self.rows[side, e, at] = rows[e * self.per : (e + 1) * self.per]

    def multiply(self, unit):
        group, e = unit // self.GROUP, unit % self.GROUP
        side = group % 2

        @pl.when(unit == 0)
        def _():
            self.hold().wait()

        self.plain[side, e] = inner(self.rows[side, e], self.held[e], 1, 1)

        @pl.when(e == self.GROUP - 1)
        def _():
            for copy in self.stores(group, side):
                copy.start()

    def run(self, unit):
        pl.when(unit < self.pairs)(lambda: self.pick(unit))
        pl.when(unit >= self.GROUP)(lambda: self.multiply(unit - self.GROUP))

    def finish(self):
        groups = self.pairs // self.GROUP
        for group in (groups - 2, groups - 1):
            for copy in self.stores(group, group % 2):
                copy.wait()


class OutputWork:
    def __init__(self, places, hidden, weight, out, scratch):
        self.places, self.hidden, self.weight, self.out = places, hidden, weight, out
        self.rows, self.held, self.narrow, self.block, self.in_sems, self.out_sems = scratch
        self.experts, self.slots, _ = hidden.shape
        self.pairs = out.shape[0]
        self.per = self.slots // self.pairs
        self.width = weight.shape[2]
        self.units = 2 * self.experts + self.pairs

    @staticmethod
    def scratch(hidden, weight, out):
        experts, slots, narrow = hidden.shape
        return [
            pltpu.VMEM((experts, slots, weight.shape[2]), weight.dtype),
            pltpu.VMEM((2,) + weight.shape[1:], weight.dtype),
            pltpu.VMEM((2, slots, narrow), hidden.dtype),
            pltpu.VMEM((2,) + out.shape[1:], out.dtype),
            pltpu.SemaphoreType.DMA((2, 2)),
            pltpu.SemaphoreType.DMA((2,)),
        ]

    def loads(self, e):
        slot = e % 2
        return [
            pltpu.make_async_copy(self.weight.at[e], self.held.at[slot], self.in_sems.at[slot, 0]),
            pltpu.make_async_copy(self.hidden.at[e], self.narrow.at[slot], self.in_sems.at[slot, 1]),
        ]

    def store(self, pair):
        return pltpu.make_async_copy(self.block.at[pair % 2], self.out.at[pair], self.out_sems.at[pair % 2])

    def begin(self):
        for copy in self.loads(0):
            copy.start()

    def run(self, unit):
        half = self.width // 2

        @pl.when(unit < 2 * self.experts)
        def _():
            e, side = unit // 2, unit % 2

            @pl.when(side == 0)
            def _():
                @pl.when(e + 1 < self.experts)
                def _():
                    for copy in self.loads(e + 1):
                        copy.start()

                for copy in self.loads(e):
                    copy.wait()

            at = pl.ds(pl.multiple_of(side * half, half), half)
            self.rows[e, :, at] = inner(self.narrow[e % 2], self.held[e % 2, :, at]).astype(self.rows.dtype)

        @pl.when(unit >= 2 * self.experts)
        def _():
            pair = unit - 2 * self.experts

            @pl.when(pair >= 2)
            def _():
                self.store(pair - 2).wait()

            at = pl.ds(pl.multiple_of(pair * self.per, self.per), self.per)
            rows = jnp.concatenate([self.rows[e, at] for e in range(self.experts)], axis=0)
            self.block[pair % 2] = inner(one_hot(self.places[pair], self.per), rows, 0, 0).astype(self.block.dtype)
            self.store(pair).start()

    def finish(self):
        for pair in (self.pairs - 2, self.pairs - 1):
            self.store(pair).wait()


def expert_weight_grads(rows, grads, weighted, gate_back, up_back):
    experts, slots, width = rows.shape
    hidden = weighted.shape[2]
    parts = 4
    part = width // parts

    def kernel(x, c, low, gate, up, gate_out, up_out, down_out):
        gate_out[0] = inner(x[0], gate[0], 0, 0)
        up_out[0] = inner(x[0], up[0], 0, 0)
        down_out[0] = inner(low[0], c[0], 0, 0)

    source = pl.BlockSpec((1, slots, part), lambda e, i: (e, 0, i))
    whole = pl.BlockSpec((1, slots, hidden), lambda e, i: (e, 0, 0))
    tall = pl.BlockSpec((1, part, hidden), lambda e, i: (e, i, 0))
    flat = pl.BlockSpec((1, hidden, part), lambda e, i: (e, 0, i))
    return pl.pallas_call(
        kernel,
        out_shape=[
            jax.ShapeDtypeStruct((experts, width, hidden), jnp.float32),
            jax.ShapeDtypeStruct((experts, width, hidden), jnp.float32),
            jax.ShapeDtypeStruct((experts, hidden, width), jnp.float32),
        ],
        grid=(experts, parts),
        in_specs=[source, source, whole, whole, whole],
        out_specs=[tall, tall, flat],
        compiler_params=local_params(),
        cost_estimate=pl.CostEstimate(
            flops=6 * experts * slots * width * hidden, bytes_accessed=24 * experts * width * hidden, transcendentals=0
        ),
        name="expert_weight_grads",
    )(rows, grads, weighted, gate_back, up_back)


class ColumnsFlow:
    SENDS = 24 + 1 + 8
    RECVS = 8 + 1 + 8
    LOCALS = 4

    def __init__(self, place, sources, rows_in, wide, tall, send, recv, local):
        self.p, self.sources, self.rows_in, self.wide, self.tall = place, sources, rows_in, wide, tall
        self.send, self.recv, self.local = send, recv, local
        self.rows = rows_in.shape[0]
        self.share = wide.shape[1] // len(sources)

    def wide_rows(self, col):
        return pl.ds(pl.multiple_of((self.p.dp * 8 + col) * self.rows, self.rows), self.rows)

    def piece(self, i, to, start):
        share = self.share
        src = self.sources[i].at[:, pl.ds(pl.multiple_of(to * share, share), share)]
        dst = self.wide.at[self.wide_rows(self.p.col), pl.ds(i * share, share)]
        return src, dst

    def scatter(self, step, i):
        to = (self.p.col + step) % 8
        src, dst = self.piece(i, to, step)
        return remote(
            src, dst, self.send.at[3 * step + i], self.recv.at[self.p.col], (self.p.dp, to // 4, to % 4)
        )

    def keep(self, i):
        src, dst = self.piece(i, self.p.col, 0)
        return pltpu.make_async_copy(src, dst, self.local.at[i])

    def tall_rows(self, k):
        return self.tall.at[pl.ds(pl.multiple_of(self.p.column(k) * self.rows, self.rows), self.rows)]

    def swap(self):
        group = self.p.dp * 2 + self.p.blk
        dst = self.tall.at[pl.ds(pl.multiple_of(self.p.z * self.rows, self.rows), self.rows)]
        return remote(
            self.rows_in, dst, self.send.at[24], self.recv.at[8], (self.p.z, group // 4, group % 4)
        )

    def stay(self):
        return pltpu.make_async_copy(self.rows_in, self.tall_rows(0), self.local.at[3])

    def at_home(self):
        group = self.p.dp * 2 + self.p.blk
        return (self.p.z == self.p.dp) & (group == self.p.col)

    def band(self, which, k):
        if which == 0:
            height = 8 * self.rows
            return self.wide.at[pl.ds(pl.multiple_of(self.p.column(k) * height, height), height)]
        return self.tall_rows(k)

    def across(self, which, k):
        ref = self.band(which, 0)
        slot = 4 * which + k - 1
        return remote(ref, ref, self.send.at[25 + slot], self.recv.at[9 + slot], self.p.at(k))

    def part(self, which, k, first):
        ref = self.band(which, k)
        half = ref.shape[0] // 2
        return ref.at[pl.ds(0 if first else half, half)]

    def turn(self, which, k):
        ref = self.part(which, k, k == 1)
        slot = 4 * which + 1 + k
        return remote(ref, ref, self.send.at[25 + slot], self.recv.at[9 + slot], self.p.at(3 - k))

    def got(self, sem, ref):
        remote(ref, ref, self.send.at[0], self.recv.at[sem], self.p.at(0, 1 - self.p.blk)).wait_recv()

    def begin(self):
        home = self.at_home()

        @pl.when(home)
        def _():
            self.stay().start()

        @pl.when(jnp.logical_not(home))
        def _():
            self.swap().start()

        @pl.loop(1, 8)
        def _(step):
            for i in range(3):
                self.scatter(step, i).start()

        for i in range(3):
            self.keep(i).start()

    def settle(self):
        home = self.at_home()

        @pl.when(home)
        def _():
            self.stay().wait()

        @pl.when(jnp.logical_not(home))
        def _():
            self.got(8, self.tall_rows(0))

        self.across(1, 1).start()
        self.across(1, 2).start()
        for i in range(3):
            self.keep(i).wait()

        @pl.loop(1, 8)
        def _(step):
            col = (self.p.col + step) % 8
            self.got(col, self.wide.at[self.wide_rows(col)])

        self.across(0, 1).start()
        self.across(0, 2).start()

    def turns(self):
        for which in (1, 0):
            for k in (1, 2):
                self.got(9 + 4 * which + k - 1, self.band(which, k))
                self.turn(which, k).start()

    def finish(self):
        for which in (1, 0):
            for k in (1, 2):
                self.got(9 + 4 * which + 1 + k, self.part(which, 3, k == 1))
                self.turn(which, k).wait_send()
                self.across(which, k).wait_send()

        @pl.when(jnp.logical_not(self.at_home()))
        def _():
            self.swap().wait_send()

        @pl.loop(1, 8)
        def _(step):
            for i in range(3):
                self.scatter(step, i).wait_send()


class SumsFlow:
    SENDS = 8 + 24 + 1
    RECVS = 8 + 8 + 1
    LOCALS = 12

    def __init__(self, place, wide, tall, wide_out, tall_out, scratch):
        self.p = place
        self.parts = (wide, tall)
        self.outs = (wide_out, tall_out)
        self.acc, self.half_in, self.side_in = scratch[0:2], scratch[2:4], scratch[4:6]
        self.send, self.recv, self.local = scratch[6:9]
        self.rows = tall_out.shape[0]

    @staticmethod
    def scratch(wide, tall):
        shapes = []
        for kind in ((4, 1), (2, 2), (2, 1)):
            for part in (wide, tall):
                shapes.append(pltpu.VMEM((kind[0], part.shape[1] // kind[1], part.shape[2]), part.dtype))
        return shapes + [
            pltpu.SemaphoreType.DMA((SumsFlow.SENDS,)),
            pltpu.SemaphoreType.DMA((SumsFlow.RECVS,)),
            pltpu.SemaphoreType.DMA((SumsFlow.LOCALS,)),
        ]

    def load(self, which, k):
        return pltpu.make_async_copy(
            self.parts[which].at[self.p.column(k)], self.acc[which].at[k], self.local.at[4 * which + k]
        )

    def halves(self, ref):
        half = ref.shape[0] // 2
        return ref.at[pl.ds(0, half)], ref.at[pl.ds(half, half)]

    def corner(self, which, k):
        src = self.halves(self.acc[which].at[3])[k - 1]
        slot = 4 * which + k - 1
        return remote(src, self.half_in[which].at[k - 1], self.send.at[slot], self.recv.at[slot], self.p.at(k))

    def side(self, which, k):
        slot = 4 * which + 1 + k
        return remote(
            self.acc[which].at[k], self.side_in[which].at[k - 1], self.send.at[slot], self.recv.at[slot], self.p.at(k)
        )

    def deal(self, step, i):
        to = (self.p.col + step) % 8
        src, dst = self.piece(to, i)
        return remote(
            src, dst, self.send.at[8 + 3 * step + i], self.recv.at[8 + self.p.col], (self.p.dp, to // 4, to % 4)
        )

    def piece(self, to, i):
        share = self.outs[0].shape[2] // 8
        rows = pl.ds(pl.multiple_of(to * self.rows, self.rows), self.rows)
        dst = self.outs[0].at[i, :, pl.ds(pl.multiple_of(self.p.col * share, share), share)]
        return self.acc[0].at[0, rows, pl.ds(i * share, share)], dst

    def keep(self, i):
        src, dst = self.piece(self.p.col, i)
        return pltpu.make_async_copy(src, dst, self.local.at[8 + i])

    def swap(self):
        return remote(
            self.acc[1].at[0], self.outs[1], self.send.at[32], self.recv.at[16], (self.p.col // 2, self.p.col % 2, self.p.dp)
        )

    def stay(self):
        return pltpu.make_async_copy(self.acc[1].at[0], self.outs[1], self.local.at[11])

    def at_home(self):
        return (self.p.col // 2 == self.p.dp) & (self.p.col % 2 == self.p.blk) & (self.p.z == self.p.dp)

    def begin(self):
        for which in (1, 0):
            for k in (3, 2, 1, 0):
                self.load(which, k).start()
        for which in (1, 0):
            self.load(which, 3).wait()
            self.corner(which, 1).start()
            self.corner(which, 2).start()

    def sides(self):
        for which in (1, 0):
            for k, other in ((2, 1), (1, 2)):
                self.load(which, k).wait()
                self.corner(which, other).wait_recv()
                target = self.halves(self.acc[which].at[k])[other - 1]
                add_rows(target, [target, self.half_in[which].at[other - 1]], target.shape[0])
                self.side(which, k).start()

    def total(self):
        for which in (1, 0):
            self.load(which, 0).wait()
            self.side(which, 1).wait_recv()
            self.side(which, 2).wait_recv()
            mine = self.acc[which].at[0]
            add_rows(mine, [mine, self.side_in[which].at[0], self.side_in[which].at[1]], mine.shape[0])
            if which == 1:
                home = self.at_home()

                @pl.when(home)
                def _():
                    self.stay().start()

                @pl.when(jnp.logical_not(home))
                def _():
                    self.swap().start()

        @pl.loop(1, 8)
        def _(step):
            for i in range(3):
                self.deal(step, i).start()

        for i in range(3):
            self.keep(i).start()

    def finish(self):
        home = self.at_home()

        @pl.when(home)
        def _():
            self.stay().wait()

        @pl.when(jnp.logical_not(home))
        def _():
            self.swap().wait()

        for i in range(3):
            self.keep(i).wait()

        @pl.loop(1, 8)
        def _(step):
            col = (self.p.col + step) % 8
            landed = self.acc[0].at[0, pl.ds(0, self.rows)]
            remote(
                landed, landed, self.send.at[0], self.recv.at[8 + col], self.p.at(0, 1 - self.p.blk)
            ).wait_recv()
            for i in range(3):
                self.deal(step, i).wait_send()

        for which in (1, 0):
            for k in (1, 2):
                self.corner(which, k).wait_send()
                self.side(which, k).wait_send()

    def steps(self):
        idle = lambda: None
        return [self.begin, self.sides, idle, idle, self.total, idle, idle, idle, idle, idle, idle, idle, idle, idle, idle, idle, self.finish]


class DealFlow:
    def __init__(self, place, src, out, send, recv, local):
        self.p, self.src, self.out, self.send, self.recv, self.local = place, src, out, send, recv, local
        self.me = (place.dp * 2 + place.blk) * 4 + place.z

    def copy(self, step):
        to = (self.me + step) % 32
        return remote(
            self.src.at[to], self.out.at[self.me], self.send.at[step], self.recv.at[self.me], (to // 8, (to // 4) % 2, to % 4)
        )

    def keep(self):
        return pltpu.make_async_copy(self.src.at[self.me], self.out.at[self.me], self.local.at[0])

    def begin(self):
        self.keep().start()

        @pl.loop(1, 32)
        def _(step):
            self.copy(step).start()

    def finish(self):
        self.keep().wait()

        @pl.loop(1, 32)
        def _(step):
            landed = self.out.at[(self.me + step) % 32]
            remote(
                landed,
                landed,
                self.send.at[0],
                self.recv.at[(self.me + step) % 32],
                self.p.at(0, 1 - self.p.blk),
            ).wait_recv()
            self.copy(step).wait_send()

    @staticmethod
    def scratch():
        return [pltpu.SemaphoreType.DMA((32,)), pltpu.SemaphoreType.DMA((32,)), pltpu.SemaphoreType.DMA((1,))]

    def steps(self, length=18):
        return [self.begin] + [lambda: None] * (length - 2) + [self.finish]


def hbm_call(kernel, shapes, scratch, name, collective_id, args, aliases=None, in_vmem=(), out_vmem=()):
    return pl.pallas_call(
        kernel,
        out_shape=shapes,
        in_specs=[
            pl.BlockSpec(memory_space=pltpu.VMEM if i in in_vmem else pl.ANY) for i in range(len(args))
        ],
        out_specs=[
            pl.BlockSpec(memory_space=pltpu.VMEM if i in out_vmem else pl.ANY) for i in range(len(shapes))
        ],
        scratch_shapes=scratch,
        input_output_aliases=aliases or {},
        compiler_params=pltpu.CompilerParams(
            collective_id=collective_id, has_side_effects=True, vmem_limit_bytes=VMEM_BYTES
        ),
        name=name,
    )(*args)


def gather_sems():
    return [pltpu.SemaphoreType.DMA((GatherFlow.SENDS,)), pltpu.SemaphoreType.DMA((GatherFlow.RECVS,))]


def plane_sems(count):
    return gather_sems() + [pltpu.SemaphoreType.DMA((count,))]


def opening_call(tokens, small, cotangent, query_weight, key_weight, value_weight, output_weight):
    width = tokens.shape[1]
    rows = query_weight.shape[0]

    def kernel(tok, sml, cot, wq, wk, wv, wo, tok_out, sml_out, cot_out, wide, tall, *sems):
        place = Place()
        entry_barrier(place, "all")
        weights = ColumnsFlow(place, (wq, wk, wv), wo, wide, tall, *sems[7:10])
        line = GatherFlow(place, tok, tok_out, sems[0], sems[1], False)
        params = GatherFlow(place, sml, sml_out, sems[2], sems[3], True, True)
        plane = PlaneFlow(place, [(place.z, cot)], cot_out, *sems[4:7])
        params.begin()
        weights.begin()
        for d in range(1, 4):
            params.along(d)
        plane.begin()
        for d in range(4):
            params.turn(d)
        plane.turns()
        weights.settle()
        line.begin()
        for d in range(4):
            params.corner(d)
        plane.corners()
        line.along(1)
        params.finish()
        line.along(2)
        weights.turns()
        line.along(3)
        plane.finish()
        line.finish()
        weights.finish()

    shapes = [
        jax.ShapeDtypeStruct((8,) + tokens.shape, tokens.dtype),
        jax.ShapeDtypeStruct((32,) + small.shape, small.dtype),
        jax.ShapeDtypeStruct((32,) + cotangent.shape, cotangent.dtype),
        jax.ShapeDtypeStruct((32 * rows, 3 * width // 8), tokens.dtype),
        jax.ShapeDtypeStruct((4 * rows, width), tokens.dtype),
    ]
    scratch = gather_sems() * 2 + plane_sems(1)
    scratch += [
        pltpu.SemaphoreType.DMA((ColumnsFlow.SENDS,)),
        pltpu.SemaphoreType.DMA((ColumnsFlow.RECVS,)),
        pltpu.SemaphoreType.DMA((ColumnsFlow.LOCALS,)),
    ]
    return hbm_call(
        kernel,
        shapes,
        scratch,
        "opening",
        1,
        (tokens, small, cotangent, query_weight, key_weight, value_weight, output_weight),
    )


def attention_call(tokens_all, gains, wide, tall, head_gains, cosine, sine, cotangent, gathered):
    count, tok_rows, width = tokens_all.shape
    rows = count * tok_rows
    share = tall.shape[0]
    heads = share // HEAD_DIM
    block = 2 * tok_rows
    blocks = rows // block
    scale = 1.0 / math.sqrt(HEAD_DIM)
    bf16, f32 = jnp.bfloat16, jnp.float32
    line = ScatterFlow.scratch(tok_rows, width, bf16, False)

    def kernel(tok, gain, wide_in, tall_in, head_gain, cos, sin, cot, _, *refs):
        outs, scratch = refs[:8], refs[8:]
        normed_out, unit_out, row_out, context_out, scale_out, log_out, attended, gathered_out = outs
        held, wide_ref, tall_ref, normed, unit, qkv, context, part, sums, landed = scratch[:10]
        ins, stores, send, recv = scratch[10:14]
        place = Place()
        entry_barrier(place, "all")
        flow = ScatterFlow(place, part, attended, scratch[14 : 14 + len(line)], False)
        others = GatherFlow(
            place, cot, gathered_out, scratch[-2], scratch[-1], True, others=True
        )

        def block_in(i):
            return pltpu.make_async_copy(tok.at[pl.ds(2 * i, 2)], held.at[i], ins.at[i])

        weights = [
            pltpu.make_async_copy(wide_in, wide_ref, ins.at[blocks]),
            pltpu.make_async_copy(tall_in, tall_ref, ins.at[blocks + 1]),
        ]
        for i in range(blocks):
            block_in(i).start()
        for copy in weights:
            copy.start()
        for copy in weights:
            copy.wait()
        sums[...] = jnp.zeros_like(sums)

        @pl.loop(0, blocks)
        def _(i):
            block_in(i).wait()
            at = pl.ds(pl.multiple_of(i * block, block), block)
            values = held[i].reshape(block, width).astype(f32)
            mean = jnp.mean(values * values, axis=1, keepdims=True)
            low = (values * lax.rsqrt(mean + NORM_EPSILON) * gain[...]).astype(bf16)
            normed[at] = low
            linear = inner(low, wide_ref[...])
            unit[at] = linear[:, : 2 * share]
            qkv[at, 2 * share :] = linear[:, 2 * share :].astype(bf16)
            for n in range(2):
                part_lin = linear[:, n * share : (n + 1) * share]
                sums[n : n + 1, at] = jnp.sum(jnp.transpose(part_lin * part_lin), axis=0, keepdims=True)

        def exchange(step):
            to = (place.col + step) % 8
            return remote(
                sums, landed.at[place.col], send.at[step], recv.at[place.col], (place.dp, to // 4, to % 4)
            )

        @pl.loop(1, 8)
        def _(step):
            exchange(step).start()

        landed[place.col] = sums[...]

        @pl.loop(1, 8)
        def _(step):
            col = (place.col + step) % 8
            remote(sums, landed.at[col], send.at[0], recv.at[col], place.at(0, 1 - place.blk)).wait_recv()
            exchange(step).wait_send()

        others.begin()
        total = landed[0]
        for col in range(1, 8):
            total = total + landed[col]
        scales = jnp.transpose(lax.rsqrt(total / width + NORM_EPSILON))
        scale_out[...] = scales

        @pl.loop(0, blocks)
        def _(i):
            at = pl.ds(pl.multiple_of(i * block, block), block)
            for n in range(2):
                for h in range(heads):
                    lanes = pl.ds(n * share + h * HEAD_DIM, HEAD_DIM)
                    mine = unit[at, lanes] * scale_out[at, n : n + 1]
                    unit[at, lanes] = mine
                    scaled = mine * head_gain[n : n + 1, h * HEAD_DIM : (h + 1) * HEAD_DIM]
                    turned = scaled * cos[at] + pltpu.roll(scaled, HEAD_DIM // 2, 1) * sin[at]
                    qkv[at, lanes] = turned.astype(bf16)

        out_copies = [
            pltpu.make_async_copy(src, dst, stores.at[n])
            for n, (src, dst) in enumerate(((normed, normed_out), (unit, unit_out), (qkv, row_out)))
        ]
        for copy in out_copies:
            copy.start()
        for h in range(heads):
            for i in range(blocks):
                seen = (i + 1) * block
                queries = qkv[i * block : seen, h * HEAD_DIM : (h + 1) * HEAD_DIM]
                keys = qkv[:seen, share + h * HEAD_DIM : share + (h + 1) * HEAD_DIM]
                values = qkv[:seen, 2 * share + h * HEAD_DIM : 2 * share + (h + 1) * HEAD_DIM]
                scores = inner(queries, keys, 1, 1) * scale
                row = lax.broadcasted_iota(jnp.int32, scores.shape, 0) + i * block
                column = lax.broadcasted_iota(jnp.int32, scores.shape, 1)
                scores = jnp.where(column <= row, scores, MASKED)
                peak = jnp.max(scores, axis=1, keepdims=True)
                exponent = jnp.exp(scores - peak)
                sum_row = jnp.sum(exponent, axis=1, keepdims=True)
                low = (exponent / sum_row).astype(bf16)
                context[i * block : seen, h * HEAD_DIM : (h + 1) * HEAD_DIM] = inner(low, values).astype(bf16)
                log_out[i * block : seen, h : h + 1] = peak + jnp.log(sum_row)
            if h == 0:
                others.along(1)

        @pl.loop(0, blocks)
        def _(i):
            at = pl.ds(pl.multiple_of(i * block, block), block)
            rows_here = inner(context[at], tall_ref[...]).astype(bf16)
            part[pl.ds(2 * i, 2)] = rows_here.reshape(2, tok_rows, width)

        last = pltpu.make_async_copy(context, context_out, stores.at[3])
        last.start()
        flow.begin()
        others.along(2)
        flow.stage3(0)
        flow.stage3(1)
        flow.chain(0)
        others.along(3)
        others.turn(1)
        flow.stage3(2)
        flow.chain(1)
        flow.chain(2)
        others.turn(2)
        others.corner(1)
        flow.stage3(3)
        flow.final()
        others.turn(3)
        others.corner(2)
        others.corner(3)
        others.finish()
        for copy in out_copies + [last]:
            copy.wait()

    shapes = [
        jax.ShapeDtypeStruct((rows, width), bf16),
        jax.ShapeDtypeStruct((rows, 2 * share), f32),
        jax.ShapeDtypeStruct((rows, 3 * share), bf16),
        jax.ShapeDtypeStruct((rows, share), bf16),
        jax.ShapeDtypeStruct((rows, 8), f32),
        jax.ShapeDtypeStruct((rows, 8), f32),
        jax.ShapeDtypeStruct((tok_rows, width), f32),
        jax.ShapeDtypeStruct(gathered.shape, gathered.dtype),
    ]
    scratch = [
        pltpu.VMEM((blocks, 2, tok_rows, width), bf16),
        pltpu.VMEM(wide.shape, bf16),
        pltpu.VMEM(tall.shape, bf16),
        pltpu.VMEM((rows, width), bf16),
        pltpu.VMEM((rows, 2 * share), f32),
        pltpu.VMEM((rows, 3 * share), bf16),
        pltpu.VMEM((rows, share), bf16),
        pltpu.VMEM((8, tok_rows, width), bf16),
        pltpu.VMEM((8, rows), f32),
        pltpu.VMEM((8, 8, rows), f32),
        pltpu.SemaphoreType.DMA((blocks + 2,)),
        pltpu.SemaphoreType.DMA((4,)),
        pltpu.SemaphoreType.DMA((8,)),
        pltpu.SemaphoreType.DMA((8,)),
    ]
    args = (tokens_all, gains, wide, tall, head_gains, cosine, sine, cotangent, gathered)
    return hbm_call(
        kernel, shapes, scratch + line + gather_sems(), "attention", 5, args, {8: 7}, (1, 4, 5, 6), (4, 5)
    )


def closing_call(normed_part, wide, tall, out_part):
    height = out_part.shape[1] // 2
    line = ScatterFlow.scratch(normed_part.shape[1], normed_part.shape[2], normed_part.dtype, False)
    half = ScatterFlow.scratch(height, out_part.shape[2], out_part.dtype, True)
    sums = SumsFlow.scratch(wide, tall)
    rows = tall.shape[1]

    def kernel(part, wide_in, tall_in, mixed_in, out, wide_out, tall_out, mixed, *scratch):
        place = Place()
        entry_barrier(place, "all")
        first, second = len(line), len(line) + len(half)
        weights = SumsFlow(place, wide_in, tall_in, wide_out, tall_out, scratch[second:])
        flow = ScatterFlow(place, part, out, scratch[:first], False)
        plane = ScatterFlow(place, mixed_in, mixed, scratch[first:second], True, (height, height))
        weights.begin()
        flow.begin()
        plane.begin()
        flow.stage3(0)
        flow.stage3(1)
        weights.sides()
        plane.stage1(0)
        plane.stage1(1)
        flow.chain(0)
        flow.stage3(2)
        plane.stage1(2)
        plane.stage1(3)
        weights.total()
        flow.chain(1)
        flow.chain(2)
        plane.stage2(0)
        plane.stage2(1)
        flow.stage3(3)
        plane.stage2(2)
        plane.stage2(3)
        flow.final()
        for i in range(4):
            plane.stage3(i)
        weights.finish()
        plane.settle_plane()

    shapes = [
        jax.ShapeDtypeStruct(normed_part.shape[1:], jnp.float32),
        jax.ShapeDtypeStruct((3, rows, 8 * wide.shape[2] // 3), wide.dtype),
        jax.ShapeDtypeStruct((rows, tall.shape[2]), tall.dtype),
        jax.ShapeDtypeStruct((4, height, out_part.shape[2]), out_part.dtype),
    ]
    return hbm_call(kernel, shapes, line + half + sums, "closing", 2, (normed_part, wide, tall, out_part))


def run_beside(steps, work):
    steps[0]()
    work.begin()

    @pl.loop(0, work.units)
    def _(unit):
        for i, step in enumerate(steps[1:-1]):
            pl.when(unit == i)(step)
        work.run(unit)

    steps[-1]()
    work.finish()


def features_call(features, probs, places, cotangent_all, down_weight, per):
    experts, hidden, width = down_weight.shape
    slots = places.shape[0] * per

    def kernel(feature_ref, prob_ref, place_ref, cot, weight, feature_out, prob_out, rows, plain, *scratch):
        place = Place()
        entry_barrier(place, "planes")
        small = GatherFlow(place, prob_ref, prob_out, scratch[2], scratch[3], True)
        flow = GatherFlow(place, feature_ref, feature_out, scratch[0], scratch[1], True)
        work = PickWork(place_ref, cot, weight, rows, plain, scratch[4:])

        def both(i):
            def act():
                small.steps()[i]()
                flow.steps()[i]()

            return act

        run_beside([both(i) for i in range(len(flow.steps()))], work)

    shapes = [
        jax.ShapeDtypeStruct((32,) + features.shape, features.dtype),
        jax.ShapeDtypeStruct((32,) + probs.shape, probs.dtype),
        jax.ShapeDtypeStruct((experts, slots, width), features.dtype),
        jax.ShapeDtypeStruct((experts, slots, hidden), jnp.float32),
    ]
    scratch = gather_sems() * 2 + PickWork.scratch(cotangent_all, down_weight, per)
    return hbm_call(
        kernel, shapes, scratch, "features", 6, (features, probs, places, cotangent_all, down_weight), None, (2,)
    )


def experts_back_call(part, dealt, places, hidden, weight):
    sums = ScatterFlow.scratch(part.shape[1], part.shape[2], part.dtype, True)
    out_shape = jax.ShapeDtypeStruct((places.shape[0], places.shape[2], part.shape[2]), part.dtype)

    def kernel(part_ref, dealt_ref, place_ref, hidden_ref, weight_ref, out, dealt_out, mixed, *scratch):
        place = Place()
        entry_barrier(place, "all")
        deal = DealFlow(place, dealt_ref, dealt_out, *scratch[:3])
        flow = ScatterFlow(place, part_ref, out, scratch[3 : 3 + len(sums)], True)
        work = OutputWork(place_ref, hidden_ref, weight_ref, mixed, scratch[3 + len(sums) :])
        deal.begin()
        run_beside(flow.steps(), work)
        deal.finish()

    shapes = [
        jax.ShapeDtypeStruct(part.shape[1:], jnp.float32),
        jax.ShapeDtypeStruct(dealt.shape, dealt.dtype),
        out_shape,
    ]
    scratch = DealFlow.scratch() + sums + OutputWork.scratch(hidden, weight, out_shape)
    return hbm_call(
        kernel, shapes, scratch, "experts_back", 3, (part, dealt, places, hidden, weight), None, (2,)
    )


def residual_grad_call(grad, logit_grad, out_part):
    height = out_part.shape[1] // 2
    sums = ScatterFlow.scratch(height, out_part.shape[2], out_part.dtype, True)

    def kernel(grad_ref, logit_ref, part_ref, grad_out, logit_out, out, *scratch):
        place = Place()
        entry_barrier(place, "planes")
        line = GatherFlow(place, grad_ref, grad_out, scratch[0], scratch[1], False)
        logits = GatherFlow(place, logit_ref, logit_out, scratch[2], scratch[3], True)
        flow = ScatterFlow(place, part_ref, out, scratch[4:], True, (0, height))
        line.begin()
        logits.begin()
        flow.begin()
        flow.stage1(0)
        flow.stage1(1)
        line.along(1)
        logits.along(1)
        logits.turn(0)
        flow.stage1(2)
        flow.stage1(3)
        flow.stage2(0)
        line.along(2)
        logits.along(2)
        logits.turn(1)
        flow.stage2(1)
        flow.stage2(2)
        line.along(3)
        logits.along(3)
        logits.turn(2)
        logits.turn(3)
        flow.stage3(0)
        flow.stage2(3)
        flow.stage3(1)
        for d in range(4):
            logits.corner(d)
        flow.stage3(2)
        line.finish()
        logits.finish()
        flow.stage3(3)
        flow.settle_plane()

    shapes = [
        jax.ShapeDtypeStruct((8,) + grad.shape, grad.dtype),
        jax.ShapeDtypeStruct((32,) + logit_grad.shape, logit_grad.dtype),
        jax.ShapeDtypeStruct((4, height, out_part.shape[2]), out_part.dtype),
    ]
    return hbm_call(kernel, shapes, gather_sems() * 2 + sums, "residual_grad", 7, (grad, logit_grad, out_part))


def column_sum(values, name, collective_id):
    def kernel(src, out, landed, send, recv):
        place = Place()
        entry_barrier(place, "column")

        def copy(step):
            to = (place.col + step) % 8
            return remote(
                src, landed.at[place.col], send.at[step], recv.at[place.col], (place.dp, to // 4, to % 4)
            )

        @pl.loop(1, 8)
        def _(step):
            copy(step).start()

        landed[place.col] = src[...]

        @pl.loop(1, 8)
        def _(step):
            col = (place.col + step) % 8
            remote(src, landed.at[col], send.at[0], recv.at[col], place.at(0, 1 - place.blk)).wait_recv()
            copy(step).wait_send()

        total = landed[0]
        for col in range(1, 8):
            total = total + landed[col]
        out[...] = total

    return pl.pallas_call(
        kernel,
        out_shape=jax.ShapeDtypeStruct(values.shape, values.dtype),
        in_specs=[pl.BlockSpec(memory_space=pltpu.VMEM)],
        out_specs=pl.BlockSpec(memory_space=pltpu.VMEM),
        scratch_shapes=[
            pltpu.VMEM((8,) + values.shape, values.dtype),
            pltpu.SemaphoreType.DMA((8,)),
            pltpu.SemaphoreType.DMA((8,)),
        ],
        compiler_params=pltpu.CompilerParams(collective_id=collective_id, has_side_effects=True),
        name=name,
    )(values)


def deal_sum(values, collective_id):
    def kernel(src, out, landed, send, recv, local):
        place = Place()
        entry_barrier(place, "all")
        flow = DealFlow(place, src, landed, send, recv, local)
        flow.begin()
        flow.finish()
        total = landed[0]
        for index in range(1, 32):
            total = total + landed[index]
        out[...] = total

    return pl.pallas_call(
        kernel,
        out_shape=jax.ShapeDtypeStruct(values.shape[1:], values.dtype),
        in_specs=[pl.BlockSpec(memory_space=pltpu.VMEM)],
        out_specs=pl.BlockSpec(memory_space=pltpu.VMEM),
        scratch_shapes=[pltpu.VMEM(values.shape, values.dtype)] + DealFlow.scratch(),
        compiler_params=pltpu.CompilerParams(collective_id=collective_id, has_side_effects=True),
        name="gain_gradients",
    )(values)


def product(left, right, sums, batches=((), ()), out=jnp.float32):
    return lax.dot_general(left, right, (sums, batches), preferred_element_type=out)


def shift_line(rows, step):
    size = lax.axis_size(SP)
    return lax.ppermute(rows, SP, [(i, (i + step) % size) for i in range(size)])


HEAD_BATCH = ((1,), (1,))
BATCH = ((0,), (0,))


def rotate_heads(values, cosine, sine):
    rows, width = values.shape
    heads = values.reshape(rows, width // HEAD_DIM, HEAD_DIM)
    return rotate(heads, cosine, sine).reshape(rows, width)


def body_fast(
    tokens,
    query_weight,
    key_weight,
    value_weight,
    output_weight,
    router_weight,
    attention_gain,
    query_gain,
    key_gain,
    feature_gain,
    gate_weight,
    up_weight,
    down_weight,
    routes,
    cotangent,
):
    tok_rows, model_width = tokens.shape
    column_size = 8
    devices = 32
    share = model_width // column_size
    heads_here = share // HEAD_DIM
    seq_rows = tok_rows * column_size
    experts_here = gate_weight.shape[0]
    own_rows = query_weight.shape[0]
    score_scale = 1.0 / math.sqrt(HEAD_DIM)
    column = lax.axis_index(BLK) * 4 + lax.axis_index(SP)
    f32, bf16 = jnp.float32, jnp.bfloat16

    gains = jnp.stack([attention_gain, query_gain, key_gain, feature_gain], axis=1)
    named_here = routes.astype(bf16).reshape(own_rows, tok_rows * TOPK // own_rows)
    filled = EXPERTS + 4 + named_here.shape[1]
    small = jnp.concatenate(
        [router_weight, gains, named_here, jnp.zeros((own_rows, 128 - filled), bf16)], axis=1
    )
    tokens_all, small_all, cotangent_all, wide_weight, tall_weight = opening_call(
        tokens, small, cotangent, query_weight, key_weight, value_weight, output_weight
    )
    routes_all = small_all[:, :, EXPERTS + 4 : filled].astype(jnp.int32).reshape(devices, tok_rows, TOPK)
    small_all = small_all.reshape(model_width, 128)
    router_full = small_all[:, :EXPERTS]
    gain_all = small_all[:, EXPERTS : EXPERTS + 4].astype(f32)
    gain_attention, gain_feature = gain_all[:, 0], gain_all[:, 3]
    gain_share = lax.dynamic_slice_in_dim(gain_all, column * share, share, axis=0)
    gain_query, gain_key = gain_share[:, 1], gain_share[:, 2]

    half_cos, half_sin = rope_tables(jnp.arange(seq_rows, dtype=jnp.int32), HEAD_DIM)
    cosine = jnp.concatenate([half_cos, half_cos], axis=1)
    sine = jnp.concatenate([-half_sin, half_sin], axis=1)
    head_gains = gain_share[:, 1:3].T
    normed_all, unit_rows, head_rows, context, scales, logs, attended, cotangent_all = attention_call(
        tokens_all,
        gain_attention[None],
        wide_weight,
        tall_weight,
        head_gains,
        cosine,
        sine,
        cotangent,
        cotangent_all,
    )
    query_u, key_u = unit_rows[:, :share], unit_rows[:, share:]
    queries, keys, values = head_rows[:, :share], head_rows[:, share : 2 * share], head_rows[:, 2 * share :]
    query_r, key_r = scales[:, :1], scales[:, 1:2]

    def split(rows):
        return rows.reshape(seq_rows, heads_here, HEAD_DIM)

    places_row = jnp.arange(seq_rows, dtype=jnp.int32)
    causal = places_row[None, :] <= places_row[:, None]

    tokens_f = tokens.astype(f32)
    residual = tokens_f + attended
    features_f, feature_pull = jax.vjp(norm_apply, residual, gain_feature)
    features = features_f.astype(bf16)
    logits = jnp.dot(features, router_full, preferred_element_type=f32)
    router_probs = jax.nn.softmax(logits, axis=-1)

    first_expert = (lax.axis_index(DP) * 4 + lax.axis_index(SP)) * experts_here
    expert_ids = first_expert + jnp.arange(experts_here, dtype=jnp.int32)
    named = jnp.any(routes_all[:, None] == expert_ids[None, :, None, None], axis=3)
    earlier = (jnp.arange(tok_rows)[:, None] < jnp.arange(tok_rows)[None, :]).astype(bf16)
    rank = product(named.astype(bf16), earlier, ((2,), (0,))).astype(jnp.int32)
    pairs, pair_rows, per = devices // 2, 2 * tok_rows, 2 * CAP
    places = jnp.where(named, rank, -per).reshape(pairs, 2, experts_here, tok_rows)
    places = places + CAP * jnp.arange(2, dtype=jnp.int32)[None, :, None, None]
    places = places.transpose(0, 2, 1, 3).reshape(pairs, experts_here, pair_rows)
    cotangent_all = cotangent_all.reshape(pairs, pair_rows, model_width)
    features_all, probs_all, grad_rows, plain_grads = features_call(
        features, router_probs.reshape(tok_rows // 2, 2 * EXPERTS), places, cotangent_all, down_weight, per
    )
    probs_all = probs_all.reshape(pairs, pair_rows, EXPERTS)
    probs_here = lax.dynamic_slice_in_dim(probs_all, first_expert, experts_here, axis=2).transpose(0, 2, 1)
    features_all = features_all.reshape(pairs, pair_rows, model_width)
    expert_rows, row_probs = pick_rows(places, probs_here, features_all, per)
    weighted_hidden, gate_grad, up_grad, input_rows, row_grads = run_experts(
        expert_rows, plain_grads, row_probs, gate_weight, up_weight
    )
    input_part, token_grad = put_rows_back(places, input_rows, row_grads)
    input_part = input_part.reshape(devices, tok_rows, model_width)
    input_grad, prob_parts, out_part = experts_back_call(
        input_part, token_grad, places, weighted_hidden, down_weight
    )
    out_part = out_part.reshape(devices, tok_rows, model_width)

    prob_parts = prob_parts.reshape(4, 2, 4, 8, tok_rows)[:, :, :, :experts_here]
    prob_grad = jnp.sum(prob_parts, axis=1).reshape(EXPERTS, tok_rows).T
    logit_grad = (
        router_probs * (prob_grad - jnp.sum(prob_grad * router_probs, axis=-1, keepdims=True))
    ).astype(bf16)
    feature_grad = jnp.dot(logit_grad, router_full.T, preferred_element_type=f32) + input_grad
    residual_part, feature_gain_grad = feature_pull(feature_grad)
    residual_grad = cotangent.astype(f32) + residual_part
    attended_grad = residual_grad.astype(bf16)
    grads_all, logit_all, first_sums = residual_grad_call(
        attended_grad, logit_grad.reshape(tok_rows // 2, 2 * EXPERTS), out_part
    )

    def along_line(sums):
        total = lax.dynamic_index_in_dim(sums, lax.axis_index(SP), axis=0, keepdims=False).astype(f32)
        for j in (1, 2, 3):
            block = lax.dynamic_index_in_dim(sums, (lax.axis_index(SP) + j) % 4, axis=0, keepdims=False)
            total = total + shift_line(block, j).astype(f32)
        return total

    first_half = along_line(first_sums)
    own_index = (lax.axis_index(DP) * 2 + lax.axis_index(BLK)) * 4 + lax.axis_index(SP)
    own_features = lax.dynamic_slice_in_dim(
        features_all.reshape(devices * tok_rows, model_width), own_index * own_rows, own_rows, axis=1
    )
    router_grad = product(own_features, logit_all.reshape(devices * tok_rows, EXPERTS), ((0,), (0,)))

    grads_all = grads_all.reshape(seq_rows, model_width)
    tall_grad = product(context, grads_all, ((0,), (0,))).astype(bf16)
    context_grad = product(grads_all, tall_weight, ((1,), (1,))).astype(bf16)
    scores = product(split(queries), split(keys), ((2,), (2,)), HEAD_BATCH) * score_scale
    attn_weights = jnp.where(causal[None], jnp.exp(scores - logs[:, :heads_here].T[:, :, None]), 0.0)
    attn_low = attn_weights.astype(bf16)
    prob_dots = product(split(context_grad), split(values), ((2,), (2,)), HEAD_BATCH)
    row_delta = jnp.sum(attn_weights * prob_dots, axis=-1, keepdims=True)
    score_grad = (attn_weights * (prob_dots - row_delta)).astype(bf16)
    query_back = product(score_grad, split(keys), ((2,), (0,)), ((0,), (1,))).transpose(1, 0, 2) * score_scale
    key_back = product(score_grad, split(queries), ((1,), (0,)), ((0,), (1,))).transpose(1, 0, 2) * score_scale
    value_low = product(attn_low, split(context_grad), ((1,), (0,)), ((0,), (1,))).transpose(1, 0, 2)
    value_low = value_low.astype(bf16).reshape(seq_rows, share)

    def unrotate(grad):
        grad = grad.astype(bf16).astype(f32).reshape(seq_rows, share)
        return rotate_heads(grad, half_cos, -half_sin)

    query_back, key_back = unrotate(query_back), unrotate(key_back)
    query_gain_grad = jnp.sum(query_back * query_u, axis=0)
    key_gain_grad = jnp.sum(key_back * key_u, axis=0)
    query_w, key_w = query_back * gain_query, key_back * gain_key
    dots = jnp.stack([jnp.sum(query_w * query_u, axis=1), jnp.sum(key_w * key_u, axis=1)])
    dots, first_half = lax.optimization_barrier((dots, first_half))
    dots = column_sum(dots.reshape(16, seq_rows // 8), "dot_sums", 8).reshape(2, seq_rows) / model_width
    query_low = (query_r * (query_w - query_u * dots[0][:, None])).astype(bf16)
    key_low = (key_r * (key_w - key_u * dots[1][:, None])).astype(bf16)
    linear_grad = jnp.concatenate([query_low, key_low, value_low], axis=1)
    wide_grad = product(normed_all, linear_grad, ((0,), (0,))).astype(bf16)
    normed_part = product(linear_grad, wide_weight, ((1,), (1,))).astype(bf16)
    normed_grad, wide_back, tall_back, second_sums = closing_call(
        normed_part.reshape(column_size, tok_rows, model_width),
        wide_grad.reshape(4, model_width // 4, 3 * share),
        tall_grad.reshape(4, share // 4, model_width),
        out_part,
    )
    _, attention_pull = jax.vjp(norm_apply, tokens_f, gain_attention)
    tokens_part, attention_gain_grad = attention_pull(normed_grad)
    input_gradient = residual_grad + tokens_part
    def spread(share_grad):
        placed = jnp.zeros((model_width,), f32)
        return lax.dynamic_update_slice(placed, share_grad, (column * share,))

    gain_grads = jnp.stack(
        [attention_gain_grad, spread(query_gain_grad), spread(key_gain_grad), feature_gain_grad]
    )
    gain_grads = gain_grads.reshape(4, devices, own_rows).transpose(1, 0, 2)
    gain_grads = jnp.pad(gain_grads, ((0, 0), (0, 4), (0, 128 - own_rows)))
    gain_sums = deal_sum(gain_grads, 9)
    second_sums, gain_sums, weighted_hidden = lax.optimization_barrier((second_sums, gain_sums, weighted_hidden))
    mixture = jnp.concatenate([first_half, along_line(second_sums)], axis=0)
    block_output = (residual + mixture).astype(bf16)
    gate_grad_local, up_grad_local, down_grad_local = expert_weight_grads(
        expert_rows, grad_rows, weighted_hidden, gate_grad, up_grad
    )
    return (
        block_output,
        input_gradient,
        wide_back[0].astype(f32),
        wide_back[1].astype(f32),
        wide_back[2].astype(f32),
        tall_back.astype(f32),
        router_grad,
        gain_sums[0, :own_rows],
        gain_sums[1, :own_rows],
        gain_sums[2, :own_rows],
        gain_sums[3, :own_rows],
        gate_grad_local,
        up_grad_local,
        down_grad_local,
    )


def body(
    tokens,
    query_weight,
    key_weight,
    value_weight,
    output_weight,
    router_weight,
    attention_gain,
    query_gain,
    key_gain,
    feature_gain,
    gate_weight,
    up_weight,
    down_weight,
    routes,
    cotangent,
):
    sp_size = lax.axis_size(SP)
    blk_size = lax.axis_size(BLK)
    dp_size = lax.axis_size(DP)
    tok_rows = tokens.shape[0]
    model_width = tokens.shape[1]
    heads_here = HEADS // sp_size
    head_width = heads_here * HEAD_DIM
    experts_here = gate_weight.shape[0]
    capacity = CAP
    score_scale = 1.0 / math.sqrt(HEAD_DIM)
    (
        query_full,
        key_full,
        value_full,
        output_full,
        router_full,
        gain_attention,
        gain_query,
        gain_key,
        gain_feature,
    ) = (
        lax.all_gather(query_weight, AXES, axis=0, tiled=True),
        lax.all_gather(key_weight, AXES, axis=0, tiled=True),
        lax.all_gather(value_weight, AXES, axis=0, tiled=True),
        lax.all_gather(output_weight, AXES, axis=0, tiled=True),
        lax.all_gather(router_weight, AXES, axis=0, tiled=True),
        lax.all_gather(attention_gain, AXES, axis=0, tiled=True),
        lax.all_gather(query_gain, AXES, axis=0, tiled=True),
        lax.all_gather(key_gain, AXES, axis=0, tiled=True),
        lax.all_gather(feature_gain, AXES, axis=0, tiled=True),
    )
    gain_attention = gain_attention.astype(jnp.float32)
    gain_query = gain_query.astype(jnp.float32)
    gain_key = gain_key.astype(jnp.float32)
    gain_feature = gain_feature.astype(jnp.float32)
    tokens_f = tokens.astype(jnp.float32)
    normed_f, attention_pull = jax.vjp(norm_apply, tokens_f, gain_attention)
    normed = normed_f.astype(jnp.bfloat16)
    query_lin = jnp.dot(normed, query_full, preferred_element_type=jnp.float32)
    key_lin = jnp.dot(normed, key_full, preferred_element_type=jnp.float32)
    value_rows = jnp.dot(normed, value_full, preferred_element_type=jnp.float32).astype(
        jnp.bfloat16
    )
    seq_start = (lax.axis_index(BLK) * sp_size + lax.axis_index(SP)) * tok_rows
    cosine, sine = rope_tables(seq_start + jnp.arange(tok_rows, dtype=jnp.int32), HEAD_DIM)

    def rotated(linear, norm_gain):
        normalized = norm_apply(linear, norm_gain).reshape(
            tok_rows, model_width // HEAD_DIM, HEAD_DIM
        )
        return rotate(normalized, cosine, sine).reshape(tok_rows, model_width)

    query_rot, query_pull = jax.vjp(rotated, query_lin, gain_query)
    key_rot, key_pull = jax.vjp(rotated, key_lin, gain_key)
    query_heads, key_heads, value_heads = (
        lax.all_to_all(
            query_rot.astype(jnp.bfloat16).reshape(tok_rows, sp_size, head_width),
            SP,
            split_axis=1,
            concat_axis=0,
            tiled=True,
        ),
        lax.all_to_all(
            key_rot.astype(jnp.bfloat16).reshape(tok_rows, sp_size, head_width),
            SP,
            split_axis=1,
            concat_axis=0,
            tiled=True,
        ),
        lax.all_to_all(
            value_rows.reshape(tok_rows, sp_size, head_width),
            SP,
            split_axis=1,
            concat_axis=0,
            tiled=True,
        ),
    )
    head_rows = sp_size * tok_rows
    keys_all, values_all = (
        lax.all_gather(key_heads, BLK, axis=0, tiled=True),
        lax.all_gather(value_heads, BLK, axis=0, tiled=True),
    )
    key_rows = keys_all.shape[0]
    keys_all = keys_all.reshape(key_rows, heads_here, HEAD_DIM)
    values_all = values_all.reshape(key_rows, heads_here, HEAD_DIM)
    block_rows = math.gcd(512, head_rows)
    blocks = head_rows // block_rows
    query_base = lax.axis_index(BLK) * head_rows
    key_places = jnp.arange(key_rows, dtype=jnp.int32)
    query_blocks = query_heads.reshape(blocks, block_rows, heads_here, HEAD_DIM)
    block_starts = jnp.arange(blocks, dtype=jnp.int32) * block_rows

    def masked_scores(block_queries, block_start):
        scores = (
            jnp.einsum("qhd,khd->hqk", block_queries, keys_all, preferred_element_type=jnp.float32)
            * score_scale
        )
        query_places = query_base + block_start + jnp.arange(block_rows, dtype=jnp.int32)
        causal = key_places[None, :] <= query_places[:, None]
        return jnp.where(causal[None], scores, MASKED)

    def attend_block(block_input):
        block_queries, block_start = block_input
        scores = masked_scores(block_queries, block_start)
        row_peak = jnp.max(scores, axis=-1, keepdims=True)
        exponent = jnp.exp(scores - row_peak)
        row_total = jnp.sum(exponent, axis=-1, keepdims=True)
        attn_weights = (exponent / row_total).astype(jnp.bfloat16)
        context = jnp.einsum(
            "hqk,khd->qhd", attn_weights, values_all, preferred_element_type=jnp.float32
        )
        return (context.astype(jnp.bfloat16), (row_peak + jnp.log(row_total))[..., 0])

    context_blocks, logsum = lax.map(attend_block, (query_blocks, block_starts))
    context_rows = lax.all_to_all(
        context_blocks.reshape(head_rows, 1, head_width),
        SP,
        split_axis=0,
        concat_axis=1,
        tiled=True,
    ).reshape(tok_rows, model_width)
    attended = jnp.dot(context_rows, output_full, preferred_element_type=jnp.float32)
    residual = tokens_f + attended
    features_f, feature_pull = jax.vjp(norm_apply, residual, gain_feature)
    features = features_f.astype(jnp.bfloat16)
    logits = jnp.dot(features, router_full, preferred_element_type=jnp.float32)
    router_probs = jax.nn.softmax(logits, axis=-1)
    flat_experts, slot_rank = rank_slots(routes)
    slot_index = flat_experts * capacity + slot_rank
    token_of = jnp.arange(tok_rows * TOPK, dtype=jnp.int32) // TOPK
    slot_token = jnp.zeros((EXPERTS * capacity,), jnp.int32).at[slot_index].set(token_of)
    slot_used = jnp.zeros((EXPERTS * capacity,), jnp.bool_).at[slot_index].set(True)
    slot_rows = jnp.where(slot_used[:, None], features[slot_token], jnp.zeros((), jnp.bfloat16))

    def spread_halves(per_slot):
        grouped = per_slot.reshape(dp_size, 1, sp_size, experts_here, capacity, model_width)
        grouped = jnp.broadcast_to(
            grouped, (dp_size, blk_size, sp_size, experts_here, capacity, model_width)
        )
        return grouped.reshape(dp_size * blk_size * sp_size, experts_here, capacity, model_width)

    def join_halves(returned):
        grouped = returned.reshape(
            dp_size, blk_size, sp_size, experts_here, capacity, model_width
        ).astype(jnp.float32)
        return jnp.sum(grouped, axis=1).reshape(EXPERTS * capacity, model_width)

    send_rows = spread_halves(slot_rows)
    arrived = lax.all_to_all(
        send_rows, AXES, split_axis=0, concat_axis=0, tiled=True
    )
    gate_values = jnp.einsum(
        "secd,edf->secf", arrived, gate_weight, preferred_element_type=jnp.float32
    )
    up_values = jnp.einsum("secd,edf->secf", arrived, up_weight, preferred_element_type=jnp.float32)
    hidden = (jax.nn.silu(gate_values) * up_values).astype(jnp.bfloat16)
    part_out = jnp.einsum(
        "secf,efd->secd", hidden, down_weight, preferred_element_type=jnp.float32
    ).astype(jnp.bfloat16)
    returned = lax.all_to_all(
        part_out, AXES, split_axis=0, concat_axis=0, tiled=True
    )
    expert_out = join_halves(returned)
    route_rows = expert_out[slot_index].reshape(tok_rows, TOPK, model_width)
    route_probs = jnp.take_along_axis(router_probs, routes, axis=1)
    block_output = (residual + jnp.sum(route_probs[:, :, None] * route_rows, axis=1)).astype(
        jnp.bfloat16
    )
    out_grad = cotangent.astype(jnp.float32)
    route_grad = (
        (route_probs[:, :, None] * out_grad[:, None, :])
        .astype(jnp.bfloat16)
        .reshape(tok_rows * TOPK, model_width)
    )
    prob_route = jnp.sum(out_grad[:, None, :] * route_rows, axis=-1)
    expert_ids = jnp.arange(EXPERTS, dtype=jnp.int32)
    prob_grad = jnp.sum(
        jnp.where(routes[:, :, None] == expert_ids[None, None, :], prob_route[:, :, None], 0.0),
        axis=1,
    )
    logit_grad = (
        router_probs * (prob_grad - jnp.sum(prob_grad * router_probs, axis=-1, keepdims=True))
    ).astype(jnp.bfloat16)
    router_grad_full = jnp.dot(features.T, logit_grad, preferred_element_type=jnp.float32)
    gradient_slots = (
        jnp.zeros((EXPERTS * capacity, model_width), jnp.bfloat16).at[slot_index].set(route_grad)
    )
    gradient_send = spread_halves(gradient_slots)
    gradient_arrived, rows_arrived = (
        lax.all_to_all(gradient_send, AXES, split_axis=0, concat_axis=0, tiled=True),
        lax.all_to_all(send_rows, AXES, split_axis=0, concat_axis=0, tiled=True),
    )
    gate_values = jnp.einsum(
        "secd,edf->secf", rows_arrived, gate_weight, preferred_element_type=jnp.float32
    )
    up_values = jnp.einsum(
        "secd,edf->secf", rows_arrived, up_weight, preferred_element_type=jnp.float32
    )
    sigmoid_values = jax.nn.sigmoid(gate_values)
    silu_values = gate_values * sigmoid_values
    hidden = (silu_values * up_values).astype(jnp.bfloat16)
    hidden_grad = jnp.einsum(
        "secd,efd->secf", gradient_arrived, down_weight, preferred_element_type=jnp.float32
    ).astype(jnp.bfloat16)
    down_grad_local = jnp.einsum(
        "secf,secd->efd", hidden, gradient_arrived, preferred_element_type=jnp.float32
    )
    hidden_wide = hidden_grad.astype(jnp.float32)
    gate_grad = (
        hidden_wide * up_values * sigmoid_values * (1.0 + gate_values * (1.0 - sigmoid_values))
    ).astype(jnp.bfloat16)
    up_grad = (hidden_wide * silu_values).astype(jnp.bfloat16)
    gate_grad_local = jnp.einsum(
        "secd,secf->edf", rows_arrived, gate_grad, preferred_element_type=jnp.float32
    )
    up_grad_local = jnp.einsum(
        "secd,secf->edf", rows_arrived, up_grad, preferred_element_type=jnp.float32
    )
    input_parts = (
        jnp.einsum("secf,edf->secd", gate_grad, gate_weight, preferred_element_type=jnp.float32)
        + jnp.einsum("secf,edf->secd", up_grad, up_weight, preferred_element_type=jnp.float32)
    ).astype(jnp.bfloat16)
    returned_grads = lax.all_to_all(
        input_parts, AXES, split_axis=0, concat_axis=0, tiled=True
    )
    slot_input_grad = join_halves(returned_grads)
    expert_input_grad = slot_input_grad[slot_index].reshape(tok_rows, TOPK, model_width)
    feature_grad = jnp.dot(logit_grad, router_full.T, preferred_element_type=jnp.float32) + jnp.sum(
        expert_input_grad, axis=1
    )
    residual_part, feature_gain_grad = feature_pull(feature_grad)
    residual_grad = out_grad + residual_part
    attended_grad = residual_grad.astype(jnp.bfloat16)
    output_grad_full = jnp.dot(context_rows.T, attended_grad, preferred_element_type=jnp.float32)
    context_grad = jnp.dot(attended_grad, output_full.T, preferred_element_type=jnp.float32).astype(
        jnp.bfloat16
    )
    context_heads_grad = lax.all_to_all(
        context_grad.reshape(tok_rows, sp_size, head_width),
        SP,
        split_axis=1,
        concat_axis=0,
        tiled=True,
    )
    context_heads_grad = context_heads_grad.reshape(blocks, block_rows, heads_here, HEAD_DIM)

    def backward_block(carry, block_input):
        key_total, value_total = carry
        block_queries, block_grads, block_logsum, block_start = block_input
        scores = masked_scores(block_queries, block_start)
        attn_weights = jnp.exp(scores - block_logsum[..., None])
        prob_dots = jnp.einsum(
            "qhd,khd->hqk", block_grads, values_all, preferred_element_type=jnp.float32
        )
        row_delta = jnp.sum(attn_weights * prob_dots, axis=-1, keepdims=True)
        score_grad = (attn_weights * (prob_dots - row_delta)).astype(jnp.bfloat16)
        query_grad = (
            jnp.einsum("hqk,khd->qhd", score_grad, keys_all, preferred_element_type=jnp.float32)
            * score_scale
        )
        key_total = (
            key_total
            + jnp.einsum(
                "hqk,qhd->khd", score_grad, block_queries, preferred_element_type=jnp.float32
            )
            * score_scale
        )
        value_total = value_total + jnp.einsum(
            "hqk,qhd->khd",
            attn_weights.astype(jnp.bfloat16),
            block_grads,
            preferred_element_type=jnp.float32,
        )
        return ((key_total, value_total), query_grad.astype(jnp.bfloat16))

    zero_keys = jnp.zeros((key_rows, heads_here, HEAD_DIM), jnp.float32)
    (key_total, value_total), query_grads = lax.scan(
        backward_block,
        (zero_keys, zero_keys),
        (query_blocks, context_heads_grad, logsum, block_starts),
    )
    key_mine, value_mine = (
        lax.psum_scatter(key_total, BLK, scatter_dimension=0, tiled=True),
        lax.psum_scatter(value_total, BLK, scatter_dimension=0, tiled=True),
    )
    query_back, key_back, value_back = (
        lax.all_to_all(
            query_grads.reshape(head_rows, 1, head_width),
            SP,
            split_axis=0,
            concat_axis=1,
            tiled=True,
        ),
        lax.all_to_all(
            key_mine.astype(jnp.bfloat16).reshape(head_rows, 1, head_width),
            SP,
            split_axis=0,
            concat_axis=1,
            tiled=True,
        ),
        lax.all_to_all(
            value_mine.astype(jnp.bfloat16).reshape(head_rows, 1, head_width),
            SP,
            split_axis=0,
            concat_axis=1,
            tiled=True,
        ),
    )
    query_lin_grad, query_gain_grad = query_pull(
        query_back.reshape(tok_rows, model_width).astype(jnp.float32)
    )
    key_lin_grad, key_gain_grad = key_pull(
        key_back.reshape(tok_rows, model_width).astype(jnp.float32)
    )
    query_lin_low = query_lin_grad.astype(jnp.bfloat16)
    key_lin_low = key_lin_grad.astype(jnp.bfloat16)
    value_low = value_back.reshape(tok_rows, model_width)
    query_grad_full = jnp.dot(normed.T, query_lin_low, preferred_element_type=jnp.float32)
    key_grad_full = jnp.dot(normed.T, key_lin_low, preferred_element_type=jnp.float32)
    value_grad_full = jnp.dot(normed.T, value_low, preferred_element_type=jnp.float32)
    normed_grad = jnp.dot(query_lin_low, query_full.T, preferred_element_type=jnp.float32)
    normed_grad = normed_grad + jnp.dot(key_lin_low, key_full.T, preferred_element_type=jnp.float32)
    normed_grad = normed_grad + jnp.dot(value_low, value_full.T, preferred_element_type=jnp.float32)
    tokens_part, attention_gain_grad = attention_pull(normed_grad)
    input_gradient = residual_grad + tokens_part
    summed = (
        lax.psum_scatter(query_grad_full, AXES, scatter_dimension=0, tiled=True),
        lax.psum_scatter(key_grad_full, AXES, scatter_dimension=0, tiled=True),
        lax.psum_scatter(value_grad_full, AXES, scatter_dimension=0, tiled=True),
        lax.psum_scatter(output_grad_full, AXES, scatter_dimension=0, tiled=True),
        lax.psum_scatter(router_grad_full, AXES, scatter_dimension=0, tiled=True),
        lax.psum_scatter(attention_gain_grad, AXES, scatter_dimension=0, tiled=True),
        lax.psum_scatter(query_gain_grad, AXES, scatter_dimension=0, tiled=True),
        lax.psum_scatter(key_gain_grad, AXES, scatter_dimension=0, tiled=True),
        lax.psum_scatter(feature_gain_grad, AXES, scatter_dimension=0, tiled=True),
    )
    return (
        block_output,
        input_gradient,
        summed[0],
        summed[1],
        summed[2],
        summed[3],
        summed[4],
        summed[5],
        summed[6],
        summed[7],
        summed[8],
        gate_grad_local,
        up_grad_local,
        down_grad_local,
    )


def solution(mesh):
    in_specs = (
        P(AXES, None),
        P(AXES, None),
        P(AXES, None),
        P(AXES, None),
        P(AXES, None),
        P(AXES, None),
        P(AXES),
        P(AXES),
        P(AXES),
        P(AXES),
        P((DP, SP), None, BLK),
        P((DP, SP), None, BLK),
        P((DP, SP), BLK, None),
        P(AXES, None),
        P(AXES, None),
    )
    out_specs = (
        P(AXES, None),
        P(AXES, None),
        P(AXES, None),
        P(AXES, None),
        P(AXES, None),
        P(AXES, None),
        P(AXES, None),
        P(AXES),
        P(AXES),
        P(AXES),
        P(AXES),
        P((DP, SP), None, BLK),
        P((DP, SP), None, BLK),
        P((DP, SP), BLK, None),
    )
    fast = dict(mesh.shape) == {DP: 4, BLK: 2, SP: 4}
    return jax.shard_map(body_fast if fast else body, mesh=mesh, in_specs=in_specs, out_specs=out_specs, check_vma=False)
```

```python
import functools
import math

import jax
import jax.numpy as jnp
from jax import lax
from jax.experimental import pallas as pl
from jax.experimental.pallas import tpu as pltpu
from jax.sharding import PartitionSpec as P

DP, BLK, SP = AXES = ("dp", "blk", "sp")

HEADS = 16
HEAD_DIM = 128
EXPERTS = 64
TOPK = 8
CAP = 24


NORM_EPSILON = 1e-05
ROPE_BASE = 10000.0
MASKED = -1e30


def norm_apply(values, norm_gain):
    return (
        values
        * lax.rsqrt(jnp.mean(values * values, axis=-1, keepdims=True) + NORM_EPSILON)
        * norm_gain
    )


def rope_tables(positions, head_size):
    half_size = head_size // 2
    frequencies = jnp.exp(
        -math.log(ROPE_BASE) * 2.0 * jnp.arange(half_size, dtype=jnp.float32) / head_size
    )
    angles = positions.astype(jnp.float32)[:, None] * frequencies[None, :]
    return (jnp.cos(angles), jnp.sin(angles))


def rotate(values, cosine, sine):
    half_size = values.shape[-1] // 2
    first_half = values[..., :half_size]
    second_half = values[..., half_size:]
    cosine_row = cosine[:, None, :]
    sine_row = sine[:, None, :]
    return jnp.concatenate(
        [
            first_half * cosine_row - second_half * sine_row,
            second_half * cosine_row + first_half * sine_row,
        ],
        axis=-1,
    )


def rank_slots(route_rows):
    flat_experts = route_rows.reshape(-1)
    onehot = (flat_experts[:, None] == jnp.arange(EXPERTS, dtype=jnp.int32)[None, :]).astype(
        jnp.int32
    )
    return (flat_experts, jnp.sum(jnp.cumsum(onehot, axis=0) * onehot, axis=1) - 1)


MESH_ID = pl.DeviceIdType.MESH
VMEM_BYTES = 60 * 1024 * 1024


class Place:
    def __init__(self):
        self.dp = lax.axis_index(DP)
        self.blk = lax.axis_index(BLK)
        self.z = lax.axis_index(SP)
        self.x = self.dp % 2
        self.y = self.dp // 2
        self.col = self.blk * 4 + self.z

    def column(self, k):
        if k == 0:
            return self.dp
        if k == 1:
            return self.dp + 1 - 2 * self.x
        if k == 2:
            return self.dp + 2 - 4 * self.y
        return 3 - self.dp

    def at(self, k=0, blk=None, z=None):
        return (self.column(k), self.blk if blk is None else blk, self.z if z is None else z)


def entry_barrier(place, reach):
    barrier = pltpu.get_barrier_semaphore()

    def tell(target):
        pl.semaphore_signal(barrier, inc=1, device_id=target, device_id_type=MESH_ID)

    if reach == "all":
        me = (place.dp * 2 + place.blk) * 4 + place.z

        @pl.loop(1, 32)
        def _(step):
            other = (me + step) % 32
            tell((other // 8, (other // 4) % 2, other % 4))

        pl.semaphore_wait(barrier, 31)
    elif reach == "column":

        @pl.loop(1, 8)
        def _(step):
            other = (place.col + step) % 8
            tell((place.dp, other // 4, other % 4))

        pl.semaphore_wait(barrier, 7)
    else:
        tell_partners(place, barrier)
        wait_partners(place, barrier)


def tell_partners(place, semaphore):
    def tell(target):
        pl.semaphore_signal(semaphore, inc=1, device_id=target, device_id_type=MESH_ID)

    tell(place.at(0, 1 - place.blk))
    tell(place.at(1))
    tell(place.at(2))

    @pl.when(place.z > 0)
    def _():
        tell(place.at(z=place.z - 1))

    @pl.when(place.z < 3)
    def _():
        tell(place.at(z=place.z + 1))


def wait_partners(place, semaphore):
    ends = (3 - place.z) // 3 + place.z // 3
    pl.semaphore_wait(semaphore, 5 - ends)


def remote(src, dst, send_sem, recv_sem, target):
    return pltpu.make_async_remote_copy(
        src_ref=src,
        dst_ref=dst,
        send_sem=send_sem,
        recv_sem=recv_sem,
        device_id=target,
        device_id_type=MESH_ID,
    )


class GatherFlow:
    SENDS = 40
    RECVS = 37

    def __init__(self, place, src, out, send, recv, full, direct=False, others=False):
        self.p, self.src, self.out, self.send, self.recv, self.full = place, src, out, send, recv, full
        self.direct, self.others = direct, others
        self.half = src.shape[0] // 2

    def slot(self, k, blk, s):
        if self.full:
            return (self.p.column(k) * 2 + blk) * 4 + s
        return blk * 4 + s

    def block(self, k, s, blk=None):
        return self.out.at[self.slot(k, self.p.blk if blk is None else blk, s)]

    def copies(self, k, s, own=False):
        src = self.src if own else self.block(k, s)
        return src, self.block(k, s)

    def up(self, s, own=False):
        src, dst = self.copies(0, s, own)
        return remote(src, dst, self.send.at[s], self.recv.at[s], self.p.at(z=jnp.minimum(self.p.z + 1, 3)))

    def down(self, s, own=False):
        src, dst = self.copies(0, s, own)
        return remote(src, dst, self.send.at[4 + s], self.recv.at[s], self.p.at(z=jnp.maximum(self.p.z - 1, 0)))

    def across_x(self, s, own=False):
        src, dst = self.copies(0, s, own)
        return remote(src, dst, self.send.at[8 + s], self.recv.at[4 + s], self.p.at(1))

    def across_y(self, s, own=False):
        src, dst = self.copies(0, s, own)
        return remote(src, dst, self.send.at[12 + s], self.recv.at[8 + s], self.p.at(2))

    def turn_y(self, s):
        ref = self.block(1, s).at[pl.ds(0, self.half)]
        return remote(ref, ref, self.send.at[16 + s], self.recv.at[12 + s], self.p.at(2))

    def turn_x(self, s):
        ref = self.block(2, s).at[pl.ds(self.half, self.half)]
        return remote(ref, ref, self.send.at[20 + s], self.recv.at[16 + s], self.p.at(1))

    def core(self, k, s, own=False):
        src, dst = self.copies(k, s, own)
        return remote(
            src, dst, self.send.at[24 + 4 * k + s], self.recv.at[20 + 4 * k + s], self.p.at(0, 1 - self.p.blk)
        )

    def got(self, sem, ref):
        remote(ref, ref, self.send.at[0], self.recv.at[sem], self.p.at(0, 1 - self.p.blk)).wait_recv()

    def own_copy(self):
        return pltpu.make_async_copy(self.src, self.block(0, self.p.z), self.recv.at[36])

    def spread(self, s, own=False):
        if self.full:
            self.across_x(s, own).start()
            self.across_y(s, own).start()
        self.core(0, s, own).start()

    def straight(self, step):
        z = self.p.z
        return remote(
            self.src, self.block(0, z), self.send.at[step - 1], self.recv.at[z], self.p.at(z=(z + step) % 4)
        )

    def begin(self):
        z = self.p.z
        if self.direct:
            for step in (1, 2, 3):
                self.straight(step).start()
            self.spread(z, True)
            self.own_copy().start()
            return

        @pl.when(z < 3)
        def _():
            self.up(z, True).start()

        @pl.when(z > 0)
        def _():
            self.down(z, True).start()

        if not self.others:
            self.spread(z, True)
            self.own_copy().start()

    def along(self, d):
        z = self.p.z

        @pl.when(z >= d)
        def _():
            s = z - d
            self.got(s, self.block(0, s))

            if not self.direct:

                @pl.when(z < 3)
                def _():
                    self.up(s).start()

            self.spread(s)

        @pl.when(z + d <= 3)
        def _():
            s = z + d
            self.got(s, self.block(0, s))

            if not self.direct:

                @pl.when(z > 0)
                def _():
                    self.down(s).start()

            self.spread(s)

    def each(self, d, act):
        z = self.p.z
        if d == 0:
            if not self.others:
                act(z)
            return

        @pl.when(z >= d)
        def _():
            act(z - d)

        @pl.when(z + d <= 3)
        def _():
            act(z + d)

    def turn(self, d):
        if not self.full:
            return

        def act(s):
            self.got(4 + s, self.block(1, s))
            self.turn_y(s).start()
            self.core(1, s).start()
            self.got(8 + s, self.block(2, s))
            self.turn_x(s).start()
            self.core(2, s).start()

        self.each(d, act)

    def corner(self, d):
        if not self.full:
            return

        def act(s):
            self.got(12 + s, self.block(3, s).at[pl.ds(0, self.half)])
            self.got(16 + s, self.block(3, s).at[pl.ds(self.half, self.half)])
            self.core(3, s).start()

        self.each(d, act)

    def settle_plane(self, s):
        for k in range(4 if self.full else 1):
            self.got(20 + 4 * k + s, self.block(k, s, 1 - self.p.blk))
            self.core(k, s).wait_send()
        if self.full:
            self.across_x(s).wait_send()
            self.across_y(s).wait_send()
            self.turn_x(s).wait_send()
            self.turn_y(s).wait_send()

    def finish(self):
        z = self.p.z

        @pl.loop(0, 4)
        def _(s):
            pl.when((s != z) | (not self.others))(lambda: self.settle_plane(s))
            if not self.direct:

                @pl.when((s <= z) & (z < 3))
                def _():
                    self.up(s).wait_send()

                @pl.when((s >= z) & (z > 0))
                def _():
                    self.down(s).wait_send()

        if self.direct:
            for step in (1, 2, 3):
                self.straight(step).wait_send()
        if not self.others:
            self.own_copy().wait()

    def steps(self):
        return [
            self.begin,
            lambda: self.along(1),
            lambda: self.turn(0),
            lambda: self.along(2),
            lambda: self.turn(1),
            lambda: self.along(3),
            lambda: self.corner(0),
            lambda: self.turn(2),
            lambda: self.corner(1),
            lambda: self.turn(3),
            lambda: self.corner(2),
            lambda: self.corner(3),
            self.finish,
        ]


class PlaneFlow(GatherFlow):
    def __init__(self, place, blocks, out, send, recv, local):
        super().__init__(place, blocks[0][1], out, send, recv, True)
        self.blocks, self.local = blocks, local

    def begin(self):
        for i, (s, src) in enumerate(self.blocks):
            self.src = src
            self.spread(s, True)
            pltpu.make_async_copy(src, self.block(0, s), self.local.at[i]).start()

    def turns(self):
        for s, _ in self.blocks:
            self.got(4 + s, self.block(1, s))
            self.turn_y(s).start()
            self.core(1, s).start()
            self.got(8 + s, self.block(2, s))
            self.turn_x(s).start()
            self.core(2, s).start()

    def corners(self):
        for s, _ in self.blocks:
            self.got(12 + s, self.block(3, s).at[pl.ds(0, self.half)])
            self.got(16 + s, self.block(3, s).at[pl.ds(self.half, self.half)])
            self.core(3, s).start()

    def finish(self):
        for i, (s, src) in enumerate(self.blocks):
            self.settle_plane(s)
            pltpu.make_async_copy(src, self.block(0, s), self.local.at[i]).wait()


class PlaneFlow(GatherFlow):
    def __init__(self, place, blocks, out, send, recv, local):
        super().__init__(place, blocks[0][1], out, send, recv, True)
        self.blocks, self.local = blocks, local

    def begin(self):
        for i, (s, src) in enumerate(self.blocks):
            self.src = src
            self.spread(s, True)
            pltpu.make_async_copy(src, self.block(0, s), self.local.at[i]).start()

    def turns(self):
        for s, _ in self.blocks:
            self.got(4 + s, self.block(1, s))
            self.turn_y(s).start()
            self.core(1, s).start()
            self.got(8 + s, self.block(2, s))
            self.turn_x(s).start()
            self.core(2, s).start()

    def corners(self):
        for s, _ in self.blocks:
            self.got(12 + s, self.block(3, s).at[pl.ds(0, self.half)])
            self.got(16 + s, self.block(3, s).at[pl.ds(self.half, self.half)])
            self.core(3, s).start()

    def finish(self):
        for i, (s, src) in enumerate(self.blocks):
            self.settle_plane(s)
            pltpu.make_async_copy(src, self.block(0, s), self.local.at[i]).wait()


def run_flows(flows):
    lists = [flow.steps() for flow in flows]
    for position in range(max(len(steps) for steps in lists)):
        for steps in lists:
            if position < len(steps):
                steps[position]()


def add_rows(dst, terms, rows):
    @pl.loop(0, rows // 16)
    def _(i):
        at = pl.ds(pl.multiple_of(i * 16, 16), 16)
        total = terms[0][at, :].astype(jnp.float32)
        for term in terms[1:]:
            total = total + term[at, :].astype(jnp.float32)
        dst[at, :] = total.astype(dst.dtype)


class ScatterFlow:
    SENDS = 16 + 8 + 8 + 4 + 4
    RECVS = 16 + 8 + 8 + 4 + 4
    LOCALS = 20

    def __init__(self, place, part, out, scratch, full, band=None):
        self.p, self.part, self.out, self.full = place, part, out, full
        if full:
            (self.acc, self.near, self.half_in, self.side_in, self.line_in, self.sum, self.send, self.recv, self.local) = scratch
        else:
            (self.acc, self.near, self.line_in, self.sum, self.send, self.recv, self.local) = scratch
        self.columns = 4 if full else 1
        first, self.rows = band or (0, part.shape[1])
        self.band = pl.ds(first, self.rows)
        self.half = self.rows // 2

    @staticmethod
    def scratch(rows, width, dtype, full):
        columns = 4 if full else 1
        shapes = [
            pltpu.VMEM((columns, 4, rows, width), dtype),
            pltpu.VMEM((columns, 4, rows, width), dtype),
        ]
        if full:
            shapes += [pltpu.VMEM((2, 4, rows // 2, width), dtype), pltpu.VMEM((2, 4, rows, width), dtype)]
        return shapes + [
            pltpu.VMEM((2, 4, rows, width), dtype),
            pltpu.VMEM((rows, width), jnp.float32),
            pltpu.SemaphoreType.DMA((ScatterFlow.SENDS,)),
            pltpu.SemaphoreType.DMA((ScatterFlow.RECVS,)),
            pltpu.SemaphoreType.DMA((ScatterFlow.LOCALS,)),
        ]

    def slot(self, k, blk, s):
        if self.full:
            return (self.p.column(k) * 2 + blk) * 4 + s
        return blk * 4 + s

    def order(self, i):
        z = self.p.z
        return [3 * (1 - z // 2), (2 + 3 * z) % 5, 1 + z % 2, z][i]

    def load(self, k, s):
        return pltpu.make_async_copy(
            self.part.at[self.slot(k, self.p.blk, s), self.band], self.acc.at[k, s], self.local.at[4 * k + s]
        )

    def core(self, k, s):
        return remote(
            self.part.at[self.slot(k, 1 - self.p.blk, s), self.band],
            self.near.at[k, s],
            self.send.at[4 * k + s],
            self.recv.at[4 * k + s],
            self.p.at(0, 1 - self.p.blk),
        )

    def half_x(self, s):
        return remote(
            self.acc.at[3, s, pl.ds(0, self.half)],
            self.half_in.at[0, s],
            self.send.at[16 + s],
            self.recv.at[16 + s],
            self.p.at(1),
        )

    def half_y(self, s):
        return remote(
            self.acc.at[3, s, pl.ds(self.half, self.half)],
            self.half_in.at[1, s],
            self.send.at[20 + s],
            self.recv.at[20 + s],
            self.p.at(2),
        )

    def side_x(self, s):
        return remote(
            self.acc.at[1, s], self.side_in.at[0, s], self.send.at[24 + s], self.recv.at[24 + s], self.p.at(1)
        )

    def side_y(self, s):
        return remote(
            self.acc.at[2, s], self.side_in.at[1, s], self.send.at[28 + s], self.recv.at[28 + s], self.p.at(2)
        )

    def line_up(self, s):
        return remote(
            self.acc.at[0, s],
            self.line_in.at[0, s],
            self.send.at[32 + s],
            self.recv.at[32 + s],
            self.p.at(z=jnp.minimum(self.p.z + 1, 3)),
        )

    def line_down(self, s):
        return remote(
            self.acc.at[0, s],
            self.line_in.at[1, s],
            self.send.at[36 + s],
            self.recv.at[36 + s],
            self.p.at(z=jnp.maximum(self.p.z - 1, 0)),
        )

    def begin(self):
        for i in range(4):
            s = self.order(i)
            for k in reversed(range(self.columns)):
                self.core(k, s).start()
                self.load(k, s).start()

    def arrive(self, k, s):
        self.load(k, s).wait()
        self.core(k, s).wait_recv()
        return [self.acc.at[k, s], self.near.at[k, s]]

    def stage1(self, i):
        if not self.full:
            return
        s = self.order(i)
        add_rows(self.acc.at[3, s], self.arrive(3, s), self.rows)
        self.half_x(s).start()
        self.half_y(s).start()

    def stage2(self, i):
        if not self.full:
            return
        s = self.order(i)
        first, second = pl.ds(0, self.half), pl.ds(self.half, self.half)
        terms = self.arrive(2, s)
        late = [term.at[first] for term in terms] + [self.half_in.at[0, s]]
        rest = [term.at[second] for term in terms]
        add_rows(rest[0], rest, self.half)
        self.half_x(s).wait_recv()
        add_rows(late[0], late, self.half)
        self.side_y(s).start()
        terms = self.arrive(1, s)
        late = [term.at[second] for term in terms] + [self.half_in.at[1, s]]
        rest = [term.at[first] for term in terms]
        add_rows(rest[0], rest, self.half)
        self.half_y(s).wait_recv()
        add_rows(late[0], late, self.half)
        self.side_x(s).start()

    def stage3(self, i):
        s = self.order(i)
        z = self.p.z
        terms = self.arrive(0, s)
        if self.full:
            self.side_x(s).wait_recv()
            self.side_y(s).wait_recv()
            terms = terms + [self.side_in.at[0, s], self.side_in.at[1, s]]
        add_rows(self.acc.at[0, s], terms, self.rows)
        if i < 3:

            @pl.when(z == 0)
            def _():
                self.line_up(s).start()

            @pl.when(z == 3)
            def _():
                self.line_down(s).start()

    def chain(self, i):
        s = self.order(i)
        z = self.p.z

        @pl.when((z > 0) & (z < s) & (z < 3))
        def _():
            self.line_up(s).wait_recv()
            add_rows(self.acc.at[0, s], [self.acc.at[0, s], self.line_in.at[0, s]], self.rows)
            self.line_up(s).start()

        @pl.when((z < 3) & (z > s) & (z > 0))
        def _():
            self.line_down(s).wait_recv()
            add_rows(self.acc.at[0, s], [self.acc.at[0, s], self.line_in.at[1, s]], self.rows)
            self.line_down(s).start()

    def final(self):
        z = self.p.z
        mine, above, below = self.acc.at[0, z], self.line_in.at[0, z], self.line_in.at[1, z]

        @pl.when(z > 0)
        def _():
            self.line_up(z).wait_recv()

        @pl.when(z < 3)
        def _():
            self.line_down(z).wait_recv()

        @pl.when(z == 0)
        def _():
            add_rows(self.sum, [mine, below], self.rows)

        @pl.when(z == 3)
        def _():
            add_rows(self.sum, [mine, above], self.rows)

        @pl.when((z > 0) & (z < 3))
        def _():
            add_rows(self.sum, [mine, above, below], self.rows)

        done = pltpu.make_async_copy(self.sum, self.out, self.local.at[0])
        done.start()

        @pl.loop(0, 4)
        def _(s):
            for k in range(self.columns):
                self.core(k, s).wait_send()
            if self.full:
                self.half_x(s).wait_send()
                self.half_y(s).wait_send()
                self.side_x(s).wait_send()
                self.side_y(s).wait_send()

            @pl.when(s > z)
            def _():
                self.line_up(s).wait_send()

            @pl.when(s < z)
            def _():
                self.line_down(s).wait_send()

        done.wait()

    def steps(self):
        plan = [
            (self.stage1, 0),
            (self.stage1, 1),
            (self.stage2, 0),
            (self.stage1, 2),
            (self.stage2, 1),
            (self.stage3, 0),
            (self.stage1, 3),
            (self.stage2, 2),
            (self.stage3, 1),
            (self.chain, 0),
            (self.stage2, 3),
            (self.stage3, 2),
            (self.chain, 1),
            (self.chain, 2),
            (self.stage3, 3),
        ]
        return [self.begin] + [functools.partial(act, i) for act, i in plan] + [self.final]


def local_params():
    return pltpu.CompilerParams(vmem_limit_bytes=VMEM_BYTES)


def inner(left, right, left_dim=1, right_dim=0):
    return lax.dot_general(
        left, right, (((left_dim,), (right_dim,)), ((), ())), preferred_element_type=jnp.float32
    )


def is_place(places, per):
    return lax.broadcasted_iota(jnp.int32, (per, places.shape[1]), 0) == places


def one_hot(places, per):
    experts = places.shape[0]
    hot = [is_place(places[e : e + 1], per).astype(jnp.float32) for e in range(experts)]
    return jnp.concatenate(hot, axis=0).astype(jnp.bfloat16)


def pick_rows(places, probs, features, per):
    pairs, experts, pair_rows = places.shape
    width = features.shape[-1]
    step = 2

    def kernel(place_ref, prob_ref, feature_ref, row_ref, row_prob_ref):
        for i in range(step):
            rows = inner(one_hot(place_ref[i], per), feature_ref[i]).astype(row_ref.dtype)
            for e in range(experts):
                at = pl.ds(i * per, per)
                row_ref[e, at] = rows[e * per : (e + 1) * per]
                hot = is_place(place_ref[i, e : e + 1], per)
                prob = jnp.concatenate([prob_ref[2 * i, e : e + 1], prob_ref[2 * i + 1, e : e + 1]], axis=1)
                row_prob_ref[e, at] = jnp.sum(jnp.where(hot, prob, 0.0), axis=1, keepdims=True)

    return pl.pallas_call(
        kernel,
        out_shape=[
            jax.ShapeDtypeStruct((experts, pairs * per, width), features.dtype),
            jax.ShapeDtypeStruct((experts, pairs * per, 1), jnp.float32),
        ],
        grid=(pairs // step,),
        in_specs=[
            pl.BlockSpec((step, experts, pair_rows), lambda p: (p, 0, 0)),
            pl.BlockSpec((2 * step, experts, pair_rows // 2), lambda p: (p, 0, 0)),
            pl.BlockSpec((step, pair_rows, width), lambda p: (p, 0, 0)),
        ],
        out_specs=[
            pl.BlockSpec((experts, step * per, width), lambda p: (0, p, 0)),
            pl.BlockSpec((experts, step * per, 1), lambda p: (0, p, 0)),
        ],
        compiler_params=local_params(),
        name="pick_rows",
    )(places, probs, features)


def put_rows_back(places, rows, row_grads):
    pairs, experts, pair_rows = places.shape
    _, slots, width = rows.shape
    per = slots // pairs
    step = 2
    half = pair_rows // 2

    def kernel(place_ref, row_ref, grad_ref, sum_ref, prob_ref):
        for i in range(step):
            at = pl.ds(i * per, per)
            gathered = jnp.concatenate([row_ref[e, at] for e in range(experts)], axis=0)
            sum_ref[i] = inner(one_hot(place_ref[i], per), gathered, 0, 0).astype(sum_ref.dtype)
            prob_ref[2 * i : 2 * i + 2] = jnp.zeros((2, 8, half), jnp.float32)
            for e in range(experts):
                hot = is_place(place_ref[i, e : e + 1], per)
                line = jnp.sum(jnp.where(hot, grad_ref[e, at], 0.0), axis=0, keepdims=True)
                prob_ref[2 * i, e : e + 1] = line[:, :half]
                prob_ref[2 * i + 1, e : e + 1] = line[:, half:]

    return pl.pallas_call(
        kernel,
        out_shape=[
            jax.ShapeDtypeStruct((pairs, pair_rows, width), rows.dtype),
            jax.ShapeDtypeStruct((2 * pairs, 8, half), jnp.float32),
        ],
        grid=(pairs // step,),
        in_specs=[
            pl.BlockSpec((step, experts, pair_rows), lambda p: (p, 0, 0)),
            pl.BlockSpec((experts, step * per, width), lambda p: (0, p, 0)),
            pl.BlockSpec((experts, step * per, 1), lambda p: (0, p, 0)),
        ],
        out_specs=[
            pl.BlockSpec((step, pair_rows, width), lambda p: (p, 0, 0)),
            pl.BlockSpec((2 * step, 8, half), lambda p: (p, 0, 0)),
        ],
        compiler_params=local_params(),
        name="put_rows_back",
    )(places, rows, row_grads)


def run_experts(rows, plain_grads, probs, gate_weight, up_weight):
    experts, slots, width = rows.shape
    hidden = gate_weight.shape[2]
    parts = 2
    part = slots // parts

    def kernel(x, plain_ref, p, wg, wu, weighted, gate_back, up_back, back, prob_back):
        gate = inner(x[0], wg[0])
        up = inner(x[0], wu[0])
        plain = plain_ref[0]
        prob = p[0]
        sig = jax.nn.sigmoid(gate)
        act = gate * sig
        hid = act * up
        prob_back[0] = jnp.sum(hid * plain, axis=1, keepdims=True)
        weighted[0] = (hid * prob).astype(jnp.bfloat16)
        grad = plain * prob
        gate_low = (grad * up * sig * (1.0 + gate * (1.0 - sig))).astype(jnp.bfloat16)
        up_low = (grad * act).astype(jnp.bfloat16)
        gate_back[0] = gate_low
        up_back[0] = up_low
        back[0] = (inner(gate_low, wg[0], 1, 1) + inner(up_low, wu[0], 1, 1)).astype(jnp.bfloat16)

    def block(size):
        return pl.BlockSpec((1, part, size), lambda e, i: (e, i, 0))

    weight = pl.BlockSpec((1, width, hidden), lambda e, i: (e, 0, 0))
    narrow = jax.ShapeDtypeStruct((experts, slots, hidden), rows.dtype)
    return pl.pallas_call(
        kernel,
        out_shape=[
            narrow,
            narrow,
            narrow,
            jax.ShapeDtypeStruct(rows.shape, rows.dtype),
            jax.ShapeDtypeStruct((experts, slots, 1), jnp.float32),
        ],
        grid=(experts, parts),
        in_specs=[block(width), block(hidden), block(1), weight, weight],
        out_specs=[block(hidden)] * 3 + [block(width), block(1)],
        compiler_params=local_params(),
        name="run_experts",
    )(rows, plain_grads, probs, gate_weight, up_weight)


class PickWork:
    GROUP = 4

    def __init__(self, places, source, weight, rows_out, plain_out, scratch):
        self.places, self.source, self.weight = places, source, weight
        self.rows_out, self.plain_out = rows_out, plain_out
        self.block, self.rows, self.plain, self.held, self.in_sems, self.out_sems, self.held_sem = scratch
        self.pairs = source.shape[0]
        self.units = self.pairs + self.GROUP
        self.experts = weight.shape[0]
        self.per = self.rows.shape[2] // self.GROUP

    @staticmethod
    def scratch(source, weight, per):
        experts, hidden, width = weight.shape
        group = PickWork.GROUP * per
        return [
            pltpu.VMEM((2,) + source.shape[1:], source.dtype),
            pltpu.VMEM((2, experts, group, width), source.dtype),
            pltpu.VMEM((2, experts, group, hidden), jnp.float32),
            pltpu.VMEM(weight.shape, weight.dtype),
            pltpu.SemaphoreType.DMA((2,)),
            pltpu.SemaphoreType.DMA((2, 2)),
            pltpu.SemaphoreType.DMA((1,)),
        ]

    def load(self, unit, slot):
        return pltpu.make_async_copy(self.source.at[unit], self.block.at[slot], self.in_sems.at[slot])

    def hold(self):
        return pltpu.make_async_copy(self.weight, self.held, self.held_sem.at[0])

    def stores(self, group, slot):
        height = self.GROUP * self.per
        at = pl.ds(pl.multiple_of(group * height, height), height)
        return [
            pltpu.make_async_copy(self.rows.at[slot], self.rows_out.at[:, at], self.out_sems.at[slot, 0]),
            pltpu.make_async_copy(self.plain.at[slot], self.plain_out.at[:, at], self.out_sems.at[slot, 1]),
        ]

    def begin(self):
        self.hold().start()
        self.load(0, 0).start()

    def pick(self, unit):
        slot, group, turn = unit % 2, unit // self.GROUP, unit % self.GROUP
        side = group % 2

        @pl.when(unit + 1 < self.pairs)
        def _():
            self.load(unit + 1, 1 - slot).start()

        @pl.when((turn == 0) & (group >= 2))
        def _():
            for copy in self.stores(group - 2, side):
                copy.wait()

        self.load(unit, slot).wait()
        rows = inner(one_hot(self.places[unit], self.per), self.block[slot]).astype(self.rows.dtype)
        for e in range(self.experts):
            at = pl.ds(pl.multiple_of(turn * self.per, self.per), self.per)
            self.rows[side, e, at] = rows[e * self.per : (e + 1) * self.per]

    def multiply(self, unit):
        group, e = unit // self.GROUP, unit % self.GROUP
        side = group % 2

        @pl.when(unit == 0)
        def _():
            self.hold().wait()

        self.plain[side, e] = inner(self.rows[side, e], self.held[e], 1, 1)

        @pl.when(e == self.GROUP - 1)
        def _():
            for copy in self.stores(group, side):
                copy.start()

    def run(self, unit):
        pl.when(unit < self.pairs)(lambda: self.pick(unit))
        pl.when(unit >= self.GROUP)(lambda: self.multiply(unit - self.GROUP))

    def finish(self):
        groups = self.pairs // self.GROUP
        for group in (groups - 2, groups - 1):
            for copy in self.stores(group, group % 2):
                copy.wait()


class OutputWork:
    def __init__(self, places, hidden, weight, out, scratch):
        self.places, self.hidden, self.weight, self.out = places, hidden, weight, out
        self.rows, self.held, self.narrow, self.block, self.in_sems, self.out_sems = scratch
        self.experts, self.slots, _ = hidden.shape
        self.pairs = out.shape[0]
        self.per = self.slots // self.pairs
        self.width = weight.shape[2]
        self.units = 2 * self.experts + self.pairs

    @staticmethod
    def scratch(hidden, weight, out):
        experts, slots, narrow = hidden.shape
        return [
            pltpu.VMEM((experts, slots, weight.shape[2]), weight.dtype),
            pltpu.VMEM((2,) + weight.shape[1:], weight.dtype),
            pltpu.VMEM((2, slots, narrow), hidden.dtype),
            pltpu.VMEM((2,) + out.shape[1:], out.dtype),
            pltpu.SemaphoreType.DMA((2, 2)),
            pltpu.SemaphoreType.DMA((2,)),
        ]

    def loads(self, e):
        slot = e % 2
        return [
            pltpu.make_async_copy(self.weight.at[e], self.held.at[slot], self.in_sems.at[slot, 0]),
            pltpu.make_async_copy(self.hidden.at[e], self.narrow.at[slot], self.in_sems.at[slot, 1]),
        ]

    def store(self, pair):
        return pltpu.make_async_copy(self.block.at[pair % 2], self.out.at[pair], self.out_sems.at[pair % 2])

    def begin(self):
        for copy in self.loads(0):
            copy.start()

    def run(self, unit):
        half = self.width // 2

        @pl.when(unit < 2 * self.experts)
        def _():
            e, side = unit // 2, unit % 2

            @pl.when(side == 0)
            def _():
                @pl.when(e + 1 < self.experts)
                def _():
                    for copy in self.loads(e + 1):
                        copy.start()

                for copy in self.loads(e):
                    copy.wait()

            at = pl.ds(pl.multiple_of(side * half, half), half)
            self.rows[e, :, at] = inner(self.narrow[e % 2], self.held[e % 2, :, at]).astype(self.rows.dtype)

        @pl.when(unit >= 2 * self.experts)
        def _():
            pair = unit - 2 * self.experts

            @pl.when(pair >= 2)
            def _():
                self.store(pair - 2).wait()

            at = pl.ds(pl.multiple_of(pair * self.per, self.per), self.per)
            rows = jnp.concatenate([self.rows[e, at] for e in range(self.experts)], axis=0)
            self.block[pair % 2] = inner(one_hot(self.places[pair], self.per), rows, 0, 0).astype(self.block.dtype)
            self.store(pair).start()

    def finish(self):
        for pair in (self.pairs - 2, self.pairs - 1):
            self.store(pair).wait()


def expert_weight_grads(rows, grads, weighted, gate_back, up_back):
    experts, slots, width = rows.shape
    hidden = weighted.shape[2]
    parts = 4
    part = width // parts

    def kernel(x, c, low, gate, up, gate_out, up_out, down_out):
        gate_out[0] = inner(x[0], gate[0], 0, 0)
        up_out[0] = inner(x[0], up[0], 0, 0)
        down_out[0] = inner(low[0], c[0], 0, 0)

    source = pl.BlockSpec((1, slots, part), lambda e, i: (e, 0, i))
    whole = pl.BlockSpec((1, slots, hidden), lambda e, i: (e, 0, 0))
    tall = pl.BlockSpec((1, part, hidden), lambda e, i: (e, i, 0))
    flat = pl.BlockSpec((1, hidden, part), lambda e, i: (e, 0, i))
    return pl.pallas_call(
        kernel,
        out_shape=[
            jax.ShapeDtypeStruct((experts, width, hidden), jnp.float32),
            jax.ShapeDtypeStruct((experts, width, hidden), jnp.float32),
            jax.ShapeDtypeStruct((experts, hidden, width), jnp.float32),
        ],
        grid=(experts, parts),
        in_specs=[source, source, whole, whole, whole],
        out_specs=[tall, tall, flat],
        compiler_params=local_params(),
        cost_estimate=pl.CostEstimate(
            flops=6 * experts * slots * width * hidden, bytes_accessed=24 * experts * width * hidden, transcendentals=0
        ),
        name="expert_weight_grads",
    )(rows, grads, weighted, gate_back, up_back)


class ColumnsFlow:
    SENDS = 24 + 1 + 16
    RECVS = 24 + 1 + 16
    LOCALS = 4

    def __init__(self, place, sources, rows_in, wide, tall, send, recv, local):
        self.p, self.sources, self.rows_in, self.wide, self.tall = place, sources, rows_in, wide, tall
        self.send, self.recv, self.local = send, recv, local
        self.rows = rows_in.shape[0]
        self.share = wide.shape[1] // len(sources)

    def spot(self, i, col):
        rows = pl.ds(pl.multiple_of((self.p.dp * 8 + col) * self.rows, self.rows), self.rows)
        return self.wide.at[rows, pl.ds(i * self.share, self.share)]

    def piece(self, i, to):
        return self.sources[i].at[:, pl.ds(pl.multiple_of(to * self.share, self.share), self.share)]

    def scatter(self, step, i):
        to = (self.p.col + step) % 8
        return remote(
            self.piece(i, to),
            self.spot(i, self.p.col),
            self.send.at[3 * step + i],
            self.recv.at[3 * self.p.col + i],
            (self.p.dp, to // 4, to % 4),
        )

    def keep(self, i):
        return pltpu.make_async_copy(self.piece(i, self.p.col), self.spot(i, self.p.col), self.local.at[i])

    def tall_rows(self, k):
        return self.tall.at[pl.ds(pl.multiple_of(self.p.column(k) * self.rows, self.rows), self.rows)]

    def swap(self):
        group = self.p.dp * 2 + self.p.blk
        dst = self.tall.at[pl.ds(pl.multiple_of(self.p.z * self.rows, self.rows), self.rows)]
        return remote(
            self.rows_in, dst, self.send.at[24], self.recv.at[24], (self.p.z, group // 4, group % 4)
        )

    def stay(self):
        return pltpu.make_async_copy(self.rows_in, self.tall_rows(0), self.local.at[3])

    def at_home(self):
        group = self.p.dp * 2 + self.p.blk
        return (self.p.z == self.p.dp) & (group == self.p.col)

    def band(self, i, k, first=0, parts=1):
        if i == 3:
            height, ref = self.rows, self.tall
        else:
            height, ref = 8 * self.rows, self.wide
        part = height // parts
        rows = pl.ds(pl.multiple_of(self.p.column(k) * height + first * part, part), part)
        return ref.at[rows] if i == 3 else ref.at[rows, pl.ds(i * self.share, self.share)]

    def across(self, i, k):
        ref = self.band(i, 0)
        slot = 25 + 4 * i + k - 1
        return remote(ref, ref, self.send.at[slot], self.recv.at[slot], self.p.at(k))

    def turn(self, i, k):
        ref = self.band(i, k, k - 1, 2)
        slot = 25 + 4 * i + 1 + k
        return remote(ref, ref, self.send.at[slot], self.recv.at[slot], self.p.at(3 - k))

    def got(self, sem, ref):
        remote(ref, ref, self.send.at[0], self.recv.at[sem], self.p.at(0, 1 - self.p.blk)).wait_recv()

    def begin(self):
        home = self.at_home()

        @pl.when(home)
        def _():
            self.stay().start()

        @pl.when(jnp.logical_not(home))
        def _():
            self.swap().start()

        for i in range(3):

            @pl.loop(1, 8)
            def _(step):
                self.scatter(step, i).start()

            self.keep(i).start()

    def settle(self, i):
        if i == 3:
            home = self.at_home()

            @pl.when(home)
            def _():
                self.stay().wait()

            @pl.when(jnp.logical_not(home))
            def _():
                self.got(24, self.tall_rows(0))

        else:
            self.keep(i).wait()

            @pl.loop(1, 8)
            def _(step):
                col = (self.p.col + step) % 8
                self.got(3 * col + i, self.spot(i, col))

        self.across(i, 1).start()
        self.across(i, 2).start()

    def turns(self, i):
        for k in (1, 2):
            self.got(25 + 4 * i + k - 1, self.band(i, k))
            self.turn(i, k).start()

    def finish(self):
        for i in (3, 0, 1, 2):
            for k in (1, 2):
                self.got(25 + 4 * i + 1 + k, self.band(i, 3, k - 1, 2))
                self.turn(i, k).wait_send()
                self.across(i, k).wait_send()

        @pl.when(jnp.logical_not(self.at_home()))
        def _():
            self.swap().wait_send()

        @pl.loop(1, 8)
        def _(step):
            for i in range(3):
                self.scatter(step, i).wait_send()


class SumsFlow:
    SENDS = 8 + 24 + 1
    RECVS = 8 + 8 + 1
    LOCALS = 12

    def __init__(self, place, wide_out, tall_out, scratch):
        self.p = place
        self.outs = (wide_out, tall_out)
        self.acc, self.half_in, self.side_in = scratch[0:2], scratch[2:4], scratch[4:6]
        self.send, self.recv, self.local = scratch[6:9]
        self.rows = tall_out.shape[0]

    @staticmethod
    def scratch(wide, tall):
        shapes = []
        for kind in ((4, 1), (2, 2), (2, 1)):
            for rows, width in (wide, tall):
                shapes.append(pltpu.VMEM((kind[0], rows // kind[1], width), jnp.bfloat16))
        return shapes + [
            pltpu.SemaphoreType.DMA((SumsFlow.SENDS,)),
            pltpu.SemaphoreType.DMA((SumsFlow.RECVS,)),
            pltpu.SemaphoreType.DMA((SumsFlow.LOCALS,)),
        ]

    def halves(self, ref):
        half = ref.shape[0] // 2
        return ref.at[pl.ds(0, half)], ref.at[pl.ds(half, half)]

    def corner(self, which, k):
        src = self.halves(self.acc[which].at[3])[k - 1]
        slot = 4 * which + k - 1
        return remote(src, self.half_in[which].at[k - 1], self.send.at[slot], self.recv.at[slot], self.p.at(k))

    def side(self, which, k):
        slot = 4 * which + 1 + k
        return remote(
            self.acc[which].at[k], self.side_in[which].at[k - 1], self.send.at[slot], self.recv.at[slot], self.p.at(k)
        )

    def deal(self, step, i):
        to = (self.p.col + step) % 8
        src, dst = self.piece(to, i)
        return remote(
            src, dst, self.send.at[8 + 3 * step + i], self.recv.at[8 + self.p.col], (self.p.dp, to // 4, to % 4)
        )

    def piece(self, to, i):
        share = self.outs[0].shape[2] // 8
        rows = pl.ds(pl.multiple_of(to * self.rows, self.rows), self.rows)
        dst = self.outs[0].at[i, :, pl.ds(pl.multiple_of(self.p.col * share, share), share)]
        return self.acc[0].at[0, rows, pl.ds(i * share, share)], dst

    def keep(self, i):
        src, dst = self.piece(self.p.col, i)
        return pltpu.make_async_copy(src, dst, self.local.at[8 + i])

    def swap(self):
        return remote(
            self.acc[1].at[0], self.outs[1], self.send.at[32], self.recv.at[16], (self.p.col // 2, self.p.col % 2, self.p.dp)
        )

    def stay(self):
        return pltpu.make_async_copy(self.acc[1].at[0], self.outs[1], self.local.at[11])

    def at_home(self):
        return (self.p.col // 2 == self.p.dp) & (self.p.col % 2 == self.p.blk) & (self.p.z == self.p.dp)

    def corners(self, which):
        self.corner(which, 1).start()
        self.corner(which, 2).start()

    def sides(self, which):
        for k, other in ((2, 1), (1, 2)):
            self.corner(which, other).wait_recv()
            target = self.halves(self.acc[which].at[k])[other - 1]
            add_rows(target, [target, self.half_in[which].at[other - 1]], target.shape[0])
            self.side(which, k).start()

    def total(self, which):
        self.side(which, 1).wait_recv()
        self.side(which, 2).wait_recv()
        mine = self.acc[which].at[0]
        add_rows(mine, [mine, self.side_in[which].at[0], self.side_in[which].at[1]], mine.shape[0])

    def hand_out_tall(self):
        home = self.at_home()

        @pl.when(home)
        def _():
            self.stay().start()

        @pl.when(jnp.logical_not(home))
        def _():
            self.swap().start()

    def hand_out_wide(self):
        @pl.loop(1, 8)
        def _(step):
            for i in range(3):
                self.deal(step, i).start()

        for i in range(3):
            self.keep(i).start()

    def finish(self):
        home = self.at_home()

        @pl.when(home)
        def _():
            self.stay().wait()

        @pl.when(jnp.logical_not(home))
        def _():
            self.swap().wait()

        for i in range(3):
            self.keep(i).wait()

        @pl.loop(1, 8)
        def _(step):
            col = (self.p.col + step) % 8
            landed = self.acc[0].at[0, pl.ds(0, self.rows)]
            remote(
                landed, landed, self.send.at[0], self.recv.at[8 + col], self.p.at(0, 1 - self.p.blk)
            ).wait_recv()
            for i in range(3):
                self.deal(step, i).wait_send()

        for which in (1, 0):
            for k in (1, 2):
                self.corner(which, k).wait_send()
                self.side(which, k).wait_send()

    def steps(self):
        idle = lambda: None
        return [self.begin, self.sides, idle, idle, self.total, idle, idle, idle, idle, idle, idle, idle, idle, idle, idle, idle, self.finish]


class DealFlow:
    def __init__(self, place, src, out, send, recv, local):
        self.p, self.src, self.out, self.send, self.recv, self.local = place, src, out, send, recv, local
        self.me = (place.dp * 2 + place.blk) * 4 + place.z

    def copy(self, step):
        to = (self.me + step) % 32
        return remote(
            self.src.at[to], self.out.at[self.me], self.send.at[step], self.recv.at[self.me], (to // 8, (to // 4) % 2, to % 4)
        )

    def keep(self):
        return pltpu.make_async_copy(self.src.at[self.me], self.out.at[self.me], self.local.at[0])

    def begin(self):
        self.keep().start()

        @pl.loop(1, 32)
        def _(step):
            self.copy(step).start()

    def finish(self):
        self.keep().wait()

        @pl.loop(1, 32)
        def _(step):
            landed = self.out.at[(self.me + step) % 32]
            remote(
                landed,
                landed,
                self.send.at[0],
                self.recv.at[(self.me + step) % 32],
                self.p.at(0, 1 - self.p.blk),
            ).wait_recv()
            self.copy(step).wait_send()

    @staticmethod
    def scratch():
        return [pltpu.SemaphoreType.DMA((32,)), pltpu.SemaphoreType.DMA((32,)), pltpu.SemaphoreType.DMA((1,))]

    def steps(self, length=18):
        return [self.begin] + [lambda: None] * (length - 2) + [self.finish]


def hbm_call(kernel, shapes, scratch, name, collective_id, args, aliases=None, in_vmem=(), out_vmem=()):
    return pl.pallas_call(
        kernel,
        out_shape=shapes,
        in_specs=[
            pl.BlockSpec(memory_space=pltpu.VMEM if i in in_vmem else pl.ANY) for i in range(len(args))
        ],
        out_specs=[
            pl.BlockSpec(memory_space=pltpu.VMEM if i in out_vmem else pl.ANY) for i in range(len(shapes))
        ],
        scratch_shapes=scratch,
        input_output_aliases=aliases or {},
        compiler_params=pltpu.CompilerParams(
            collective_id=collective_id, has_side_effects=True, vmem_limit_bytes=VMEM_BYTES
        ),
        name=name,
    )(*args)


def gather_sems():
    return [pltpu.SemaphoreType.DMA((GatherFlow.SENDS,)), pltpu.SemaphoreType.DMA((GatherFlow.RECVS,))]


def plane_sems(count):
    return gather_sems() + [pltpu.SemaphoreType.DMA((count,))]


def opening_call(tokens, small, cotangent, query_weight, key_weight, value_weight, output_weight):
    width = tokens.shape[1]
    rows = query_weight.shape[0]

    def kernel(tok, sml, cot, wq, wk, wv, wo, tok_out, sml_out, cot_out, wide, tall, *sems):
        place = Place()
        entry_barrier(place, "all")
        weights = ColumnsFlow(place, (wq, wk, wv), wo, wide, tall, *sems[7:10])
        line = GatherFlow(place, tok, tok_out, sems[0], sems[1], False)
        params = GatherFlow(place, sml, sml_out, sems[2], sems[3], True, True)
        plane = PlaneFlow(place, [(place.z, cot)], cot_out, *sems[4:7])
        params.begin()
        weights.begin()
        for d in range(1, 4):
            params.along(d)
        plane.begin()
        for d in range(4):
            params.turn(d)
        weights.settle(3)
        weights.settle(0)
        plane.turns()
        weights.settle(1)
        line.begin()
        weights.turns(3)
        for d in range(4):
            params.corner(d)
        plane.corners()
        weights.settle(2)
        weights.turns(0)
        line.along(1)
        weights.turns(1)
        params.finish()
        line.along(2)
        weights.turns(2)
        line.along(3)
        plane.finish()
        line.finish()
        weights.finish()

    shapes = [
        jax.ShapeDtypeStruct((8,) + tokens.shape, tokens.dtype),
        jax.ShapeDtypeStruct((32,) + small.shape, small.dtype),
        jax.ShapeDtypeStruct((32,) + cotangent.shape, cotangent.dtype),
        jax.ShapeDtypeStruct((32 * rows, 3 * width // 8), tokens.dtype),
        jax.ShapeDtypeStruct((4 * rows, width), tokens.dtype),
    ]
    scratch = gather_sems() * 2 + plane_sems(1)
    scratch += [
        pltpu.SemaphoreType.DMA((ColumnsFlow.SENDS,)),
        pltpu.SemaphoreType.DMA((ColumnsFlow.RECVS,)),
        pltpu.SemaphoreType.DMA((ColumnsFlow.LOCALS,)),
    ]
    return hbm_call(
        kernel,
        shapes,
        scratch,
        "opening",
        1,
        (tokens, small, cotangent, query_weight, key_weight, value_weight, output_weight),
    )


def attention_call(tokens_all, gains, wide, tall, head_gains, cosine, sine, cotangent, gathered):
    count, tok_rows, width = tokens_all.shape
    rows = count * tok_rows
    share = tall.shape[0]
    heads = share // HEAD_DIM
    block = 2 * tok_rows
    blocks = rows // block
    scale = 1.0 / math.sqrt(HEAD_DIM)
    bf16, f32 = jnp.bfloat16, jnp.float32
    line = ScatterFlow.scratch(tok_rows, width, bf16, False)

    def kernel(tok, gain, wide_in, tall_in, head_gain, cos, sin, cot, _, *refs):
        outs, scratch = refs[:8], refs[8:]
        normed_out, unit_out, row_out, context_out, scale_out, log_out, attended, gathered_out = outs
        held, wide_ref, tall_ref, normed, unit, qkv, context, part, sums, landed = scratch[:10]
        ins, stores, send, recv = scratch[10:14]
        place = Place()
        entry_barrier(place, "all")
        flow = ScatterFlow(place, part, attended, scratch[14 : 14 + len(line)], False)
        others = GatherFlow(
            place, cot, gathered_out, scratch[-2], scratch[-1], True, others=True
        )

        def block_in(i):
            return pltpu.make_async_copy(tok.at[pl.ds(2 * i, 2)], held.at[i], ins.at[i])

        weights = [
            pltpu.make_async_copy(wide_in, wide_ref, ins.at[blocks]),
            pltpu.make_async_copy(tall_in, tall_ref, ins.at[blocks + 1]),
        ]
        for i in range(blocks):
            block_in(i).start()
        for copy in weights:
            copy.start()
        for copy in weights:
            copy.wait()
        sums[...] = jnp.zeros_like(sums)

        @pl.loop(0, blocks)
        def _(i):
            block_in(i).wait()
            at = pl.ds(pl.multiple_of(i * block, block), block)
            values = held[i].reshape(block, width).astype(f32)
            mean = jnp.mean(values * values, axis=1, keepdims=True)
            low = (values * lax.rsqrt(mean + NORM_EPSILON) * gain[...]).astype(bf16)
            normed[at] = low
            linear = inner(low, wide_ref[...])
            unit[at] = linear[:, : 2 * share]
            qkv[at, 2 * share :] = linear[:, 2 * share :].astype(bf16)
            for n in range(2):
                part_lin = linear[:, n * share : (n + 1) * share]
                sums[n : n + 1, at] = jnp.sum(jnp.transpose(part_lin * part_lin), axis=0, keepdims=True)

        def exchange(step):
            to = (place.col + step) % 8
            return remote(
                sums, landed.at[place.col], send.at[step], recv.at[place.col], (place.dp, to // 4, to % 4)
            )

        @pl.loop(1, 8)
        def _(step):
            exchange(step).start()

        landed[place.col] = sums[...]

        @pl.loop(1, 8)
        def _(step):
            col = (place.col + step) % 8
            remote(sums, landed.at[col], send.at[0], recv.at[col], place.at(0, 1 - place.blk)).wait_recv()
            exchange(step).wait_send()

        others.begin()
        total = landed[0]
        for col in range(1, 8):
            total = total + landed[col]
        scales = jnp.transpose(lax.rsqrt(total / width + NORM_EPSILON))
        scale_out[...] = scales

        @pl.loop(0, blocks)
        def _(i):
            at = pl.ds(pl.multiple_of(i * block, block), block)
            for n in range(2):
                for h in range(heads):
                    lanes = pl.ds(n * share + h * HEAD_DIM, HEAD_DIM)
                    mine = unit[at, lanes] * scale_out[at, n : n + 1]
                    unit[at, lanes] = mine
                    scaled = mine * head_gain[n : n + 1, h * HEAD_DIM : (h + 1) * HEAD_DIM]
                    turned = scaled * cos[at] + pltpu.roll(scaled, HEAD_DIM // 2, 1) * sin[at]
                    qkv[at, lanes] = turned.astype(bf16)

        out_copies = [
            pltpu.make_async_copy(src, dst, stores.at[n])
            for n, (src, dst) in enumerate(((normed, normed_out), (unit, unit_out), (qkv, row_out)))
        ]
        for copy in out_copies:
            copy.start()
        for h in range(heads):
            for i in range(blocks):
                seen = (i + 1) * block
                queries = qkv[i * block : seen, h * HEAD_DIM : (h + 1) * HEAD_DIM]
                keys = qkv[:seen, share + h * HEAD_DIM : share + (h + 1) * HEAD_DIM]
                values = qkv[:seen, 2 * share + h * HEAD_DIM : 2 * share + (h + 1) * HEAD_DIM]
                scores = inner(queries, keys, 1, 1) * scale
                row = lax.broadcasted_iota(jnp.int32, scores.shape, 0) + i * block
                column = lax.broadcasted_iota(jnp.int32, scores.shape, 1)
                scores = jnp.where(column <= row, scores, MASKED)
                peak = jnp.max(scores, axis=1, keepdims=True)
                exponent = jnp.exp(scores - peak)
                sum_row = jnp.sum(exponent, axis=1, keepdims=True)
                low = (exponent / sum_row).astype(bf16)
                context[i * block : seen, h * HEAD_DIM : (h + 1) * HEAD_DIM] = inner(low, values).astype(bf16)
                log_out[i * block : seen, h : h + 1] = peak + jnp.log(sum_row)
            if h == 0:
                others.along(1)

        @pl.loop(0, blocks)
        def _(i):
            at = pl.ds(pl.multiple_of(i * block, block), block)
            rows_here = inner(context[at], tall_ref[...]).astype(bf16)
            part[pl.ds(2 * i, 2)] = rows_here.reshape(2, tok_rows, width)

        last = pltpu.make_async_copy(context, context_out, stores.at[3])
        last.start()
        flow.begin()
        others.along(2)
        flow.stage3(0)
        flow.stage3(1)
        flow.chain(0)
        others.along(3)
        others.turn(1)
        flow.stage3(2)
        flow.chain(1)
        flow.chain(2)
        others.turn(2)
        others.corner(1)
        flow.stage3(3)
        flow.final()
        others.turn(3)
        others.corner(2)
        others.corner(3)
        others.finish()
        for copy in out_copies + [last]:
            copy.wait()

    shapes = [
        jax.ShapeDtypeStruct((rows, width), bf16),
        jax.ShapeDtypeStruct((rows, 2 * share), f32),
        jax.ShapeDtypeStruct((rows, 3 * share), bf16),
        jax.ShapeDtypeStruct((rows, share), bf16),
        jax.ShapeDtypeStruct((rows, 8), f32),
        jax.ShapeDtypeStruct((rows, 8), f32),
        jax.ShapeDtypeStruct((tok_rows, width), f32),
        jax.ShapeDtypeStruct(gathered.shape, gathered.dtype),
    ]
    scratch = [
        pltpu.VMEM((blocks, 2, tok_rows, width), bf16),
        pltpu.VMEM(wide.shape, bf16),
        pltpu.VMEM(tall.shape, bf16),
        pltpu.VMEM((rows, width), bf16),
        pltpu.VMEM((rows, 2 * share), f32),
        pltpu.VMEM((rows, 3 * share), bf16),
        pltpu.VMEM((rows, share), bf16),
        pltpu.VMEM((8, tok_rows, width), bf16),
        pltpu.VMEM((8, rows), f32),
        pltpu.VMEM((8, 8, rows), f32),
        pltpu.SemaphoreType.DMA((blocks + 2,)),
        pltpu.SemaphoreType.DMA((4,)),
        pltpu.SemaphoreType.DMA((8,)),
        pltpu.SemaphoreType.DMA((8,)),
    ]
    args = (tokens_all, gains, wide, tall, head_gains, cosine, sine, cotangent, gathered)
    return hbm_call(
        kernel, shapes, scratch + line + gather_sems(), "attention", 5, args, {8: 7}, (1, 4, 5, 6), (4, 5)
    )


def run_units(work, first, last):
    @pl.loop(first, last)
    def _(unit):
        work.run(unit)


def features_call(features, probs, places, cotangent_all, down_weight, per):
    experts, hidden, width = down_weight.shape
    slots = places.shape[0] * per

    def kernel(feature_ref, prob_ref, place_ref, cot, weight, feature_out, prob_out, rows, plain, *scratch):
        place = Place()
        entry_barrier(place, "planes")
        small = GatherFlow(place, prob_ref, prob_out, scratch[2], scratch[3], True)
        flow = GatherFlow(place, feature_ref, feature_out, scratch[0], scratch[1], True)
        work = PickWork(place_ref, cot, weight, rows, plain, scratch[4:])

        flows = (small, flow)

        def along(d):
            for each in flows:
                each.along(d)

        def turn(d):
            for each in flows:
                each.turn(d)

        def corner(d):
            for each in flows:
                each.corner(d)

        for each in flows:
            each.begin()
        work.begin()
        run_units(work, 0, 4)
        along(1)
        turn(0)
        run_units(work, 4, 9)
        along(2)
        corner(0)
        run_units(work, 9, 13)
        along(3)
        turn(1)
        run_units(work, 13, work.units)
        corner(1)
        turn(2)
        corner(2)
        turn(3)
        corner(3)
        for each in flows:
            each.finish()
        work.finish()

    shapes = [
        jax.ShapeDtypeStruct((32,) + features.shape, features.dtype),
        jax.ShapeDtypeStruct((32,) + probs.shape, probs.dtype),
        jax.ShapeDtypeStruct((experts, slots, width), features.dtype),
        jax.ShapeDtypeStruct((experts, slots, hidden), jnp.float32),
    ]
    scratch = gather_sems() * 2 + PickWork.scratch(cotangent_all, down_weight, per)
    return hbm_call(
        kernel, shapes, scratch, "features", 6, (features, probs, places, cotangent_all, down_weight), None, (2,)
    )


def experts_back_call(part, dealt, places, hidden, weight):
    sums = ScatterFlow.scratch(part.shape[1], part.shape[2], part.dtype, True)
    out_shape = jax.ShapeDtypeStruct((places.shape[0], places.shape[2], part.shape[2]), part.dtype)

    def kernel(part_ref, dealt_ref, place_ref, hidden_ref, weight_ref, out, dealt_out, mixed, *scratch):
        place = Place()
        entry_barrier(place, "all")
        deal = DealFlow(place, dealt_ref, dealt_out, *scratch[:3])
        flow = ScatterFlow(place, part_ref, out, scratch[3 : 3 + len(sums)], True)
        work = OutputWork(place_ref, hidden_ref, weight_ref, mixed, scratch[3 + len(sums) :])
        deal.begin()
        flow.begin()
        work.begin()
        for i in range(4):
            flow.stage1(i)
        run_units(work, 0, 8)
        flow.stage2(0)
        flow.stage2(1)
        run_units(work, 8, 12)
        flow.stage2(2)
        flow.stage2(3)
        run_units(work, 12, 16)
        flow.stage3(0)
        flow.stage3(1)
        flow.chain(0)
        run_units(work, 16, 20)
        flow.stage3(2)
        flow.chain(1)
        flow.chain(2)
        run_units(work, 20, work.units)
        flow.stage3(3)
        flow.final()
        work.finish()
        deal.finish()

    shapes = [
        jax.ShapeDtypeStruct(part.shape[1:], jnp.float32),
        jax.ShapeDtypeStruct(dealt.shape, dealt.dtype),
        out_shape,
    ]
    scratch = DealFlow.scratch() + sums + OutputWork.scratch(hidden, weight, out_shape)
    return hbm_call(
        kernel, shapes, scratch, "experts_back", 3, (part, dealt, places, hidden, weight), None, (2,)
    )


def attention_back_call(
    grad, logit_grad, out_part, tokens, gain, feature_row, wide, tall, head_gains, cosine, sine, kept
):
    tok_rows, width = grad.shape
    rows = kept[0].shape[0]
    share = tall.shape[0]
    heads = share // HEAD_DIM
    own_rows = width // 32
    block = 2 * tok_rows
    blocks = rows // block
    band_rows = width // 4
    height = tok_rows // 2
    scale = 1.0 / math.sqrt(HEAD_DIM)
    bf16, f32 = jnp.bfloat16, jnp.float32
    line = ScatterFlow.scratch(tok_rows, width, bf16, False)
    mixed = ScatterFlow.scratch(height, width, bf16, True)
    sums = SumsFlow.scratch((band_rows, 3 * share), (share // 4, width))
    flow_scratch = line + mixed + mixed[-3:] + sums + DealFlow.scratch() + gather_sems() * 2
    flow_scratch += [pltpu.SemaphoreType.REGULAR]

    def kernel(*refs):
        grad_ref, logit_ref, part_ref, tok_in, gain_ref, feature_ref, wide_in, tall_in = refs[:8]
        head_gain, cos, sin, normed_in, unit_in, qkv_in, context_in, scale_ref, log_ref = refs[8:17]
        logit_out, first_out, second_out, normed_grad, wide_out, tall_out, gain_out = refs[17:24]
        scratch = refs[24:]
        grads, tok, wide_ref, tall_ref, normed, unit, qkv, context, context_grad = scratch[:9]
        grad_q, grad_k, grad_v, low_grads, dots, landed, deals, dealt, tall_grad = scratch[9:18]
        ins, send, recv = scratch[18:21]
        rest = list(scratch[21:])

        def take(count):
            taken = rest[:count]
            del rest[:count]
            return taken

        place = Place()
        entry_barrier(place, "all")
        line_scratch, mixed_scratch, more = take(len(line)), take(len(mixed)), take(3)
        weights = SumsFlow(place, wide_out, tall_out, take(len(sums)))
        deal = DealFlow(place, deals, dealt, *take(3))
        gather = GatherFlow(place, grad_ref, grads, *take(2), False)
        logits = GatherFlow(place, logit_ref, logit_out, *take(2), True)
        freed = take(1)[0]
        flow = ScatterFlow(place, grads, normed_grad, line_scratch, False)
        first = ScatterFlow(place, part_ref, first_out, mixed_scratch, True, (0, height))
        second = ScatterFlow(
            place, part_ref, second_out, mixed_scratch[:-3] + more, True, (height, height)
        )
        gather.begin()
        logits.begin()
        first.begin()
        sources = (tok_in, wide_in, tall_in, normed_in, unit_in, qkv_in, context_in)
        held = (tok, wide_ref, tall_ref, normed, unit, qkv, context)
        loads = [pltpu.make_async_copy(s, d, ins.at[n]) for n, (s, d) in enumerate(zip(sources, held))]
        for copy in loads:
            copy.start()
        deals[...] = jnp.zeros_like(deals)
        dots[...] = jnp.zeros_like(dots)
        first.stage1(0)
        first.stage1(1)
        gather.along(1)
        logits.along(1)
        logits.turn(0)
        first.stage1(2)
        first.stage1(3)
        first.stage2(0)
        gather.along(2)
        logits.along(2)
        logits.turn(1)
        first.stage2(1)
        first.stage2(2)
        gather.along(3)
        logits.along(3)
        logits.turn(2)
        logits.turn(3)
        first.stage3(0)
        first.stage2(3)
        first.stage3(1)
        first.chain(0)
        for d in range(4):
            logits.corner(d)
        gather.finish()
        for copy in loads:
            copy.wait()

        @pl.loop(0, blocks)
        def _(i):
            at = pl.ds(pl.multiple_of(i * block, block), block)
            values = grads[pl.ds(2 * i, 2)].reshape(block, width)
            context_grad[at] = inner(values, tall_ref[...], 1, 1).astype(bf16)

        first.stage3(2)
        first.chain(1)
        first.chain(2)
        first.stage3(3)

        @pl.loop(0, 4)
        def _(i):
            lanes = pl.ds(pl.multiple_of(i * band_rows, band_rows), band_rows)
            values = grads[:, :, lanes].reshape(rows, band_rows)
            tall_grad[:, lanes] = inner(context[...], values, 0, 0).astype(bf16)

        for k in range(4):
            at = pl.ds(pl.multiple_of(place.column(k) * own_rows, own_rows), own_rows)
            weights.acc[1][k] = tall_grad[at]
        first.final()
        tell_partners(place, freed)

        def back_block(h, i):
            seen = (i + 1) * block
            here, lanes = slice(i * block, seen), slice(h * HEAD_DIM, (h + 1) * HEAD_DIM)
            queries = qkv[here, lanes]
            keys = qkv[:seen, share + h * HEAD_DIM : share + (h + 1) * HEAD_DIM]
            values = qkv[:seen, 2 * share + h * HEAD_DIM : 2 * share + (h + 1) * HEAD_DIM]
            outer = context_grad[here, lanes]
            scores = inner(queries, keys, 1, 1) * scale
            row = lax.broadcasted_iota(jnp.int32, scores.shape, 0) + i * block
            column = lax.broadcasted_iota(jnp.int32, scores.shape, 1)
            probs = jnp.where(column <= row, jnp.exp(scores - log_ref[here, h : h + 1]), 0.0)
            prob_dots = inner(outer, values, 1, 1)
            delta = jnp.sum(probs * prob_dots, axis=1, keepdims=True)
            score_grad = (probs * (prob_dots - delta)).astype(bf16)
            grad_q[here, lanes] = inner(score_grad, keys) * scale
            key_part = inner(score_grad, queries, 0, 0) * scale
            value_part = inner(probs.astype(bf16), outer, 0, 0)
            if i == blocks - 1:
                grad_k[:, lanes] = key_part
                grad_v[:, lanes] = value_part
            else:
                grad_k[:seen, lanes] += key_part
                grad_v[:seen, lanes] += value_part

        back_block(0, 3)
        wait_partners(place, freed)
        second.begin()
        weights.corners(1)
        back_block(0, 2)
        for i in range(4):
            second.stage1(i)
        back_block(0, 1)
        back_block(0, 0)
        back_block(1, 3)
        second.stage2(0)
        weights.sides(1)
        back_block(1, 2)
        second.stage2(1)
        back_block(1, 1)
        second.stage2(2)
        back_block(1, 0)
        second.stage2(3)

        @pl.loop(0, blocks)
        def _(i):
            at = pl.ds(pl.multiple_of(i * block, block), block)
            low_grads[at, 2 * share :] = grad_v[at].astype(bf16)
            for n, grad_n in enumerate((grad_q, grad_k)):
                total = jnp.zeros((block, 1), f32)
                for h in range(heads):
                    lanes = slice(h * HEAD_DIM, (h + 1) * HEAD_DIM)
                    turned = grad_n[at, lanes].astype(bf16).astype(f32)
                    back = turned * cos[at] - pltpu.roll(turned, HEAD_DIM // 2, 1) * sin[at]
                    mine = unit[at, n * share + h * HEAD_DIM : n * share + (h + 1) * HEAD_DIM]
                    for j in range(HEAD_DIM // own_rows):
                        to = place.col * 4 + h * (HEAD_DIM // own_rows) + j
                        columns = slice(j * own_rows, (j + 1) * own_rows)
                        deals[to, 1 + n : 2 + n, :own_rows] += jnp.sum(
                            (back * mine)[:, columns], axis=0, keepdims=True
                        )
                    weighted = back * head_gain[n : n + 1, lanes]
                    grad_n[at, lanes] = weighted
                    total += jnp.sum(weighted * mine, axis=1, keepdims=True)
                dots[n : n + 1, at] = jnp.transpose(jnp.broadcast_to(total, (block, 128)))[:1]

        def exchange(step):
            to = (place.col + step) % 8
            return remote(
                dots, landed.at[place.col], send.at[step], recv.at[place.col], (place.dp, to // 4, to % 4)
            )

        @pl.loop(1, 8)
        def _(step):
            exchange(step).start()

        landed[place.col] = dots[...]
        second.stage3(0)

        @pl.loop(1, 8)
        def _(step):
            col = (place.col + step) % 8
            remote(dots, landed.at[col], send.at[0], recv.at[col], place.at(0, 1 - place.blk)).wait_recv()
            exchange(step).wait_send()

        total_dots = landed[0]
        for col in range(1, 8):
            total_dots = total_dots + landed[col]
        columns = jnp.transpose(total_dots / width)
        for n, grad_n in enumerate((grad_q, grad_k)):
            mine = unit[:, n * share : (n + 1) * share]
            low = scale_ref[:, n : n + 1] * (grad_n[...] - mine * columns[:, n : n + 1])
            low_grads[:, n * share : (n + 1) * share] = low.astype(bf16)

        def wide_grad(k):
            lanes = pl.ds(pl.multiple_of(place.column(k) * band_rows, band_rows), band_rows)
            weights.acc[0][k] = inner(normed[:, lanes], low_grads[...], 0, 0).astype(bf16)

        wide_grad(3)
        weights.corners(0)

        @pl.loop(0, blocks)
        def _(i):
            at = pl.ds(pl.multiple_of(i * block, block), block)
            values = inner(low_grads[at], wide_ref[...], 1, 1).astype(bf16)
            grads[pl.ds(2 * i, 2)] = values.reshape(2, tok_rows, width)

        flow.begin()
        wide_grad(2)
        wide_grad(1)
        second.stage3(1)
        second.chain(0)
        flow.stage3(0)
        weights.sides(0)
        flow.stage3(1)
        wide_grad(0)
        flow.chain(0)
        second.stage3(2)
        second.chain(1)
        second.chain(2)
        flow.stage3(2)
        flow.chain(1)
        weights.total(0)
        weights.hand_out_wide()
        flow.chain(2)
        flow.stage3(3)
        second.stage3(3)
        weights.total(1)
        weights.hand_out_tall()
        flow.final()

        values = tok[...].astype(f32)
        scaled = values * lax.rsqrt(jnp.mean(values * values, axis=1, keepdims=True) + NORM_EPSILON)
        attention_row = jnp.sum(scaled * flow.sum[...], axis=0, keepdims=True)
        for to in range(32):
            lanes = slice(to * own_rows, (to + 1) * own_rows)
            deals[to, 0:1, :own_rows] = attention_row[:, lanes]
            deals[to, 3:4, :own_rows] = feature_ref[:, lanes]
        deal.begin()
        second.final()
        logits.finish()
        weights.finish()
        deal.finish()
        total = dealt[0]
        for index in range(1, 32):
            total = total + dealt[index]
        gain_out[...] = total

    shapes = [
        jax.ShapeDtypeStruct((32,) + logit_grad.shape, logit_grad.dtype),
        jax.ShapeDtypeStruct((height, width), f32),
        jax.ShapeDtypeStruct((height, width), f32),
        jax.ShapeDtypeStruct((tok_rows, width), f32),
        jax.ShapeDtypeStruct((3, own_rows, width), bf16),
        jax.ShapeDtypeStruct((own_rows, width), bf16),
        jax.ShapeDtypeStruct((8, 128), f32),
    ]
    scratch = [
        pltpu.VMEM((8, tok_rows, width), bf16),
        pltpu.VMEM((tok_rows, width), bf16),
        pltpu.VMEM(wide.shape, bf16),
        pltpu.VMEM(tall.shape, bf16),
        pltpu.VMEM((rows, width), bf16),
        pltpu.VMEM((rows, 2 * share), f32),
        pltpu.VMEM((rows, 3 * share), bf16),
        pltpu.VMEM((rows, share), bf16),
        pltpu.VMEM((rows, share), bf16),
        pltpu.VMEM((rows, share), f32),
        pltpu.VMEM((rows, share), f32),
        pltpu.VMEM((rows, share), f32),
        pltpu.VMEM((rows, 3 * share), bf16),
        pltpu.VMEM((8, rows), f32),
        pltpu.VMEM((8, 8, rows), f32),
        pltpu.VMEM((32, 8, 128), f32),
        pltpu.VMEM((32, 8, 128), f32),
        pltpu.VMEM(tall.shape, bf16),
        pltpu.SemaphoreType.DMA((7,)),
        pltpu.SemaphoreType.DMA((8,)),
        pltpu.SemaphoreType.DMA((8,)),
    ]
    args = (grad, logit_grad, out_part, tokens, gain, feature_row, wide, tall, head_gains, cosine, sine)
    return hbm_call(
        kernel,
        shapes,
        scratch + flow_scratch,
        "attention_back",
        2,
        args + tuple(kept),
        None,
        (4, 5, 8, 9, 10, 15, 16),
        (6,),
    )


def product(left, right, sums, batches=((), ()), out=jnp.float32):
    return lax.dot_general(left, right, (sums, batches), preferred_element_type=out)


def body_fast(
    tokens,
    query_weight,
    key_weight,
    value_weight,
    output_weight,
    router_weight,
    attention_gain,
    query_gain,
    key_gain,
    feature_gain,
    gate_weight,
    up_weight,
    down_weight,
    routes,
    cotangent,
):
    tok_rows, model_width = tokens.shape
    column_size = 8
    devices = 32
    share = model_width // column_size
    heads_here = share // HEAD_DIM
    seq_rows = tok_rows * column_size
    experts_here = gate_weight.shape[0]
    own_rows = query_weight.shape[0]
    score_scale = 1.0 / math.sqrt(HEAD_DIM)
    column = lax.axis_index(BLK) * 4 + lax.axis_index(SP)
    f32, bf16 = jnp.float32, jnp.bfloat16

    gains = jnp.stack([attention_gain, query_gain, key_gain, feature_gain])
    named_here = routes.astype(bf16).reshape(own_rows, tok_rows * TOPK // own_rows)
    filled = EXPERTS + named_here.shape[1]
    small = jnp.concatenate([router_weight, named_here], axis=1)
    small = jnp.concatenate([small, jnp.pad(gains, ((0, 28), (0, filled - own_rows)))], axis=0)
    small = jnp.pad(small, ((0, 0), (0, 128 - filled)))
    tokens_all, small_all, cotangent_all, wide_weight, tall_weight = opening_call(
        tokens, small, cotangent, query_weight, key_weight, value_weight, output_weight
    )
    routes_all = small_all[:, :own_rows, EXPERTS:filled].astype(jnp.int32).reshape(devices, tok_rows, TOPK)
    router_full = small_all[:, :own_rows, :EXPERTS].reshape(model_width, EXPERTS)
    gain_all = small_all[:, own_rows : own_rows + 4, :own_rows].astype(f32)
    gain_all = gain_all.transpose(1, 0, 2).reshape(4, model_width)
    gain_attention, gain_feature = gain_all[0], gain_all[3]
    head_gains = lax.dynamic_slice_in_dim(gain_all[1:3], column * share, share, axis=1)

    half_cos, half_sin = rope_tables(jnp.arange(seq_rows, dtype=jnp.int32), HEAD_DIM)
    cosine = jnp.concatenate([half_cos, half_cos], axis=1)
    sine = jnp.concatenate([-half_sin, half_sin], axis=1)
    *kept, attended, cotangent_all = attention_call(
        tokens_all,
        gain_attention[None],
        wide_weight,
        tall_weight,
        head_gains,
        cosine,
        sine,
        cotangent,
        cotangent_all,
    )
    tokens_f = tokens.astype(f32)
    residual = tokens_f + attended
    features_f, feature_pull = jax.vjp(norm_apply, residual, gain_feature)
    features = features_f.astype(bf16)
    logits = jnp.dot(features, router_full, preferred_element_type=f32)
    router_probs = jax.nn.softmax(logits, axis=-1)

    first_expert = (lax.axis_index(DP) * 4 + lax.axis_index(SP)) * experts_here
    expert_ids = first_expert + jnp.arange(experts_here, dtype=jnp.int32)
    named = jnp.any(routes_all[:, None] == expert_ids[None, :, None, None], axis=3)
    earlier = (jnp.arange(tok_rows)[:, None] < jnp.arange(tok_rows)[None, :]).astype(bf16)
    rank = product(named.astype(bf16), earlier, ((2,), (0,))).astype(jnp.int32)
    pairs, pair_rows, per = devices // 2, 2 * tok_rows, 2 * CAP
    places = jnp.where(named, rank, -per).reshape(pairs, 2, experts_here, tok_rows)
    places = places + CAP * jnp.arange(2, dtype=jnp.int32)[None, :, None, None]
    places = places.transpose(0, 2, 1, 3).reshape(pairs, experts_here, pair_rows)
    cotangent_all = cotangent_all.reshape(pairs, pair_rows, model_width)
    features_all, probs_all, grad_rows, plain_grads = features_call(
        features, router_probs.T, places, cotangent_all, down_weight, per
    )
    probs_here = lax.dynamic_slice_in_dim(probs_all, first_expert, experts_here, axis=1)
    features_all = features_all.reshape(pairs, pair_rows, model_width)
    expert_rows, row_probs = pick_rows(places, probs_here, features_all, per)
    weighted_hidden, gate_grad, up_grad, input_rows, row_grads = run_experts(
        expert_rows, plain_grads, row_probs, gate_weight, up_weight
    )
    input_part, token_grad = put_rows_back(places, input_rows, row_grads)
    input_part = input_part.reshape(devices, tok_rows, model_width)
    input_grad, prob_parts, out_part = experts_back_call(
        input_part, token_grad, places, weighted_hidden, down_weight
    )
    out_part = out_part.reshape(devices, tok_rows, model_width)

    prob_parts = prob_parts.reshape(4, 2, 4, 8, tok_rows)[:, :, :, :experts_here]
    prob_grad = jnp.sum(prob_parts, axis=1).reshape(EXPERTS, tok_rows).T
    logit_grad = (
        router_probs * (prob_grad - jnp.sum(prob_grad * router_probs, axis=-1, keepdims=True))
    ).astype(bf16)
    feature_grad = jnp.dot(logit_grad, router_full.T, preferred_element_type=f32) + input_grad
    residual_part, feature_gain_grad = feature_pull(feature_grad)
    residual_grad = cotangent.astype(f32) + residual_part
    attended_grad = residual_grad.astype(bf16)
    logit_all, first_half, second_half, normed_grad, wide_back, tall_back, gain_sums = attention_back_call(
        attended_grad,
        logit_grad.reshape(tok_rows // 2, 2 * EXPERTS),
        out_part,
        tokens,
        gain_attention[None],
        feature_gain_grad[None],
        wide_weight,
        tall_weight,
        head_gains,
        cosine,
        sine,
        kept,
    )
    own_index = (lax.axis_index(DP) * 2 + lax.axis_index(BLK)) * 4 + lax.axis_index(SP)
    own_features = lax.dynamic_slice_in_dim(
        features_all.reshape(devices * tok_rows, model_width), own_index * own_rows, own_rows, axis=1
    )
    router_grad = product(own_features, logit_all.reshape(devices * tok_rows, EXPERTS), ((0,), (0,)))

    _, attention_pull = jax.vjp(lambda values: norm_apply(values, gain_attention), tokens_f)
    input_gradient = residual_grad + attention_pull(normed_grad)[0]
    block_output = (residual + jnp.concatenate([first_half, second_half], axis=0)).astype(bf16)
    gate_grad_local, up_grad_local, down_grad_local = expert_weight_grads(
        expert_rows, grad_rows, weighted_hidden, gate_grad, up_grad
    )
    return (
        block_output,
        input_gradient,
        wide_back[0].astype(f32),
        wide_back[1].astype(f32),
        wide_back[2].astype(f32),
        tall_back.astype(f32),
        router_grad,
        gain_sums[0, :own_rows],
        gain_sums[1, :own_rows],
        gain_sums[2, :own_rows],
        gain_sums[3, :own_rows],
        gate_grad_local,
        up_grad_local,
        down_grad_local,
    )


def body(
    tokens,
    query_weight,
    key_weight,
    value_weight,
    output_weight,
    router_weight,
    attention_gain,
    query_gain,
    key_gain,
    feature_gain,
    gate_weight,
    up_weight,
    down_weight,
    routes,
    cotangent,
):
    sp_size = lax.axis_size(SP)
    blk_size = lax.axis_size(BLK)
    dp_size = lax.axis_size(DP)
    tok_rows = tokens.shape[0]
    model_width = tokens.shape[1]
    heads_here = HEADS // sp_size
    head_width = heads_here * HEAD_DIM
    experts_here = gate_weight.shape[0]
    capacity = CAP
    score_scale = 1.0 / math.sqrt(HEAD_DIM)
    (
        query_full,
        key_full,
        value_full,
        output_full,
        router_full,
        gain_attention,
        gain_query,
        gain_key,
        gain_feature,
    ) = (
        lax.all_gather(query_weight, AXES, axis=0, tiled=True),
        lax.all_gather(key_weight, AXES, axis=0, tiled=True),
        lax.all_gather(value_weight, AXES, axis=0, tiled=True),
        lax.all_gather(output_weight, AXES, axis=0, tiled=True),
        lax.all_gather(router_weight, AXES, axis=0, tiled=True),
        lax.all_gather(attention_gain, AXES, axis=0, tiled=True),
        lax.all_gather(query_gain, AXES, axis=0, tiled=True),
        lax.all_gather(key_gain, AXES, axis=0, tiled=True),
        lax.all_gather(feature_gain, AXES, axis=0, tiled=True),
    )
    gain_attention = gain_attention.astype(jnp.float32)
    gain_query = gain_query.astype(jnp.float32)
    gain_key = gain_key.astype(jnp.float32)
    gain_feature = gain_feature.astype(jnp.float32)
    tokens_f = tokens.astype(jnp.float32)
    normed_f, attention_pull = jax.vjp(norm_apply, tokens_f, gain_attention)
    normed = normed_f.astype(jnp.bfloat16)
    query_lin = jnp.dot(normed, query_full, preferred_element_type=jnp.float32)
    key_lin = jnp.dot(normed, key_full, preferred_element_type=jnp.float32)
    value_rows = jnp.dot(normed, value_full, preferred_element_type=jnp.float32).astype(
        jnp.bfloat16
    )
    seq_start = (lax.axis_index(BLK) * sp_size + lax.axis_index(SP)) * tok_rows
    cosine, sine = rope_tables(seq_start + jnp.arange(tok_rows, dtype=jnp.int32), HEAD_DIM)

    def rotated(linear, norm_gain):
        normalized = norm_apply(linear, norm_gain).reshape(
            tok_rows, model_width // HEAD_DIM, HEAD_DIM
        )
        return rotate(normalized, cosine, sine).reshape(tok_rows, model_width)

    query_rot, query_pull = jax.vjp(rotated, query_lin, gain_query)
    key_rot, key_pull = jax.vjp(rotated, key_lin, gain_key)
    query_heads, key_heads, value_heads = (
        lax.all_to_all(
            query_rot.astype(jnp.bfloat16).reshape(tok_rows, sp_size, head_width),
            SP,
            split_axis=1,
            concat_axis=0,
            tiled=True,
        ),
        lax.all_to_all(
            key_rot.astype(jnp.bfloat16).reshape(tok_rows, sp_size, head_width),
            SP,
            split_axis=1,
            concat_axis=0,
            tiled=True,
        ),
        lax.all_to_all(
            value_rows.reshape(tok_rows, sp_size, head_width),
            SP,
            split_axis=1,
            concat_axis=0,
            tiled=True,
        ),
    )
    head_rows = sp_size * tok_rows
    keys_all, values_all = (
        lax.all_gather(key_heads, BLK, axis=0, tiled=True),
        lax.all_gather(value_heads, BLK, axis=0, tiled=True),
    )
    key_rows = keys_all.shape[0]
    keys_all = keys_all.reshape(key_rows, heads_here, HEAD_DIM)
    values_all = values_all.reshape(key_rows, heads_here, HEAD_DIM)
    block_rows = math.gcd(512, head_rows)
    blocks = head_rows // block_rows
    query_base = lax.axis_index(BLK) * head_rows
    key_places = jnp.arange(key_rows, dtype=jnp.int32)
    query_blocks = query_heads.reshape(blocks, block_rows, heads_here, HEAD_DIM)
    block_starts = jnp.arange(blocks, dtype=jnp.int32) * block_rows

    def masked_scores(block_queries, block_start):
        scores = (
            jnp.einsum("qhd,khd->hqk", block_queries, keys_all, preferred_element_type=jnp.float32)
            * score_scale
        )
        query_places = query_base + block_start + jnp.arange(block_rows, dtype=jnp.int32)
        causal = key_places[None, :] <= query_places[:, None]
        return jnp.where(causal[None], scores, MASKED)

    def attend_block(block_input):
        block_queries, block_start = block_input
        scores = masked_scores(block_queries, block_start)
        row_peak = jnp.max(scores, axis=-1, keepdims=True)
        exponent = jnp.exp(scores - row_peak)
        row_total = jnp.sum(exponent, axis=-1, keepdims=True)
        attn_weights = (exponent / row_total).astype(jnp.bfloat16)
        context = jnp.einsum(
            "hqk,khd->qhd", attn_weights, values_all, preferred_element_type=jnp.float32
        )
        return (context.astype(jnp.bfloat16), (row_peak + jnp.log(row_total))[..., 0])

    context_blocks, logsum = lax.map(attend_block, (query_blocks, block_starts))
    context_rows = lax.all_to_all(
        context_blocks.reshape(head_rows, 1, head_width),
        SP,
        split_axis=0,
        concat_axis=1,
        tiled=True,
    ).reshape(tok_rows, model_width)
    attended = jnp.dot(context_rows, output_full, preferred_element_type=jnp.float32)
    residual = tokens_f + attended
    features_f, feature_pull = jax.vjp(norm_apply, residual, gain_feature)
    features = features_f.astype(jnp.bfloat16)
    logits = jnp.dot(features, router_full, preferred_element_type=jnp.float32)
    router_probs = jax.nn.softmax(logits, axis=-1)
    flat_experts, slot_rank = rank_slots(routes)
    slot_index = flat_experts * capacity + slot_rank
    token_of = jnp.arange(tok_rows * TOPK, dtype=jnp.int32) // TOPK
    slot_token = jnp.zeros((EXPERTS * capacity,), jnp.int32).at[slot_index].set(token_of)
    slot_used = jnp.zeros((EXPERTS * capacity,), jnp.bool_).at[slot_index].set(True)
    slot_rows = jnp.where(slot_used[:, None], features[slot_token], jnp.zeros((), jnp.bfloat16))

    def spread_halves(per_slot):
        grouped = per_slot.reshape(dp_size, 1, sp_size, experts_here, capacity, model_width)
        grouped = jnp.broadcast_to(
            grouped, (dp_size, blk_size, sp_size, experts_here, capacity, model_width)
        )
        return grouped.reshape(dp_size * blk_size * sp_size, experts_here, capacity, model_width)

    def join_halves(returned):
        grouped = returned.reshape(
            dp_size, blk_size, sp_size, experts_here, capacity, model_width
        ).astype(jnp.float32)
        return jnp.sum(grouped, axis=1).reshape(EXPERTS * capacity, model_width)

    send_rows = spread_halves(slot_rows)
    arrived = lax.all_to_all(
        send_rows, AXES, split_axis=0, concat_axis=0, tiled=True
    )
    gate_values = jnp.einsum(
        "secd,edf->secf", arrived, gate_weight, preferred_element_type=jnp.float32
    )
    up_values = jnp.einsum("secd,edf->secf", arrived, up_weight, preferred_element_type=jnp.float32)
    hidden = (jax.nn.silu(gate_values) * up_values).astype(jnp.bfloat16)
    part_out = jnp.einsum(
        "secf,efd->secd", hidden, down_weight, preferred_element_type=jnp.float32
    ).astype(jnp.bfloat16)
    returned = lax.all_to_all(
        part_out, AXES, split_axis=0, concat_axis=0, tiled=True
    )
    expert_out = join_halves(returned)
    route_rows = expert_out[slot_index].reshape(tok_rows, TOPK, model_width)
    route_probs = jnp.take_along_axis(router_probs, routes, axis=1)
    block_output = (residual + jnp.sum(route_probs[:, :, None] * route_rows, axis=1)).astype(
        jnp.bfloat16
    )
    out_grad = cotangent.astype(jnp.float32)
    route_grad = (
        (route_probs[:, :, None] * out_grad[:, None, :])
        .astype(jnp.bfloat16)
        .reshape(tok_rows * TOPK, model_width)
    )
    prob_route = jnp.sum(out_grad[:, None, :] * route_rows, axis=-1)
    expert_ids = jnp.arange(EXPERTS, dtype=jnp.int32)
    prob_grad = jnp.sum(
        jnp.where(routes[:, :, None] == expert_ids[None, None, :], prob_route[:, :, None], 0.0),
        axis=1,
    )
    logit_grad = (
        router_probs * (prob_grad - jnp.sum(prob_grad * router_probs, axis=-1, keepdims=True))
    ).astype(jnp.bfloat16)
    router_grad_full = jnp.dot(features.T, logit_grad, preferred_element_type=jnp.float32)
    gradient_slots = (
        jnp.zeros((EXPERTS * capacity, model_width), jnp.bfloat16).at[slot_index].set(route_grad)
    )
    gradient_send = spread_halves(gradient_slots)
    gradient_arrived, rows_arrived = (
        lax.all_to_all(gradient_send, AXES, split_axis=0, concat_axis=0, tiled=True),
        lax.all_to_all(send_rows, AXES, split_axis=0, concat_axis=0, tiled=True),
    )
    gate_values = jnp.einsum(
        "secd,edf->secf", rows_arrived, gate_weight, preferred_element_type=jnp.float32
    )
    up_values = jnp.einsum(
        "secd,edf->secf", rows_arrived, up_weight, preferred_element_type=jnp.float32
    )
    sigmoid_values = jax.nn.sigmoid(gate_values)
    silu_values = gate_values * sigmoid_values
    hidden = (silu_values * up_values).astype(jnp.bfloat16)
    hidden_grad = jnp.einsum(
        "secd,efd->secf", gradient_arrived, down_weight, preferred_element_type=jnp.float32
    ).astype(jnp.bfloat16)
    down_grad_local = jnp.einsum(
        "secf,secd->efd", hidden, gradient_arrived, preferred_element_type=jnp.float32
    )
    hidden_wide = hidden_grad.astype(jnp.float32)
    gate_grad = (
        hidden_wide * up_values * sigmoid_values * (1.0 + gate_values * (1.0 - sigmoid_values))
    ).astype(jnp.bfloat16)
    up_grad = (hidden_wide * silu_values).astype(jnp.bfloat16)
    gate_grad_local = jnp.einsum(
        "secd,secf->edf", rows_arrived, gate_grad, preferred_element_type=jnp.float32
    )
    up_grad_local = jnp.einsum(
        "secd,secf->edf", rows_arrived, up_grad, preferred_element_type=jnp.float32
    )
    input_parts = (
        jnp.einsum("secf,edf->secd", gate_grad, gate_weight, preferred_element_type=jnp.float32)
        + jnp.einsum("secf,edf->secd", up_grad, up_weight, preferred_element_type=jnp.float32)
    ).astype(jnp.bfloat16)
    returned_grads = lax.all_to_all(
        input_parts, AXES, split_axis=0, concat_axis=0, tiled=True
    )
    slot_input_grad = join_halves(returned_grads)
    expert_input_grad = slot_input_grad[slot_index].reshape(tok_rows, TOPK, model_width)
    feature_grad = jnp.dot(logit_grad, router_full.T, preferred_element_type=jnp.float32) + jnp.sum(
        expert_input_grad, axis=1
    )
    residual_part, feature_gain_grad = feature_pull(feature_grad)
    residual_grad = out_grad + residual_part
    attended_grad = residual_grad.astype(jnp.bfloat16)
    output_grad_full = jnp.dot(context_rows.T, attended_grad, preferred_element_type=jnp.float32)
    context_grad = jnp.dot(attended_grad, output_full.T, preferred_element_type=jnp.float32).astype(
        jnp.bfloat16
    )
    context_heads_grad = lax.all_to_all(
        context_grad.reshape(tok_rows, sp_size, head_width),
        SP,
        split_axis=1,
        concat_axis=0,
        tiled=True,
    )
    context_heads_grad = context_heads_grad.reshape(blocks, block_rows, heads_here, HEAD_DIM)

    def backward_block(carry, block_input):
        key_total, value_total = carry
        block_queries, block_grads, block_logsum, block_start = block_input
        scores = masked_scores(block_queries, block_start)
        attn_weights = jnp.exp(scores - block_logsum[..., None])
        prob_dots = jnp.einsum(
            "qhd,khd->hqk", block_grads, values_all, preferred_element_type=jnp.float32
        )
        row_delta = jnp.sum(attn_weights * prob_dots, axis=-1, keepdims=True)
        score_grad = (attn_weights * (prob_dots - row_delta)).astype(jnp.bfloat16)
        query_grad = (
            jnp.einsum("hqk,khd->qhd", score_grad, keys_all, preferred_element_type=jnp.float32)
            * score_scale
        )
        key_total = (
            key_total
            + jnp.einsum(
                "hqk,qhd->khd", score_grad, block_queries, preferred_element_type=jnp.float32
            )
            * score_scale
        )
        value_total = value_total + jnp.einsum(
            "hqk,qhd->khd",
            attn_weights.astype(jnp.bfloat16),
            block_grads,
            preferred_element_type=jnp.float32,
        )
        return ((key_total, value_total), query_grad.astype(jnp.bfloat16))

    zero_keys = jnp.zeros((key_rows, heads_here, HEAD_DIM), jnp.float32)
    (key_total, value_total), query_grads = lax.scan(
        backward_block,
        (zero_keys, zero_keys),
        (query_blocks, context_heads_grad, logsum, block_starts),
    )
    key_mine, value_mine = (
        lax.psum_scatter(key_total, BLK, scatter_dimension=0, tiled=True),
        lax.psum_scatter(value_total, BLK, scatter_dimension=0, tiled=True),
    )
    query_back, key_back, value_back = (
        lax.all_to_all(
            query_grads.reshape(head_rows, 1, head_width),
            SP,
            split_axis=0,
            concat_axis=1,
            tiled=True,
        ),
        lax.all_to_all(
            key_mine.astype(jnp.bfloat16).reshape(head_rows, 1, head_width),
            SP,
            split_axis=0,
            concat_axis=1,
            tiled=True,
        ),
        lax.all_to_all(
            value_mine.astype(jnp.bfloat16).reshape(head_rows, 1, head_width),
            SP,
            split_axis=0,
            concat_axis=1,
            tiled=True,
        ),
    )
    query_lin_grad, query_gain_grad = query_pull(
        query_back.reshape(tok_rows, model_width).astype(jnp.float32)
    )
    key_lin_grad, key_gain_grad = key_pull(
        key_back.reshape(tok_rows, model_width).astype(jnp.float32)
    )
    query_lin_low = query_lin_grad.astype(jnp.bfloat16)
    key_lin_low = key_lin_grad.astype(jnp.bfloat16)
    value_low = value_back.reshape(tok_rows, model_width)
    query_grad_full = jnp.dot(normed.T, query_lin_low, preferred_element_type=jnp.float32)
    key_grad_full = jnp.dot(normed.T, key_lin_low, preferred_element_type=jnp.float32)
    value_grad_full = jnp.dot(normed.T, value_low, preferred_element_type=jnp.float32)
    normed_grad = jnp.dot(query_lin_low, query_full.T, preferred_element_type=jnp.float32)
    normed_grad = normed_grad + jnp.dot(key_lin_low, key_full.T, preferred_element_type=jnp.float32)
    normed_grad = normed_grad + jnp.dot(value_low, value_full.T, preferred_element_type=jnp.float32)
    tokens_part, attention_gain_grad = attention_pull(normed_grad)
    input_gradient = residual_grad + tokens_part
    summed = (
        lax.psum_scatter(query_grad_full, AXES, scatter_dimension=0, tiled=True),
        lax.psum_scatter(key_grad_full, AXES, scatter_dimension=0, tiled=True),
        lax.psum_scatter(value_grad_full, AXES, scatter_dimension=0, tiled=True),
        lax.psum_scatter(output_grad_full, AXES, scatter_dimension=0, tiled=True),
        lax.psum_scatter(router_grad_full, AXES, scatter_dimension=0, tiled=True),
        lax.psum_scatter(attention_gain_grad, AXES, scatter_dimension=0, tiled=True),
        lax.psum_scatter(query_gain_grad, AXES, scatter_dimension=0, tiled=True),
        lax.psum_scatter(key_gain_grad, AXES, scatter_dimension=0, tiled=True),
        lax.psum_scatter(feature_gain_grad, AXES, scatter_dimension=0, tiled=True),
    )
    return (
        block_output,
        input_gradient,
        summed[0],
        summed[1],
        summed[2],
        summed[3],
        summed[4],
        summed[5],
        summed[6],
        summed[7],
        summed[8],
        gate_grad_local,
        up_grad_local,
        down_grad_local,
    )


def solution(mesh):
    in_specs = (
        P(AXES, None),
        P(AXES, None),
        P(AXES, None),
        P(AXES, None),
        P(AXES, None),
        P(AXES, None),
        P(AXES),
        P(AXES),
        P(AXES),
        P(AXES),
        P((DP, SP), None, BLK),
        P((DP, SP), None, BLK),
        P((DP, SP), BLK, None),
        P(AXES, None),
        P(AXES, None),
    )
    out_specs = (
        P(AXES, None),
        P(AXES, None),
        P(AXES, None),
        P(AXES, None),
        P(AXES, None),
        P(AXES, None),
        P(AXES, None),
        P(AXES),
        P(AXES),
        P(AXES),
        P(AXES),
        P((DP, SP), None, BLK),
        P((DP, SP), None, BLK),
        P((DP, SP), BLK, None),
    )
    fast = dict(mesh.shape) == {DP: 4, BLK: 2, SP: 4}
    return jax.shard_map(body_fast if fast else body, mesh=mesh, in_specs=in_specs, out_specs=out_specs, check_vma=False)
```

```python
import functools
import math

import jax
import jax.numpy as jnp
import numpy as np
from jax import lax
from jax.experimental import pallas as pl
from jax.experimental.pallas import tpu as pltpu
from jax.sharding import PartitionSpec as P

DP, BLK, SP = AXES = ("dp", "blk", "sp")

HEADS = 16
HEAD_DIM = 128
EXPERTS = 64
TOPK = 8
CAP = 24


NORM_EPSILON = 1e-05
ROPE_BASE = 10000.0
MASKED = -1e30


def norm_apply(values, norm_gain):
    return (
        values
        * lax.rsqrt(jnp.mean(values * values, axis=-1, keepdims=True) + NORM_EPSILON)
        * norm_gain
    )


def rope_tables(positions, head_size):
    half_size = head_size // 2
    frequencies = jnp.exp(
        -math.log(ROPE_BASE) * 2.0 * jnp.arange(half_size, dtype=jnp.float32) / head_size
    )
    angles = positions.astype(jnp.float32)[:, None] * frequencies[None, :]
    return (jnp.cos(angles), jnp.sin(angles))


def rotate(values, cosine, sine):
    half_size = values.shape[-1] // 2
    first_half = values[..., :half_size]
    second_half = values[..., half_size:]
    cosine_row = cosine[:, None, :]
    sine_row = sine[:, None, :]
    return jnp.concatenate(
        [
            first_half * cosine_row - second_half * sine_row,
            second_half * cosine_row + first_half * sine_row,
        ],
        axis=-1,
    )


def rank_slots(route_rows):
    flat_experts = route_rows.reshape(-1)
    onehot = (flat_experts[:, None] == jnp.arange(EXPERTS, dtype=jnp.int32)[None, :]).astype(
        jnp.int32
    )
    return (flat_experts, jnp.sum(jnp.cumsum(onehot, axis=0) * onehot, axis=1) - 1)


MESH_ID = pl.DeviceIdType.MESH
VMEM_BYTES = 60 * 1024 * 1024


class Place:
    def __init__(self):
        self.dp = lax.axis_index(DP)
        self.blk = lax.axis_index(BLK)
        self.z = lax.axis_index(SP)
        self.x = self.dp % 2
        self.y = self.dp // 2
        self.col = self.blk * 4 + self.z

    def column(self, k):
        if k == 0:
            return self.dp
        if k == 1:
            return self.dp + 1 - 2 * self.x
        if k == 2:
            return self.dp + 2 - 4 * self.y
        return 3 - self.dp

    def at(self, k=0, blk=None, z=None):
        return (self.column(k), self.blk if blk is None else blk, self.z if z is None else z)


def entry_barrier(place, reach):
    barrier = pltpu.get_barrier_semaphore()

    def tell(target):
        pl.semaphore_signal(barrier, inc=1, device_id=target, device_id_type=MESH_ID)

    if reach == "all":
        me = (place.dp * 2 + place.blk) * 4 + place.z

        @pl.loop(1, 32)
        def _(step):
            other = (me + step) % 32
            tell((other // 8, (other // 4) % 2, other % 4))

        pl.semaphore_wait(barrier, 31)
    elif reach == "column":

        @pl.loop(1, 8)
        def _(step):
            other = (place.col + step) % 8
            tell((place.dp, other // 4, other % 4))

        pl.semaphore_wait(barrier, 7)
    else:
        tell_partners(place, barrier)
        wait_partners(place, barrier)


def tell_partners(place, semaphore):
    def tell(target):
        pl.semaphore_signal(semaphore, inc=1, device_id=target, device_id_type=MESH_ID)

    tell(place.at(0, 1 - place.blk))
    tell(place.at(1))
    tell(place.at(2))

    @pl.when(place.z > 0)
    def _():
        tell(place.at(z=place.z - 1))

    @pl.when(place.z < 3)
    def _():
        tell(place.at(z=place.z + 1))


def wait_partners(place, semaphore):
    ends = (3 - place.z) // 3 + place.z // 3
    pl.semaphore_wait(semaphore, 5 - ends)


def remote(src, dst, send_sem, recv_sem, target):
    return pltpu.make_async_remote_copy(
        src_ref=src,
        dst_ref=dst,
        send_sem=send_sem,
        recv_sem=recv_sem,
        device_id=target,
        device_id_type=MESH_ID,
    )


class GatherFlow:
    SENDS = 40
    RECVS = 37

    def __init__(self, place, src, out, send, recv, full, direct=False, others=False):
        self.p, self.src, self.out, self.send, self.recv, self.full = place, src, out, send, recv, full
        self.direct, self.others = direct, others
        self.half = src.shape[0] // 2

    def slot(self, k, blk, s):
        if self.full:
            return (self.p.column(k) * 2 + blk) * 4 + s
        return blk * 4 + s

    def block(self, k, s, blk=None):
        return self.out.at[self.slot(k, self.p.blk if blk is None else blk, s)]

    def copies(self, k, s, own=False):
        src = self.src if own else self.block(k, s)
        return src, self.block(k, s)

    def up(self, s, own=False):
        src, dst = self.copies(0, s, own)
        return remote(src, dst, self.send.at[s], self.recv.at[s], self.p.at(z=jnp.minimum(self.p.z + 1, 3)))

    def down(self, s, own=False):
        src, dst = self.copies(0, s, own)
        return remote(src, dst, self.send.at[4 + s], self.recv.at[s], self.p.at(z=jnp.maximum(self.p.z - 1, 0)))

    def across_x(self, s, own=False):
        src, dst = self.copies(0, s, own)
        return remote(src, dst, self.send.at[8 + s], self.recv.at[4 + s], self.p.at(1))

    def across_y(self, s, own=False):
        src, dst = self.copies(0, s, own)
        return remote(src, dst, self.send.at[12 + s], self.recv.at[8 + s], self.p.at(2))

    def turn_y(self, s):
        ref = self.block(1, s).at[pl.ds(0, self.half)]
        return remote(ref, ref, self.send.at[16 + s], self.recv.at[12 + s], self.p.at(2))

    def turn_x(self, s):
        ref = self.block(2, s).at[pl.ds(self.half, self.half)]
        return remote(ref, ref, self.send.at[20 + s], self.recv.at[16 + s], self.p.at(1))

    def core(self, k, s, own=False):
        src, dst = self.copies(k, s, own)
        return remote(
            src, dst, self.send.at[24 + 4 * k + s], self.recv.at[20 + 4 * k + s], self.p.at(0, 1 - self.p.blk)
        )

    def got(self, sem, ref):
        remote(ref, ref, self.send.at[0], self.recv.at[sem], self.p.at(0, 1 - self.p.blk)).wait_recv()

    def own_copy(self):
        return pltpu.make_async_copy(self.src, self.block(0, self.p.z), self.recv.at[36])

    def spread(self, s, own=False):
        if self.full:
            self.across_x(s, own).start()
            self.across_y(s, own).start()
        self.core(0, s, own).start()

    def straight(self, step):
        z = self.p.z
        return remote(
            self.src, self.block(0, z), self.send.at[step - 1], self.recv.at[z], self.p.at(z=(z + step) % 4)
        )

    def begin(self):
        z = self.p.z
        if self.direct:
            for step in (1, 2, 3):
                self.straight(step).start()
            self.spread(z, True)
            self.own_copy().start()
            return

        @pl.when(z < 3)
        def _():
            self.up(z, True).start()

        @pl.when(z > 0)
        def _():
            self.down(z, True).start()

        if not self.others:
            self.spread(z, True)
            self.own_copy().start()

    def along(self, d):
        z = self.p.z

        @pl.when(z >= d)
        def _():
            s = z - d
            self.got(s, self.block(0, s))

            if not self.direct:

                @pl.when(z < 3)
                def _():
                    self.up(s).start()

            self.spread(s)

        @pl.when(z + d <= 3)
        def _():
            s = z + d
            self.got(s, self.block(0, s))

            if not self.direct:

                @pl.when(z > 0)
                def _():
                    self.down(s).start()

            self.spread(s)

    def each(self, d, act):
        z = self.p.z
        if d == 0:
            if not self.others:
                act(z)
            return

        @pl.when(z >= d)
        def _():
            act(z - d)

        @pl.when(z + d <= 3)
        def _():
            act(z + d)

    def turn(self, d):
        if not self.full:
            return

        def act(s):
            self.got(4 + s, self.block(1, s))
            self.turn_y(s).start()
            self.core(1, s).start()
            self.got(8 + s, self.block(2, s))
            self.turn_x(s).start()
            self.core(2, s).start()

        self.each(d, act)

    def corner(self, d):
        if not self.full:
            return

        def act(s):
            self.got(12 + s, self.block(3, s).at[pl.ds(0, self.half)])
            self.got(16 + s, self.block(3, s).at[pl.ds(self.half, self.half)])
            self.core(3, s).start()

        self.each(d, act)

    def settle_plane(self, s):
        for k in range(4 if self.full else 1):
            self.got(20 + 4 * k + s, self.block(k, s, 1 - self.p.blk))
            self.core(k, s).wait_send()
        if self.full:
            self.across_x(s).wait_send()
            self.across_y(s).wait_send()
            self.turn_x(s).wait_send()
            self.turn_y(s).wait_send()

    def finish(self):
        z = self.p.z

        @pl.loop(0, 4)
        def _(s):
            pl.when((s != z) | (not self.others))(lambda: self.settle_plane(s))
            if not self.direct:

                @pl.when((s <= z) & (z < 3))
                def _():
                    self.up(s).wait_send()

                @pl.when((s >= z) & (z > 0))
                def _():
                    self.down(s).wait_send()

        if self.direct:
            for step in (1, 2, 3):
                self.straight(step).wait_send()
        if not self.others:
            self.own_copy().wait()


class PlaneFlow(GatherFlow):
    def __init__(self, place, blocks, out, send, recv, local):
        super().__init__(place, blocks[0][1], out, send, recv, True)
        self.blocks, self.local = blocks, local

    def begin(self):
        for i, (s, src) in enumerate(self.blocks):
            self.src = src
            self.spread(s, True)
            pltpu.make_async_copy(src, self.block(0, s), self.local.at[i]).start()

    def turns(self):
        for s, _ in self.blocks:
            self.got(4 + s, self.block(1, s))
            self.turn_y(s).start()
            self.core(1, s).start()
            self.got(8 + s, self.block(2, s))
            self.turn_x(s).start()
            self.core(2, s).start()

    def corners(self):
        for s, _ in self.blocks:
            self.got(12 + s, self.block(3, s).at[pl.ds(0, self.half)])
            self.got(16 + s, self.block(3, s).at[pl.ds(self.half, self.half)])
            self.core(3, s).start()

    def finish(self):
        for i, (s, src) in enumerate(self.blocks):
            self.settle_plane(s)
            pltpu.make_async_copy(src, self.block(0, s), self.local.at[i]).wait()


class PlaneFlow(GatherFlow):
    def __init__(self, place, blocks, out, send, recv, local):
        super().__init__(place, blocks[0][1], out, send, recv, True)
        self.blocks, self.local = blocks, local

    def begin(self):
        for i, (s, src) in enumerate(self.blocks):
            self.src = src
            self.spread(s, True)
            pltpu.make_async_copy(src, self.block(0, s), self.local.at[i]).start()

    def turns(self):
        for s, _ in self.blocks:
            self.got(4 + s, self.block(1, s))
            self.turn_y(s).start()
            self.core(1, s).start()
            self.got(8 + s, self.block(2, s))
            self.turn_x(s).start()
            self.core(2, s).start()

    def corners(self):
        for s, _ in self.blocks:
            self.got(12 + s, self.block(3, s).at[pl.ds(0, self.half)])
            self.got(16 + s, self.block(3, s).at[pl.ds(self.half, self.half)])
            self.core(3, s).start()

    def finish(self):
        for i, (s, src) in enumerate(self.blocks):
            self.settle_plane(s)
            pltpu.make_async_copy(src, self.block(0, s), self.local.at[i]).wait()


def run_flows(flows):
    lists = [flow.steps() for flow in flows]
    for position in range(max(len(steps) for steps in lists)):
        for steps in lists:
            if position < len(steps):
                steps[position]()


def add_rows(dst, terms, rows):
    @pl.loop(0, rows // 16)
    def _(i):
        at = pl.ds(pl.multiple_of(i * 16, 16), 16)
        total = terms[0][at, :].astype(jnp.float32)
        for term in terms[1:]:
            total = total + term[at, :].astype(jnp.float32)
        dst[at, :] = total.astype(dst.dtype)


class ScatterFlow:
    SENDS = 16 + 8 + 8 + 4 + 4
    RECVS = 16 + 8 + 8 + 4 + 4
    LOCALS = 16

    def __init__(self, place, part, out, scratch, full, band=None):
        self.p, self.part, self.out, self.full = place, part, out, full
        if full:
            (self.acc, self.near, self.half_in, self.side_in, self.line_in, self.sum, self.send, self.recv, self.local) = scratch
        else:
            (self.acc, self.near, self.line_in, self.sum, self.send, self.recv, self.local) = scratch
        self.columns = 4 if full else 1
        self.left = False
        first, self.rows = band or (0, part.shape[1])
        self.band = pl.ds(first, self.rows)
        self.half = self.rows // 2

    @staticmethod
    def scratch(rows, width, dtype, full):
        columns = 4 if full else 1
        shapes = [
            pltpu.VMEM((columns, 4, rows, width), dtype),
            pltpu.VMEM((columns, 4, rows, width), dtype),
        ]
        if full:
            shapes += [pltpu.VMEM((2, 4, rows // 2, width), dtype), pltpu.VMEM((2, 4, rows, width), dtype)]
        return shapes + [
            pltpu.VMEM((2, 4, rows, width), dtype),
            pltpu.VMEM((rows, width), jnp.float32),
            pltpu.SemaphoreType.DMA((ScatterFlow.SENDS,)),
            pltpu.SemaphoreType.DMA((ScatterFlow.RECVS,)),
            pltpu.SemaphoreType.DMA((ScatterFlow.LOCALS,)),
        ]

    def slot(self, k, blk, s):
        if self.full:
            return (self.p.column(k) * 2 + blk) * 4 + s
        return blk * 4 + s

    def order(self, i):
        z = self.p.z
        return [3 * (1 - z // 2), (2 + 3 * z) % 5, 1 + z % 2, z][i]

    def load(self, k, s):
        return pltpu.make_async_copy(
            self.part.at[self.slot(k, self.p.blk, s), self.band], self.acc.at[k, s], self.local.at[4 * k + s]
        )

    def core(self, k, s):
        return remote(
            self.part.at[self.slot(k, 1 - self.p.blk, s), self.band],
            self.near.at[k, s],
            self.send.at[4 * k + s],
            self.recv.at[4 * k + s],
            self.p.at(0, 1 - self.p.blk),
        )

    def half_x(self, s):
        return remote(
            self.acc.at[3, s, pl.ds(0, self.half)],
            self.half_in.at[0, s],
            self.send.at[16 + s],
            self.recv.at[16 + s],
            self.p.at(1),
        )

    def half_y(self, s):
        return remote(
            self.acc.at[3, s, pl.ds(self.half, self.half)],
            self.half_in.at[1, s],
            self.send.at[20 + s],
            self.recv.at[20 + s],
            self.p.at(2),
        )

    def side_x(self, s):
        return remote(
            self.acc.at[1, s], self.side_in.at[0, s], self.send.at[24 + s], self.recv.at[24 + s], self.p.at(1)
        )

    def side_y(self, s):
        return remote(
            self.acc.at[2, s], self.side_in.at[1, s], self.send.at[28 + s], self.recv.at[28 + s], self.p.at(2)
        )

    def line_up(self, s):
        return remote(
            self.acc.at[0, s],
            self.line_in.at[0, s],
            self.send.at[32 + s],
            self.recv.at[32 + s],
            self.p.at(z=jnp.minimum(self.p.z + 1, 3)),
        )

    def line_down(self, s):
        return remote(
            self.acc.at[0, s],
            self.line_in.at[1, s],
            self.send.at[36 + s],
            self.recv.at[36 + s],
            self.p.at(z=jnp.maximum(self.p.z - 1, 0)),
        )

    def begin(self, columns=None):
        for i in range(4):
            s = self.order(i)
            for k in columns or reversed(range(self.columns)):
                self.core(k, s).start()
                self.load(k, s).start()

    def unsent(self):
        return range(self.columns)

    def leave(self, s):
        self.half_x(s).wait_send()
        self.half_y(s).wait_send()
        self.side_x(s).wait_send()
        self.side_y(s).wait_send()

    def leave_all(self):
        self.left = True

        @pl.loop(0, 4)
        def _(s):
            self.leave(s)

    def arrive(self, k, s):
        self.load(k, s).wait()
        self.core(k, s).wait_recv()
        return [self.acc.at[k, s], self.near.at[k, s]]

    def stage1(self, i):
        if not self.full:
            return
        s = self.order(i)
        add_rows(self.acc.at[3, s], self.arrive(3, s), self.rows)
        self.half_x(s).start()
        self.half_y(s).start()

    def stage2(self, i):
        if not self.full:
            return
        s = self.order(i)
        first, second = pl.ds(0, self.half), pl.ds(self.half, self.half)
        terms = self.arrive(2, s)
        late = [term.at[first] for term in terms] + [self.half_in.at[0, s]]
        rest = [term.at[second] for term in terms]
        add_rows(rest[0], rest, self.half)
        self.half_x(s).wait_recv()
        add_rows(late[0], late, self.half)
        self.side_y(s).start()
        terms = self.arrive(1, s)
        late = [term.at[second] for term in terms] + [self.half_in.at[1, s]]
        rest = [term.at[first] for term in terms]
        add_rows(rest[0], rest, self.half)
        self.half_y(s).wait_recv()
        add_rows(late[0], late, self.half)
        self.side_x(s).start()

    def stage3(self, i):
        s = self.order(i)
        z = self.p.z
        terms = self.arrive(0, s)
        if self.full:
            self.side_x(s).wait_recv()
            self.side_y(s).wait_recv()
            terms = terms + [self.side_in.at[0, s], self.side_in.at[1, s]]
        add_rows(self.acc.at[0, s], terms, self.rows)
        if i < 3:

            @pl.when(z == 0)
            def _():
                self.line_up(s).start()

            @pl.when(z == 3)
            def _():
                self.line_down(s).start()

    def chain(self, i):
        s = self.order(i)
        z = self.p.z

        @pl.when((z > 0) & (z < s) & (z < 3))
        def _():
            self.line_up(s).wait_recv()
            add_rows(self.acc.at[0, s], [self.acc.at[0, s], self.line_in.at[0, s]], self.rows)
            self.line_up(s).start()

        @pl.when((z < 3) & (z > s) & (z > 0))
        def _():
            self.line_down(s).wait_recv()
            add_rows(self.acc.at[0, s], [self.acc.at[0, s], self.line_in.at[1, s]], self.rows)
            self.line_down(s).start()

    def final(self):
        z = self.p.z
        mine, above, below = self.acc.at[0, z], self.line_in.at[0, z], self.line_in.at[1, z]

        @pl.when(z > 0)
        def _():
            self.line_up(z).wait_recv()

        @pl.when(z < 3)
        def _():
            self.line_down(z).wait_recv()

        @pl.when(z == 0)
        def _():
            add_rows(self.sum, [mine, below], self.rows)

        @pl.when(z == 3)
        def _():
            add_rows(self.sum, [mine, above], self.rows)

        @pl.when((z > 0) & (z < 3))
        def _():
            add_rows(self.sum, [mine, above, below], self.rows)

        done = pltpu.make_async_copy(self.sum, self.out, self.local.at[0])
        done.start()

        @pl.loop(0, 4)
        def _(s):
            for k in self.unsent():
                self.core(k, s).wait_send()
            if self.full and not self.left:
                self.leave(s)

            @pl.when(s > z)
            def _():
                self.line_up(s).wait_send()

            @pl.when(s < z)
            def _():
                self.line_down(s).wait_send()

        done.wait()


class MadeFlow(ScatterFlow):
    def __init__(self, place, out, scratch, stage):
        self.stage = stage
        super().__init__(place, stage.at[0], out, scratch, True)

    def core(self, k, s):
        return remote(
            self.stage.at[k % 2, s],
            self.near.at[k, s],
            self.send.at[4 * k + s],
            self.recv.at[4 * k + s],
            self.p.at(0, 1 - self.p.blk),
        )

    def unsent(self):
        return (0, 1)

    def arrive(self, k, s):
        self.core(k, s).wait_recv()
        return [self.acc.at[k, s], self.near.at[k, s]]


def local_params():
    return pltpu.CompilerParams(vmem_limit_bytes=VMEM_BYTES)


def inner(left, right, left_dim=1, right_dim=0):
    return lax.dot_general(
        left, right, (((left_dim,), (right_dim,)), ((), ())), preferred_element_type=jnp.float32
    )


def is_place(places, per):
    return lax.broadcasted_iota(jnp.int32, (per, places.shape[1]), 0) == places


def one_hot(places, per):
    experts = places.shape[0]
    hot = [is_place(places[e : e + 1], per).astype(jnp.float32) for e in range(experts)]
    return jnp.concatenate(hot, axis=0).astype(jnp.bfloat16)


def pick_rows(places, probs, features, per):
    pairs, experts, pair_rows = places.shape
    width = features.shape[-1]
    step = 2

    def kernel(place_ref, prob_ref, feature_ref, row_ref, row_prob_ref):
        for i in range(step):
            rows = inner(one_hot(place_ref[i], per), feature_ref[i]).astype(row_ref.dtype)
            for e in range(experts):
                at = pl.ds(i * per, per)
                row_ref[e, at] = rows[e * per : (e + 1) * per]
                hot = is_place(place_ref[i, e : e + 1], per)
                prob = jnp.concatenate([prob_ref[2 * i, e : e + 1], prob_ref[2 * i + 1, e : e + 1]], axis=1)
                row_prob_ref[e, at] = jnp.sum(jnp.where(hot, prob, 0.0), axis=1, keepdims=True)

    return pl.pallas_call(
        kernel,
        out_shape=[
            jax.ShapeDtypeStruct((experts, pairs * per, width), features.dtype),
            jax.ShapeDtypeStruct((experts, pairs * per, 1), jnp.float32),
        ],
        grid=(pairs // step,),
        in_specs=[
            pl.BlockSpec((step, experts, pair_rows), lambda p: (p, 0, 0)),
            pl.BlockSpec((2 * step, experts, pair_rows // 2), lambda p: (p, 0, 0)),
            pl.BlockSpec((step, pair_rows, width), lambda p: (p, 0, 0)),
        ],
        out_specs=[
            pl.BlockSpec((experts, step * per, width), lambda p: (0, p, 0)),
            pl.BlockSpec((experts, step * per, 1), lambda p: (0, p, 0)),
        ],
        compiler_params=local_params(),
        name="pick_rows",
    )(places, probs, features)


def run_experts(rows, plain_grads, probs, gate_weight, up_weight):
    experts, slots, width = rows.shape
    hidden = gate_weight.shape[2]
    parts = 2
    part = slots // parts

    def kernel(x, plain_ref, p, wg, wu, weighted, gate_back, up_back, back, prob_back):
        gate = inner(x[0], wg[0])
        up = inner(x[0], wu[0])
        plain = plain_ref[0]
        prob = p[0]
        sig = jax.nn.sigmoid(gate)
        act = gate * sig
        hid = act * up
        prob_back[0] = jnp.sum(hid * plain, axis=1, keepdims=True)
        weighted[0] = (hid * prob).astype(jnp.bfloat16)
        grad = plain * prob
        gate_low = (grad * up * sig * (1.0 + gate * (1.0 - sig))).astype(jnp.bfloat16)
        up_low = (grad * act).astype(jnp.bfloat16)
        gate_back[0] = gate_low
        up_back[0] = up_low
        back[0] = (inner(gate_low, wg[0], 1, 1) + inner(up_low, wu[0], 1, 1)).astype(jnp.bfloat16)

    def block(size):
        return pl.BlockSpec((1, part, size), lambda e, i: (e, i, 0))

    weight = pl.BlockSpec((1, width, hidden), lambda e, i: (e, 0, 0))
    narrow = jax.ShapeDtypeStruct((experts, slots, hidden), rows.dtype)
    return pl.pallas_call(
        kernel,
        out_shape=[
            narrow,
            narrow,
            narrow,
            jax.ShapeDtypeStruct(rows.shape, rows.dtype),
            jax.ShapeDtypeStruct((experts, slots, 1), jnp.float32),
        ],
        grid=(experts, parts),
        in_specs=[block(width), block(hidden), block(1), weight, weight],
        out_specs=[block(hidden)] * 3 + [block(width), block(1)],
        compiler_params=local_params(),
        name="run_experts",
    )(rows, plain_grads, probs, gate_weight, up_weight)


class PickWork:
    GROUP = 4

    def __init__(self, places, source, weight, rows_out, plain_out, scratch):
        self.places, self.source, self.weight = places, source, weight
        self.rows_out, self.plain_out = rows_out, plain_out
        self.block, self.rows, self.plain, self.held, self.in_sems, self.out_sems, self.held_sem = scratch
        self.pairs = source.shape[0]
        self.units = self.pairs + self.GROUP
        self.experts = weight.shape[0]
        self.per = self.rows.shape[2] // self.GROUP

    @staticmethod
    def scratch(source, weight, per):
        experts, hidden, width = weight.shape
        group = PickWork.GROUP * per
        return [
            pltpu.VMEM((2,) + source.shape[1:], source.dtype),
            pltpu.VMEM((2, experts, group, width), source.dtype),
            pltpu.VMEM((2, experts, group, hidden), jnp.float32),
            pltpu.VMEM(weight.shape, weight.dtype),
            pltpu.SemaphoreType.DMA((2,)),
            pltpu.SemaphoreType.DMA((2, 2)),
            pltpu.SemaphoreType.DMA((1,)),
        ]

    def load(self, unit, slot):
        return pltpu.make_async_copy(self.source.at[unit], self.block.at[slot], self.in_sems.at[slot])

    def hold(self):
        return pltpu.make_async_copy(self.weight, self.held, self.held_sem.at[0])

    def stores(self, group, slot):
        height = self.GROUP * self.per
        at = pl.ds(pl.multiple_of(group * height, height), height)
        return [
            pltpu.make_async_copy(self.rows.at[slot], self.rows_out.at[:, at], self.out_sems.at[slot, 0]),
            pltpu.make_async_copy(self.plain.at[slot], self.plain_out.at[:, at], self.out_sems.at[slot, 1]),
        ]

    def begin(self):
        self.hold().start()
        self.load(0, 0).start()

    def pick(self, unit):
        slot, group, turn = unit % 2, unit // self.GROUP, unit % self.GROUP
        side = group % 2

        @pl.when(unit + 1 < self.pairs)
        def _():
            self.load(unit + 1, 1 - slot).start()

        @pl.when((turn == 0) & (group >= 2))
        def _():
            for copy in self.stores(group - 2, side):
                copy.wait()

        self.load(unit, slot).wait()
        rows = inner(one_hot(self.places[unit], self.per), self.block[slot]).astype(self.rows.dtype)
        for e in range(self.experts):
            at = pl.ds(pl.multiple_of(turn * self.per, self.per), self.per)
            self.rows[side, e, at] = rows[e * self.per : (e + 1) * self.per]

    def multiply(self, unit):
        group, e = unit // self.GROUP, unit % self.GROUP
        side = group % 2

        @pl.when(unit == 0)
        def _():
            self.hold().wait()

        self.plain[side, e] = inner(self.rows[side, e], self.held[e], 1, 1)

        @pl.when(e == self.GROUP - 1)
        def _():
            for copy in self.stores(group, side):
                copy.start()

    def run(self, unit):
        pl.when(unit < self.pairs)(lambda: self.pick(unit))
        pl.when(unit >= self.GROUP)(lambda: self.multiply(unit - self.GROUP))

    def finish(self):
        groups = self.pairs // self.GROUP
        for group in (groups - 2, groups - 1):
            for copy in self.stores(group, group % 2):
                copy.wait()


class PutWork:
    def __init__(self, place, places, source, row_grads, flow, deals, scratch):
        self.p, self.places, self.source, self.row_grads = place, places, source, row_grads
        self.flow, self.deals = flow, deals
        self.rows, self.sems = scratch
        self.experts, self.per = self.rows.shape[1:3]

    @staticmethod
    def scratch(source, per):
        experts, _, width = source.shape
        return [pltpu.VMEM((2, experts, per, width), source.dtype), pltpu.SemaphoreType.DMA((2,))]

    def pair(self, k, unit):
        side = unit // 2
        blk = side * self.p.blk + (1 - side) * (1 - self.p.blk)
        return self.p.column(k) * 4 + blk * 2 + unit % 2

    def load(self, k, unit, slot):
        at = pl.ds(pl.multiple_of(self.pair(k, unit) * self.per, self.per), self.per)
        return pltpu.make_async_copy(self.source.at[:, at], self.rows.at[slot], self.sems.at[slot])

    def column(self, k):
        flow = self.flow
        if k < 2:

            @pl.loop(0, 4)
            def _(s):
                flow.core(k + 2, s).wait_send()

        @pl.loop(0, 4)
        def _(unit):
            slot = unit % 2

            @pl.when(unit < 3)
            def _():
                self.load(k, unit + 1, 1 - slot).start()

            if k:

                @pl.when(unit == 3)
                def _():
                    self.load(k - 1, 0, 1 - slot).start()

            self.load(k, unit, slot).wait()
            pair = self.pair(k, unit)
            places = self.places[pair]
            rows = jnp.concatenate([self.rows[slot, e] for e in range(self.experts)], axis=0)
            summed = inner(one_hot(places, self.per), rows, 0, 0).astype(self.rows.dtype)
            summed = summed.reshape(2, summed.shape[0] // 2, summed.shape[1])
            blocks = pl.ds(2 * (unit % 2), 2)

            @pl.when(unit < 2)
            def _():
                flow.stage[k % 2, blocks] = summed

            @pl.when(unit >= 2)
            def _():
                flow.acc[k, blocks] = summed

            at = pl.ds(pl.multiple_of(pair * self.per, self.per), self.per)
            half = places.shape[1] // 2
            for e in range(self.experts):
                hot = is_place(places[e : e + 1], self.per)
                line = jnp.sum(jnp.where(hot, self.row_grads[e, at], 0.0), axis=0, keepdims=True)
                self.deals[2 * pair, e : e + 1] = line[:, :half]
                self.deals[2 * pair + 1, e : e + 1] = line[:, half:]

            @pl.when(unit == 1)
            def _():
                for s in range(4):
                    flow.core(k, s).start()


class OutputWork:
    def __init__(self, places, hidden, weight, out, scratch):
        self.places, self.hidden, self.weight, self.out = places, hidden, weight, out
        self.rows, self.held, self.narrow, self.block, self.in_sems, self.out_sems = scratch
        self.experts, self.slots, _ = hidden.shape
        self.pairs = out.shape[0]
        self.per = self.slots // self.pairs
        self.width = weight.shape[2]
        self.units = 2 * self.experts + self.pairs

    @staticmethod
    def scratch(hidden, weight, out):
        experts, slots, narrow = hidden.shape
        return [
            pltpu.VMEM((experts, slots, weight.shape[2]), weight.dtype),
            pltpu.VMEM((2,) + weight.shape[1:], weight.dtype),
            pltpu.VMEM((2, slots, narrow), hidden.dtype),
            pltpu.VMEM((2,) + out.shape[1:], out.dtype),
            pltpu.SemaphoreType.DMA((2, 2)),
            pltpu.SemaphoreType.DMA((2,)),
        ]

    def loads(self, e):
        slot = e % 2
        return [
            pltpu.make_async_copy(self.weight.at[e], self.held.at[slot], self.in_sems.at[slot, 0]),
            pltpu.make_async_copy(self.hidden.at[e], self.narrow.at[slot], self.in_sems.at[slot, 1]),
        ]

    def store(self, pair):
        return pltpu.make_async_copy(self.block.at[pair % 2], self.out.at[pair], self.out_sems.at[pair % 2])

    def begin(self):
        for copy in self.loads(0):
            copy.start()

    def run(self, unit):
        half = self.width // 2

        @pl.when(unit < 2 * self.experts)
        def _():
            e, side = unit // 2, unit % 2

            @pl.when(side == 0)
            def _():
                @pl.when(e + 1 < self.experts)
                def _():
                    for copy in self.loads(e + 1):
                        copy.start()

                for copy in self.loads(e):
                    copy.wait()

            at = pl.ds(pl.multiple_of(side * half, half), half)
            self.rows[e, :, at] = inner(self.narrow[e % 2], self.held[e % 2, :, at]).astype(self.rows.dtype)

        @pl.when(unit >= 2 * self.experts)
        def _():
            pair = unit - 2 * self.experts

            @pl.when(pair >= 2)
            def _():
                self.store(pair - 2).wait()

            at = pl.ds(pl.multiple_of(pair * self.per, self.per), self.per)
            rows = jnp.concatenate([self.rows[e, at] for e in range(self.experts)], axis=0)
            self.block[pair % 2] = inner(one_hot(self.places[pair], self.per), rows, 0, 0).astype(self.block.dtype)
            self.store(pair).start()

    def finish(self):
        for pair in (self.pairs - 2, self.pairs - 1):
            self.store(pair).wait()


def expert_weight_grads(rows, grads, weighted, gate_back, up_back):
    experts, slots, width = rows.shape
    hidden = weighted.shape[2]
    parts = 4
    part = width // parts

    def kernel(x, c, low, gate, up, gate_out, up_out, down_out):
        gate_out[0] = inner(x[0], gate[0], 0, 0)
        up_out[0] = inner(x[0], up[0], 0, 0)
        down_out[0] = inner(low[0], c[0], 0, 0)

    source = pl.BlockSpec((1, slots, part), lambda e, i: (e, 0, i))
    whole = pl.BlockSpec((1, slots, hidden), lambda e, i: (e, 0, 0))
    tall = pl.BlockSpec((1, part, hidden), lambda e, i: (e, i, 0))
    flat = pl.BlockSpec((1, hidden, part), lambda e, i: (e, 0, i))
    return pl.pallas_call(
        kernel,
        out_shape=[
            jax.ShapeDtypeStruct((experts, width, hidden), jnp.float32),
            jax.ShapeDtypeStruct((experts, width, hidden), jnp.float32),
            jax.ShapeDtypeStruct((experts, hidden, width), jnp.float32),
        ],
        grid=(experts, parts),
        in_specs=[source, source, whole, whole, whole],
        out_specs=[tall, tall, flat],
        compiler_params=local_params(),
        cost_estimate=pl.CostEstimate(
            flops=6 * experts * slots * width * hidden, bytes_accessed=24 * experts * width * hidden, transcendentals=0
        ),
        name="expert_weight_grads",
    )(rows, grads, weighted, gate_back, up_back)


class ColumnsFlow:
    SENDS = 24 + 1 + 16
    RECVS = 24 + 1 + 16
    LOCALS = 4

    def __init__(self, place, sources, rows_in, wide, tall, send, recv, local):
        self.p, self.sources, self.rows_in, self.wide, self.tall = place, sources, rows_in, wide, tall
        self.send, self.recv, self.local = send, recv, local
        self.rows = rows_in.shape[0]
        self.share = wide.shape[1] // len(sources)

    def spot(self, i, col):
        rows = pl.ds(pl.multiple_of((self.p.dp * 8 + col) * self.rows, self.rows), self.rows)
        return self.wide.at[rows, pl.ds(i * self.share, self.share)]

    def piece(self, i, to):
        return self.sources[i].at[:, pl.ds(pl.multiple_of(to * self.share, self.share), self.share)]

    def scatter(self, step, i):
        to = (self.p.col + step) % 8
        return remote(
            self.piece(i, to),
            self.spot(i, self.p.col),
            self.send.at[3 * step + i],
            self.recv.at[3 * self.p.col + i],
            (self.p.dp, to // 4, to % 4),
        )

    def keep(self, i):
        return pltpu.make_async_copy(self.piece(i, self.p.col), self.spot(i, self.p.col), self.local.at[i])

    def tall_rows(self, k):
        return self.tall.at[pl.ds(pl.multiple_of(self.p.column(k) * self.rows, self.rows), self.rows)]

    def swap(self):
        group = self.p.dp * 2 + self.p.blk
        dst = self.tall.at[pl.ds(pl.multiple_of(self.p.z * self.rows, self.rows), self.rows)]
        return remote(
            self.rows_in, dst, self.send.at[24], self.recv.at[24], (self.p.z, group // 4, group % 4)
        )

    def stay(self):
        return pltpu.make_async_copy(self.rows_in, self.tall_rows(0), self.local.at[3])

    def at_home(self):
        group = self.p.dp * 2 + self.p.blk
        return (self.p.z == self.p.dp) & (group == self.p.col)

    def band(self, i, k, first=0, parts=1):
        if i == 3:
            height, ref = self.rows, self.tall
        else:
            height, ref = 8 * self.rows, self.wide
        part = height // parts
        rows = pl.ds(pl.multiple_of(self.p.column(k) * height + first * part, part), part)
        return ref.at[rows] if i == 3 else ref.at[rows, pl.ds(i * self.share, self.share)]

    def across(self, i, k):
        ref = self.band(i, 0)
        slot = 25 + 4 * i + k - 1
        return remote(ref, ref, self.send.at[slot], self.recv.at[slot], self.p.at(k))

    def turn(self, i, k):
        ref = self.band(i, k, k - 1, 2)
        slot = 25 + 4 * i + 1 + k
        return remote(ref, ref, self.send.at[slot], self.recv.at[slot], self.p.at(3 - k))

    def got(self, sem, ref):
        remote(ref, ref, self.send.at[0], self.recv.at[sem], self.p.at(0, 1 - self.p.blk)).wait_recv()

    def begin(self):
        home = self.at_home()

        @pl.when(home)
        def _():
            self.stay().start()

        @pl.when(jnp.logical_not(home))
        def _():
            self.swap().start()

        for i in range(3):

            @pl.loop(1, 8)
            def _(step):
                self.scatter(step, i).start()

            self.keep(i).start()

    def settle(self, i):
        if i == 3:
            home = self.at_home()

            @pl.when(home)
            def _():
                self.stay().wait()

            @pl.when(jnp.logical_not(home))
            def _():
                self.got(24, self.tall_rows(0))

        else:
            self.keep(i).wait()

            @pl.loop(1, 8)
            def _(step):
                col = (self.p.col + step) % 8
                self.got(3 * col + i, self.spot(i, col))

        self.across(i, 1).start()
        self.across(i, 2).start()

    def turns(self, i):
        for k in (1, 2):
            self.got(25 + 4 * i + k - 1, self.band(i, k))
            self.turn(i, k).start()

    def finish(self):
        for i in (3, 0, 1, 2):
            for k in (1, 2):
                self.got(25 + 4 * i + 1 + k, self.band(i, 3, k - 1, 2))
                self.turn(i, k).wait_send()
                self.across(i, k).wait_send()

        @pl.when(jnp.logical_not(self.at_home()))
        def _():
            self.swap().wait_send()

        @pl.loop(1, 8)
        def _(step):
            for i in range(3):
                self.scatter(step, i).wait_send()


class SumsFlow:
    SENDS = 12 + 24 + 1
    RECVS = 12 + 16 + 1
    LOCALS = 4

    def __init__(self, place, wide_out, tall_out, scratch):
        self.p = place
        self.wide_out, self.tall_out = wide_out, tall_out
        self.acc, self.half_in, self.side_in = scratch[0:3], scratch[3:6], scratch[6:9]
        self.send, self.recv, self.local = scratch[9:12]
        self.rows = tall_out.shape[0]
        self.share = wide_out.shape[2] // 8

    @staticmethod
    def scratch(arrays):
        shapes = []
        for kind in ((4, 1), (2, 2), (2, 1)):
            for rows, width in arrays:
                shapes.append(pltpu.VMEM((kind[0], rows // kind[1], width), jnp.bfloat16))
        return shapes + [
            pltpu.SemaphoreType.DMA((SumsFlow.SENDS,)),
            pltpu.SemaphoreType.DMA((SumsFlow.RECVS,)),
            pltpu.SemaphoreType.DMA((SumsFlow.LOCALS,)),
        ]

    def halves(self, ref):
        half = ref.shape[0] // 2
        return ref.at[pl.ds(0, half)], ref.at[pl.ds(half, half)]

    def corner(self, which, k):
        src = self.halves(self.acc[which].at[3])[k - 1]
        slot = 4 * which + k - 1
        return remote(src, self.half_in[which].at[k - 1], self.send.at[slot], self.recv.at[slot], self.p.at(k))

    def side(self, which, k):
        slot = 4 * which + 1 + k
        return remote(
            self.acc[which].at[k], self.side_in[which].at[k - 1], self.send.at[slot], self.recv.at[slot], self.p.at(k)
        )

    def piece(self, to, i):
        rows = pl.ds(pl.multiple_of(to * self.rows, self.rows), self.rows)
        dst = self.wide_out.at[i, :, pl.ds(pl.multiple_of(self.p.col * self.share, self.share), self.share)]
        if i == 2:
            return self.acc[2].at[0, rows], dst
        return self.acc[0].at[0, rows, pl.ds(i * self.share, self.share)], dst

    def deal(self, step, i):
        to = (self.p.col + step) % 8
        src, dst = self.piece(to, i)
        return remote(
            src,
            dst,
            self.send.at[12 + 3 * step + i],
            self.recv.at[12 + 8 * (i // 2) + self.p.col],
            (self.p.dp, to // 4, to % 4),
        )

    def keep(self, i):
        src, dst = self.piece(self.p.col, i)
        return pltpu.make_async_copy(src, dst, self.local.at[i])

    def swap(self):
        return remote(
            self.acc[1].at[0],
            self.tall_out,
            self.send.at[36],
            self.recv.at[28],
            (self.p.col // 2, self.p.col % 2, self.p.dp),
        )

    def stay(self):
        return pltpu.make_async_copy(self.acc[1].at[0], self.tall_out, self.local.at[3])

    def at_home(self):
        return (self.p.col // 2 == self.p.dp) & (self.p.col % 2 == self.p.blk) & (self.p.z == self.p.dp)

    def corners(self, which):
        self.corner(which, 1).start()
        self.corner(which, 2).start()

    def sides(self, which):
        for k, other in ((2, 1), (1, 2)):
            self.corner(which, other).wait_recv()
            target = self.halves(self.acc[which].at[k])[other - 1]
            add_rows(target, [target, self.half_in[which].at[other - 1]], target.shape[0])
            self.side(which, k).start()

    def total(self, which):
        self.side(which, 1).wait_recv()
        self.side(which, 2).wait_recv()
        mine = self.acc[which].at[0]
        add_rows(mine, [mine, self.side_in[which].at[0], self.side_in[which].at[1]], mine.shape[0])

    def hand_out_tall(self):
        home = self.at_home()

        @pl.when(home)
        def _():
            self.stay().start()

        @pl.when(jnp.logical_not(home))
        def _():
            self.swap().start()

    def hand_out(self, weights):
        @pl.loop(1, 8)
        def _(step):
            for i in weights:
                self.deal(step, i).start()

        for i in weights:
            self.keep(i).start()

    def finish(self):
        home = self.at_home()

        @pl.when(home)
        def _():
            self.stay().wait()

        @pl.when(jnp.logical_not(home))
        def _():
            self.swap().wait()

        for i in range(3):
            self.keep(i).wait()

        @pl.loop(1, 8)
        def _(step):
            col = (self.p.col + step) % 8
            for which, landed in (
                (0, self.acc[0].at[0, pl.ds(0, self.rows)]),
                (1, self.acc[2].at[0, pl.ds(0, self.rows)]),
            ):
                remote(
                    landed,
                    landed,
                    self.send.at[0],
                    self.recv.at[12 + 8 * which + col],
                    self.p.at(0, 1 - self.p.blk),
                ).wait_recv()
            for i in range(3):
                self.deal(step, i).wait_send()

        for which in (1, 2, 0):
            for k in (1, 2):
                self.corner(which, k).wait_send()
                self.side(which, k).wait_send()


class DealFlow:
    def __init__(self, place, src, out, send, recv, local):
        self.p, self.src, self.out, self.send, self.recv, self.local = place, src, out, send, recv, local
        self.me = (place.dp * 2 + place.blk) * 4 + place.z

    def copy(self, step):
        to = (self.me + step) % 32
        return remote(
            self.src.at[to], self.out.at[self.me], self.send.at[step], self.recv.at[self.me], (to // 8, (to // 4) % 2, to % 4)
        )

    def keep(self):
        return pltpu.make_async_copy(self.src.at[self.me], self.out.at[self.me], self.local.at[0])

    def begin(self):
        self.keep().start()

        @pl.loop(1, 32)
        def _(step):
            self.copy(step).start()

    def finish(self):
        self.keep().wait()

        @pl.loop(1, 32)
        def _(step):
            landed = self.out.at[(self.me + step) % 32]
            remote(
                landed,
                landed,
                self.send.at[0],
                self.recv.at[(self.me + step) % 32],
                self.p.at(0, 1 - self.p.blk),
            ).wait_recv()
            self.copy(step).wait_send()

    @staticmethod
    def scratch():
        return [pltpu.SemaphoreType.DMA((32,)), pltpu.SemaphoreType.DMA((32,)), pltpu.SemaphoreType.DMA((1,))]

    def steps(self, length=18):
        return [self.begin] + [lambda: None] * (length - 2) + [self.finish]


def hbm_call(kernel, shapes, scratch, name, collective_id, args, in_vmem=(), out_vmem=()):
    return pl.pallas_call(
        kernel,
        out_shape=shapes,
        in_specs=[
            pl.BlockSpec(memory_space=pltpu.VMEM if i in in_vmem else pl.ANY) for i in range(len(args))
        ],
        out_specs=[
            pl.BlockSpec(memory_space=pltpu.VMEM if i in out_vmem else pl.ANY) for i in range(len(shapes))
        ],
        scratch_shapes=scratch,
        compiler_params=pltpu.CompilerParams(
            collective_id=collective_id, has_side_effects=True, vmem_limit_bytes=VMEM_BYTES
        ),
        name=name,
    )(*args)


def gather_sems():
    return [pltpu.SemaphoreType.DMA((GatherFlow.SENDS,)), pltpu.SemaphoreType.DMA((GatherFlow.RECVS,))]


def plane_sems(count):
    return gather_sems() + [pltpu.SemaphoreType.DMA((count,))]


def attention_call(
    tokens, small, cotangent, query_weight, key_weight, value_weight, output_weight, cosine, sine, experts
):
    tok_rows, width = tokens.shape
    own_rows = query_weight.shape[0]
    rows = 8 * tok_rows
    share = width // 8
    heads = share // HEAD_DIM
    block = 2 * tok_rows
    blocks = rows // block
    scale = 1.0 / math.sqrt(HEAD_DIM)
    bf16, f32 = jnp.bfloat16, jnp.float32
    line = ScatterFlow.scratch(tok_rows, width, bf16, False)

    def kernel(tok, sml, cot, wq, wk, wv, wo, cos, sin, *refs):
        outs, scratch = refs[:13], refs[13:]
        normed_out, unit_out, row_out, context_out, scale_out, log_out = outs[:6]
        attended, small_out, gathered_out, wide_out, tall_out, gains, place_out = outs[6:]
        held, wide_ref, tall_ref, normed, unit, qkv, context, part, sums, landed = scratch[:10]
        small_held, hits, normed_t, context_t, stores, send, recv = scratch[10:17]
        rest = list(scratch[17:])

        def take(count):
            taken = rest[:count]
            del rest[:count]
            return taken

        place = Place()
        entry_barrier(place, "all")
        flow = ScatterFlow(place, part, attended, take(len(line)), False)
        params = GatherFlow(place, sml, small_held, *take(2), True, True)
        tokens_in = GatherFlow(place, tok, held, *take(2), False)
        others = GatherFlow(place, cot, gathered_out, *take(2), True, others=True)
        plane = PlaneFlow(place, [(place.z, cot)], gathered_out, *take(3))
        weights = ColumnsFlow(place, (wq, wk, wv), wo, wide_ref, tall_ref, *take(3))
        params.begin()
        weights.begin()
        sums[...] = jnp.zeros_like(sums)
        for d in range(1, 4):
            params.along(d)
        plane.begin()
        for d in range(4):
            params.turn(d)
        weights.settle(3)
        weights.settle(0)
        plane.turns()
        weights.settle(1)
        tokens_in.begin()
        weights.turns(3)
        for d in range(4):
            params.corner(d)
        plane.corners()
        weights.settle(2)
        weights.turns(0)
        tokens_in.along(1)
        weights.turns(1)
        params.finish()
        for to in range(32):
            rows_here = small_held[to, own_rows : own_rows + 16, :own_rows].astype(f32)
            gains[:, to * own_rows : (to + 1) * own_rows] = rows_here[:4]
        tokens_in.along(2)
        weights.turns(2)
        first_expert = (place.dp * 4 + place.z) * experts

        @pl.loop(0, 32)
        def _(d):
            named = small_held[d, own_rows + 16 : own_rows + 32].astype(f32)[:TOPK]
            for e in range(experts):
                matches = jnp.where(named == (first_expert + e).astype(f32), 1.0, 0.0)
                hits[e, pl.ds(d, 1)] = jnp.sum(matches, axis=0, keepdims=True)

        earlier = lax.broadcasted_iota(jnp.int32, (tok_rows, tok_rows), 0)
        earlier = earlier < lax.broadcasted_iota(jnp.int32, (tok_rows, tok_rows), 1)
        earlier = earlier.astype(f32).astype(bf16)
        for e in range(experts):
            hit = hits[e]
            rank = inner(hit.astype(bf16), earlier)
            place_out[e] = jnp.where(hit > 0.5, rank, -1.0).astype(jnp.int32)

        tokens_in.along(3)
        plane.finish()
        weights.finish()
        tokens_in.finish()
        others.begin()
        head_gain = gains[1:3, pl.ds(pl.multiple_of(place.col * share, share), share)]

        @pl.loop(0, blocks)
        def _(i):
            at = pl.ds(pl.multiple_of(i * block, block), block)
            values = held[pl.ds(2 * i, 2)].reshape(block, width).astype(f32)
            mean = jnp.mean(values * values, axis=1, keepdims=True)
            low = (values * lax.rsqrt(mean + NORM_EPSILON) * gains[0:1]).astype(bf16)
            normed[at] = low
            linear = inner(low, wide_ref[...])
            unit[at] = linear[:, : 2 * share]
            qkv[at, 2 * share :] = linear[:, 2 * share :].astype(bf16)
            for n in range(2):
                part_lin = linear[:, n * share : (n + 1) * share]
                sums[n : n + 1, at] = jnp.sum(jnp.transpose(part_lin * part_lin), axis=0, keepdims=True)

        def exchange(step):
            to = (place.col + step) % 8
            return remote(
                sums, landed.at[place.col], send.at[step], recv.at[place.col], (place.dp, to // 4, to % 4)
            )

        @pl.loop(1, 8)
        def _(step):
            exchange(step).start()

        landed[place.col] = sums[...]

        @pl.loop(1, 8)
        def _(step):
            col = (place.col + step) % 8
            remote(sums, landed.at[col], send.at[0], recv.at[col], place.at(0, 1 - place.blk)).wait_recv()
            exchange(step).wait_send()

        total = landed[0]
        for col in range(1, 8):
            total = total + landed[col]
        scales = jnp.transpose(lax.rsqrt(total / width + NORM_EPSILON))
        scale_out[...] = scales

        @pl.loop(0, blocks)
        def _(i):
            at = pl.ds(pl.multiple_of(i * block, block), block)
            for n in range(2):
                for h in range(heads):
                    lanes = pl.ds(n * share + h * HEAD_DIM, HEAD_DIM)
                    mine = unit[at, lanes] * scale_out[at, n : n + 1]
                    unit[at, lanes] = mine
                    scaled = mine * head_gain[n : n + 1, h * HEAD_DIM : (h + 1) * HEAD_DIM]
                    turned = scaled * cos[at] + pltpu.roll(scaled, HEAD_DIM // 2, 1) * sin[at]
                    qkv[at, lanes] = turned.astype(bf16)

        out_copies = [
            pltpu.make_async_copy(src, dst, stores.at[n])
            for n, (src, dst) in enumerate(
                (
                    (unit, unit_out),
                    (qkv, row_out),
                    (wide_ref, wide_out),
                    (tall_ref, tall_out),
                    (small_held, small_out),
                )
            )
        ]
        for copy in out_copies:
            copy.start()
        for h in range(heads):
            for i in range(blocks):
                seen = (i + 1) * block
                queries = qkv[i * block : seen, h * HEAD_DIM : (h + 1) * HEAD_DIM]
                keys = qkv[:seen, share + h * HEAD_DIM : share + (h + 1) * HEAD_DIM]
                values = qkv[:seen, 2 * share + h * HEAD_DIM : 2 * share + (h + 1) * HEAD_DIM]
                scores = inner(queries, keys, 1, 1) * scale
                row = lax.broadcasted_iota(jnp.int32, scores.shape, 0) + i * block
                column = lax.broadcasted_iota(jnp.int32, scores.shape, 1)
                scores = jnp.where(column <= row, scores, MASKED)
                peak = jnp.max(scores, axis=1, keepdims=True)
                exponent = jnp.exp(scores - peak)
                sum_row = jnp.sum(exponent, axis=1, keepdims=True)
                low = (exponent / sum_row).astype(bf16)
                context[i * block : seen, h * HEAD_DIM : (h + 1) * HEAD_DIM] = inner(low, values).astype(bf16)
                log_out[i * block : seen, h : h + 1] = peak + jnp.log(sum_row)
            if h == 0:
                others.along(1)

        @pl.loop(0, blocks)
        def _(i):
            at = pl.ds(pl.multiple_of(i * block, block), block)
            rows_here = inner(context[at], tall_ref[...]).astype(bf16)
            part[pl.ds(2 * i, 2)] = rows_here.reshape(2, tok_rows, width)

        flow.begin()
        others.along(2)
        for i in range(blocks):
            at = slice(i * block, (i + 1) * block)
            normed_t[:, at] = jnp.transpose(normed[at])
            context_t[:, at] = jnp.transpose(context[at])
        last = [
            pltpu.make_async_copy(normed_t, normed_out, stores.at[5]),
            pltpu.make_async_copy(context_t, context_out, stores.at[6]),
        ]
        for copy in last:
            copy.start()
        flow.stage3(0)
        flow.stage3(1)
        flow.chain(0)
        others.along(3)
        others.turn(1)
        flow.stage3(2)
        flow.chain(1)
        flow.chain(2)
        others.turn(2)
        others.corner(1)
        flow.stage3(3)
        flow.final()
        others.turn(3)
        others.corner(2)
        others.corner(3)
        others.finish()
        for copy in out_copies + last:
            copy.wait()

    shapes = [
        jax.ShapeDtypeStruct((width, rows), bf16),
        jax.ShapeDtypeStruct((rows, 2 * share), f32),
        jax.ShapeDtypeStruct((rows, 3 * share), bf16),
        jax.ShapeDtypeStruct((share, rows), bf16),
        jax.ShapeDtypeStruct((rows, 8), f32),
        jax.ShapeDtypeStruct((rows, 8), f32),
        jax.ShapeDtypeStruct((tok_rows, width), f32),
        jax.ShapeDtypeStruct((32,) + small.shape, bf16),
        jax.ShapeDtypeStruct((32,) + cotangent.shape, bf16),
        jax.ShapeDtypeStruct((width, 3 * share), bf16),
        jax.ShapeDtypeStruct((share, width), bf16),
        jax.ShapeDtypeStruct((4, width), f32),
        jax.ShapeDtypeStruct((experts, 32, tok_rows), jnp.int32),
    ]
    scratch = [
        pltpu.VMEM((8, tok_rows, width), bf16),
        pltpu.VMEM((width, 3 * share), bf16),
        pltpu.VMEM((share, width), bf16),
        pltpu.VMEM((rows, width), bf16),
        pltpu.VMEM((rows, 2 * share), f32),
        pltpu.VMEM((rows, 3 * share), bf16),
        pltpu.VMEM((rows, share), bf16),
        pltpu.VMEM((8, tok_rows, width), bf16),
        pltpu.VMEM((8, rows), f32),
        pltpu.VMEM((8, 8, rows), f32),
        pltpu.VMEM((32,) + small.shape, bf16),
        pltpu.VMEM((experts, 32, tok_rows), f32),
        pltpu.VMEM((width, rows), bf16),
        pltpu.VMEM((share, rows), bf16),
        pltpu.SemaphoreType.DMA((7,)),
        pltpu.SemaphoreType.DMA((8,)),
        pltpu.SemaphoreType.DMA((8,)),
    ]
    scratch += line + gather_sems() * 3 + plane_sems(1)
    scratch += [
        pltpu.SemaphoreType.DMA((ColumnsFlow.SENDS,)),
        pltpu.SemaphoreType.DMA((ColumnsFlow.RECVS,)),
        pltpu.SemaphoreType.DMA((ColumnsFlow.LOCALS,)),
    ]
    args = (tokens, small, cotangent, query_weight, key_weight, value_weight, output_weight, cosine, sine)
    return hbm_call(kernel, shapes, scratch, "attention", 5, args, (7, 8), (4, 5, 11, 12))


def run_units(work, first, last):
    @pl.loop(first, last)
    def _(unit):
        work.run(unit)


def features_call(features, probs, places, cotangent_all, down_weight, per):
    experts, hidden, width = down_weight.shape
    slots = places.shape[0] * per

    def kernel(feature_ref, prob_ref, place_ref, cot, weight, feature_out, prob_out, rows, plain, *scratch):
        place = Place()
        entry_barrier(place, "planes")
        small = GatherFlow(place, prob_ref, prob_out, scratch[2], scratch[3], True)
        flow = GatherFlow(place, feature_ref, feature_out, scratch[0], scratch[1], True)
        work = PickWork(place_ref, cot, weight, rows, plain, scratch[4:])

        flows = (small, flow)

        def along(d):
            for each in flows:
                each.along(d)

        def turn(d):
            for each in flows:
                each.turn(d)

        def corner(d):
            for each in flows:
                each.corner(d)

        for each in flows:
            each.begin()
        work.begin()
        run_units(work, 0, 4)
        along(1)
        turn(0)
        run_units(work, 4, 9)
        along(2)
        corner(0)
        run_units(work, 9, 13)
        along(3)
        turn(1)
        run_units(work, 13, work.units)
        corner(1)
        turn(2)
        corner(2)
        turn(3)
        corner(3)
        for each in flows:
            each.finish()
        work.finish()

    shapes = [
        jax.ShapeDtypeStruct((32,) + features.shape, features.dtype),
        jax.ShapeDtypeStruct((32,) + probs.shape, probs.dtype),
        jax.ShapeDtypeStruct((experts, slots, width), features.dtype),
        jax.ShapeDtypeStruct((experts, slots, hidden), jnp.float32),
    ]
    scratch = gather_sems() * 2 + PickWork.scratch(cotangent_all, down_weight, per)
    return hbm_call(
        kernel, shapes, scratch, "features", 6, (features, probs, places, cotangent_all, down_weight), (2,)
    )


def experts_back_call(input_rows, row_grads, places, hidden, weight, tok_rows):
    width = input_rows.shape[2]
    pairs, experts, pair_rows = places.shape
    per = input_rows.shape[1] // pairs
    sums = ScatterFlow.scratch(tok_rows, width, input_rows.dtype, True)
    out_shape = jax.ShapeDtypeStruct((pairs, pair_rows, width), input_rows.dtype)
    dealt = jax.ShapeDtypeStruct((2 * pairs, 8, tok_rows), jnp.float32)
    put_scratch = PutWork.scratch(input_rows, per)

    def kernel(source, grad_ref, place_ref, hidden_ref, weight_ref, out, dealt_out, mixed, *scratch):
        place = Place()
        entry_barrier(place, "all")
        stage, deals = scratch[:2]
        rest = scratch[2 + len(put_scratch) + 3 :]
        deal = DealFlow(place, deals, dealt_out, *scratch[2 + len(put_scratch) :][:3])
        flow = MadeFlow(place, out, rest[: len(sums)], stage)
        put = PutWork(place, place_ref, source, grad_ref, flow, deals, scratch[2 : 2 + len(put_scratch)])
        work = OutputWork(place_ref, hidden_ref, weight_ref, mixed, rest[len(sums) :])
        put.load(3, 0, 0).start()
        work.begin()
        deals[...] = jnp.zeros_like(deals)
        put.column(3)
        put.column(2)
        for i in range(4):
            flow.stage1(i)
        put.column(1)
        put.column(0)
        deal.begin()
        flow.stage2(0)
        flow.stage2(1)
        run_units(work, 0, 8)
        flow.stage2(2)
        flow.stage2(3)
        run_units(work, 8, 16)
        flow.stage3(0)
        flow.stage3(1)
        flow.chain(0)
        run_units(work, 16, 20)
        flow.stage3(2)
        flow.chain(1)
        flow.chain(2)
        run_units(work, 20, work.units)
        flow.stage3(3)
        flow.final()
        work.finish()
        deal.finish()

    shapes = [jax.ShapeDtypeStruct((tok_rows, width), jnp.float32), dealt, out_shape]
    scratch = [
        pltpu.VMEM((2, 4, tok_rows, width), input_rows.dtype),
        pltpu.VMEM(dealt.shape, jnp.float32),
    ]
    scratch += put_scratch + DealFlow.scratch() + sums + OutputWork.scratch(hidden, weight, out_shape)
    return hbm_call(
        kernel, shapes, scratch, "experts_back", 3, (input_rows, row_grads, places, hidden, weight), (1, 2)
    )


def attention_back_call(
    grad, logit_grad, out_part, tokens, gain, feature_row, wide, tall, head_gains, cosine, sine, kept
):
    tok_rows, width = grad.shape
    rows = kept[0].shape[1]
    share = tall.shape[0]
    heads = share // HEAD_DIM
    own_rows = width // 32
    block = 2 * tok_rows
    blocks = rows // block
    band_rows = width // 4
    height = tok_rows // 2
    scale = 1.0 / math.sqrt(HEAD_DIM)
    bf16, f32 = jnp.bfloat16, jnp.float32
    line = ScatterFlow.scratch(tok_rows, width, bf16, False)
    mixed = ScatterFlow.scratch(height, width, bf16, True)
    sums = SumsFlow.scratch(((band_rows, 2 * share), (share // 4, width), (band_rows, share)))
    flow_scratch = line + mixed + mixed[-5:] + sums + DealFlow.scratch() + gather_sems() * 2
    flow_scratch += [pltpu.SemaphoreType.REGULAR]

    def kernel(*refs):
        grad_ref, logit_ref, part_ref, tok_in, gain_ref, feature_ref, wide_in, tall_in = refs[:8]
        head_gain, cos, sin, normed_in, unit_in, qkv_in, context_in, scale_ref, log_ref = refs[8:17]
        logit_out, first_out, second_out, normed_grad, wide_out, tall_out, gain_out = refs[17:24]
        scratch = refs[24:]
        grads, tok, wide_ref, tall_ref, normed, unit, qkv, context, context_grad = scratch[:9]
        grad_q, grad_k, grad_v, low_grads, dots, landed, deals, dealt, tall_grad = scratch[9:18]
        ins, send, recv = scratch[18:21]
        rest = list(scratch[21:])

        def take(count):
            taken = rest[:count]
            del rest[:count]
            return taken

        place = Place()
        entry_barrier(place, "all")
        line_scratch, mixed_scratch, more = take(len(line)), take(len(mixed)), take(5)
        weights = SumsFlow(place, wide_out, tall_out, take(len(sums)))
        deal = DealFlow(place, deals, dealt, *take(3))
        gather = GatherFlow(place, grad_ref, grads, *take(2), False)
        logits = GatherFlow(place, logit_ref, logit_out, *take(2), True)
        freed = take(1)[0]
        flow = ScatterFlow(place, grads, normed_grad, line_scratch, False)
        first = ScatterFlow(place, part_ref, first_out, mixed_scratch, True, (0, height))
        second = ScatterFlow(
            place, part_ref, second_out, mixed_scratch[:-5] + more, True, (height, height)
        )
        gather.begin()
        logits.begin()
        first.begin()
        sources = (tok_in, wide_in, tall_in, normed_in, unit_in, qkv_in, context_in)
        held = (tok, wide_ref, tall_ref, normed, unit, qkv, context)
        loads = [pltpu.make_async_copy(s, d, ins.at[n]) for n, (s, d) in enumerate(zip(sources, held))]
        for copy in loads:
            copy.start()
        deals[...] = jnp.zeros_like(deals)
        dots[...] = jnp.zeros_like(dots)
        first.stage1(0)
        first.stage1(1)
        gather.along(1)
        logits.along(1)
        logits.turn(0)
        first.stage1(2)
        first.stage1(3)
        first.stage2(0)
        gather.along(2)
        logits.along(2)
        logits.turn(1)
        first.stage2(1)
        first.stage2(2)
        gather.along(3)
        logits.along(3)
        logits.turn(2)
        logits.turn(3)
        first.stage3(0)
        first.stage2(3)
        first.stage3(1)
        first.chain(0)
        for d in range(4):
            logits.corner(d)
        gather.finish()
        for copy in loads:
            copy.wait()
        first.stage3(2)
        first.chain(1)
        first.stage3(3)
        tell_partners(place, freed)

        @pl.loop(0, blocks)
        def _(i):
            at = pl.ds(pl.multiple_of(i * block, block), block)
            values = grads[pl.ds(2 * i, 2)].reshape(block, width)
            context_grad[at] = inner(values, tall_ref[...], 1, 1).astype(bf16)

        wait_partners(place, freed)
        first.leave_all()
        second.begin((3, 2, 1))
        first.chain(2)

        @pl.loop(0, 4)
        def _(i):
            lanes = pl.ds(pl.multiple_of(i * band_rows, band_rows), band_rows)
            values = grads[:, :, lanes].reshape(rows, band_rows)
            tall_grad[:, lanes] = inner(context[...], values).astype(bf16)

        for k in range(4):
            at = pl.ds(pl.multiple_of(place.column(k) * own_rows, own_rows), own_rows)
            weights.acc[1][k] = tall_grad[at]
        weights.corners(1)
        first.final()
        second.begin((0,))

        def back_block(h, i):
            seen = (i + 1) * block
            here, lanes = slice(i * block, seen), slice(h * HEAD_DIM, (h + 1) * HEAD_DIM)
            queries = qkv[here, lanes]
            keys = qkv[:seen, share + h * HEAD_DIM : share + (h + 1) * HEAD_DIM]
            values = qkv[:seen, 2 * share + h * HEAD_DIM : 2 * share + (h + 1) * HEAD_DIM]
            outer = context_grad[here, lanes]
            scores = inner(queries, keys, 1, 1) * scale
            row = lax.broadcasted_iota(jnp.int32, scores.shape, 0) + i * block
            column = lax.broadcasted_iota(jnp.int32, scores.shape, 1)
            probs = jnp.where(column <= row, jnp.exp(scores - log_ref[here, h : h + 1]), 0.0)
            prob_dots = inner(outer, values, 1, 1)
            delta = jnp.sum(probs * prob_dots, axis=1, keepdims=True)
            score_grad = (probs * (prob_dots - delta)).astype(bf16)
            grad_q[here, lanes] = inner(score_grad, keys) * scale
            key_part = inner(score_grad, queries, 0, 0) * scale
            value_part = inner(probs.astype(bf16), outer, 0, 0)
            if i == blocks - 1:
                grad_k[:, lanes] = key_part
                grad_v[:, lanes] = value_part
            else:
                grad_k[:seen, lanes] += key_part
                grad_v[:seen, lanes] += value_part

        back_block(0, 3)
        back_block(0, 2)
        second.stage1(0)
        second.stage1(1)
        back_block(0, 1)
        back_block(0, 0)
        second.stage1(2)
        second.stage1(3)
        back_block(1, 3)
        back_block(1, 2)
        weights.sides(1)
        second.stage2(0)
        back_block(1, 1)
        back_block(1, 0)
        low_grads[:, 2 * share :] = grad_v[...].astype(bf16)

        def band_grad(which, k):
            band = pl.ds(pl.multiple_of(place.column(k) * band_rows, band_rows), band_rows)
            lanes = slice(2 * share, 3 * share) if which == 2 else slice(0, 2 * share)
            weights.acc[which][k] = inner(normed[band], low_grads[:, lanes]).astype(bf16)

        for k in (3, 2, 1, 0):
            band_grad(2, k)

        second.stage2(1)

        @pl.loop(0, blocks)
        def _(i):
            at = pl.ds(pl.multiple_of(i * block, block), block)
            for n, grad_n in enumerate((grad_q, grad_k)):
                total = jnp.zeros((block, 1), f32)
                for h in range(heads):
                    lanes = slice(h * HEAD_DIM, (h + 1) * HEAD_DIM)
                    turned = grad_n[at, lanes].astype(bf16).astype(f32)
                    back = turned * cos[at] - pltpu.roll(turned, HEAD_DIM // 2, 1) * sin[at]
                    mine = unit[at, n * share + h * HEAD_DIM : n * share + (h + 1) * HEAD_DIM]
                    for j in range(HEAD_DIM // own_rows):
                        to = place.col * 4 + h * (HEAD_DIM // own_rows) + j
                        columns = slice(j * own_rows, (j + 1) * own_rows)
                        deals[to, 1 + n : 2 + n, :own_rows] += jnp.sum(
                            (back * mine)[:, columns], axis=0, keepdims=True
                        )
                    weighted = back * head_gain[n : n + 1, lanes]
                    grad_n[at, lanes] = weighted
                    total += jnp.sum(weighted * mine, axis=1, keepdims=True)
                dots[n : n + 1, at] = jnp.transpose(jnp.broadcast_to(total, (block, 128)))[:1]

        def exchange(step):
            to = (place.col + step) % 8
            return remote(
                dots, landed.at[place.col], send.at[step], recv.at[place.col], (place.dp, to // 4, to % 4)
            )

        @pl.loop(1, 8)
        def _(step):
            exchange(step).start()

        landed[place.col] = dots[...]

        @pl.loop(1, 8)
        def _(step):
            col = (place.col + step) % 8
            remote(dots, landed.at[col], send.at[0], recv.at[col], place.at(0, 1 - place.blk)).wait_recv()
            exchange(step).wait_send()

        total_dots = landed[0]
        for col in range(1, 8):
            total_dots = total_dots + landed[col]
        columns = jnp.transpose(total_dots / width)
        for n, grad_n in enumerate((grad_q, grad_k)):
            mine = unit[:, n * share : (n + 1) * share]
            low = scale_ref[:, n : n + 1] * (grad_n[...] - mine * columns[:, n : n + 1])
            low_grads[:, n * share : (n + 1) * share] = low.astype(bf16)

        weights.corners(2)
        band_grad(0, 3)
        weights.corners(0)

        @pl.loop(0, blocks)
        def _(i):
            at = pl.ds(pl.multiple_of(i * block, block), block)
            values = inner(low_grads[at], wide_ref[...], 1, 1).astype(bf16)
            grads[pl.ds(2 * i, 2)] = values.reshape(2, tok_rows, width)

        flow.begin()
        weights.sides(2)
        band_grad(0, 2)
        band_grad(0, 1)
        flow.stage3(0)
        weights.sides(0)
        flow.stage3(1)
        band_grad(0, 0)
        second.stage2(2)
        flow.chain(0)
        weights.total(2)
        weights.hand_out((2,))
        second.stage2(3)
        flow.stage3(2)
        flow.chain(1)
        weights.total(0)
        weights.hand_out((0, 1))
        second.stage3(0)
        second.stage3(1)
        flow.chain(2)
        flow.stage3(3)
        second.chain(0)
        second.stage3(2)
        second.chain(1)
        second.chain(2)
        weights.total(1)
        weights.hand_out_tall()
        flow.final()

        values = tok[...].astype(f32)
        scaled = values * lax.rsqrt(jnp.mean(values * values, axis=1, keepdims=True) + NORM_EPSILON)
        attention_row = jnp.sum(scaled * flow.sum[...], axis=0, keepdims=True)
        for to in range(32):
            lanes = slice(to * own_rows, (to + 1) * own_rows)
            deals[to, 0:1, :own_rows] = attention_row[:, lanes]
            deals[to, 3:4, :own_rows] = feature_ref[:, lanes]
        deal.begin()
        second.stage3(3)
        second.final()
        logits.finish()
        weights.finish()
        deal.finish()
        total = dealt[0]
        for index in range(1, 32):
            total = total + dealt[index]
        gain_out[...] = total

    shapes = [
        jax.ShapeDtypeStruct((32,) + logit_grad.shape, logit_grad.dtype),
        jax.ShapeDtypeStruct((height, width), f32),
        jax.ShapeDtypeStruct((height, width), f32),
        jax.ShapeDtypeStruct((tok_rows, width), f32),
        jax.ShapeDtypeStruct((3, own_rows, width), bf16),
        jax.ShapeDtypeStruct((own_rows, width), bf16),
        jax.ShapeDtypeStruct((8, 128), f32),
    ]
    scratch = [
        pltpu.VMEM((8, tok_rows, width), bf16),
        pltpu.VMEM((tok_rows, width), bf16),
        pltpu.VMEM(wide.shape, bf16),
        pltpu.VMEM(tall.shape, bf16),
        pltpu.VMEM((width, rows), bf16),
        pltpu.VMEM((rows, 2 * share), f32),
        pltpu.VMEM((rows, 3 * share), bf16),
        pltpu.VMEM((share, rows), bf16),
        pltpu.VMEM((rows, share), bf16),
        pltpu.VMEM((rows, share), f32),
        pltpu.VMEM((rows, share), f32),
        pltpu.VMEM((rows, share), f32),
        pltpu.VMEM((rows, 3 * share), bf16),
        pltpu.VMEM((8, rows), f32),
        pltpu.VMEM((8, 8, rows), f32),
        pltpu.VMEM((32, 8, 128), f32),
        pltpu.VMEM((32, 8, 128), f32),
        pltpu.VMEM(tall.shape, bf16),
        pltpu.SemaphoreType.DMA((7,)),
        pltpu.SemaphoreType.DMA((8,)),
        pltpu.SemaphoreType.DMA((8,)),
    ]
    args = (grad, logit_grad, out_part, tokens, gain, feature_row, wide, tall, head_gains, cosine, sine)
    return hbm_call(
        kernel,
        shapes,
        scratch + flow_scratch,
        "attention_back",
        2,
        args + tuple(kept),
        (4, 5, 8, 9, 10, 15, 16),
        (6,),
    )


def turn_tables(count):
    half = HEAD_DIM // 2
    frequencies = np.exp(-math.log(ROPE_BASE) * 2.0 * np.arange(half) / HEAD_DIM).astype(np.float32)
    angles = np.arange(count, dtype=np.float32)[:, None] * frequencies[None, :]
    return np.cos(angles), np.sin(angles)


def product(left, right, sums, batches=((), ()), out=jnp.float32):
    return lax.dot_general(left, right, (sums, batches), preferred_element_type=out)


def body_fast(
    tokens,
    query_weight,
    key_weight,
    value_weight,
    output_weight,
    router_weight,
    attention_gain,
    query_gain,
    key_gain,
    feature_gain,
    gate_weight,
    up_weight,
    down_weight,
    routes,
    cotangent,
):
    tok_rows, model_width = tokens.shape
    column_size = 8
    devices = 32
    share = model_width // column_size
    heads_here = share // HEAD_DIM
    seq_rows = tok_rows * column_size
    experts_here = gate_weight.shape[0]
    own_rows = query_weight.shape[0]
    score_scale = 1.0 / math.sqrt(HEAD_DIM)
    column = lax.axis_index(BLK) * 4 + lax.axis_index(SP)
    f32, bf16 = jnp.float32, jnp.bfloat16

    gains = jnp.stack([attention_gain, query_gain, key_gain, feature_gain])
    small = jnp.concatenate(
        [
            jnp.pad(router_weight, ((0, 0), (0, 128 - EXPERTS))),
            jnp.pad(gains, ((0, 12), (0, 128 - own_rows))),
            jnp.pad(routes.T.astype(bf16), ((0, 16 - TOPK), (0, 0))),
        ],
        axis=0,
    )
    half_cos, half_sin = turn_tables(seq_rows)
    cosine = np.concatenate([half_cos, half_cos], axis=1)
    sine = np.concatenate([-half_sin, half_sin], axis=1)
    *kept, attended, small_all, cotangent_all, wide_weight, tall_weight, gain_all, slots = attention_call(
        tokens, small, cotangent, query_weight, key_weight, value_weight, output_weight, cosine, sine, experts_here
    )
    router_full = small_all[:, :own_rows, :EXPERTS].reshape(model_width, EXPERTS)
    gain_attention, gain_feature = gain_all[0], gain_all[3]
    head_gains = lax.dynamic_slice_in_dim(gain_all[1:3], column * share, share, axis=1)

    tokens_f = tokens.astype(f32)
    residual = tokens_f + attended
    features_f, feature_pull = jax.vjp(norm_apply, residual, gain_feature)
    features = features_f.astype(bf16)
    logits = jnp.dot(features, router_full, preferred_element_type=f32)
    router_probs = jax.nn.softmax(logits, axis=-1)

    first_expert = (lax.axis_index(DP) * 4 + lax.axis_index(SP)) * experts_here
    pairs, pair_rows, per = devices // 2, 2 * tok_rows, 2 * CAP
    slots = slots.reshape(experts_here, pairs, 2, tok_rows).transpose(1, 0, 2, 3)
    second = CAP * jnp.arange(2, dtype=jnp.int32)[None, None, :, None]
    places = jnp.where(slots < 0, -1, slots + second).reshape(pairs, experts_here, pair_rows)
    cotangent_all = cotangent_all.reshape(pairs, pair_rows, model_width)
    features_all, probs_all, grad_rows, plain_grads = features_call(
        features, router_probs.T, places, cotangent_all, down_weight, per
    )
    probs_here = lax.dynamic_slice_in_dim(probs_all, first_expert, experts_here, axis=1)
    features_all = features_all.reshape(pairs, pair_rows, model_width)
    expert_rows, row_probs = pick_rows(places, probs_here, features_all, per)
    weighted_hidden, gate_grad, up_grad, input_rows, row_grads = run_experts(
        expert_rows, plain_grads, row_probs, gate_weight, up_weight
    )
    input_grad, prob_parts, out_part = experts_back_call(
        input_rows, row_grads, places, weighted_hidden, down_weight, tok_rows
    )
    out_part = out_part.reshape(devices, tok_rows, model_width)

    prob_parts = prob_parts.reshape(4, 2, 4, 8, tok_rows)[:, :, :, :experts_here]
    prob_grad = jnp.sum(prob_parts, axis=1).reshape(EXPERTS, tok_rows).T
    logit_grad = (
        router_probs * (prob_grad - jnp.sum(prob_grad * router_probs, axis=-1, keepdims=True))
    ).astype(bf16)
    feature_grad = jnp.dot(logit_grad, router_full.T, preferred_element_type=f32) + input_grad
    residual_part, feature_gain_grad = feature_pull(feature_grad)
    residual_grad = cotangent.astype(f32) + residual_part
    attended_grad = residual_grad.astype(bf16)
    logit_all, first_half, second_half, normed_grad, wide_back, tall_back, gain_sums = attention_back_call(
        attended_grad,
        logit_grad.reshape(tok_rows // 2, 2 * EXPERTS),
        out_part,
        tokens,
        gain_attention[None],
        feature_gain_grad[None],
        wide_weight,
        tall_weight,
        head_gains,
        cosine,
        sine,
        kept,
    )
    own_index = (lax.axis_index(DP) * 2 + lax.axis_index(BLK)) * 4 + lax.axis_index(SP)
    own_features = lax.dynamic_slice_in_dim(
        features_all.reshape(devices * tok_rows, model_width), own_index * own_rows, own_rows, axis=1
    )
    router_grad = product(own_features, logit_all.reshape(devices * tok_rows, EXPERTS), ((0,), (0,)))

    _, attention_pull = jax.vjp(lambda values: norm_apply(values, gain_attention), tokens_f)
    input_gradient = residual_grad + attention_pull(normed_grad)[0]
    block_output = (residual + jnp.concatenate([first_half, second_half], axis=0)).astype(bf16)
    gate_grad_local, up_grad_local, down_grad_local = expert_weight_grads(
        expert_rows, grad_rows, weighted_hidden, gate_grad, up_grad
    )
    return (
        block_output,
        input_gradient,
        wide_back[0].astype(f32),
        wide_back[1].astype(f32),
        wide_back[2].astype(f32),
        tall_back.astype(f32),
        router_grad,
        gain_sums[0, :own_rows],
        gain_sums[1, :own_rows],
        gain_sums[2, :own_rows],
        gain_sums[3, :own_rows],
        gate_grad_local,
        up_grad_local,
        down_grad_local,
    )


def body(
    tokens,
    query_weight,
    key_weight,
    value_weight,
    output_weight,
    router_weight,
    attention_gain,
    query_gain,
    key_gain,
    feature_gain,
    gate_weight,
    up_weight,
    down_weight,
    routes,
    cotangent,
):
    sp_size = lax.axis_size(SP)
    blk_size = lax.axis_size(BLK)
    dp_size = lax.axis_size(DP)
    tok_rows = tokens.shape[0]
    model_width = tokens.shape[1]
    heads_here = HEADS // sp_size
    head_width = heads_here * HEAD_DIM
    experts_here = gate_weight.shape[0]
    capacity = CAP
    score_scale = 1.0 / math.sqrt(HEAD_DIM)
    (
        query_full,
        key_full,
        value_full,
        output_full,
        router_full,
        gain_attention,
        gain_query,
        gain_key,
        gain_feature,
    ) = (
        lax.all_gather(query_weight, AXES, axis=0, tiled=True),
        lax.all_gather(key_weight, AXES, axis=0, tiled=True),
        lax.all_gather(value_weight, AXES, axis=0, tiled=True),
        lax.all_gather(output_weight, AXES, axis=0, tiled=True),
        lax.all_gather(router_weight, AXES, axis=0, tiled=True),
        lax.all_gather(attention_gain, AXES, axis=0, tiled=True),
        lax.all_gather(query_gain, AXES, axis=0, tiled=True),
        lax.all_gather(key_gain, AXES, axis=0, tiled=True),
        lax.all_gather(feature_gain, AXES, axis=0, tiled=True),
    )
    gain_attention = gain_attention.astype(jnp.float32)
    gain_query = gain_query.astype(jnp.float32)
    gain_key = gain_key.astype(jnp.float32)
    gain_feature = gain_feature.astype(jnp.float32)
    tokens_f = tokens.astype(jnp.float32)
    normed_f, attention_pull = jax.vjp(norm_apply, tokens_f, gain_attention)
    normed = normed_f.astype(jnp.bfloat16)
    query_lin = jnp.dot(normed, query_full, preferred_element_type=jnp.float32)
    key_lin = jnp.dot(normed, key_full, preferred_element_type=jnp.float32)
    value_rows = jnp.dot(normed, value_full, preferred_element_type=jnp.float32).astype(
        jnp.bfloat16
    )
    seq_start = (lax.axis_index(BLK) * sp_size + lax.axis_index(SP)) * tok_rows
    cosine, sine = rope_tables(seq_start + jnp.arange(tok_rows, dtype=jnp.int32), HEAD_DIM)

    def rotated(linear, norm_gain):
        normalized = norm_apply(linear, norm_gain).reshape(
            tok_rows, model_width // HEAD_DIM, HEAD_DIM
        )
        return rotate(normalized, cosine, sine).reshape(tok_rows, model_width)

    query_rot, query_pull = jax.vjp(rotated, query_lin, gain_query)
    key_rot, key_pull = jax.vjp(rotated, key_lin, gain_key)
    query_heads, key_heads, value_heads = (
        lax.all_to_all(
            query_rot.astype(jnp.bfloat16).reshape(tok_rows, sp_size, head_width),
            SP,
            split_axis=1,
            concat_axis=0,
            tiled=True,
        ),
        lax.all_to_all(
            key_rot.astype(jnp.bfloat16).reshape(tok_rows, sp_size, head_width),
            SP,
            split_axis=1,
            concat_axis=0,
            tiled=True,
        ),
        lax.all_to_all(
            value_rows.reshape(tok_rows, sp_size, head_width),
            SP,
            split_axis=1,
            concat_axis=0,
            tiled=True,
        ),
    )
    head_rows = sp_size * tok_rows
    keys_all, values_all = (
        lax.all_gather(key_heads, BLK, axis=0, tiled=True),
        lax.all_gather(value_heads, BLK, axis=0, tiled=True),
    )
    key_rows = keys_all.shape[0]
    keys_all = keys_all.reshape(key_rows, heads_here, HEAD_DIM)
    values_all = values_all.reshape(key_rows, heads_here, HEAD_DIM)
    block_rows = math.gcd(512, head_rows)
    blocks = head_rows // block_rows
    query_base = lax.axis_index(BLK) * head_rows
    key_places = jnp.arange(key_rows, dtype=jnp.int32)
    query_blocks = query_heads.reshape(blocks, block_rows, heads_here, HEAD_DIM)
    block_starts = jnp.arange(blocks, dtype=jnp.int32) * block_rows

    def masked_scores(block_queries, block_start):
        scores = (
            jnp.einsum("qhd,khd->hqk", block_queries, keys_all, preferred_element_type=jnp.float32)
            * score_scale
        )
        query_places = query_base + block_start + jnp.arange(block_rows, dtype=jnp.int32)
        causal = key_places[None, :] <= query_places[:, None]
        return jnp.where(causal[None], scores, MASKED)

    def attend_block(block_input):
        block_queries, block_start = block_input
        scores = masked_scores(block_queries, block_start)
        row_peak = jnp.max(scores, axis=-1, keepdims=True)
        exponent = jnp.exp(scores - row_peak)
        row_total = jnp.sum(exponent, axis=-1, keepdims=True)
        attn_weights = (exponent / row_total).astype(jnp.bfloat16)
        context = jnp.einsum(
            "hqk,khd->qhd", attn_weights, values_all, preferred_element_type=jnp.float32
        )
        return (context.astype(jnp.bfloat16), (row_peak + jnp.log(row_total))[..., 0])

    context_blocks, logsum = lax.map(attend_block, (query_blocks, block_starts))
    context_rows = lax.all_to_all(
        context_blocks.reshape(head_rows, 1, head_width),
        SP,
        split_axis=0,
        concat_axis=1,
        tiled=True,
    ).reshape(tok_rows, model_width)
    attended = jnp.dot(context_rows, output_full, preferred_element_type=jnp.float32)
    residual = tokens_f + attended
    features_f, feature_pull = jax.vjp(norm_apply, residual, gain_feature)
    features = features_f.astype(jnp.bfloat16)
    logits = jnp.dot(features, router_full, preferred_element_type=jnp.float32)
    router_probs = jax.nn.softmax(logits, axis=-1)
    flat_experts, slot_rank = rank_slots(routes)
    slot_index = flat_experts * capacity + slot_rank
    token_of = jnp.arange(tok_rows * TOPK, dtype=jnp.int32) // TOPK
    slot_token = jnp.zeros((EXPERTS * capacity,), jnp.int32).at[slot_index].set(token_of)
    slot_used = jnp.zeros((EXPERTS * capacity,), jnp.bool_).at[slot_index].set(True)
    slot_rows = jnp.where(slot_used[:, None], features[slot_token], jnp.zeros((), jnp.bfloat16))

    def spread_halves(per_slot):
        grouped = per_slot.reshape(dp_size, 1, sp_size, experts_here, capacity, model_width)
        grouped = jnp.broadcast_to(
            grouped, (dp_size, blk_size, sp_size, experts_here, capacity, model_width)
        )
        return grouped.reshape(dp_size * blk_size * sp_size, experts_here, capacity, model_width)

    def join_halves(returned):
        grouped = returned.reshape(
            dp_size, blk_size, sp_size, experts_here, capacity, model_width
        ).astype(jnp.float32)
        return jnp.sum(grouped, axis=1).reshape(EXPERTS * capacity, model_width)

    send_rows = spread_halves(slot_rows)
    arrived = lax.all_to_all(
        send_rows, AXES, split_axis=0, concat_axis=0, tiled=True
    )
    gate_values = jnp.einsum(
        "secd,edf->secf", arrived, gate_weight, preferred_element_type=jnp.float32
    )
    up_values = jnp.einsum("secd,edf->secf", arrived, up_weight, preferred_element_type=jnp.float32)
    hidden = (jax.nn.silu(gate_values) * up_values).astype(jnp.bfloat16)
    part_out = jnp.einsum(
        "secf,efd->secd", hidden, down_weight, preferred_element_type=jnp.float32
    ).astype(jnp.bfloat16)
    returned = lax.all_to_all(
        part_out, AXES, split_axis=0, concat_axis=0, tiled=True
    )
    expert_out = join_halves(returned)
    route_rows = expert_out[slot_index].reshape(tok_rows, TOPK, model_width)
    route_probs = jnp.take_along_axis(router_probs, routes, axis=1)
    block_output = (residual + jnp.sum(route_probs[:, :, None] * route_rows, axis=1)).astype(
        jnp.bfloat16
    )
    out_grad = cotangent.astype(jnp.float32)
    route_grad = (
        (route_probs[:, :, None] * out_grad[:, None, :])
        .astype(jnp.bfloat16)
        .reshape(tok_rows * TOPK, model_width)
    )
    prob_route = jnp.sum(out_grad[:, None, :] * route_rows, axis=-1)
    expert_ids = jnp.arange(EXPERTS, dtype=jnp.int32)
    prob_grad = jnp.sum(
        jnp.where(routes[:, :, None] == expert_ids[None, None, :], prob_route[:, :, None], 0.0),
        axis=1,
    )
    logit_grad = (
        router_probs * (prob_grad - jnp.sum(prob_grad * router_probs, axis=-1, keepdims=True))
    ).astype(jnp.bfloat16)
    router_grad_full = jnp.dot(features.T, logit_grad, preferred_element_type=jnp.float32)
    gradient_slots = (
        jnp.zeros((EXPERTS * capacity, model_width), jnp.bfloat16).at[slot_index].set(route_grad)
    )
    gradient_send = spread_halves(gradient_slots)
    gradient_arrived, rows_arrived = (
        lax.all_to_all(gradient_send, AXES, split_axis=0, concat_axis=0, tiled=True),
        lax.all_to_all(send_rows, AXES, split_axis=0, concat_axis=0, tiled=True),
    )
    gate_values = jnp.einsum(
        "secd,edf->secf", rows_arrived, gate_weight, preferred_element_type=jnp.float32
    )
    up_values = jnp.einsum(
        "secd,edf->secf", rows_arrived, up_weight, preferred_element_type=jnp.float32
    )
    sigmoid_values = jax.nn.sigmoid(gate_values)
    silu_values = gate_values * sigmoid_values
    hidden = (silu_values * up_values).astype(jnp.bfloat16)
    hidden_grad = jnp.einsum(
        "secd,efd->secf", gradient_arrived, down_weight, preferred_element_type=jnp.float32
    ).astype(jnp.bfloat16)
    down_grad_local = jnp.einsum(
        "secf,secd->efd", hidden, gradient_arrived, preferred_element_type=jnp.float32
    )
    hidden_wide = hidden_grad.astype(jnp.float32)
    gate_grad = (
        hidden_wide * up_values * sigmoid_values * (1.0 + gate_values * (1.0 - sigmoid_values))
    ).astype(jnp.bfloat16)
    up_grad = (hidden_wide * silu_values).astype(jnp.bfloat16)
    gate_grad_local = jnp.einsum(
        "secd,secf->edf", rows_arrived, gate_grad, preferred_element_type=jnp.float32
    )
    up_grad_local = jnp.einsum(
        "secd,secf->edf", rows_arrived, up_grad, preferred_element_type=jnp.float32
    )
    input_parts = (
        jnp.einsum("secf,edf->secd", gate_grad, gate_weight, preferred_element_type=jnp.float32)
        + jnp.einsum("secf,edf->secd", up_grad, up_weight, preferred_element_type=jnp.float32)
    ).astype(jnp.bfloat16)
    returned_grads = lax.all_to_all(
        input_parts, AXES, split_axis=0, concat_axis=0, tiled=True
    )
    slot_input_grad = join_halves(returned_grads)
    expert_input_grad = slot_input_grad[slot_index].reshape(tok_rows, TOPK, model_width)
    feature_grad = jnp.dot(logit_grad, router_full.T, preferred_element_type=jnp.float32) + jnp.sum(
        expert_input_grad, axis=1
    )
    residual_part, feature_gain_grad = feature_pull(feature_grad)
    residual_grad = out_grad + residual_part
    attended_grad = residual_grad.astype(jnp.bfloat16)
    output_grad_full = jnp.dot(context_rows.T, attended_grad, preferred_element_type=jnp.float32)
    context_grad = jnp.dot(attended_grad, output_full.T, preferred_element_type=jnp.float32).astype(
        jnp.bfloat16
    )
    context_heads_grad = lax.all_to_all(
        context_grad.reshape(tok_rows, sp_size, head_width),
        SP,
        split_axis=1,
        concat_axis=0,
        tiled=True,
    )
    context_heads_grad = context_heads_grad.reshape(blocks, block_rows, heads_here, HEAD_DIM)

    def backward_block(carry, block_input):
        key_total, value_total = carry
        block_queries, block_grads, block_logsum, block_start = block_input
        scores = masked_scores(block_queries, block_start)
        attn_weights = jnp.exp(scores - block_logsum[..., None])
        prob_dots = jnp.einsum(
            "qhd,khd->hqk", block_grads, values_all, preferred_element_type=jnp.float32
        )
        row_delta = jnp.sum(attn_weights * prob_dots, axis=-1, keepdims=True)
        score_grad = (attn_weights * (prob_dots - row_delta)).astype(jnp.bfloat16)
        query_grad = (
            jnp.einsum("hqk,khd->qhd", score_grad, keys_all, preferred_element_type=jnp.float32)
            * score_scale
        )
        key_total = (
            key_total
            + jnp.einsum(
                "hqk,qhd->khd", score_grad, block_queries, preferred_element_type=jnp.float32
            )
            * score_scale
        )
        value_total = value_total + jnp.einsum(
            "hqk,qhd->khd",
            attn_weights.astype(jnp.bfloat16),
            block_grads,
            preferred_element_type=jnp.float32,
        )
        return ((key_total, value_total), query_grad.astype(jnp.bfloat16))

    zero_keys = jnp.zeros((key_rows, heads_here, HEAD_DIM), jnp.float32)
    (key_total, value_total), query_grads = lax.scan(
        backward_block,
        (zero_keys, zero_keys),
        (query_blocks, context_heads_grad, logsum, block_starts),
    )
    key_mine, value_mine = (
        lax.psum_scatter(key_total, BLK, scatter_dimension=0, tiled=True),
        lax.psum_scatter(value_total, BLK, scatter_dimension=0, tiled=True),
    )
    query_back, key_back, value_back = (
        lax.all_to_all(
            query_grads.reshape(head_rows, 1, head_width),
            SP,
            split_axis=0,
            concat_axis=1,
            tiled=True,
        ),
        lax.all_to_all(
            key_mine.astype(jnp.bfloat16).reshape(head_rows, 1, head_width),
            SP,
            split_axis=0,
            concat_axis=1,
            tiled=True,
        ),
        lax.all_to_all(
            value_mine.astype(jnp.bfloat16).reshape(head_rows, 1, head_width),
            SP,
            split_axis=0,
            concat_axis=1,
            tiled=True,
        ),
    )
    query_lin_grad, query_gain_grad = query_pull(
        query_back.reshape(tok_rows, model_width).astype(jnp.float32)
    )
    key_lin_grad, key_gain_grad = key_pull(
        key_back.reshape(tok_rows, model_width).astype(jnp.float32)
    )
    query_lin_low = query_lin_grad.astype(jnp.bfloat16)
    key_lin_low = key_lin_grad.astype(jnp.bfloat16)
    value_low = value_back.reshape(tok_rows, model_width)
    query_grad_full = jnp.dot(normed.T, query_lin_low, preferred_element_type=jnp.float32)
    key_grad_full = jnp.dot(normed.T, key_lin_low, preferred_element_type=jnp.float32)
    value_grad_full = jnp.dot(normed.T, value_low, preferred_element_type=jnp.float32)
    normed_grad = jnp.dot(query_lin_low, query_full.T, preferred_element_type=jnp.float32)
    normed_grad = normed_grad + jnp.dot(key_lin_low, key_full.T, preferred_element_type=jnp.float32)
    normed_grad = normed_grad + jnp.dot(value_low, value_full.T, preferred_element_type=jnp.float32)
    tokens_part, attention_gain_grad = attention_pull(normed_grad)
    input_gradient = residual_grad + tokens_part
    summed = (
        lax.psum_scatter(query_grad_full, AXES, scatter_dimension=0, tiled=True),
        lax.psum_scatter(key_grad_full, AXES, scatter_dimension=0, tiled=True),
        lax.psum_scatter(value_grad_full, AXES, scatter_dimension=0, tiled=True),
        lax.psum_scatter(output_grad_full, AXES, scatter_dimension=0, tiled=True),
        lax.psum_scatter(router_grad_full, AXES, scatter_dimension=0, tiled=True),
        lax.psum_scatter(attention_gain_grad, AXES, scatter_dimension=0, tiled=True),
        lax.psum_scatter(query_gain_grad, AXES, scatter_dimension=0, tiled=True),
        lax.psum_scatter(key_gain_grad, AXES, scatter_dimension=0, tiled=True),
        lax.psum_scatter(feature_gain_grad, AXES, scatter_dimension=0, tiled=True),
    )
    return (
        block_output,
        input_gradient,
        summed[0],
        summed[1],
        summed[2],
        summed[3],
        summed[4],
        summed[5],
        summed[6],
        summed[7],
        summed[8],
        gate_grad_local,
        up_grad_local,
        down_grad_local,
    )


def solution(mesh):
    in_specs = (
        P(AXES, None),
        P(AXES, None),
        P(AXES, None),
        P(AXES, None),
        P(AXES, None),
        P(AXES, None),
        P(AXES),
        P(AXES),
        P(AXES),
        P(AXES),
        P((DP, SP), None, BLK),
        P((DP, SP), None, BLK),
        P((DP, SP), BLK, None),
        P(AXES, None),
        P(AXES, None),
    )
    out_specs = (
        P(AXES, None),
        P(AXES, None),
        P(AXES, None),
        P(AXES, None),
        P(AXES, None),
        P(AXES, None),
        P(AXES, None),
        P(AXES),
        P(AXES),
        P(AXES),
        P(AXES),
        P((DP, SP), None, BLK),
        P((DP, SP), None, BLK),
        P((DP, SP), BLK, None),
    )
    fast = dict(mesh.shape) == {DP: 4, BLK: 2, SP: 4}
    return jax.shard_map(body_fast if fast else body, mesh=mesh, in_specs=in_specs, out_specs=out_specs, check_vma=False)
```

```python
import functools
import math

import jax
import jax.numpy as jnp
import numpy as np
from jax import lax
from jax.experimental import pallas as pl
from jax.experimental.pallas import tpu as pltpu
from jax.sharding import PartitionSpec as P

DP, BLK, SP = AXES = ("dp", "blk", "sp")

HEADS = 16
HEAD_DIM = 128
EXPERTS = 64
TOPK = 8
CAP = 24


NORM_EPSILON = 1e-05
ROPE_BASE = 10000.0
MASKED = -1e30


def norm_apply(values, norm_gain):
    return (
        values
        * lax.rsqrt(jnp.mean(values * values, axis=-1, keepdims=True) + NORM_EPSILON)
        * norm_gain
    )


def rope_tables(positions, head_size):
    half_size = head_size // 2
    frequencies = jnp.exp(
        -math.log(ROPE_BASE) * 2.0 * jnp.arange(half_size, dtype=jnp.float32) / head_size
    )
    angles = positions.astype(jnp.float32)[:, None] * frequencies[None, :]
    return (jnp.cos(angles), jnp.sin(angles))


def rotate(values, cosine, sine):
    half_size = values.shape[-1] // 2
    first_half = values[..., :half_size]
    second_half = values[..., half_size:]
    cosine_row = cosine[:, None, :]
    sine_row = sine[:, None, :]
    return jnp.concatenate(
        [
            first_half * cosine_row - second_half * sine_row,
            second_half * cosine_row + first_half * sine_row,
        ],
        axis=-1,
    )


def rank_slots(route_rows):
    flat_experts = route_rows.reshape(-1)
    onehot = (flat_experts[:, None] == jnp.arange(EXPERTS, dtype=jnp.int32)[None, :]).astype(
        jnp.int32
    )
    return (flat_experts, jnp.sum(jnp.cumsum(onehot, axis=0) * onehot, axis=1) - 1)


MESH_ID = pl.DeviceIdType.MESH
VMEM_BYTES = 60 * 1024 * 1024


class Place:
    def __init__(self):
        self.dp = lax.axis_index(DP)
        self.blk = lax.axis_index(BLK)
        self.z = lax.axis_index(SP)
        self.x = self.dp % 2
        self.y = self.dp // 2
        self.col = self.blk * 4 + self.z

    def column(self, k):
        if k == 0:
            return self.dp
        if k == 1:
            return self.dp + 1 - 2 * self.x
        if k == 2:
            return self.dp + 2 - 4 * self.y
        return 3 - self.dp

    def at(self, k=0, blk=None, z=None):
        return (self.column(k), self.blk if blk is None else blk, self.z if z is None else z)


def entry_barrier(place, reach):
    barrier = pltpu.get_barrier_semaphore()

    def tell(target):
        pl.semaphore_signal(barrier, inc=1, device_id=target, device_id_type=MESH_ID)

    if reach == "all":
        me = (place.dp * 2 + place.blk) * 4 + place.z

        @pl.loop(1, 32)
        def _(step):
            other = (me + step) % 32
            tell((other // 8, (other // 4) % 2, other % 4))

        pl.semaphore_wait(barrier, 31)
    elif reach == "column":

        @pl.loop(1, 8)
        def _(step):
            other = (place.col + step) % 8
            tell((place.dp, other // 4, other % 4))

        pl.semaphore_wait(barrier, 7)
    else:
        tell_partners(place, barrier)
        wait_partners(place, barrier)


def tell_partners(place, semaphore):
    def tell(target):
        pl.semaphore_signal(semaphore, inc=1, device_id=target, device_id_type=MESH_ID)

    tell(place.at(0, 1 - place.blk))
    tell(place.at(1))
    tell(place.at(2))

    @pl.when(place.z > 0)
    def _():
        tell(place.at(z=place.z - 1))

    @pl.when(place.z < 3)
    def _():
        tell(place.at(z=place.z + 1))


def wait_partners(place, semaphore):
    ends = (3 - place.z) // 3 + place.z // 3
    pl.semaphore_wait(semaphore, 5 - ends)


def remote(src, dst, send_sem, recv_sem, target):
    return pltpu.make_async_remote_copy(
        src_ref=src,
        dst_ref=dst,
        send_sem=send_sem,
        recv_sem=recv_sem,
        device_id=target,
        device_id_type=MESH_ID,
    )


class GatherFlow:
    SENDS = 40
    RECVS = 37

    def __init__(self, place, src, out, send, recv, full, direct=False, others=False):
        self.p, self.src, self.out, self.send, self.recv, self.full = place, src, out, send, recv, full
        self.direct, self.others = direct, others
        self.half = src.shape[0] // 2

    def slot(self, k, blk, s):
        if self.full:
            return (self.p.column(k) * 2 + blk) * 4 + s
        return blk * 4 + s

    def block(self, k, s, blk=None):
        return self.out.at[self.slot(k, self.p.blk if blk is None else blk, s)]

    def copies(self, k, s, own=False):
        src = self.src if own else self.block(k, s)
        return src, self.block(k, s)

    def up(self, s, own=False):
        src, dst = self.copies(0, s, own)
        return remote(src, dst, self.send.at[s], self.recv.at[s], self.p.at(z=jnp.minimum(self.p.z + 1, 3)))

    def down(self, s, own=False):
        src, dst = self.copies(0, s, own)
        return remote(src, dst, self.send.at[4 + s], self.recv.at[s], self.p.at(z=jnp.maximum(self.p.z - 1, 0)))

    def across_x(self, s, own=False):
        src, dst = self.copies(0, s, own)
        return remote(src, dst, self.send.at[8 + s], self.recv.at[4 + s], self.p.at(1))

    def across_y(self, s, own=False):
        src, dst = self.copies(0, s, own)
        return remote(src, dst, self.send.at[12 + s], self.recv.at[8 + s], self.p.at(2))

    def turn_y(self, s):
        ref = self.block(1, s).at[pl.ds(0, self.half)]
        return remote(ref, ref, self.send.at[16 + s], self.recv.at[12 + s], self.p.at(2))

    def turn_x(self, s):
        ref = self.block(2, s).at[pl.ds(self.half, self.half)]
        return remote(ref, ref, self.send.at[20 + s], self.recv.at[16 + s], self.p.at(1))

    def core(self, k, s, own=False):
        src, dst = self.copies(k, s, own)
        return remote(
            src, dst, self.send.at[24 + 4 * k + s], self.recv.at[20 + 4 * k + s], self.p.at(0, 1 - self.p.blk)
        )

    def got(self, sem, ref):
        remote(ref, ref, self.send.at[0], self.recv.at[sem], self.p.at(0, 1 - self.p.blk)).wait_recv()

    def own_copy(self):
        return pltpu.make_async_copy(self.src, self.block(0, self.p.z), self.recv.at[36])

    def spread(self, s, own=False):
        if self.full:
            self.across_x(s, own).start()
            self.across_y(s, own).start()
        self.core(0, s, own).start()

    def straight(self, step):
        z = self.p.z
        return remote(
            self.src, self.block(0, z), self.send.at[step - 1], self.recv.at[z], self.p.at(z=(z + step) % 4)
        )

    def begin(self):
        z = self.p.z
        if self.direct:
            for step in (1, 2, 3):
                self.straight(step).start()
            self.spread(z, True)
            self.own_copy().start()
            return

        @pl.when(z < 3)
        def _():
            self.up(z, True).start()

        @pl.when(z > 0)
        def _():
            self.down(z, True).start()

        if not self.others:
            self.spread(z, True)
            self.own_copy().start()

    def along(self, d):
        z = self.p.z

        @pl.when(z >= d)
        def _():
            s = z - d
            self.got(s, self.block(0, s))

            if not self.direct:

                @pl.when(z < 3)
                def _():
                    self.up(s).start()

            self.spread(s)

        @pl.when(z + d <= 3)
        def _():
            s = z + d
            self.got(s, self.block(0, s))

            if not self.direct:

                @pl.when(z > 0)
                def _():
                    self.down(s).start()

            self.spread(s)

    def each(self, d, act):
        z = self.p.z
        if d == 0:
            if not self.others:
                act(z)
            return

        @pl.when(z >= d)
        def _():
            act(z - d)

        @pl.when(z + d <= 3)
        def _():
            act(z + d)

    def turn(self, d):
        if not self.full:
            return

        def act(s):
            self.got(4 + s, self.block(1, s))
            self.turn_y(s).start()
            self.core(1, s).start()
            self.got(8 + s, self.block(2, s))
            self.turn_x(s).start()
            self.core(2, s).start()

        self.each(d, act)

    def corner(self, d):
        if not self.full:
            return

        def act(s):
            self.got(12 + s, self.block(3, s).at[pl.ds(0, self.half)])
            self.got(16 + s, self.block(3, s).at[pl.ds(self.half, self.half)])
            self.core(3, s).start()

        self.each(d, act)

    def settle_plane(self, s):
        for k in range(4 if self.full else 1):
            self.got(20 + 4 * k + s, self.block(k, s, 1 - self.p.blk))
            self.core(k, s).wait_send()
        if self.full:
            self.across_x(s).wait_send()
            self.across_y(s).wait_send()
            self.turn_x(s).wait_send()
            self.turn_y(s).wait_send()

    def finish(self):
        z = self.p.z

        @pl.loop(0, 4)
        def _(s):
            pl.when((s != z) | (not self.others))(lambda: self.settle_plane(s))
            if not self.direct:

                @pl.when((s <= z) & (z < 3))
                def _():
                    self.up(s).wait_send()

                @pl.when((s >= z) & (z > 0))
                def _():
                    self.down(s).wait_send()

        if self.direct:
            for step in (1, 2, 3):
                self.straight(step).wait_send()
        if not self.others:
            self.own_copy().wait()


class PlaneFlow(GatherFlow):
    def __init__(self, place, blocks, out, send, recv, local):
        super().__init__(place, blocks[0][1], out, send, recv, True)
        self.blocks, self.local = blocks, local

    def begin(self):
        for i, (s, src) in enumerate(self.blocks):
            self.src = src
            self.spread(s, True)
            pltpu.make_async_copy(src, self.block(0, s), self.local.at[i]).start()

    def turns(self):
        for s, _ in self.blocks:
            self.got(4 + s, self.block(1, s))
            self.turn_y(s).start()
            self.core(1, s).start()
            self.got(8 + s, self.block(2, s))
            self.turn_x(s).start()
            self.core(2, s).start()

    def corners(self):
        for s, _ in self.blocks:
            self.got(12 + s, self.block(3, s).at[pl.ds(0, self.half)])
            self.got(16 + s, self.block(3, s).at[pl.ds(self.half, self.half)])
            self.core(3, s).start()

    def finish(self):
        for i, (s, src) in enumerate(self.blocks):
            self.settle_plane(s)
            pltpu.make_async_copy(src, self.block(0, s), self.local.at[i]).wait()


class PlaneFlow(GatherFlow):
    def __init__(self, place, blocks, out, send, recv, local):
        super().__init__(place, blocks[0][1], out, send, recv, True)
        self.blocks, self.local = blocks, local

    def begin(self):
        for i, (s, src) in enumerate(self.blocks):
            self.src = src
            self.spread(s, True)
            pltpu.make_async_copy(src, self.block(0, s), self.local.at[i]).start()

    def turns(self):
        for s, _ in self.blocks:
            self.got(4 + s, self.block(1, s))
            self.turn_y(s).start()
            self.core(1, s).start()
            self.got(8 + s, self.block(2, s))
            self.turn_x(s).start()
            self.core(2, s).start()

    def corners(self):
        for s, _ in self.blocks:
            self.got(12 + s, self.block(3, s).at[pl.ds(0, self.half)])
            self.got(16 + s, self.block(3, s).at[pl.ds(self.half, self.half)])
            self.core(3, s).start()

    def finish(self):
        for i, (s, src) in enumerate(self.blocks):
            self.settle_plane(s)
            pltpu.make_async_copy(src, self.block(0, s), self.local.at[i]).wait()


def run_flows(flows):
    lists = [flow.steps() for flow in flows]
    for position in range(max(len(steps) for steps in lists)):
        for steps in lists:
            if position < len(steps):
                steps[position]()


def add_rows(dst, terms, rows):
    @pl.loop(0, rows // 16)
    def _(i):
        at = pl.ds(pl.multiple_of(i * 16, 16), 16)
        total = terms[0][at, :].astype(jnp.float32)
        for term in terms[1:]:
            total = total + term[at, :].astype(jnp.float32)
        dst[at, :] = total.astype(dst.dtype)


class ScatterFlow:
    SENDS = 16 + 8 + 8 + 4 + 4
    RECVS = 16 + 8 + 8 + 4 + 4
    LOCALS = 16

    def __init__(self, place, part, out, scratch, full, band=None):
        self.p, self.part, self.out, self.full = place, part, out, full
        if full:
            (self.acc, self.near, self.half_in, self.side_in, self.line_in, self.sum, self.send, self.recv, self.local) = scratch
        else:
            (self.acc, self.near, self.line_in, self.sum, self.send, self.recv, self.local) = scratch
        self.columns = 4 if full else 1
        self.left = False
        first, self.rows = band or (0, part.shape[1])
        self.band = pl.ds(first, self.rows)
        self.half = self.rows // 2

    @staticmethod
    def scratch(rows, width, dtype, full):
        columns = 4 if full else 1
        shapes = [
            pltpu.VMEM((columns, 4, rows, width), dtype),
            pltpu.VMEM((columns, 4, rows, width), dtype),
        ]
        if full:
            shapes += [pltpu.VMEM((2, 4, rows // 2, width), dtype), pltpu.VMEM((2, 4, rows, width), dtype)]
        return shapes + [
            pltpu.VMEM((2, 4, rows, width), dtype),
            pltpu.VMEM((rows, width), jnp.float32),
            pltpu.SemaphoreType.DMA((ScatterFlow.SENDS,)),
            pltpu.SemaphoreType.DMA((ScatterFlow.RECVS,)),
            pltpu.SemaphoreType.DMA((ScatterFlow.LOCALS,)),
        ]

    def slot(self, k, blk, s):
        if self.full:
            return (self.p.column(k) * 2 + blk) * 4 + s
        return blk * 4 + s

    def order(self, i):
        z = self.p.z
        return [3 * (1 - z // 2), (2 + 3 * z) % 5, 1 + z % 2, z][i]

    def load(self, k, s):
        return pltpu.make_async_copy(
            self.part.at[self.slot(k, self.p.blk, s), self.band], self.acc.at[k, s], self.local.at[4 * k + s]
        )

    def core(self, k, s):
        return remote(
            self.part.at[self.slot(k, 1 - self.p.blk, s), self.band],
            self.near.at[k, s],
            self.send.at[4 * k + s],
            self.recv.at[4 * k + s],
            self.p.at(0, 1 - self.p.blk),
        )

    def half_x(self, s):
        return remote(
            self.acc.at[3, s, pl.ds(0, self.half)],
            self.half_in.at[0, s],
            self.send.at[16 + s],
            self.recv.at[16 + s],
            self.p.at(1),
        )

    def half_y(self, s):
        return remote(
            self.acc.at[3, s, pl.ds(self.half, self.half)],
            self.half_in.at[1, s],
            self.send.at[20 + s],
            self.recv.at[20 + s],
            self.p.at(2),
        )

    def side_x(self, s):
        return remote(
            self.acc.at[1, s], self.side_in.at[0, s], self.send.at[24 + s], self.recv.at[24 + s], self.p.at(1)
        )

    def side_y(self, s):
        return remote(
            self.acc.at[2, s], self.side_in.at[1, s], self.send.at[28 + s], self.recv.at[28 + s], self.p.at(2)
        )

    def line_up(self, s):
        return remote(
            self.acc.at[0, s],
            self.line_in.at[0, s],
            self.send.at[32 + s],
            self.recv.at[32 + s],
            self.p.at(z=jnp.minimum(self.p.z + 1, 3)),
        )

    def line_down(self, s):
        return remote(
            self.acc.at[0, s],
            self.line_in.at[1, s],
            self.send.at[36 + s],
            self.recv.at[36 + s],
            self.p.at(z=jnp.maximum(self.p.z - 1, 0)),
        )

    def begin(self, columns=None):
        for i in range(4):
            s = self.order(i)
            for k in columns or reversed(range(self.columns)):
                self.core(k, s).start()
                self.load(k, s).start()

    def unsent(self):
        return range(self.columns)

    def leave(self, s):
        self.half_x(s).wait_send()
        self.half_y(s).wait_send()
        self.side_x(s).wait_send()
        self.side_y(s).wait_send()

    def leave_all(self):
        self.left = True

        @pl.loop(0, 4)
        def _(s):
            self.leave(s)

    def arrive(self, k, s):
        self.load(k, s).wait()
        self.core(k, s).wait_recv()
        return [self.acc.at[k, s], self.near.at[k, s]]

    def stage1(self, i):
        if not self.full:
            return
        s = self.order(i)
        add_rows(self.acc.at[3, s], self.arrive(3, s), self.rows)
        self.half_x(s).start()
        self.half_y(s).start()

    def stage2(self, i):
        if not self.full:
            return
        s = self.order(i)
        first, second = pl.ds(0, self.half), pl.ds(self.half, self.half)
        terms = self.arrive(2, s)
        late = [term.at[first] for term in terms] + [self.half_in.at[0, s]]
        rest = [term.at[second] for term in terms]
        add_rows(rest[0], rest, self.half)
        self.half_x(s).wait_recv()
        add_rows(late[0], late, self.half)
        self.side_y(s).start()
        terms = self.arrive(1, s)
        late = [term.at[second] for term in terms] + [self.half_in.at[1, s]]
        rest = [term.at[first] for term in terms]
        add_rows(rest[0], rest, self.half)
        self.half_y(s).wait_recv()
        add_rows(late[0], late, self.half)
        self.side_x(s).start()

    def stage3(self, i):
        s = self.order(i)
        z = self.p.z
        terms = self.arrive(0, s)
        if self.full:
            self.side_x(s).wait_recv()
            self.side_y(s).wait_recv()
            terms = terms + [self.side_in.at[0, s], self.side_in.at[1, s]]
        add_rows(self.acc.at[0, s], terms, self.rows)
        if i < 3:

            @pl.when(z == 0)
            def _():
                self.line_up(s).start()

            @pl.when(z == 3)
            def _():
                self.line_down(s).start()

    def chain(self, i):
        s = self.order(i)
        z = self.p.z

        @pl.when((z > 0) & (z < s) & (z < 3))
        def _():
            self.line_up(s).wait_recv()
            add_rows(self.acc.at[0, s], [self.acc.at[0, s], self.line_in.at[0, s]], self.rows)
            self.line_up(s).start()

        @pl.when((z < 3) & (z > s) & (z > 0))
        def _():
            self.line_down(s).wait_recv()
            add_rows(self.acc.at[0, s], [self.acc.at[0, s], self.line_in.at[1, s]], self.rows)
            self.line_down(s).start()

    def final(self):
        z = self.p.z
        mine, above, below = self.acc.at[0, z], self.line_in.at[0, z], self.line_in.at[1, z]

        @pl.when(z > 0)
        def _():
            self.line_up(z).wait_recv()

        @pl.when(z < 3)
        def _():
            self.line_down(z).wait_recv()

        @pl.when(z == 0)
        def _():
            add_rows(self.sum, [mine, below], self.rows)

        @pl.when(z == 3)
        def _():
            add_rows(self.sum, [mine, above], self.rows)

        @pl.when((z > 0) & (z < 3))
        def _():
            add_rows(self.sum, [mine, above, below], self.rows)

        done = pltpu.make_async_copy(self.sum, self.out, self.local.at[0])
        done.start()

        @pl.loop(0, 4)
        def _(s):
            for k in self.unsent():
                self.core(k, s).wait_send()
            if self.full and not self.left:
                self.leave(s)

            @pl.when(s > z)
            def _():
                self.line_up(s).wait_send()

            @pl.when(s < z)
            def _():
                self.line_down(s).wait_send()

        done.wait()


class MadeFlow(ScatterFlow):
    def __init__(self, place, out, scratch, stage):
        self.stage = stage
        super().__init__(place, stage.at[0], out, scratch, True)

    def core(self, k, s):
        return remote(
            self.stage.at[k % 2, s],
            self.near.at[k, s],
            self.send.at[4 * k + s],
            self.recv.at[4 * k + s],
            self.p.at(0, 1 - self.p.blk),
        )

    def unsent(self):
        return (0, 1)

    def arrive(self, k, s):
        self.core(k, s).wait_recv()
        return [self.acc.at[k, s], self.near.at[k, s]]


def local_params():
    return pltpu.CompilerParams(vmem_limit_bytes=VMEM_BYTES)


def inner(left, right, left_dim=1, right_dim=0):
    return lax.dot_general(
        left, right, (((left_dim,), (right_dim,)), ((), ())), preferred_element_type=jnp.float32
    )


def is_place(places, per):
    return lax.broadcasted_iota(jnp.int32, (per, places.shape[1]), 0) == places


def one_hot(places, per):
    experts = places.shape[0]
    hot = [is_place(places[e : e + 1], per).astype(jnp.float32) for e in range(experts)]
    return jnp.concatenate(hot, axis=0).astype(jnp.bfloat16)


def pick_rows(places, probs, features, per):
    pairs, experts, pair_rows = places.shape
    width = features.shape[-1]
    step = 4

    def kernel(place_ref, prob_ref, feature_ref, row_ref, row_prob_ref):
        for i in range(step):
            rows = inner(one_hot(place_ref[i], per), feature_ref[i]).astype(row_ref.dtype)
            for e in range(experts):
                at = pl.ds(i * per, per)
                row_ref[e, at] = rows[e * per : (e + 1) * per]
                hot = is_place(place_ref[i, e : e + 1], per)
                prob = jnp.concatenate([prob_ref[2 * i, e : e + 1], prob_ref[2 * i + 1, e : e + 1]], axis=1)
                row_prob_ref[e, at] = jnp.sum(jnp.where(hot, prob, 0.0), axis=1, keepdims=True)

    return pl.pallas_call(
        kernel,
        out_shape=[
            jax.ShapeDtypeStruct((experts, pairs * per, width), features.dtype),
            jax.ShapeDtypeStruct((experts, pairs * per, 1), jnp.float32),
        ],
        grid=(pairs // step,),
        in_specs=[
            pl.BlockSpec((step, experts, pair_rows), lambda p: (p, 0, 0)),
            pl.BlockSpec((2 * step, experts, pair_rows // 2), lambda p: (p, 0, 0)),
            pl.BlockSpec((step, pair_rows, width), lambda p: (p, 0, 0)),
        ],
        out_specs=[
            pl.BlockSpec((experts, step * per, width), lambda p: (0, p, 0)),
            pl.BlockSpec((experts, step * per, 1), lambda p: (0, p, 0)),
        ],
        compiler_params=local_params(),
        name="pick_rows",
    )(places, probs, features)


def run_experts(rows, plain_grads, probs, gate_weight, up_weight):
    experts, slots, width = rows.shape
    hidden = gate_weight.shape[2]
    parts = 2
    part = slots // parts

    def kernel(x, plain_ref, p, wg, wu, weighted, gate_back, up_back, back, prob_back):
        gate = inner(x[0], wg[0])
        up = inner(x[0], wu[0])
        plain = plain_ref[0]
        prob = p[0]
        sig = jax.nn.sigmoid(gate)
        act = gate * sig
        hid = act * up
        prob_back[0] = jnp.sum(hid * plain, axis=1, keepdims=True)
        weighted[0] = (hid * prob).astype(jnp.bfloat16)
        grad = plain * prob
        gate_low = (grad * up * sig * (1.0 + gate * (1.0 - sig))).astype(jnp.bfloat16)
        up_low = (grad * act).astype(jnp.bfloat16)
        gate_back[0] = gate_low
        up_back[0] = up_low
        back[0] = (inner(gate_low, wg[0], 1, 1) + inner(up_low, wu[0], 1, 1)).astype(jnp.bfloat16)

    def block(size):
        return pl.BlockSpec((1, part, size), lambda e, i: (e, i, 0))

    weight = pl.BlockSpec((1, width, hidden), lambda e, i: (e, 0, 0))
    narrow = jax.ShapeDtypeStruct((experts, slots, hidden), rows.dtype)
    return pl.pallas_call(
        kernel,
        out_shape=[
            narrow,
            narrow,
            narrow,
            jax.ShapeDtypeStruct(rows.shape, rows.dtype),
            jax.ShapeDtypeStruct((experts, slots, 1), jnp.float32),
        ],
        grid=(experts, parts),
        in_specs=[block(width), block(hidden), block(1), weight, weight],
        out_specs=[block(hidden)] * 3 + [block(width), block(1)],
        compiler_params=local_params(),
        name="run_experts",
    )(rows, plain_grads, probs, gate_weight, up_weight)


class PickWork:
    GROUP = 4

    def __init__(self, places, source, weight, rows_out, plain_out, scratch):
        self.places, self.source, self.weight = places, source, weight
        self.rows_out, self.plain_out = rows_out, plain_out
        self.block, self.rows, self.plain, self.held, self.in_sems, self.out_sems, self.held_sem = scratch
        self.pairs = source.shape[0]
        self.units = self.pairs + self.GROUP
        self.experts = weight.shape[0]
        self.per = self.rows.shape[2] // self.GROUP

    @staticmethod
    def scratch(source, weight, per):
        experts, hidden, width = weight.shape
        group = PickWork.GROUP * per
        return [
            pltpu.VMEM((2,) + source.shape[1:], source.dtype),
            pltpu.VMEM((2, experts, group, width), source.dtype),
            pltpu.VMEM((2, experts, group, hidden), jnp.float32),
            pltpu.VMEM(weight.shape, weight.dtype),
            pltpu.SemaphoreType.DMA((2,)),
            pltpu.SemaphoreType.DMA((2, 2)),
            pltpu.SemaphoreType.DMA((1,)),
        ]

    def load(self, unit, slot):
        return pltpu.make_async_copy(self.source.at[unit], self.block.at[slot], self.in_sems.at[slot])

    def hold(self):
        return pltpu.make_async_copy(self.weight, self.held, self.held_sem.at[0])

    def stores(self, group, slot):
        height = self.GROUP * self.per
        at = pl.ds(pl.multiple_of(group * height, height), height)
        return [
            pltpu.make_async_copy(self.rows.at[slot], self.rows_out.at[:, at], self.out_sems.at[slot, 0]),
            pltpu.make_async_copy(self.plain.at[slot], self.plain_out.at[:, at], self.out_sems.at[slot, 1]),
        ]

    def begin(self):
        self.hold().start()
        self.load(0, 0).start()

    def pick(self, unit):
        slot, group, turn = unit % 2, unit // self.GROUP, unit % self.GROUP
        side = group % 2

        @pl.when(unit + 1 < self.pairs)
        def _():
            self.load(unit + 1, 1 - slot).start()

        @pl.when((turn == 0) & (group >= 2))
        def _():
            for copy in self.stores(group - 2, side):
                copy.wait()

        self.load(unit, slot).wait()
        rows = inner(one_hot(self.places[unit], self.per), self.block[slot]).astype(self.rows.dtype)
        for e in range(self.experts):
            at = pl.ds(pl.multiple_of(turn * self.per, self.per), self.per)
            self.rows[side, e, at] = rows[e * self.per : (e + 1) * self.per]

    def multiply(self, unit):
        group, e = unit // self.GROUP, unit % self.GROUP
        side = group % 2

        @pl.when(unit == 0)
        def _():
            self.hold().wait()

        self.plain[side, e] = inner(self.rows[side, e], self.held[e], 1, 1)

        @pl.when(e == self.GROUP - 1)
        def _():
            for copy in self.stores(group, side):
                copy.start()

    def run(self, unit):
        pl.when(unit < self.pairs)(lambda: self.pick(unit))
        pl.when(unit >= self.GROUP)(lambda: self.multiply(unit - self.GROUP))

    def finish(self):
        groups = self.pairs // self.GROUP
        for group in (groups - 2, groups - 1):
            for copy in self.stores(group, group % 2):
                copy.wait()


class PutWork:
    def __init__(self, place, places, source, row_grads, flow, deals, scratch):
        self.p, self.places, self.source, self.row_grads = place, places, source, row_grads
        self.flow, self.deals = flow, deals
        self.rows, self.sems = scratch
        self.experts, self.per = self.rows.shape[1:3]

    @staticmethod
    def scratch(source, per):
        experts, _, width = source.shape
        return [pltpu.VMEM((2, experts, per, width), source.dtype), pltpu.SemaphoreType.DMA((2,))]

    def pair(self, k, unit):
        side = unit // 2
        blk = side * self.p.blk + (1 - side) * (1 - self.p.blk)
        return self.p.column(k) * 4 + blk * 2 + unit % 2

    def load(self, k, unit, slot):
        at = pl.ds(pl.multiple_of(self.pair(k, unit) * self.per, self.per), self.per)
        return pltpu.make_async_copy(self.source.at[:, at], self.rows.at[slot], self.sems.at[slot])

    def column(self, k):
        flow = self.flow
        if k < 2:

            @pl.loop(0, 4)
            def _(s):
                flow.core(k + 2, s).wait_send()

        @pl.loop(0, 4)
        def _(unit):
            slot = unit % 2

            @pl.when(unit < 3)
            def _():
                self.load(k, unit + 1, 1 - slot).start()

            if k:

                @pl.when(unit == 3)
                def _():
                    self.load(k - 1, 0, 1 - slot).start()

            self.load(k, unit, slot).wait()
            pair = self.pair(k, unit)
            places = self.places[pair]
            rows = jnp.concatenate([self.rows[slot, e] for e in range(self.experts)], axis=0)
            summed = inner(one_hot(places, self.per), rows, 0, 0).astype(self.rows.dtype)
            summed = summed.reshape(2, summed.shape[0] // 2, summed.shape[1])
            blocks = pl.ds(2 * (unit % 2), 2)

            @pl.when(unit < 2)
            def _():
                flow.stage[k % 2, blocks] = summed

            @pl.when(unit >= 2)
            def _():
                flow.acc[k, blocks] = summed

            at = pl.ds(pl.multiple_of(pair * self.per, self.per), self.per)
            half = places.shape[1] // 2
            for e in range(self.experts):
                hot = is_place(places[e : e + 1], self.per)
                line = jnp.sum(jnp.where(hot, self.row_grads[e, at], 0.0), axis=0, keepdims=True)
                self.deals[2 * pair, e : e + 1] = line[:, :half]
                self.deals[2 * pair + 1, e : e + 1] = line[:, half:]

            @pl.when(unit == 1)
            def _():
                for s in range(4):
                    flow.core(k, s).start()


class OutputWork:
    def __init__(self, places, hidden, weight, out, scratch):
        self.places, self.hidden, self.weight, self.out = places, hidden, weight, out
        self.rows, self.held, self.narrow, self.block, self.in_sems, self.out_sems = scratch
        self.experts, self.slots, _ = hidden.shape
        self.pairs = out.shape[0]
        self.per = self.slots // self.pairs
        self.width = weight.shape[2]
        self.units = 2 * self.experts + self.pairs

    @staticmethod
    def scratch(hidden, weight, out):
        experts, slots, narrow = hidden.shape
        return [
            pltpu.VMEM((experts, slots, weight.shape[2]), weight.dtype),
            pltpu.VMEM((2,) + weight.shape[1:], weight.dtype),
            pltpu.VMEM((2, slots, narrow), hidden.dtype),
            pltpu.VMEM((2,) + out.shape[1:], out.dtype),
            pltpu.SemaphoreType.DMA((2, 2)),
            pltpu.SemaphoreType.DMA((2,)),
        ]

    def loads(self, e):
        slot = e % 2
        return [
            pltpu.make_async_copy(self.weight.at[e], self.held.at[slot], self.in_sems.at[slot, 0]),
            pltpu.make_async_copy(self.hidden.at[e], self.narrow.at[slot], self.in_sems.at[slot, 1]),
        ]

    def store(self, pair):
        return pltpu.make_async_copy(self.block.at[pair % 2], self.out.at[pair], self.out_sems.at[pair % 2])

    def begin(self):
        for copy in self.loads(0):
            copy.start()

    def run(self, unit):
        half = self.width // 2

        @pl.when(unit < 2 * self.experts)
        def _():
            e, side = unit // 2, unit % 2

            @pl.when(side == 0)
            def _():
                @pl.when(e + 1 < self.experts)
                def _():
                    for copy in self.loads(e + 1):
                        copy.start()

                for copy in self.loads(e):
                    copy.wait()

            at = pl.ds(pl.multiple_of(side * half, half), half)
            self.rows[e, :, at] = inner(self.narrow[e % 2], self.held[e % 2, :, at]).astype(self.rows.dtype)

        @pl.when(unit >= 2 * self.experts)
        def _():
            pair = unit - 2 * self.experts

            @pl.when(pair >= 2)
            def _():
                self.store(pair - 2).wait()

            at = pl.ds(pl.multiple_of(pair * self.per, self.per), self.per)
            rows = jnp.concatenate([self.rows[e, at] for e in range(self.experts)], axis=0)
            self.block[pair % 2] = inner(one_hot(self.places[pair], self.per), rows, 0, 0).astype(self.block.dtype)
            self.store(pair).start()

    def finish(self):
        for pair in (self.pairs - 2, self.pairs - 1):
            self.store(pair).wait()


def expert_weight_grads(rows, grads, weighted, gate_back, up_back):
    experts, slots, width = rows.shape
    hidden = weighted.shape[2]
    parts = 4
    part = width // parts

    def kernel(x, c, low, gate, up, gate_out, up_out, down_out):
        gate_out[0] = inner(x[0], gate[0], 0, 0)
        up_out[0] = inner(x[0], up[0], 0, 0)
        down_out[0] = inner(low[0], c[0], 0, 0)

    source = pl.BlockSpec((1, slots, part), lambda e, i: (e, 0, i))
    whole = pl.BlockSpec((1, slots, hidden), lambda e, i: (e, 0, 0))
    tall = pl.BlockSpec((1, part, hidden), lambda e, i: (e, i, 0))
    flat = pl.BlockSpec((1, hidden, part), lambda e, i: (e, 0, i))
    return pl.pallas_call(
        kernel,
        out_shape=[
            jax.ShapeDtypeStruct((experts, width, hidden), jnp.float32),
            jax.ShapeDtypeStruct((experts, width, hidden), jnp.float32),
            jax.ShapeDtypeStruct((experts, hidden, width), jnp.float32),
        ],
        grid=(experts, parts),
        in_specs=[source, source, whole, whole, whole],
        out_specs=[tall, tall, flat],
        compiler_params=local_params(),
        cost_estimate=pl.CostEstimate(
            flops=6 * experts * slots * width * hidden, bytes_accessed=24 * experts * width * hidden, transcendentals=0
        ),
        name="expert_weight_grads",
    )(rows, grads, weighted, gate_back, up_back)


class ColumnsFlow:
    SENDS = 24 + 1 + 16
    RECVS = 24 + 1 + 16
    LOCALS = 4

    def __init__(self, place, sources, rows_in, wide, tall, send, recv, local):
        self.p, self.sources, self.rows_in, self.wide, self.tall = place, sources, rows_in, wide, tall
        self.send, self.recv, self.local = send, recv, local
        self.rows = rows_in.shape[0]
        self.share = wide.shape[1] // len(sources)

    def spot(self, i, col):
        rows = pl.ds(pl.multiple_of((self.p.dp * 8 + col) * self.rows, self.rows), self.rows)
        return self.wide.at[rows, pl.ds(i * self.share, self.share)]

    def piece(self, i, to):
        return self.sources[i].at[:, pl.ds(pl.multiple_of(to * self.share, self.share), self.share)]

    def scatter(self, step, i):
        to = (self.p.col + step) % 8
        return remote(
            self.piece(i, to),
            self.spot(i, self.p.col),
            self.send.at[3 * step + i],
            self.recv.at[3 * self.p.col + i],
            (self.p.dp, to // 4, to % 4),
        )

    def keep(self, i):
        return pltpu.make_async_copy(self.piece(i, self.p.col), self.spot(i, self.p.col), self.local.at[i])

    def tall_rows(self, k):
        return self.tall.at[pl.ds(pl.multiple_of(self.p.column(k) * self.rows, self.rows), self.rows)]

    def swap(self):
        group = self.p.dp * 2 + self.p.blk
        dst = self.tall.at[pl.ds(pl.multiple_of(self.p.z * self.rows, self.rows), self.rows)]
        return remote(
            self.rows_in, dst, self.send.at[24], self.recv.at[24], (self.p.z, group // 4, group % 4)
        )

    def stay(self):
        return pltpu.make_async_copy(self.rows_in, self.tall_rows(0), self.local.at[3])

    def at_home(self):
        group = self.p.dp * 2 + self.p.blk
        return (self.p.z == self.p.dp) & (group == self.p.col)

    def band(self, i, k, first=0, parts=1):
        if i == 3:
            height, ref = self.rows, self.tall
        else:
            height, ref = 8 * self.rows, self.wide
        part = height // parts
        rows = pl.ds(pl.multiple_of(self.p.column(k) * height + first * part, part), part)
        return ref.at[rows] if i == 3 else ref.at[rows, pl.ds(i * self.share, self.share)]

    def across(self, i, k):
        ref = self.band(i, 0)
        slot = 25 + 4 * i + k - 1
        return remote(ref, ref, self.send.at[slot], self.recv.at[slot], self.p.at(k))

    def turn(self, i, k):
        ref = self.band(i, k, k - 1, 2)
        slot = 25 + 4 * i + 1 + k
        return remote(ref, ref, self.send.at[slot], self.recv.at[slot], self.p.at(3 - k))

    def got(self, sem, ref):
        remote(ref, ref, self.send.at[0], self.recv.at[sem], self.p.at(0, 1 - self.p.blk)).wait_recv()

    def begin(self):
        home = self.at_home()

        @pl.when(home)
        def _():
            self.stay().start()

        @pl.when(jnp.logical_not(home))
        def _():
            self.swap().start()

        for i in range(3):

            @pl.loop(1, 8)
            def _(step):
                self.scatter(step, i).start()

            self.keep(i).start()

    def settle(self, i):
        if i == 3:
            home = self.at_home()

            @pl.when(home)
            def _():
                self.stay().wait()

            @pl.when(jnp.logical_not(home))
            def _():
                self.got(24, self.tall_rows(0))

        else:
            self.keep(i).wait()

            @pl.loop(1, 8)
            def _(step):
                col = (self.p.col + step) % 8
                self.got(3 * col + i, self.spot(i, col))

        self.across(i, 1).start()
        self.across(i, 2).start()

    def turns(self, i):
        for k in (1, 2):
            self.got(25 + 4 * i + k - 1, self.band(i, k))
            self.turn(i, k).start()

    def finish(self):
        for i in (3, 0, 1, 2):
            for k in (1, 2):
                self.got(25 + 4 * i + 1 + k, self.band(i, 3, k - 1, 2))
                self.turn(i, k).wait_send()
                self.across(i, k).wait_send()

        @pl.when(jnp.logical_not(self.at_home()))
        def _():
            self.swap().wait_send()

        @pl.loop(1, 8)
        def _(step):
            for i in range(3):
                self.scatter(step, i).wait_send()


class SumsFlow:
    SENDS = 12 + 24 + 1
    RECVS = 12 + 16 + 1
    LOCALS = 4

    def __init__(self, place, wide_out, tall_out, scratch):
        self.p = place
        self.wide_out, self.tall_out = wide_out, tall_out
        self.acc, self.half_in, self.side_in = scratch[0:3], scratch[3:6], scratch[6:9]
        self.send, self.recv, self.local = scratch[9:12]
        self.rows = tall_out.shape[0]
        self.share = wide_out.shape[2] // 8

    @staticmethod
    def scratch(arrays):
        shapes = []
        for kind in ((4, 1), (2, 2), (2, 1)):
            for rows, width in arrays:
                shapes.append(pltpu.VMEM((kind[0], rows // kind[1], width), jnp.bfloat16))
        return shapes + [
            pltpu.SemaphoreType.DMA((SumsFlow.SENDS,)),
            pltpu.SemaphoreType.DMA((SumsFlow.RECVS,)),
            pltpu.SemaphoreType.DMA((SumsFlow.LOCALS,)),
        ]

    def halves(self, ref):
        half = ref.shape[0] // 2
        return ref.at[pl.ds(0, half)], ref.at[pl.ds(half, half)]

    def corner(self, which, k):
        src = self.halves(self.acc[which].at[3])[k - 1]
        slot = 4 * which + k - 1
        return remote(src, self.half_in[which].at[k - 1], self.send.at[slot], self.recv.at[slot], self.p.at(k))

    def side(self, which, k):
        slot = 4 * which + 1 + k
        return remote(
            self.acc[which].at[k], self.side_in[which].at[k - 1], self.send.at[slot], self.recv.at[slot], self.p.at(k)
        )

    def piece(self, to, i):
        rows = pl.ds(pl.multiple_of(to * self.rows, self.rows), self.rows)
        dst = self.wide_out.at[i, :, pl.ds(pl.multiple_of(self.p.col * self.share, self.share), self.share)]
        if i == 2:
            return self.acc[2].at[0, rows], dst
        return self.acc[0].at[0, rows, pl.ds(i * self.share, self.share)], dst

    def deal(self, step, i):
        to = (self.p.col + step) % 8
        src, dst = self.piece(to, i)
        return remote(
            src,
            dst,
            self.send.at[12 + 3 * step + i],
            self.recv.at[12 + 8 * (i // 2) + self.p.col],
            (self.p.dp, to // 4, to % 4),
        )

    def keep(self, i):
        src, dst = self.piece(self.p.col, i)
        return pltpu.make_async_copy(src, dst, self.local.at[i])

    def swap(self):
        return remote(
            self.acc[1].at[0],
            self.tall_out,
            self.send.at[36],
            self.recv.at[28],
            (self.p.col // 2, self.p.col % 2, self.p.dp),
        )

    def stay(self):
        return pltpu.make_async_copy(self.acc[1].at[0], self.tall_out, self.local.at[3])

    def at_home(self):
        return (self.p.col // 2 == self.p.dp) & (self.p.col % 2 == self.p.blk) & (self.p.z == self.p.dp)

    def corners(self, which):
        self.corner(which, 1).start()
        self.corner(which, 2).start()

    def sides(self, which):
        for k, other in ((2, 1), (1, 2)):
            self.corner(which, other).wait_recv()
            target = self.halves(self.acc[which].at[k])[other - 1]
            add_rows(target, [target, self.half_in[which].at[other - 1]], target.shape[0])
            self.side(which, k).start()

    def total(self, which):
        self.side(which, 1).wait_recv()
        self.side(which, 2).wait_recv()
        mine = self.acc[which].at[0]
        add_rows(mine, [mine, self.side_in[which].at[0], self.side_in[which].at[1]], mine.shape[0])

    def hand_out_tall(self):
        home = self.at_home()

        @pl.when(home)
        def _():
            self.stay().start()

        @pl.when(jnp.logical_not(home))
        def _():
            self.swap().start()

    def hand_out(self, weights):
        @pl.loop(1, 8)
        def _(step):
            for i in weights:
                self.deal(step, i).start()

        for i in weights:
            self.keep(i).start()

    def finish(self):
        home = self.at_home()

        @pl.when(home)
        def _():
            self.stay().wait()

        @pl.when(jnp.logical_not(home))
        def _():
            self.swap().wait()

        for i in range(3):
            self.keep(i).wait()

        @pl.loop(1, 8)
        def _(step):
            col = (self.p.col + step) % 8
            for which, landed in (
                (0, self.acc[0].at[0, pl.ds(0, self.rows)]),
                (1, self.acc[2].at[0, pl.ds(0, self.rows)]),
            ):
                remote(
                    landed,
                    landed,
                    self.send.at[0],
                    self.recv.at[12 + 8 * which + col],
                    self.p.at(0, 1 - self.p.blk),
                ).wait_recv()
            for i in range(3):
                self.deal(step, i).wait_send()

        for which in (1, 2, 0):
            for k in (1, 2):
                self.corner(which, k).wait_send()
                self.side(which, k).wait_send()


class DealFlow:
    def __init__(self, place, src, out, send, recv, local):
        self.p, self.src, self.out, self.send, self.recv, self.local = place, src, out, send, recv, local
        self.me = (place.dp * 2 + place.blk) * 4 + place.z

    def copy(self, step):
        to = (self.me + step) % 32
        return remote(
            self.src.at[to], self.out.at[self.me], self.send.at[step], self.recv.at[self.me], (to // 8, (to // 4) % 2, to % 4)
        )

    def keep(self):
        return pltpu.make_async_copy(self.src.at[self.me], self.out.at[self.me], self.local.at[0])

    def begin(self):
        self.keep().start()

        @pl.loop(1, 32)
        def _(step):
            self.copy(step).start()

    def finish(self):
        self.keep().wait()

        @pl.loop(1, 32)
        def _(step):
            landed = self.out.at[(self.me + step) % 32]
            remote(
                landed,
                landed,
                self.send.at[0],
                self.recv.at[(self.me + step) % 32],
                self.p.at(0, 1 - self.p.blk),
            ).wait_recv()
            self.copy(step).wait_send()

    @staticmethod
    def scratch():
        return [pltpu.SemaphoreType.DMA((32,)), pltpu.SemaphoreType.DMA((32,)), pltpu.SemaphoreType.DMA((1,))]

    def steps(self, length=18):
        return [self.begin] + [lambda: None] * (length - 2) + [self.finish]


def hbm_call(kernel, shapes, scratch, name, collective_id, args, in_vmem=(), out_vmem=()):
    return pl.pallas_call(
        kernel,
        out_shape=shapes,
        in_specs=[
            pl.BlockSpec(memory_space=pltpu.VMEM if i in in_vmem else pl.ANY) for i in range(len(args))
        ],
        out_specs=[
            pl.BlockSpec(memory_space=pltpu.VMEM if i in out_vmem else pl.ANY) for i in range(len(shapes))
        ],
        scratch_shapes=scratch,
        compiler_params=pltpu.CompilerParams(
            collective_id=collective_id, has_side_effects=True, vmem_limit_bytes=VMEM_BYTES
        ),
        name=name,
    )(*args)


def gather_sems():
    return [pltpu.SemaphoreType.DMA((GatherFlow.SENDS,)), pltpu.SemaphoreType.DMA((GatherFlow.RECVS,))]


def plane_sems(count):
    return gather_sems() + [pltpu.SemaphoreType.DMA((count,))]


def attention_call(
    tokens, small, cotangent, query_weight, key_weight, value_weight, output_weight, cosine, sine, experts
):
    tok_rows, width = tokens.shape
    own_rows = query_weight.shape[0]
    rows = 8 * tok_rows
    share = width // 8
    heads = share // HEAD_DIM
    block = 2 * tok_rows
    blocks = rows // block
    scale = 1.0 / math.sqrt(HEAD_DIM)
    bf16, f32 = jnp.bfloat16, jnp.float32
    line = ScatterFlow.scratch(tok_rows, width, bf16, False)

    def kernel(tok, sml, cot, wq, wk, wv, wo, cos, sin, *refs):
        outs, scratch = refs[:14], refs[14:]
        normed_out, unit_out, row_out, context_out, scale_out, log_out = outs[:6]
        attended, small_out, gathered_out, wide_out, tall_out, gains, place_out, head_out = outs[6:]
        held, wide_ref, tall_ref, normed, unit, qkv, context, part, sums, landed = scratch[:10]
        small_held, hits, normed_t, context_t, stores, send, recv = scratch[10:17]
        rest = list(scratch[17:])

        def take(count):
            taken = rest[:count]
            del rest[:count]
            return taken

        place = Place()
        entry_barrier(place, "all")
        flow = ScatterFlow(place, part, attended, take(len(line)), False)
        params = GatherFlow(place, sml, small_held, *take(2), True, True)
        tokens_in = GatherFlow(place, tok, held, *take(2), False)
        others = GatherFlow(place, cot, gathered_out, *take(2), True, others=True)
        plane = PlaneFlow(place, [(place.z, cot)], gathered_out, *take(3))
        weights = ColumnsFlow(place, (wq, wk, wv), wo, wide_ref, tall_ref, *take(3))
        params.begin()
        weights.begin()
        sums[...] = jnp.zeros_like(sums)
        for d in range(1, 4):
            params.along(d)
        plane.begin()
        for d in range(4):
            params.turn(d)
        weights.settle(3)
        weights.settle(0)
        plane.turns()
        weights.settle(1)
        tokens_in.begin()
        weights.turns(3)
        for d in range(4):
            params.corner(d)
        plane.corners()
        weights.settle(2)
        weights.turns(0)
        tokens_in.along(1)
        weights.turns(1)
        params.finish()
        for to in range(32):
            rows_here = small_held[to, own_rows : own_rows + 16, :own_rows].astype(f32)
            gains[:, to * own_rows : (to + 1) * own_rows] = rows_here[:4]
        tokens_in.along(2)
        weights.turns(2)
        first_expert = (place.dp * 4 + place.z) * experts

        @pl.loop(0, 32)
        def _(d):
            named = small_held[d, own_rows + 16 : own_rows + 32].astype(f32)[:TOPK]
            for e in range(experts):
                matches = jnp.where(named == (first_expert + e).astype(f32), 1.0, 0.0)
                hits[e, pl.ds(d, 1)] = jnp.sum(matches, axis=0, keepdims=True)

        earlier = lax.broadcasted_iota(jnp.int32, (tok_rows, tok_rows), 0)
        earlier = earlier < lax.broadcasted_iota(jnp.int32, (tok_rows, tok_rows), 1)
        earlier = earlier.astype(f32).astype(bf16)
        for e in range(experts):
            hit = hits[e]
            rank = inner(hit.astype(bf16), earlier)
            shift = lax.broadcasted_iota(jnp.int32, hit.shape, 0) % 2 * CAP
            slots = jnp.where(hit > 0.5, rank.astype(jnp.int32) + shift, -1)
            for d in range(32):
                lanes = slice(d % 2 * tok_rows, (d % 2 + 1) * tok_rows)
                place_out[d // 2, e : e + 1, lanes] = slots[d : d + 1]

        tokens_in.along(3)
        plane.finish()
        weights.finish()
        tokens_in.finish()
        others.begin()
        head_gain = gains[1:3, pl.ds(pl.multiple_of(place.col * share, share), share)]
        head_out[...] = head_gain

        @pl.loop(0, blocks)
        def _(i):
            at = pl.ds(pl.multiple_of(i * block, block), block)
            values = held[pl.ds(2 * i, 2)].reshape(block, width).astype(f32)
            mean = jnp.mean(values * values, axis=1, keepdims=True)
            low = (values * lax.rsqrt(mean + NORM_EPSILON) * gains[0:1]).astype(bf16)
            normed[at] = low
            linear = inner(low, wide_ref[...])
            unit[at] = linear[:, : 2 * share]
            qkv[at, 2 * share :] = linear[:, 2 * share :].astype(bf16)
            for n in range(2):
                part_lin = linear[:, n * share : (n + 1) * share]
                sums[n : n + 1, at] = jnp.sum(jnp.transpose(part_lin * part_lin), axis=0, keepdims=True)

        def exchange(step):
            to = (place.col + step) % 8
            return remote(
                sums, landed.at[place.col], send.at[step], recv.at[place.col], (place.dp, to // 4, to % 4)
            )

        @pl.loop(1, 8)
        def _(step):
            exchange(step).start()

        landed[place.col] = sums[...]

        @pl.loop(1, 8)
        def _(step):
            col = (place.col + step) % 8
            remote(sums, landed.at[col], send.at[0], recv.at[col], place.at(0, 1 - place.blk)).wait_recv()
            exchange(step).wait_send()

        total = landed[0]
        for col in range(1, 8):
            total = total + landed[col]
        scales = jnp.transpose(lax.rsqrt(total / width + NORM_EPSILON))
        scale_out[...] = scales

        @pl.loop(0, blocks)
        def _(i):
            at = pl.ds(pl.multiple_of(i * block, block), block)
            for n in range(2):
                for h in range(heads):
                    lanes = pl.ds(n * share + h * HEAD_DIM, HEAD_DIM)
                    mine = unit[at, lanes] * scale_out[at, n : n + 1]
                    unit[at, lanes] = mine
                    scaled = mine * head_gain[n : n + 1, h * HEAD_DIM : (h + 1) * HEAD_DIM]
                    turned = scaled * cos[at] + pltpu.roll(scaled, HEAD_DIM // 2, 1) * sin[at]
                    qkv[at, lanes] = turned.astype(bf16)

        out_copies = [
            pltpu.make_async_copy(src, dst, stores.at[n])
            for n, (src, dst) in enumerate(
                (
                    (unit, unit_out),
                    (qkv, row_out),
                    (wide_ref, wide_out),
                    (tall_ref, tall_out),
                    (small_held, small_out),
                )
            )
        ]
        for copy in out_copies:
            copy.start()
        for h in range(heads):
            for i in range(blocks):
                seen = (i + 1) * block
                queries = qkv[i * block : seen, h * HEAD_DIM : (h + 1) * HEAD_DIM]
                keys = qkv[:seen, share + h * HEAD_DIM : share + (h + 1) * HEAD_DIM]
                values = qkv[:seen, 2 * share + h * HEAD_DIM : 2 * share + (h + 1) * HEAD_DIM]
                scores = inner(queries, keys, 1, 1) * scale
                row = lax.broadcasted_iota(jnp.int32, scores.shape, 0) + i * block
                column = lax.broadcasted_iota(jnp.int32, scores.shape, 1)
                scores = jnp.where(column <= row, scores, MASKED)
                peak = jnp.max(scores, axis=1, keepdims=True)
                exponent = jnp.exp(scores - peak)
                sum_row = jnp.sum(exponent, axis=1, keepdims=True)
                low = (exponent / sum_row).astype(bf16)
                context[i * block : seen, h * HEAD_DIM : (h + 1) * HEAD_DIM] = inner(low, values).astype(bf16)
                log_out[i * block : seen, h : h + 1] = peak + jnp.log(sum_row)
            if h == 0:
                others.along(1)

        @pl.loop(0, blocks)
        def _(i):
            at = pl.ds(pl.multiple_of(i * block, block), block)
            rows_here = inner(context[at], tall_ref[...]).astype(bf16)
            part[pl.ds(2 * i, 2)] = rows_here.reshape(2, tok_rows, width)

        flow.begin()
        others.along(2)
        for i in range(blocks):
            at = slice(i * block, (i + 1) * block)
            normed_t[:, at] = jnp.transpose(normed[at])
            context_t[:, at] = jnp.transpose(context[at])
        last = [
            pltpu.make_async_copy(normed_t, normed_out, stores.at[5]),
            pltpu.make_async_copy(context_t, context_out, stores.at[6]),
        ]
        for copy in last:
            copy.start()
        flow.stage3(0)
        flow.stage3(1)
        flow.chain(0)
        others.along(3)
        others.turn(1)
        flow.stage3(2)
        flow.chain(1)
        flow.chain(2)
        others.turn(2)
        others.corner(1)
        flow.stage3(3)
        flow.final()
        others.turn(3)
        others.corner(2)
        others.corner(3)
        others.finish()
        for copy in out_copies + last:
            copy.wait()

    shapes = [
        jax.ShapeDtypeStruct((width, rows), bf16),
        jax.ShapeDtypeStruct((rows, 2 * share), f32),
        jax.ShapeDtypeStruct((rows, 3 * share), bf16),
        jax.ShapeDtypeStruct((share, rows), bf16),
        jax.ShapeDtypeStruct((rows, 8), f32),
        jax.ShapeDtypeStruct((rows, 8), f32),
        jax.ShapeDtypeStruct((tok_rows, width), f32),
        jax.ShapeDtypeStruct((32,) + small.shape, bf16),
        jax.ShapeDtypeStruct((32,) + cotangent.shape, bf16),
        jax.ShapeDtypeStruct((width, 3 * share), bf16),
        jax.ShapeDtypeStruct((share, width), bf16),
        jax.ShapeDtypeStruct((4, width), f32),
        jax.ShapeDtypeStruct((16, experts, 2 * tok_rows), jnp.int32),
        jax.ShapeDtypeStruct((2, share), f32),
    ]
    scratch = [
        pltpu.VMEM((8, tok_rows, width), bf16),
        pltpu.VMEM((width, 3 * share), bf16),
        pltpu.VMEM((share, width), bf16),
        pltpu.VMEM((rows, width), bf16),
        pltpu.VMEM((rows, 2 * share), f32),
        pltpu.VMEM((rows, 3 * share), bf16),
        pltpu.VMEM((rows, share), bf16),
        pltpu.VMEM((8, tok_rows, width), bf16),
        pltpu.VMEM((8, rows), f32),
        pltpu.VMEM((8, 8, rows), f32),
        pltpu.VMEM((32,) + small.shape, bf16),
        pltpu.VMEM((experts, 32, tok_rows), f32),
        pltpu.VMEM((width, rows), bf16),
        pltpu.VMEM((share, rows), bf16),
        pltpu.SemaphoreType.DMA((7,)),
        pltpu.SemaphoreType.DMA((8,)),
        pltpu.SemaphoreType.DMA((8,)),
    ]
    scratch += line + gather_sems() * 3 + plane_sems(1)
    scratch += [
        pltpu.SemaphoreType.DMA((ColumnsFlow.SENDS,)),
        pltpu.SemaphoreType.DMA((ColumnsFlow.RECVS,)),
        pltpu.SemaphoreType.DMA((ColumnsFlow.LOCALS,)),
    ]
    args = (tokens, small, cotangent, query_weight, key_weight, value_weight, output_weight, cosine, sine)
    return hbm_call(kernel, shapes, scratch, "attention", 5, args, (7, 8), (4, 5, 11, 12, 13))


def run_units(work, first, last):
    @pl.loop(first, last)
    def _(unit):
        work.run(unit)


def features_call(features, probs, places, cotangent_all, down_weight, per):
    experts, hidden, width = down_weight.shape
    slots = places.shape[0] * per

    def kernel(feature_ref, prob_ref, place_ref, cot, weight, feature_out, prob_out, rows, plain, *scratch):
        place = Place()
        entry_barrier(place, "planes")
        small = GatherFlow(place, prob_ref, prob_out, scratch[2], scratch[3], True)
        flow = GatherFlow(place, feature_ref, feature_out, scratch[0], scratch[1], True)
        work = PickWork(place_ref, cot, weight, rows, plain, scratch[4:])

        flows = (small, flow)

        def along(d):
            for each in flows:
                each.along(d)

        def turn(d):
            for each in flows:
                each.turn(d)

        def corner(d):
            for each in flows:
                each.corner(d)

        for each in flows:
            each.begin()
        work.begin()
        run_units(work, 0, 4)
        along(1)
        turn(0)
        run_units(work, 4, 9)
        along(2)
        corner(0)
        run_units(work, 9, 13)
        along(3)
        turn(1)
        run_units(work, 13, work.units)
        corner(1)
        turn(2)
        corner(2)
        turn(3)
        corner(3)
        for each in flows:
            each.finish()
        work.finish()

    shapes = [
        jax.ShapeDtypeStruct((32,) + features.shape, features.dtype),
        jax.ShapeDtypeStruct((32,) + probs.shape, probs.dtype),
        jax.ShapeDtypeStruct((experts, slots, width), features.dtype),
        jax.ShapeDtypeStruct((experts, slots, hidden), jnp.float32),
    ]
    scratch = gather_sems() * 2 + PickWork.scratch(cotangent_all, down_weight, per)
    return hbm_call(
        kernel, shapes, scratch, "features", 6, (features, probs, places, cotangent_all, down_weight), (2,)
    )


def experts_back_call(input_rows, row_grads, places, hidden, weight, tok_rows):
    width = input_rows.shape[2]
    pairs, experts, pair_rows = places.shape
    per = input_rows.shape[1] // pairs
    sums = ScatterFlow.scratch(tok_rows, width, input_rows.dtype, True)
    out_shape = jax.ShapeDtypeStruct((pairs, pair_rows, width), input_rows.dtype)
    dealt = jax.ShapeDtypeStruct((2 * pairs, 8, tok_rows), jnp.float32)
    put_scratch = PutWork.scratch(input_rows, per)

    def kernel(source, grad_ref, place_ref, hidden_ref, weight_ref, out, dealt_out, mixed, *scratch):
        place = Place()
        entry_barrier(place, "all")
        stage, deals = scratch[:2]
        rest = scratch[2 + len(put_scratch) + 3 :]
        deal = DealFlow(place, deals, dealt_out, *scratch[2 + len(put_scratch) :][:3])
        flow = MadeFlow(place, out, rest[: len(sums)], stage)
        put = PutWork(place, place_ref, source, grad_ref, flow, deals, scratch[2 : 2 + len(put_scratch)])
        work = OutputWork(place_ref, hidden_ref, weight_ref, mixed, rest[len(sums) :])
        put.load(3, 0, 0).start()
        work.begin()
        deals[...] = jnp.zeros_like(deals)
        put.column(3)
        put.column(2)
        for i in range(4):
            flow.stage1(i)
        put.column(1)
        put.column(0)
        deal.begin()
        flow.stage2(0)
        flow.stage2(1)
        run_units(work, 0, 8)
        flow.stage2(2)
        flow.stage2(3)
        run_units(work, 8, 16)
        flow.stage3(0)
        flow.stage3(1)
        flow.chain(0)
        run_units(work, 16, 20)
        flow.stage3(2)
        flow.chain(1)
        flow.chain(2)
        run_units(work, 20, work.units)
        flow.stage3(3)
        flow.final()
        work.finish()
        deal.finish()

    shapes = [jax.ShapeDtypeStruct((tok_rows, width), jnp.float32), dealt, out_shape]
    scratch = [
        pltpu.VMEM((2, 4, tok_rows, width), input_rows.dtype),
        pltpu.VMEM(dealt.shape, jnp.float32),
    ]
    scratch += put_scratch + DealFlow.scratch() + sums + OutputWork.scratch(hidden, weight, out_shape)
    return hbm_call(
        kernel, shapes, scratch, "experts_back", 3, (input_rows, row_grads, places, hidden, weight), (1, 2)
    )


def attention_back_call(
    grad, logit_grad, out_part, tokens, gain, feature_row, wide, tall, head_gains, cosine, sine, kept
):
    tok_rows, width = grad.shape
    rows = kept[0].shape[1]
    share = tall.shape[0]
    heads = share // HEAD_DIM
    own_rows = width // 32
    block = 2 * tok_rows
    blocks = rows // block
    band_rows = width // 4
    height = tok_rows // 2
    scale = 1.0 / math.sqrt(HEAD_DIM)
    bf16, f32 = jnp.bfloat16, jnp.float32
    line = ScatterFlow.scratch(tok_rows, width, bf16, False)
    mixed = ScatterFlow.scratch(height, width, bf16, True)
    sums = SumsFlow.scratch(((band_rows, 2 * share), (share // 4, width), (band_rows, share)))
    flow_scratch = line + mixed + mixed[-5:] + sums + DealFlow.scratch() + gather_sems() * 2
    flow_scratch += [pltpu.SemaphoreType.REGULAR]

    def kernel(*refs):
        grad_ref, logit_ref, part_ref, tok_in, gain_ref, feature_ref, wide_in, tall_in = refs[:8]
        head_gain, cos, sin, normed_in, unit_in, qkv_in, context_in, scale_ref, log_ref = refs[8:17]
        logit_out, first_out, second_out, normed_grad, wide_out, tall_out, gain_out = refs[17:24]
        scratch = refs[24:]
        grads, tok, wide_ref, tall_ref, normed, unit, qkv, context, context_grad = scratch[:9]
        grad_q, grad_k, grad_v, low_grads, dots, landed, deals, dealt, tall_grad = scratch[9:18]
        ins, send, recv = scratch[18:21]
        rest = list(scratch[21:])

        def take(count):
            taken = rest[:count]
            del rest[:count]
            return taken

        place = Place()
        entry_barrier(place, "all")
        line_scratch, mixed_scratch, more = take(len(line)), take(len(mixed)), take(5)
        weights = SumsFlow(place, wide_out, tall_out, take(len(sums)))
        deal = DealFlow(place, deals, dealt, *take(3))
        gather = GatherFlow(place, grad_ref, grads, *take(2), False)
        logits = GatherFlow(place, logit_ref, logit_out, *take(2), True)
        freed = take(1)[0]
        flow = ScatterFlow(place, grads, normed_grad, line_scratch, False)
        first = ScatterFlow(place, part_ref, first_out, mixed_scratch, True, (0, height))
        second = ScatterFlow(
            place, part_ref, second_out, mixed_scratch[:-5] + more, True, (height, height)
        )
        gather.begin()
        logits.begin()
        first.begin()
        sources = (tok_in, wide_in, tall_in, normed_in, unit_in, qkv_in, context_in)
        held = (tok, wide_ref, tall_ref, normed, unit, qkv, context)
        loads = [pltpu.make_async_copy(s, d, ins.at[n]) for n, (s, d) in enumerate(zip(sources, held))]
        for copy in loads:
            copy.start()
        deals[...] = jnp.zeros_like(deals)
        dots[...] = jnp.zeros_like(dots)
        first.stage1(0)
        first.stage1(1)
        gather.along(1)
        logits.along(1)
        logits.turn(0)
        first.stage1(2)
        first.stage1(3)
        first.stage2(0)
        gather.along(2)
        logits.along(2)
        logits.turn(1)
        first.stage2(1)
        first.stage2(2)
        gather.along(3)
        logits.along(3)
        logits.turn(2)
        logits.turn(3)
        first.stage3(0)
        first.stage2(3)
        first.stage3(1)
        first.chain(0)
        for d in range(4):
            logits.corner(d)
        gather.finish()
        for copy in loads:
            copy.wait()
        first.stage3(2)
        first.chain(1)
        first.stage3(3)
        tell_partners(place, freed)

        @pl.loop(0, blocks)
        def _(i):
            at = pl.ds(pl.multiple_of(i * block, block), block)
            values = grads[pl.ds(2 * i, 2)].reshape(block, width)
            context_grad[at] = inner(values, tall_ref[...], 1, 1).astype(bf16)

        wait_partners(place, freed)
        first.leave_all()
        second.begin((3, 2, 1))
        first.chain(2)

        @pl.loop(0, 4)
        def _(i):
            lanes = pl.ds(pl.multiple_of(i * band_rows, band_rows), band_rows)
            values = grads[:, :, lanes].reshape(rows, band_rows)
            tall_grad[:, lanes] = inner(context[...], values).astype(bf16)

        for k in range(4):
            at = pl.ds(pl.multiple_of(place.column(k) * own_rows, own_rows), own_rows)
            weights.acc[1][k] = tall_grad[at]
        weights.corners(1)
        first.final()
        second.begin((0,))

        def back_block(h, i):
            seen = (i + 1) * block
            here, lanes = slice(i * block, seen), slice(h * HEAD_DIM, (h + 1) * HEAD_DIM)
            queries = qkv[here, lanes]
            keys = qkv[:seen, share + h * HEAD_DIM : share + (h + 1) * HEAD_DIM]
            values = qkv[:seen, 2 * share + h * HEAD_DIM : 2 * share + (h + 1) * HEAD_DIM]
            outer = context_grad[here, lanes]
            scores = inner(queries, keys, 1, 1) * scale
            row = lax.broadcasted_iota(jnp.int32, scores.shape, 0) + i * block
            column = lax.broadcasted_iota(jnp.int32, scores.shape, 1)
            probs = jnp.where(column <= row, jnp.exp(scores - log_ref[here, h : h + 1]), 0.0)
            prob_dots = inner(outer, values, 1, 1)
            delta = jnp.sum(probs * prob_dots, axis=1, keepdims=True)
            score_grad = (probs * (prob_dots - delta)).astype(bf16)
            grad_q[here, lanes] = inner(score_grad, keys) * scale
            key_part = inner(score_grad, queries, 0, 0) * scale
            value_part = inner(probs.astype(bf16), outer, 0, 0)
            if i == blocks - 1:
                grad_k[:, lanes] = key_part
                grad_v[:, lanes] = value_part
            else:
                grad_k[:seen, lanes] += key_part
                grad_v[:seen, lanes] += value_part

        back_block(0, 3)
        back_block(0, 2)
        second.stage1(0)
        second.stage1(1)
        back_block(0, 1)
        back_block(0, 0)
        second.stage1(2)
        second.stage1(3)
        back_block(1, 3)
        back_block(1, 2)
        weights.sides(1)
        second.stage2(0)
        back_block(1, 1)
        back_block(1, 0)
        low_grads[:, 2 * share :] = grad_v[...].astype(bf16)

        def band_grad(which, k):
            band = pl.ds(pl.multiple_of(place.column(k) * band_rows, band_rows), band_rows)
            lanes = slice(2 * share, 3 * share) if which == 2 else slice(0, 2 * share)
            weights.acc[which][k] = inner(normed[band], low_grads[:, lanes]).astype(bf16)

        for k in (3, 2, 1, 0):
            band_grad(2, k)

        second.stage2(1)

        @pl.loop(0, blocks)
        def _(i):
            at = pl.ds(pl.multiple_of(i * block, block), block)
            for n, grad_n in enumerate((grad_q, grad_k)):
                total = jnp.zeros((block, 1), f32)
                for h in range(heads):
                    lanes = slice(h * HEAD_DIM, (h + 1) * HEAD_DIM)
                    turned = grad_n[at, lanes].astype(bf16).astype(f32)
                    back = turned * cos[at] - pltpu.roll(turned, HEAD_DIM // 2, 1) * sin[at]
                    mine = unit[at, n * share + h * HEAD_DIM : n * share + (h + 1) * HEAD_DIM]
                    for j in range(HEAD_DIM // own_rows):
                        to = place.col * 4 + h * (HEAD_DIM // own_rows) + j
                        columns = slice(j * own_rows, (j + 1) * own_rows)
                        deals[to, 1 + n : 2 + n, :own_rows] += jnp.sum(
                            (back * mine)[:, columns], axis=0, keepdims=True
                        )
                    weighted = back * head_gain[n : n + 1, lanes]
                    grad_n[at, lanes] = weighted
                    total += jnp.sum(weighted * mine, axis=1, keepdims=True)
                dots[n : n + 1, at] = jnp.transpose(jnp.broadcast_to(total, (block, 128)))[:1]

        def exchange(step):
            to = (place.col + step) % 8
            return remote(
                dots, landed.at[place.col], send.at[step], recv.at[place.col], (place.dp, to // 4, to % 4)
            )

        @pl.loop(1, 8)
        def _(step):
            exchange(step).start()

        landed[place.col] = dots[...]

        @pl.loop(1, 8)
        def _(step):
            col = (place.col + step) % 8
            remote(dots, landed.at[col], send.at[0], recv.at[col], place.at(0, 1 - place.blk)).wait_recv()
            exchange(step).wait_send()

        total_dots = landed[0]
        for col in range(1, 8):
            total_dots = total_dots + landed[col]
        columns = jnp.transpose(total_dots / width)
        for n, grad_n in enumerate((grad_q, grad_k)):
            mine = unit[:, n * share : (n + 1) * share]
            low = scale_ref[:, n : n + 1] * (grad_n[...] - mine * columns[:, n : n + 1])
            low_grads[:, n * share : (n + 1) * share] = low.astype(bf16)

        weights.corners(2)
        band_grad(0, 3)
        weights.corners(0)

        @pl.loop(0, blocks)
        def _(i):
            at = pl.ds(pl.multiple_of(i * block, block), block)
            values = inner(low_grads[at], wide_ref[...], 1, 1).astype(bf16)
            grads[pl.ds(2 * i, 2)] = values.reshape(2, tok_rows, width)

        flow.begin()
        weights.sides(2)
        band_grad(0, 2)
        band_grad(0, 1)
        flow.stage3(0)
        weights.sides(0)
        flow.stage3(1)
        band_grad(0, 0)
        second.stage2(2)
        flow.chain(0)
        weights.total(2)
        weights.hand_out((2,))
        second.stage2(3)
        flow.stage3(2)
        flow.chain(1)
        weights.total(0)
        weights.hand_out((0, 1))
        second.stage3(0)
        second.stage3(1)
        flow.chain(2)
        flow.stage3(3)
        second.chain(0)
        second.stage3(2)
        second.chain(1)
        second.chain(2)
        weights.total(1)
        weights.hand_out_tall()
        flow.final()

        values = tok[...].astype(f32)
        scaled = values * lax.rsqrt(jnp.mean(values * values, axis=1, keepdims=True) + NORM_EPSILON)
        attention_row = jnp.sum(scaled * flow.sum[...], axis=0, keepdims=True)
        for to in range(32):
            lanes = slice(to * own_rows, (to + 1) * own_rows)
            deals[to, 0:1, :own_rows] = attention_row[:, lanes]
            deals[to, 3:4, :own_rows] = feature_ref[:, lanes]
        deal.begin()
        second.stage3(3)
        second.final()
        logits.finish()
        weights.finish()
        deal.finish()
        total = dealt[0]
        for index in range(1, 32):
            total = total + dealt[index]
        gain_out[...] = total

    shapes = [
        jax.ShapeDtypeStruct((32,) + logit_grad.shape, logit_grad.dtype),
        jax.ShapeDtypeStruct((height, width), f32),
        jax.ShapeDtypeStruct((height, width), f32),
        jax.ShapeDtypeStruct((tok_rows, width), f32),
        jax.ShapeDtypeStruct((3, own_rows, width), bf16),
        jax.ShapeDtypeStruct((own_rows, width), bf16),
        jax.ShapeDtypeStruct((8, 128), f32),
    ]
    scratch = [
        pltpu.VMEM((8, tok_rows, width), bf16),
        pltpu.VMEM((tok_rows, width), bf16),
        pltpu.VMEM(wide.shape, bf16),
        pltpu.VMEM(tall.shape, bf16),
        pltpu.VMEM((width, rows), bf16),
        pltpu.VMEM((rows, 2 * share), f32),
        pltpu.VMEM((rows, 3 * share), bf16),
        pltpu.VMEM((share, rows), bf16),
        pltpu.VMEM((rows, share), bf16),
        pltpu.VMEM((rows, share), f32),
        pltpu.VMEM((rows, share), f32),
        pltpu.VMEM((rows, share), f32),
        pltpu.VMEM((rows, 3 * share), bf16),
        pltpu.VMEM((8, rows), f32),
        pltpu.VMEM((8, 8, rows), f32),
        pltpu.VMEM((32, 8, 128), f32),
        pltpu.VMEM((32, 8, 128), f32),
        pltpu.VMEM(tall.shape, bf16),
        pltpu.SemaphoreType.DMA((7,)),
        pltpu.SemaphoreType.DMA((8,)),
        pltpu.SemaphoreType.DMA((8,)),
    ]
    args = (grad, logit_grad, out_part, tokens, gain, feature_row, wide, tall, head_gains, cosine, sine)
    return hbm_call(
        kernel,
        shapes,
        scratch + flow_scratch,
        "attention_back",
        2,
        args + tuple(kept),
        (4, 5, 8, 9, 10, 15, 16),
        (6,),
    )


def turn_tables(count):
    half = HEAD_DIM // 2
    frequencies = np.exp(-math.log(ROPE_BASE) * 2.0 * np.arange(half) / HEAD_DIM).astype(np.float32)
    angles = np.arange(count, dtype=np.float32)[:, None] * frequencies[None, :]
    return np.cos(angles), np.sin(angles)


def product(left, right, sums, batches=((), ()), out=jnp.float32):
    return lax.dot_general(left, right, (sums, batches), preferred_element_type=out)


def body_fast(
    tokens,
    query_weight,
    key_weight,
    value_weight,
    output_weight,
    router_weight,
    attention_gain,
    query_gain,
    key_gain,
    feature_gain,
    gate_weight,
    up_weight,
    down_weight,
    routes,
    cotangent,
):
    tok_rows, model_width = tokens.shape
    column_size = 8
    devices = 32
    share = model_width // column_size
    heads_here = share // HEAD_DIM
    seq_rows = tok_rows * column_size
    experts_here = gate_weight.shape[0]
    own_rows = query_weight.shape[0]
    score_scale = 1.0 / math.sqrt(HEAD_DIM)
    column = lax.axis_index(BLK) * 4 + lax.axis_index(SP)
    f32, bf16 = jnp.float32, jnp.bfloat16

    gains = jnp.stack([attention_gain, query_gain, key_gain, feature_gain])
    small = jnp.concatenate(
        [
            jnp.pad(router_weight, ((0, 0), (0, 128 - EXPERTS))),
            jnp.pad(gains, ((0, 12), (0, 128 - own_rows))),
            jnp.pad(routes.T.astype(bf16), ((0, 16 - TOPK), (0, 0))),
        ],
        axis=0,
    )
    half_cos, half_sin = turn_tables(seq_rows)
    cosine = np.concatenate([half_cos, half_cos], axis=1)
    sine = np.concatenate([-half_sin, half_sin], axis=1)
    (
        *kept,
        attended,
        small_all,
        cotangent_all,
        wide_weight,
        tall_weight,
        gain_all,
        places,
        head_gains,
    ) = attention_call(
        tokens, small, cotangent, query_weight, key_weight, value_weight, output_weight, cosine, sine, experts_here
    )
    router_full = small_all[:, :own_rows, :EXPERTS].reshape(model_width, EXPERTS)
    gain_attention, gain_feature = gain_all[0], gain_all[3]

    tokens_f = tokens.astype(f32)
    residual = tokens_f + attended
    features_f, feature_pull = jax.vjp(norm_apply, residual, gain_feature)
    features = features_f.astype(bf16)
    logits = jnp.dot(features, router_full, preferred_element_type=f32)
    router_probs = jax.nn.softmax(logits, axis=-1)

    first_expert = (lax.axis_index(DP) * 4 + lax.axis_index(SP)) * experts_here
    pairs, pair_rows, per = devices // 2, 2 * tok_rows, 2 * CAP
    cotangent_all = cotangent_all.reshape(pairs, pair_rows, model_width)
    features_all, probs_all, grad_rows, plain_grads = features_call(
        features, router_probs.T, places, cotangent_all, down_weight, per
    )
    probs_here = lax.dynamic_slice_in_dim(probs_all, first_expert, experts_here, axis=1)
    features_all = features_all.reshape(pairs, pair_rows, model_width)
    expert_rows, row_probs = pick_rows(places, probs_here, features_all, per)
    weighted_hidden, gate_grad, up_grad, input_rows, row_grads = run_experts(
        expert_rows, plain_grads, row_probs, gate_weight, up_weight
    )
    input_grad, prob_parts, out_part = experts_back_call(
        input_rows, row_grads, places, weighted_hidden, down_weight, tok_rows
    )
    out_part = out_part.reshape(devices, tok_rows, model_width)

    prob_parts = prob_parts.reshape(4, 2, 4, 8, tok_rows)[:, :, :, :experts_here]
    prob_grad = jnp.sum(prob_parts, axis=1).reshape(EXPERTS, tok_rows).T
    logit_grad = (
        router_probs * (prob_grad - jnp.sum(prob_grad * router_probs, axis=-1, keepdims=True))
    ).astype(bf16)
    feature_grad = jnp.dot(logit_grad, router_full.T, preferred_element_type=f32) + input_grad
    residual_part, feature_gain_grad = feature_pull(feature_grad)
    residual_grad = cotangent.astype(f32) + residual_part
    attended_grad = residual_grad.astype(bf16)
    logit_all, first_half, second_half, normed_grad, wide_back, tall_back, gain_sums = attention_back_call(
        attended_grad,
        logit_grad.reshape(tok_rows // 2, 2 * EXPERTS),
        out_part,
        tokens,
        gain_attention[None],
        feature_gain_grad[None],
        wide_weight,
        tall_weight,
        head_gains,
        cosine,
        sine,
        kept,
    )
    own_index = (lax.axis_index(DP) * 2 + lax.axis_index(BLK)) * 4 + lax.axis_index(SP)
    own_features = lax.dynamic_slice_in_dim(
        features_all.reshape(devices * tok_rows, model_width), own_index * own_rows, own_rows, axis=1
    )
    router_grad = product(own_features, logit_all.reshape(devices * tok_rows, EXPERTS), ((0,), (0,)))

    _, attention_pull = jax.vjp(lambda values: norm_apply(values, gain_attention), tokens_f)
    input_gradient = residual_grad + attention_pull(normed_grad)[0]
    block_output = (residual + jnp.concatenate([first_half, second_half], axis=0)).astype(bf16)
    gate_grad_local, up_grad_local, down_grad_local = expert_weight_grads(
        expert_rows, grad_rows, weighted_hidden, gate_grad, up_grad
    )
    return (
        block_output,
        input_gradient,
        wide_back[0].astype(f32),
        wide_back[1].astype(f32),
        wide_back[2].astype(f32),
        tall_back.astype(f32),
        router_grad,
        gain_sums[0, :own_rows],
        gain_sums[1, :own_rows],
        gain_sums[2, :own_rows],
        gain_sums[3, :own_rows],
        gate_grad_local,
        up_grad_local,
        down_grad_local,
    )


def body(
    tokens,
    query_weight,
    key_weight,
    value_weight,
    output_weight,
    router_weight,
    attention_gain,
    query_gain,
    key_gain,
    feature_gain,
    gate_weight,
    up_weight,
    down_weight,
    routes,
    cotangent,
):
    sp_size = lax.axis_size(SP)
    blk_size = lax.axis_size(BLK)
    dp_size = lax.axis_size(DP)
    tok_rows = tokens.shape[0]
    model_width = tokens.shape[1]
    heads_here = HEADS // sp_size
    head_width = heads_here * HEAD_DIM
    experts_here = gate_weight.shape[0]
    capacity = CAP
    score_scale = 1.0 / math.sqrt(HEAD_DIM)
    (
        query_full,
        key_full,
        value_full,
        output_full,
        router_full,
        gain_attention,
        gain_query,
        gain_key,
        gain_feature,
    ) = (
        lax.all_gather(query_weight, AXES, axis=0, tiled=True),
        lax.all_gather(key_weight, AXES, axis=0, tiled=True),
        lax.all_gather(value_weight, AXES, axis=0, tiled=True),
        lax.all_gather(output_weight, AXES, axis=0, tiled=True),
        lax.all_gather(router_weight, AXES, axis=0, tiled=True),
        lax.all_gather(attention_gain, AXES, axis=0, tiled=True),
        lax.all_gather(query_gain, AXES, axis=0, tiled=True),
        lax.all_gather(key_gain, AXES, axis=0, tiled=True),
        lax.all_gather(feature_gain, AXES, axis=0, tiled=True),
    )
    gain_attention = gain_attention.astype(jnp.float32)
    gain_query = gain_query.astype(jnp.float32)
    gain_key = gain_key.astype(jnp.float32)
    gain_feature = gain_feature.astype(jnp.float32)
    tokens_f = tokens.astype(jnp.float32)
    normed_f, attention_pull = jax.vjp(norm_apply, tokens_f, gain_attention)
    normed = normed_f.astype(jnp.bfloat16)
    query_lin = jnp.dot(normed, query_full, preferred_element_type=jnp.float32)
    key_lin = jnp.dot(normed, key_full, preferred_element_type=jnp.float32)
    value_rows = jnp.dot(normed, value_full, preferred_element_type=jnp.float32).astype(
        jnp.bfloat16
    )
    seq_start = (lax.axis_index(BLK) * sp_size + lax.axis_index(SP)) * tok_rows
    cosine, sine = rope_tables(seq_start + jnp.arange(tok_rows, dtype=jnp.int32), HEAD_DIM)

    def rotated(linear, norm_gain):
        normalized = norm_apply(linear, norm_gain).reshape(
            tok_rows, model_width // HEAD_DIM, HEAD_DIM
        )
        return rotate(normalized, cosine, sine).reshape(tok_rows, model_width)

    query_rot, query_pull = jax.vjp(rotated, query_lin, gain_query)
    key_rot, key_pull = jax.vjp(rotated, key_lin, gain_key)
    query_heads, key_heads, value_heads = (
        lax.all_to_all(
            query_rot.astype(jnp.bfloat16).reshape(tok_rows, sp_size, head_width),
            SP,
            split_axis=1,
            concat_axis=0,
            tiled=True,
        ),
        lax.all_to_all(
            key_rot.astype(jnp.bfloat16).reshape(tok_rows, sp_size, head_width),
            SP,
            split_axis=1,
            concat_axis=0,
            tiled=True,
        ),
        lax.all_to_all(
            value_rows.reshape(tok_rows, sp_size, head_width),
            SP,
            split_axis=1,
            concat_axis=0,
            tiled=True,
        ),
    )
    head_rows = sp_size * tok_rows
    keys_all, values_all = (
        lax.all_gather(key_heads, BLK, axis=0, tiled=True),
        lax.all_gather(value_heads, BLK, axis=0, tiled=True),
    )
    key_rows = keys_all.shape[0]
    keys_all = keys_all.reshape(key_rows, heads_here, HEAD_DIM)
    values_all = values_all.reshape(key_rows, heads_here, HEAD_DIM)
    block_rows = math.gcd(512, head_rows)
    blocks = head_rows // block_rows
    query_base = lax.axis_index(BLK) * head_rows
    key_places = jnp.arange(key_rows, dtype=jnp.int32)
    query_blocks = query_heads.reshape(blocks, block_rows, heads_here, HEAD_DIM)
    block_starts = jnp.arange(blocks, dtype=jnp.int32) * block_rows

    def masked_scores(block_queries, block_start):
        scores = (
            jnp.einsum("qhd,khd->hqk", block_queries, keys_all, preferred_element_type=jnp.float32)
            * score_scale
        )
        query_places = query_base + block_start + jnp.arange(block_rows, dtype=jnp.int32)
        causal = key_places[None, :] <= query_places[:, None]
        return jnp.where(causal[None], scores, MASKED)

    def attend_block(block_input):
        block_queries, block_start = block_input
        scores = masked_scores(block_queries, block_start)
        row_peak = jnp.max(scores, axis=-1, keepdims=True)
        exponent = jnp.exp(scores - row_peak)
        row_total = jnp.sum(exponent, axis=-1, keepdims=True)
        attn_weights = (exponent / row_total).astype(jnp.bfloat16)
        context = jnp.einsum(
            "hqk,khd->qhd", attn_weights, values_all, preferred_element_type=jnp.float32
        )
        return (context.astype(jnp.bfloat16), (row_peak + jnp.log(row_total))[..., 0])

    context_blocks, logsum = lax.map(attend_block, (query_blocks, block_starts))
    context_rows = lax.all_to_all(
        context_blocks.reshape(head_rows, 1, head_width),
        SP,
        split_axis=0,
        concat_axis=1,
        tiled=True,
    ).reshape(tok_rows, model_width)
    attended = jnp.dot(context_rows, output_full, preferred_element_type=jnp.float32)
    residual = tokens_f + attended
    features_f, feature_pull = jax.vjp(norm_apply, residual, gain_feature)
    features = features_f.astype(jnp.bfloat16)
    logits = jnp.dot(features, router_full, preferred_element_type=jnp.float32)
    router_probs = jax.nn.softmax(logits, axis=-1)
    flat_experts, slot_rank = rank_slots(routes)
    slot_index = flat_experts * capacity + slot_rank
    token_of = jnp.arange(tok_rows * TOPK, dtype=jnp.int32) // TOPK
    slot_token = jnp.zeros((EXPERTS * capacity,), jnp.int32).at[slot_index].set(token_of)
    slot_used = jnp.zeros((EXPERTS * capacity,), jnp.bool_).at[slot_index].set(True)
    slot_rows = jnp.where(slot_used[:, None], features[slot_token], jnp.zeros((), jnp.bfloat16))

    def spread_halves(per_slot):
        grouped = per_slot.reshape(dp_size, 1, sp_size, experts_here, capacity, model_width)
        grouped = jnp.broadcast_to(
            grouped, (dp_size, blk_size, sp_size, experts_here, capacity, model_width)
        )
        return grouped.reshape(dp_size * blk_size * sp_size, experts_here, capacity, model_width)

    def join_halves(returned):
        grouped = returned.reshape(
            dp_size, blk_size, sp_size, experts_here, capacity, model_width
        ).astype(jnp.float32)
        return jnp.sum(grouped, axis=1).reshape(EXPERTS * capacity, model_width)

    send_rows = spread_halves(slot_rows)
    arrived = lax.all_to_all(
        send_rows, AXES, split_axis=0, concat_axis=0, tiled=True
    )
    gate_values = jnp.einsum(
        "secd,edf->secf", arrived, gate_weight, preferred_element_type=jnp.float32
    )
    up_values = jnp.einsum("secd,edf->secf", arrived, up_weight, preferred_element_type=jnp.float32)
    hidden = (jax.nn.silu(gate_values) * up_values).astype(jnp.bfloat16)
    part_out = jnp.einsum(
        "secf,efd->secd", hidden, down_weight, preferred_element_type=jnp.float32
    ).astype(jnp.bfloat16)
    returned = lax.all_to_all(
        part_out, AXES, split_axis=0, concat_axis=0, tiled=True
    )
    expert_out = join_halves(returned)
    route_rows = expert_out[slot_index].reshape(tok_rows, TOPK, model_width)
    route_probs = jnp.take_along_axis(router_probs, routes, axis=1)
    block_output = (residual + jnp.sum(route_probs[:, :, None] * route_rows, axis=1)).astype(
        jnp.bfloat16
    )
    out_grad = cotangent.astype(jnp.float32)
    route_grad = (
        (route_probs[:, :, None] * out_grad[:, None, :])
        .astype(jnp.bfloat16)
        .reshape(tok_rows * TOPK, model_width)
    )
    prob_route = jnp.sum(out_grad[:, None, :] * route_rows, axis=-1)
    expert_ids = jnp.arange(EXPERTS, dtype=jnp.int32)
    prob_grad = jnp.sum(
        jnp.where(routes[:, :, None] == expert_ids[None, None, :], prob_route[:, :, None], 0.0),
        axis=1,
    )
    logit_grad = (
        router_probs * (prob_grad - jnp.sum(prob_grad * router_probs, axis=-1, keepdims=True))
    ).astype(jnp.bfloat16)
    router_grad_full = jnp.dot(features.T, logit_grad, preferred_element_type=jnp.float32)
    gradient_slots = (
        jnp.zeros((EXPERTS * capacity, model_width), jnp.bfloat16).at[slot_index].set(route_grad)
    )
    gradient_send = spread_halves(gradient_slots)
    gradient_arrived, rows_arrived = (
        lax.all_to_all(gradient_send, AXES, split_axis=0, concat_axis=0, tiled=True),
        lax.all_to_all(send_rows, AXES, split_axis=0, concat_axis=0, tiled=True),
    )
    gate_values = jnp.einsum(
        "secd,edf->secf", rows_arrived, gate_weight, preferred_element_type=jnp.float32
    )
    up_values = jnp.einsum(
        "secd,edf->secf", rows_arrived, up_weight, preferred_element_type=jnp.float32
    )
    sigmoid_values = jax.nn.sigmoid(gate_values)
    silu_values = gate_values * sigmoid_values
    hidden = (silu_values * up_values).astype(jnp.bfloat16)
    hidden_grad = jnp.einsum(
        "secd,efd->secf", gradient_arrived, down_weight, preferred_element_type=jnp.float32
    ).astype(jnp.bfloat16)
    down_grad_local = jnp.einsum(
        "secf,secd->efd", hidden, gradient_arrived, preferred_element_type=jnp.float32
    )
    hidden_wide = hidden_grad.astype(jnp.float32)
    gate_grad = (
        hidden_wide * up_values * sigmoid_values * (1.0 + gate_values * (1.0 - sigmoid_values))
    ).astype(jnp.bfloat16)
    up_grad = (hidden_wide * silu_values).astype(jnp.bfloat16)
    gate_grad_local = jnp.einsum(
        "secd,secf->edf", rows_arrived, gate_grad, preferred_element_type=jnp.float32
    )
    up_grad_local = jnp.einsum(
        "secd,secf->edf", rows_arrived, up_grad, preferred_element_type=jnp.float32
    )
    input_parts = (
        jnp.einsum("secf,edf->secd", gate_grad, gate_weight, preferred_element_type=jnp.float32)
        + jnp.einsum("secf,edf->secd", up_grad, up_weight, preferred_element_type=jnp.float32)
    ).astype(jnp.bfloat16)
    returned_grads = lax.all_to_all(
        input_parts, AXES, split_axis=0, concat_axis=0, tiled=True
    )
    slot_input_grad = join_halves(returned_grads)
    expert_input_grad = slot_input_grad[slot_index].reshape(tok_rows, TOPK, model_width)
    feature_grad = jnp.dot(logit_grad, router_full.T, preferred_element_type=jnp.float32) + jnp.sum(
        expert_input_grad, axis=1
    )
    residual_part, feature_gain_grad = feature_pull(feature_grad)
    residual_grad = out_grad + residual_part
    attended_grad = residual_grad.astype(jnp.bfloat16)
    output_grad_full = jnp.dot(context_rows.T, attended_grad, preferred_element_type=jnp.float32)
    context_grad = jnp.dot(attended_grad, output_full.T, preferred_element_type=jnp.float32).astype(
        jnp.bfloat16
    )
    context_heads_grad = lax.all_to_all(
        context_grad.reshape(tok_rows, sp_size, head_width),
        SP,
        split_axis=1,
        concat_axis=0,
        tiled=True,
    )
    context_heads_grad = context_heads_grad.reshape(blocks, block_rows, heads_here, HEAD_DIM)

    def backward_block(carry, block_input):
        key_total, value_total = carry
        block_queries, block_grads, block_logsum, block_start = block_input
        scores = masked_scores(block_queries, block_start)
        attn_weights = jnp.exp(scores - block_logsum[..., None])
        prob_dots = jnp.einsum(
            "qhd,khd->hqk", block_grads, values_all, preferred_element_type=jnp.float32
        )
        row_delta = jnp.sum(attn_weights * prob_dots, axis=-1, keepdims=True)
        score_grad = (attn_weights * (prob_dots - row_delta)).astype(jnp.bfloat16)
        query_grad = (
            jnp.einsum("hqk,khd->qhd", score_grad, keys_all, preferred_element_type=jnp.float32)
            * score_scale
        )
        key_total = (
            key_total
            + jnp.einsum(
                "hqk,qhd->khd", score_grad, block_queries, preferred_element_type=jnp.float32
            )
            * score_scale
        )
        value_total = value_total + jnp.einsum(
            "hqk,qhd->khd",
            attn_weights.astype(jnp.bfloat16),
            block_grads,
            preferred_element_type=jnp.float32,
        )
        return ((key_total, value_total), query_grad.astype(jnp.bfloat16))

    zero_keys = jnp.zeros((key_rows, heads_here, HEAD_DIM), jnp.float32)
    (key_total, value_total), query_grads = lax.scan(
        backward_block,
        (zero_keys, zero_keys),
        (query_blocks, context_heads_grad, logsum, block_starts),
    )
    key_mine, value_mine = (
        lax.psum_scatter(key_total, BLK, scatter_dimension=0, tiled=True),
        lax.psum_scatter(value_total, BLK, scatter_dimension=0, tiled=True),
    )
    query_back, key_back, value_back = (
        lax.all_to_all(
            query_grads.reshape(head_rows, 1, head_width),
            SP,
            split_axis=0,
            concat_axis=1,
            tiled=True,
        ),
        lax.all_to_all(
            key_mine.astype(jnp.bfloat16).reshape(head_rows, 1, head_width),
            SP,
            split_axis=0,
            concat_axis=1,
            tiled=True,
        ),
        lax.all_to_all(
            value_mine.astype(jnp.bfloat16).reshape(head_rows, 1, head_width),
            SP,
            split_axis=0,
            concat_axis=1,
            tiled=True,
        ),
    )
    query_lin_grad, query_gain_grad = query_pull(
        query_back.reshape(tok_rows, model_width).astype(jnp.float32)
    )
    key_lin_grad, key_gain_grad = key_pull(
        key_back.reshape(tok_rows, model_width).astype(jnp.float32)
    )
    query_lin_low = query_lin_grad.astype(jnp.bfloat16)
    key_lin_low = key_lin_grad.astype(jnp.bfloat16)
    value_low = value_back.reshape(tok_rows, model_width)
    query_grad_full = jnp.dot(normed.T, query_lin_low, preferred_element_type=jnp.float32)
    key_grad_full = jnp.dot(normed.T, key_lin_low, preferred_element_type=jnp.float32)
    value_grad_full = jnp.dot(normed.T, value_low, preferred_element_type=jnp.float32)
    normed_grad = jnp.dot(query_lin_low, query_full.T, preferred_element_type=jnp.float32)
    normed_grad = normed_grad + jnp.dot(key_lin_low, key_full.T, preferred_element_type=jnp.float32)
    normed_grad = normed_grad + jnp.dot(value_low, value_full.T, preferred_element_type=jnp.float32)
    tokens_part, attention_gain_grad = attention_pull(normed_grad)
    input_gradient = residual_grad + tokens_part
    summed = (
        lax.psum_scatter(query_grad_full, AXES, scatter_dimension=0, tiled=True),
        lax.psum_scatter(key_grad_full, AXES, scatter_dimension=0, tiled=True),
        lax.psum_scatter(value_grad_full, AXES, scatter_dimension=0, tiled=True),
        lax.psum_scatter(output_grad_full, AXES, scatter_dimension=0, tiled=True),
        lax.psum_scatter(router_grad_full, AXES, scatter_dimension=0, tiled=True),
        lax.psum_scatter(attention_gain_grad, AXES, scatter_dimension=0, tiled=True),
        lax.psum_scatter(query_gain_grad, AXES, scatter_dimension=0, tiled=True),
        lax.psum_scatter(key_gain_grad, AXES, scatter_dimension=0, tiled=True),
        lax.psum_scatter(feature_gain_grad, AXES, scatter_dimension=0, tiled=True),
    )
    return (
        block_output,
        input_gradient,
        summed[0],
        summed[1],
        summed[2],
        summed[3],
        summed[4],
        summed[5],
        summed[6],
        summed[7],
        summed[8],
        gate_grad_local,
        up_grad_local,
        down_grad_local,
    )


def solution(mesh):
    in_specs = (
        P(AXES, None),
        P(AXES, None),
        P(AXES, None),
        P(AXES, None),
        P(AXES, None),
        P(AXES, None),
        P(AXES),
        P(AXES),
        P(AXES),
        P(AXES),
        P((DP, SP), None, BLK),
        P((DP, SP), None, BLK),
        P((DP, SP), BLK, None),
        P(AXES, None),
        P(AXES, None),
    )
    out_specs = (
        P(AXES, None),
        P(AXES, None),
        P(AXES, None),
        P(AXES, None),
        P(AXES, None),
        P(AXES, None),
        P(AXES, None),
        P(AXES),
        P(AXES),
        P(AXES),
        P(AXES),
        P((DP, SP), None, BLK),
        P((DP, SP), None, BLK),
        P((DP, SP), BLK, None),
    )
    fast = dict(mesh.shape) == {DP: 4, BLK: 2, SP: 4}
    return jax.shard_map(body_fast if fast else body, mesh=mesh, in_specs=in_specs, out_specs=out_specs, check_vma=False)
```

```python
import functools
import math

import jax
import jax.numpy as jnp
import numpy as np
from jax import lax
from jax.experimental import pallas as pl
from jax.experimental.pallas import tpu as pltpu
from jax.sharding import PartitionSpec as P

DP, BLK, SP = AXES = ("dp", "blk", "sp")

HEADS = 16
HEAD_DIM = 128
EXPERTS = 64
TOPK = 8
CAP = 24


NORM_EPSILON = 1e-05
ROPE_BASE = 10000.0
MASKED = -1e30


def norm_apply(values, norm_gain):
    return (
        values
        * lax.rsqrt(jnp.mean(values * values, axis=-1, keepdims=True) + NORM_EPSILON)
        * norm_gain
    )


def rope_tables(positions, head_size):
    half_size = head_size // 2
    frequencies = jnp.exp(
        -math.log(ROPE_BASE) * 2.0 * jnp.arange(half_size, dtype=jnp.float32) / head_size
    )
    angles = positions.astype(jnp.float32)[:, None] * frequencies[None, :]
    return (jnp.cos(angles), jnp.sin(angles))


def rotate(values, cosine, sine):
    half_size = values.shape[-1] // 2
    first_half = values[..., :half_size]
    second_half = values[..., half_size:]
    cosine_row = cosine[:, None, :]
    sine_row = sine[:, None, :]
    return jnp.concatenate(
        [
            first_half * cosine_row - second_half * sine_row,
            second_half * cosine_row + first_half * sine_row,
        ],
        axis=-1,
    )


def rank_slots(route_rows):
    flat_experts = route_rows.reshape(-1)
    onehot = (flat_experts[:, None] == jnp.arange(EXPERTS, dtype=jnp.int32)[None, :]).astype(
        jnp.int32
    )
    return (flat_experts, jnp.sum(jnp.cumsum(onehot, axis=0) * onehot, axis=1) - 1)


MESH_ID = pl.DeviceIdType.MESH
VMEM_BYTES = 60 * 1024 * 1024


class Place:
    def __init__(self):
        self.dp = lax.axis_index(DP)
        self.blk = lax.axis_index(BLK)
        self.z = lax.axis_index(SP)
        self.x = self.dp % 2
        self.y = self.dp // 2
        self.col = self.blk * 4 + self.z

    def column(self, k):
        if k == 0:
            return self.dp
        if k == 1:
            return self.dp + 1 - 2 * self.x
        if k == 2:
            return self.dp + 2 - 4 * self.y
        return 3 - self.dp

    def at(self, k=0, blk=None, z=None):
        return (self.column(k), self.blk if blk is None else blk, self.z if z is None else z)


def entry_barrier(place, reach):
    barrier = pltpu.get_barrier_semaphore()

    def tell(target):
        pl.semaphore_signal(barrier, inc=1, device_id=target, device_id_type=MESH_ID)

    if reach == "all":
        me = (place.dp * 2 + place.blk) * 4 + place.z

        @pl.loop(1, 32)
        def _(step):
            other = (me + step) % 32
            tell((other // 8, (other // 4) % 2, other % 4))

        pl.semaphore_wait(barrier, 31)
    elif reach == "column":

        @pl.loop(1, 8)
        def _(step):
            other = (place.col + step) % 8
            tell((place.dp, other // 4, other % 4))

        pl.semaphore_wait(barrier, 7)
    else:
        tell_partners(place, barrier)
        wait_partners(place, barrier)


def tell_partners(place, semaphore):
    def tell(target):
        pl.semaphore_signal(semaphore, inc=1, device_id=target, device_id_type=MESH_ID)

    tell(place.at(0, 1 - place.blk))
    tell(place.at(1))
    tell(place.at(2))

    @pl.when(place.z > 0)
    def _():
        tell(place.at(z=place.z - 1))

    @pl.when(place.z < 3)
    def _():
        tell(place.at(z=place.z + 1))


def wait_partners(place, semaphore):
    ends = (3 - place.z) // 3 + place.z // 3
    pl.semaphore_wait(semaphore, 5 - ends)


def remote(src, dst, send_sem, recv_sem, target):
    return pltpu.make_async_remote_copy(
        src_ref=src,
        dst_ref=dst,
        send_sem=send_sem,
        recv_sem=recv_sem,
        device_id=target,
        device_id_type=MESH_ID,
    )


class GatherFlow:
    SENDS = 40
    RECVS = 37

    def __init__(self, place, src, out, send, recv, full, direct=False, others=False):
        self.p, self.src, self.out, self.send, self.recv, self.full = place, src, out, send, recv, full
        self.direct, self.others = direct, others
        self.half = src.shape[0] // 2

    def slot(self, k, blk, s):
        if self.full:
            return (self.p.column(k) * 2 + blk) * 4 + s
        return blk * 4 + s

    def block(self, k, s, blk=None):
        return self.out.at[self.slot(k, self.p.blk if blk is None else blk, s)]

    def copies(self, k, s, own=False):
        src = self.src if own else self.block(k, s)
        return src, self.block(k, s)

    def up(self, s, own=False):
        src, dst = self.copies(0, s, own)
        return remote(src, dst, self.send.at[s], self.recv.at[s], self.p.at(z=jnp.minimum(self.p.z + 1, 3)))

    def down(self, s, own=False):
        src, dst = self.copies(0, s, own)
        return remote(src, dst, self.send.at[4 + s], self.recv.at[s], self.p.at(z=jnp.maximum(self.p.z - 1, 0)))

    def across_x(self, s, own=False):
        src, dst = self.copies(0, s, own)
        return remote(src, dst, self.send.at[8 + s], self.recv.at[4 + s], self.p.at(1))

    def across_y(self, s, own=False):
        src, dst = self.copies(0, s, own)
        return remote(src, dst, self.send.at[12 + s], self.recv.at[8 + s], self.p.at(2))

    def turn_y(self, s):
        ref = self.block(1, s).at[pl.ds(0, self.half)]
        return remote(ref, ref, self.send.at[16 + s], self.recv.at[12 + s], self.p.at(2))

    def turn_x(self, s):
        ref = self.block(2, s).at[pl.ds(self.half, self.half)]
        return remote(ref, ref, self.send.at[20 + s], self.recv.at[16 + s], self.p.at(1))

    def core(self, k, s, own=False):
        src, dst = self.copies(k, s, own)
        return remote(
            src, dst, self.send.at[24 + 4 * k + s], self.recv.at[20 + 4 * k + s], self.p.at(0, 1 - self.p.blk)
        )

    def got(self, sem, ref):
        remote(ref, ref, self.send.at[0], self.recv.at[sem], self.p.at(0, 1 - self.p.blk)).wait_recv()

    def own_copy(self):
        return pltpu.make_async_copy(self.src, self.block(0, self.p.z), self.recv.at[36])

    def spread(self, s, own=False):
        if self.full:
            self.across_x(s, own).start()
            self.across_y(s, own).start()
        self.core(0, s, own).start()

    def straight(self, step):
        z = self.p.z
        return remote(
            self.src, self.block(0, z), self.send.at[step - 1], self.recv.at[z], self.p.at(z=(z + step) % 4)
        )

    def begin(self):
        z = self.p.z
        if self.direct:
            for step in (1, 2, 3):
                self.straight(step).start()
            self.spread(z, True)
            self.own_copy().start()
            return

        @pl.when(z < 3)
        def _():
            self.up(z, True).start()

        @pl.when(z > 0)
        def _():
            self.down(z, True).start()

        if not self.others:
            self.spread(z, True)
            self.own_copy().start()

    def along(self, d):
        z = self.p.z

        @pl.when(z >= d)
        def _():
            s = z - d
            self.got(s, self.block(0, s))

            if not self.direct:

                @pl.when(z < 3)
                def _():
                    self.up(s).start()

            self.spread(s)

        @pl.when(z + d <= 3)
        def _():
            s = z + d
            self.got(s, self.block(0, s))

            if not self.direct:

                @pl.when(z > 0)
                def _():
                    self.down(s).start()

            self.spread(s)

    def each(self, d, act):
        z = self.p.z
        if d == 0:
            if not self.others:
                act(z)
            return

        @pl.when(z >= d)
        def _():
            act(z - d)

        @pl.when(z + d <= 3)
        def _():
            act(z + d)

    def turn(self, d):
        if not self.full:
            return

        def act(s):
            self.got(4 + s, self.block(1, s))
            self.turn_y(s).start()
            self.core(1, s).start()
            self.got(8 + s, self.block(2, s))
            self.turn_x(s).start()
            self.core(2, s).start()

        self.each(d, act)

    def corner(self, d):
        if not self.full:
            return

        def act(s):
            self.got(12 + s, self.block(3, s).at[pl.ds(0, self.half)])
            self.got(16 + s, self.block(3, s).at[pl.ds(self.half, self.half)])
            self.core(3, s).start()

        self.each(d, act)

    def settle_plane(self, s):
        for k in range(4 if self.full else 1):
            self.got(20 + 4 * k + s, self.block(k, s, 1 - self.p.blk))
            self.core(k, s).wait_send()
        if self.full:
            self.across_x(s).wait_send()
            self.across_y(s).wait_send()
            self.turn_x(s).wait_send()
            self.turn_y(s).wait_send()

    def finish(self):
        z = self.p.z

        @pl.loop(0, 4)
        def _(s):
            pl.when((s != z) | (not self.others))(lambda: self.settle_plane(s))
            if not self.direct:

                @pl.when((s <= z) & (z < 3))
                def _():
                    self.up(s).wait_send()

                @pl.when((s >= z) & (z > 0))
                def _():
                    self.down(s).wait_send()

        if self.direct:
            for step in (1, 2, 3):
                self.straight(step).wait_send()
        if not self.others:
            self.own_copy().wait()


class PlaneFlow(GatherFlow):
    def __init__(self, place, blocks, out, send, recv, local):
        super().__init__(place, blocks[0][1], out, send, recv, True)
        self.blocks, self.local = blocks, local

    def begin(self):
        for i, (s, src) in enumerate(self.blocks):
            self.src = src
            self.spread(s, True)
            pltpu.make_async_copy(src, self.block(0, s), self.local.at[i]).start()

    def turns(self):
        for s, _ in self.blocks:
            self.got(4 + s, self.block(1, s))
            self.turn_y(s).start()
            self.core(1, s).start()
            self.got(8 + s, self.block(2, s))
            self.turn_x(s).start()
            self.core(2, s).start()

    def corners(self):
        for s, _ in self.blocks:
            self.got(12 + s, self.block(3, s).at[pl.ds(0, self.half)])
            self.got(16 + s, self.block(3, s).at[pl.ds(self.half, self.half)])
            self.core(3, s).start()

    def finish(self):
        for i, (s, src) in enumerate(self.blocks):
            self.settle_plane(s)
            pltpu.make_async_copy(src, self.block(0, s), self.local.at[i]).wait()


class PlaneFlow(GatherFlow):
    def __init__(self, place, blocks, out, send, recv, local):
        super().__init__(place, blocks[0][1], out, send, recv, True)
        self.blocks, self.local = blocks, local

    def begin(self):
        for i, (s, src) in enumerate(self.blocks):
            self.src = src
            self.spread(s, True)
            pltpu.make_async_copy(src, self.block(0, s), self.local.at[i]).start()

    def turns(self):
        for s, _ in self.blocks:
            self.got(4 + s, self.block(1, s))
            self.turn_y(s).start()
            self.core(1, s).start()
            self.got(8 + s, self.block(2, s))
            self.turn_x(s).start()
            self.core(2, s).start()

    def corners(self):
        for s, _ in self.blocks:
            self.got(12 + s, self.block(3, s).at[pl.ds(0, self.half)])
            self.got(16 + s, self.block(3, s).at[pl.ds(self.half, self.half)])
            self.core(3, s).start()

    def finish(self):
        for i, (s, src) in enumerate(self.blocks):
            self.settle_plane(s)
            pltpu.make_async_copy(src, self.block(0, s), self.local.at[i]).wait()


def run_flows(flows):
    lists = [flow.steps() for flow in flows]
    for position in range(max(len(steps) for steps in lists)):
        for steps in lists:
            if position < len(steps):
                steps[position]()


def add_rows(dst, terms, rows):
    @pl.loop(0, rows // 16)
    def _(i):
        at = pl.ds(pl.multiple_of(i * 16, 16), 16)
        total = terms[0][at, :].astype(jnp.float32)
        for term in terms[1:]:
            total = total + term[at, :].astype(jnp.float32)
        dst[at, :] = total.astype(dst.dtype)


class ScatterFlow:
    SENDS = 16 + 8 + 8 + 4 + 4
    RECVS = 16 + 8 + 8 + 4 + 4
    LOCALS = 16

    def __init__(self, place, part, out, scratch, full, band=None):
        self.p, self.part, self.out, self.full = place, part, out, full
        if full:
            (self.acc, self.near, self.half_in, self.side_in, self.line_in, self.sum, self.send, self.recv, self.local) = scratch
        else:
            (self.acc, self.near, self.line_in, self.sum, self.send, self.recv, self.local) = scratch
        self.columns = 4 if full else 1
        self.left = False
        first, self.rows = band or (0, part.shape[1])
        self.band = pl.ds(first, self.rows)
        self.half = self.rows // 2

    @staticmethod
    def scratch(rows, width, dtype, full):
        columns = 4 if full else 1
        shapes = [
            pltpu.VMEM((columns, 4, rows, width), dtype),
            pltpu.VMEM((columns, 4, rows, width), dtype),
        ]
        if full:
            shapes += [pltpu.VMEM((2, 4, rows // 2, width), dtype), pltpu.VMEM((2, 4, rows, width), dtype)]
        return shapes + [
            pltpu.VMEM((2, 4, rows, width), dtype),
            pltpu.VMEM((rows, width), jnp.float32),
            pltpu.SemaphoreType.DMA((ScatterFlow.SENDS,)),
            pltpu.SemaphoreType.DMA((ScatterFlow.RECVS,)),
            pltpu.SemaphoreType.DMA((ScatterFlow.LOCALS,)),
        ]

    def slot(self, k, blk, s):
        if self.full:
            return (self.p.column(k) * 2 + blk) * 4 + s
        return blk * 4 + s

    def order(self, i):
        z = self.p.z
        return [3 * (1 - z // 2), (2 + 3 * z) % 5, 1 + z % 2, z][i]

    def load(self, k, s):
        return pltpu.make_async_copy(
            self.part.at[self.slot(k, self.p.blk, s), self.band], self.acc.at[k, s], self.local.at[4 * k + s]
        )

    def core(self, k, s):
        return remote(
            self.part.at[self.slot(k, 1 - self.p.blk, s), self.band],
            self.near.at[k, s],
            self.send.at[4 * k + s],
            self.recv.at[4 * k + s],
            self.p.at(0, 1 - self.p.blk),
        )

    def half_x(self, s):
        return remote(
            self.acc.at[3, s, pl.ds(0, self.half)],
            self.half_in.at[0, s],
            self.send.at[16 + s],
            self.recv.at[16 + s],
            self.p.at(1),
        )

    def half_y(self, s):
        return remote(
            self.acc.at[3, s, pl.ds(self.half, self.half)],
            self.half_in.at[1, s],
            self.send.at[20 + s],
            self.recv.at[20 + s],
            self.p.at(2),
        )

    def side_x(self, s):
        return remote(
            self.acc.at[1, s], self.side_in.at[0, s], self.send.at[24 + s], self.recv.at[24 + s], self.p.at(1)
        )

    def side_y(self, s):
        return remote(
            self.acc.at[2, s], self.side_in.at[1, s], self.send.at[28 + s], self.recv.at[28 + s], self.p.at(2)
        )

    def line_up(self, s):
        return remote(
            self.acc.at[0, s],
            self.line_in.at[0, s],
            self.send.at[32 + s],
            self.recv.at[32 + s],
            self.p.at(z=jnp.minimum(self.p.z + 1, 3)),
        )

    def line_down(self, s):
        return remote(
            self.acc.at[0, s],
            self.line_in.at[1, s],
            self.send.at[36 + s],
            self.recv.at[36 + s],
            self.p.at(z=jnp.maximum(self.p.z - 1, 0)),
        )

    def begin(self, columns=None):
        for i in range(4):
            s = self.order(i)
            for k in columns or reversed(range(self.columns)):
                self.core(k, s).start()
                self.load(k, s).start()

    def unsent(self):
        return range(self.columns)

    def leave(self, s):
        self.half_x(s).wait_send()
        self.half_y(s).wait_send()
        self.side_x(s).wait_send()
        self.side_y(s).wait_send()

    def leave_all(self):
        self.left = True

        @pl.loop(0, 4)
        def _(s):
            self.leave(s)

    def arrive(self, k, s):
        self.load(k, s).wait()
        self.core(k, s).wait_recv()
        return [self.acc.at[k, s], self.near.at[k, s]]

    def stage1(self, i):
        if not self.full:
            return
        s = self.order(i)
        add_rows(self.acc.at[3, s], self.arrive(3, s), self.rows)
        self.half_x(s).start()
        self.half_y(s).start()

    def stage2(self, i):
        if not self.full:
            return
        s = self.order(i)
        first, second = pl.ds(0, self.half), pl.ds(self.half, self.half)
        terms = self.arrive(2, s)
        late = [term.at[first] for term in terms] + [self.half_in.at[0, s]]
        rest = [term.at[second] for term in terms]
        add_rows(rest[0], rest, self.half)
        self.half_x(s).wait_recv()
        add_rows(late[0], late, self.half)
        self.side_y(s).start()
        terms = self.arrive(1, s)
        late = [term.at[second] for term in terms] + [self.half_in.at[1, s]]
        rest = [term.at[first] for term in terms]
        add_rows(rest[0], rest, self.half)
        self.half_y(s).wait_recv()
        add_rows(late[0], late, self.half)
        self.side_x(s).start()

    def stage3(self, i):
        s = self.order(i)
        z = self.p.z
        terms = self.arrive(0, s)
        if self.full:
            self.side_x(s).wait_recv()
            self.side_y(s).wait_recv()
            terms = terms + [self.side_in.at[0, s], self.side_in.at[1, s]]
        add_rows(self.acc.at[0, s], terms, self.rows)
        if i < 3:

            @pl.when(z == 0)
            def _():
                self.line_up(s).start()

            @pl.when(z == 3)
            def _():
                self.line_down(s).start()

    def chain(self, i):
        s = self.order(i)
        z = self.p.z

        @pl.when((z > 0) & (z < s) & (z < 3))
        def _():
            self.line_up(s).wait_recv()
            add_rows(self.acc.at[0, s], [self.acc.at[0, s], self.line_in.at[0, s]], self.rows)
            self.line_up(s).start()

        @pl.when((z < 3) & (z > s) & (z > 0))
        def _():
            self.line_down(s).wait_recv()
            add_rows(self.acc.at[0, s], [self.acc.at[0, s], self.line_in.at[1, s]], self.rows)
            self.line_down(s).start()

    def final(self):
        z = self.p.z
        mine, above, below = self.acc.at[0, z], self.line_in.at[0, z], self.line_in.at[1, z]

        @pl.when(z > 0)
        def _():
            self.line_up(z).wait_recv()

        @pl.when(z < 3)
        def _():
            self.line_down(z).wait_recv()

        @pl.when(z == 0)
        def _():
            add_rows(self.sum, [mine, below], self.rows)

        @pl.when(z == 3)
        def _():
            add_rows(self.sum, [mine, above], self.rows)

        @pl.when((z > 0) & (z < 3))
        def _():
            add_rows(self.sum, [mine, above, below], self.rows)

        done = pltpu.make_async_copy(self.sum, self.out, self.local.at[0])
        done.start()

        @pl.loop(0, 4)
        def _(s):
            for k in self.unsent():
                self.core(k, s).wait_send()
            if self.full and not self.left:
                self.leave(s)

            @pl.when(s > z)
            def _():
                self.line_up(s).wait_send()

            @pl.when(s < z)
            def _():
                self.line_down(s).wait_send()

        done.wait()


class MadeFlow(ScatterFlow):
    def __init__(self, place, out, scratch, stage):
        self.stage = stage
        super().__init__(place, stage.at[0], out, scratch, True)

    def core(self, k, s):
        return remote(
            self.stage.at[k % 2, s],
            self.near.at[k, s],
            self.send.at[4 * k + s],
            self.recv.at[4 * k + s],
            self.p.at(0, 1 - self.p.blk),
        )

    def unsent(self):
        return (0, 1)

    def arrive(self, k, s):
        self.core(k, s).wait_recv()
        return [self.acc.at[k, s], self.near.at[k, s]]


def local_params():
    return pltpu.CompilerParams(vmem_limit_bytes=VMEM_BYTES)


def inner(left, right, left_dim=1, right_dim=0):
    return lax.dot_general(
        left, right, (((left_dim,), (right_dim,)), ((), ())), preferred_element_type=jnp.float32
    )


def is_place(places, per):
    return lax.broadcasted_iota(jnp.int32, (per, places.shape[1]), 0) == places


def one_hot(places, per):
    experts = places.shape[0]
    hot = [is_place(places[e : e + 1], per).astype(jnp.float32) for e in range(experts)]
    return jnp.concatenate(hot, axis=0).astype(jnp.bfloat16)


def pick_rows(places, probs, features, per):
    pairs, experts, pair_rows = places.shape
    width = features.shape[-1]
    step = 4

    def kernel(place_ref, prob_ref, feature_ref, row_ref, row_prob_ref):
        for i in range(step):
            rows = inner(one_hot(place_ref[i], per), feature_ref[i]).astype(row_ref.dtype)
            for e in range(experts):
                at = pl.ds(i * per, per)
                row_ref[e, at] = rows[e * per : (e + 1) * per]
                hot = is_place(place_ref[i, e : e + 1], per)
                prob = jnp.concatenate([prob_ref[2 * i, e : e + 1], prob_ref[2 * i + 1, e : e + 1]], axis=1)
                row_prob_ref[e, at] = jnp.sum(jnp.where(hot, prob, 0.0), axis=1, keepdims=True)

    return pl.pallas_call(
        kernel,
        out_shape=[
            jax.ShapeDtypeStruct((experts, pairs * per, width), features.dtype),
            jax.ShapeDtypeStruct((experts, pairs * per, 1), jnp.float32),
        ],
        grid=(pairs // step,),
        in_specs=[
            pl.BlockSpec((step, experts, pair_rows), lambda p: (p, 0, 0)),
            pl.BlockSpec((2 * step, experts, pair_rows // 2), lambda p: (p, 0, 0)),
            pl.BlockSpec((step, pair_rows, width), lambda p: (p, 0, 0)),
        ],
        out_specs=[
            pl.BlockSpec((experts, step * per, width), lambda p: (0, p, 0)),
            pl.BlockSpec((experts, step * per, 1), lambda p: (0, p, 0)),
        ],
        compiler_params=local_params(),
        name="pick_rows",
    )(places, probs, features)


def run_experts(rows, plain_grads, probs, gate_weight, up_weight):
    experts, slots, width = rows.shape
    hidden = gate_weight.shape[2]
    parts = 2
    part = slots // parts

    def kernel(x, plain_ref, p, wg, wu, weighted, gate_back, up_back, back, prob_back):
        gate = inner(x[0], wg[0])
        up = inner(x[0], wu[0])
        plain = plain_ref[0]
        prob = p[0]
        sig = jax.nn.sigmoid(gate)
        act = gate * sig
        hid = act * up
        prob_back[0] = jnp.sum(hid * plain, axis=1, keepdims=True)
        weighted[0] = (hid * prob).astype(jnp.bfloat16)
        grad = plain * prob
        gate_low = (grad * up * sig * (1.0 + gate * (1.0 - sig))).astype(jnp.bfloat16)
        up_low = (grad * act).astype(jnp.bfloat16)
        gate_back[0] = gate_low
        up_back[0] = up_low
        back[0] = (inner(gate_low, wg[0], 1, 1) + inner(up_low, wu[0], 1, 1)).astype(jnp.bfloat16)

    def block(size):
        return pl.BlockSpec((1, part, size), lambda e, i: (e, i, 0))

    weight = pl.BlockSpec((1, width, hidden), lambda e, i: (e, 0, 0))
    narrow = jax.ShapeDtypeStruct((experts, slots, hidden), rows.dtype)
    return pl.pallas_call(
        kernel,
        out_shape=[
            narrow,
            narrow,
            narrow,
            jax.ShapeDtypeStruct(rows.shape, rows.dtype),
            jax.ShapeDtypeStruct((experts, slots, 1), jnp.float32),
        ],
        grid=(experts, parts),
        in_specs=[block(width), block(hidden), block(1), weight, weight],
        out_specs=[block(hidden)] * 3 + [block(width), block(1)],
        compiler_params=local_params(),
        name="run_experts",
    )(rows, plain_grads, probs, gate_weight, up_weight)


class PickWork:
    GROUP = 4

    def __init__(self, places, source, weight, rows_out, plain_out, scratch):
        self.places, self.source, self.weight = places, source, weight
        self.rows_out, self.plain_out = rows_out, plain_out
        self.block, self.rows, self.plain, self.held, self.in_sems, self.out_sems, self.held_sem = scratch
        self.pairs = source.shape[0]
        self.units = self.pairs + self.GROUP
        self.experts = weight.shape[0]
        self.per = self.rows.shape[2] // self.GROUP

    @staticmethod
    def scratch(source, weight, per):
        experts, hidden, width = weight.shape
        group = PickWork.GROUP * per
        return [
            pltpu.VMEM((2,) + source.shape[1:], source.dtype),
            pltpu.VMEM((2, experts, group, width), source.dtype),
            pltpu.VMEM((2, experts, group, hidden), jnp.float32),
            pltpu.VMEM(weight.shape, weight.dtype),
            pltpu.SemaphoreType.DMA((2,)),
            pltpu.SemaphoreType.DMA((2, 2)),
            pltpu.SemaphoreType.DMA((1,)),
        ]

    def load(self, unit, slot):
        return pltpu.make_async_copy(self.source.at[unit], self.block.at[slot], self.in_sems.at[slot])

    def hold(self):
        return pltpu.make_async_copy(self.weight, self.held, self.held_sem.at[0])

    def stores(self, group, slot):
        height = self.GROUP * self.per
        at = pl.ds(pl.multiple_of(group * height, height), height)
        return [
            pltpu.make_async_copy(self.rows.at[slot], self.rows_out.at[:, at], self.out_sems.at[slot, 0]),
            pltpu.make_async_copy(self.plain.at[slot], self.plain_out.at[:, at], self.out_sems.at[slot, 1]),
        ]

    def begin(self):
        self.hold().start()
        self.load(0, 0).start()

    def pick(self, unit):
        slot, group, turn = unit % 2, unit // self.GROUP, unit % self.GROUP
        side = group % 2

        @pl.when(unit + 1 < self.pairs)
        def _():
            self.load(unit + 1, 1 - slot).start()

        @pl.when((turn == 0) & (group >= 2))
        def _():
            for copy in self.stores(group - 2, side):
                copy.wait()

        self.load(unit, slot).wait()
        rows = inner(one_hot(self.places[unit], self.per), self.block[slot]).astype(self.rows.dtype)
        for e in range(self.experts):
            at = pl.ds(pl.multiple_of(turn * self.per, self.per), self.per)
            self.rows[side, e, at] = rows[e * self.per : (e + 1) * self.per]

    def multiply(self, unit):
        group, e = unit // self.GROUP, unit % self.GROUP
        side = group % 2

        @pl.when(unit == 0)
        def _():
            self.hold().wait()

        self.plain[side, e] = inner(self.rows[side, e], self.held[e], 1, 1)

        @pl.when(e == self.GROUP - 1)
        def _():
            for copy in self.stores(group, side):
                copy.start()

    def run(self, unit):
        pl.when(unit < self.pairs)(lambda: self.pick(unit))
        pl.when(unit >= self.GROUP)(lambda: self.multiply(unit - self.GROUP))

    def finish(self):
        groups = self.pairs // self.GROUP
        for group in (groups - 2, groups - 1):
            for copy in self.stores(group, group % 2):
                copy.wait()


class PutWork:
    def __init__(self, place, places, source, row_grads, flow, deals, scratch):
        self.p, self.places, self.source, self.row_grads = place, places, source, row_grads
        self.flow, self.deals = flow, deals
        self.rows, self.sems = scratch
        self.experts, self.per = self.rows.shape[1:3]

    @staticmethod
    def scratch(source, per):
        experts, _, width = source.shape
        return [pltpu.VMEM((2, experts, per, width), source.dtype), pltpu.SemaphoreType.DMA((2,))]

    def pair(self, k, unit):
        side = unit // 2
        blk = side * self.p.blk + (1 - side) * (1 - self.p.blk)
        return self.p.column(k) * 4 + blk * 2 + unit % 2

    def load(self, k, unit, slot):
        at = pl.ds(pl.multiple_of(self.pair(k, unit) * self.per, self.per), self.per)
        return pltpu.make_async_copy(self.source.at[:, at], self.rows.at[slot], self.sems.at[slot])

    def column(self, k):
        flow = self.flow
        if k < 2:

            @pl.loop(0, 4)
            def _(s):
                flow.core(k + 2, s).wait_send()

        @pl.loop(0, 4)
        def _(unit):
            slot = unit % 2

            @pl.when(unit < 3)
            def _():
                self.load(k, unit + 1, 1 - slot).start()

            if k:

                @pl.when(unit == 3)
                def _():
                    self.load(k - 1, 0, 1 - slot).start()

            self.load(k, unit, slot).wait()
            pair = self.pair(k, unit)
            places = self.places[pair]
            rows = jnp.concatenate([self.rows[slot, e] for e in range(self.experts)], axis=0)
            summed = inner(one_hot(places, self.per), rows, 0, 0).astype(self.rows.dtype)
            summed = summed.reshape(2, summed.shape[0] // 2, summed.shape[1])
            blocks = pl.ds(2 * (unit % 2), 2)

            @pl.when(unit < 2)
            def _():
                flow.stage[k % 2, blocks] = summed

            @pl.when(unit >= 2)
            def _():
                flow.acc[k, blocks] = summed

            at = pl.ds(pl.multiple_of(pair * self.per, self.per), self.per)
            half = places.shape[1] // 2
            for e in range(self.experts):
                hot = is_place(places[e : e + 1], self.per)
                line = jnp.sum(jnp.where(hot, self.row_grads[e, at], 0.0), axis=0, keepdims=True)
                self.deals[2 * pair, e : e + 1] = line[:, :half]
                self.deals[2 * pair + 1, e : e + 1] = line[:, half:]

            @pl.when(unit == 1)
            def _():
                for s in range(4):
                    flow.core(k, s).start()


class OutputWork:
    def __init__(self, places, hidden, weight, out, scratch):
        self.places, self.hidden, self.weight, self.out = places, hidden, weight, out
        self.rows, self.held, self.narrow, self.block, self.in_sems, self.out_sems = scratch
        self.experts, self.slots, _ = hidden.shape
        self.pairs = out.shape[0]
        self.per = self.slots // self.pairs
        self.width = weight.shape[2]
        self.units = 2 * self.experts + self.pairs

    @staticmethod
    def scratch(hidden, weight, out):
        experts, slots, narrow = hidden.shape
        return [
            pltpu.VMEM((experts, slots, weight.shape[2]), weight.dtype),
            pltpu.VMEM((2,) + weight.shape[1:], weight.dtype),
            pltpu.VMEM((2, slots, narrow), hidden.dtype),
            pltpu.VMEM((2,) + out.shape[1:], out.dtype),
            pltpu.SemaphoreType.DMA((2, 2)),
            pltpu.SemaphoreType.DMA((2,)),
        ]

    def loads(self, e):
        slot = e % 2
        return [
            pltpu.make_async_copy(self.weight.at[e], self.held.at[slot], self.in_sems.at[slot, 0]),
            pltpu.make_async_copy(self.hidden.at[e], self.narrow.at[slot], self.in_sems.at[slot, 1]),
        ]

    def store(self, pair):
        return pltpu.make_async_copy(self.block.at[pair % 2], self.out.at[pair], self.out_sems.at[pair % 2])

    def begin(self):
        for copy in self.loads(0):
            copy.start()

    def run(self, unit):
        half = self.width // 2

        @pl.when(unit < 2 * self.experts)
        def _():
            e, side = unit // 2, unit % 2

            @pl.when(side == 0)
            def _():
                @pl.when(e + 1 < self.experts)
                def _():
                    for copy in self.loads(e + 1):
                        copy.start()

                for copy in self.loads(e):
                    copy.wait()

            at = pl.ds(pl.multiple_of(side * half, half), half)
            self.rows[e, :, at] = inner(self.narrow[e % 2], self.held[e % 2, :, at]).astype(self.rows.dtype)

        @pl.when(unit >= 2 * self.experts)
        def _():
            pair = unit - 2 * self.experts

            @pl.when(pair >= 2)
            def _():
                self.store(pair - 2).wait()

            at = pl.ds(pl.multiple_of(pair * self.per, self.per), self.per)
            rows = jnp.concatenate([self.rows[e, at] for e in range(self.experts)], axis=0)
            self.block[pair % 2] = inner(one_hot(self.places[pair], self.per), rows, 0, 0).astype(self.block.dtype)
            self.store(pair).start()

    def finish(self):
        for pair in (self.pairs - 2, self.pairs - 1):
            self.store(pair).wait()


def expert_weight_grads(rows, grads, weighted, gate_back, up_back):
    experts, slots, width = rows.shape
    hidden = weighted.shape[2]
    parts = 2
    part = width // parts

    def kernel(x, c, low, gate, up, gate_out, up_out, down_out):
        gate_out[0] = inner(x[0], gate[0], 0, 0)
        up_out[0] = inner(x[0], up[0], 0, 0)
        down_out[0] = inner(low[0], c[0], 0, 0)

    source = pl.BlockSpec((1, slots, part), lambda e, i: (e, 0, i))
    whole = pl.BlockSpec((1, slots, hidden), lambda e, i: (e, 0, 0))
    tall = pl.BlockSpec((1, part, hidden), lambda e, i: (e, i, 0))
    flat = pl.BlockSpec((1, hidden, part), lambda e, i: (e, 0, i))
    return pl.pallas_call(
        kernel,
        out_shape=[
            jax.ShapeDtypeStruct((experts, width, hidden), jnp.float32),
            jax.ShapeDtypeStruct((experts, width, hidden), jnp.float32),
            jax.ShapeDtypeStruct((experts, hidden, width), jnp.float32),
        ],
        grid=(experts, parts),
        in_specs=[source, source, whole, whole, whole],
        out_specs=[tall, tall, flat],
        compiler_params=local_params(),
        cost_estimate=pl.CostEstimate(
            flops=6 * experts * slots * width * hidden, bytes_accessed=24 * experts * width * hidden, transcendentals=0
        ),
        name="expert_weight_grads",
    )(rows, grads, weighted, gate_back, up_back)


class ColumnsFlow:
    SENDS = 24 + 1 + 16
    RECVS = 24 + 1 + 16
    LOCALS = 4

    def __init__(self, place, sources, rows_in, wide, tall, send, recv, local):
        self.p, self.sources, self.rows_in, self.wide, self.tall = place, sources, rows_in, wide, tall
        self.send, self.recv, self.local = send, recv, local
        self.rows = rows_in.shape[0]
        self.share = wide.shape[1] // len(sources)

    def spot(self, i, col):
        rows = pl.ds(pl.multiple_of((self.p.dp * 8 + col) * self.rows, self.rows), self.rows)
        return self.wide.at[rows, pl.ds(i * self.share, self.share)]

    def piece(self, i, to):
        return self.sources[i].at[:, pl.ds(pl.multiple_of(to * self.share, self.share), self.share)]

    def scatter(self, step, i):
        to = (self.p.col + step) % 8
        return remote(
            self.piece(i, to),
            self.spot(i, self.p.col),
            self.send.at[3 * step + i],
            self.recv.at[3 * self.p.col + i],
            (self.p.dp, to // 4, to % 4),
        )

    def keep(self, i):
        return pltpu.make_async_copy(self.piece(i, self.p.col), self.spot(i, self.p.col), self.local.at[i])

    def tall_rows(self, k):
        return self.tall.at[pl.ds(pl.multiple_of(self.p.column(k) * self.rows, self.rows), self.rows)]

    def swap(self):
        group = self.p.dp * 2 + self.p.blk
        dst = self.tall.at[pl.ds(pl.multiple_of(self.p.z * self.rows, self.rows), self.rows)]
        return remote(
            self.rows_in, dst, self.send.at[24], self.recv.at[24], (self.p.z, group // 4, group % 4)
        )

    def stay(self):
        return pltpu.make_async_copy(self.rows_in, self.tall_rows(0), self.local.at[3])

    def at_home(self):
        group = self.p.dp * 2 + self.p.blk
        return (self.p.z == self.p.dp) & (group == self.p.col)

    def band(self, i, k, first=0, parts=1):
        if i == 3:
            height, ref = self.rows, self.tall
        else:
            height, ref = 8 * self.rows, self.wide
        part = height // parts
        rows = pl.ds(pl.multiple_of(self.p.column(k) * height + first * part, part), part)
        return ref.at[rows] if i == 3 else ref.at[rows, pl.ds(i * self.share, self.share)]

    def across(self, i, k):
        ref = self.band(i, 0)
        slot = 25 + 4 * i + k - 1
        return remote(ref, ref, self.send.at[slot], self.recv.at[slot], self.p.at(k))

    def turn(self, i, k):
        ref = self.band(i, k, k - 1, 2)
        slot = 25 + 4 * i + 1 + k
        return remote(ref, ref, self.send.at[slot], self.recv.at[slot], self.p.at(3 - k))

    def got(self, sem, ref):
        remote(ref, ref, self.send.at[0], self.recv.at[sem], self.p.at(0, 1 - self.p.blk)).wait_recv()

    def begin(self):
        home = self.at_home()

        @pl.when(home)
        def _():
            self.stay().start()

        @pl.when(jnp.logical_not(home))
        def _():
            self.swap().start()

        for i in range(3):

            @pl.loop(1, 8)
            def _(step):
                self.scatter(step, i).start()

            self.keep(i).start()

    def settle(self, i):
        if i == 3:
            home = self.at_home()

            @pl.when(home)
            def _():
                self.stay().wait()

            @pl.when(jnp.logical_not(home))
            def _():
                self.got(24, self.tall_rows(0))

        else:
            self.keep(i).wait()

            @pl.loop(1, 8)
            def _(step):
                col = (self.p.col + step) % 8
                self.got(3 * col + i, self.spot(i, col))

        self.across(i, 1).start()
        self.across(i, 2).start()

    def turns(self, i):
        for k in (1, 2):
            self.got(25 + 4 * i + k - 1, self.band(i, k))
            self.turn(i, k).start()

    def finish(self):
        for i in (3, 0, 1, 2):
            for k in (1, 2):
                self.got(25 + 4 * i + 1 + k, self.band(i, 3, k - 1, 2))
                self.turn(i, k).wait_send()
                self.across(i, k).wait_send()

        @pl.when(jnp.logical_not(self.at_home()))
        def _():
            self.swap().wait_send()

        @pl.loop(1, 8)
        def _(step):
            for i in range(3):
                self.scatter(step, i).wait_send()


class SumsFlow:
    SENDS = 12 + 24 + 1
    RECVS = 12 + 16 + 1
    LOCALS = 4

    def __init__(self, place, wide_out, tall_out, scratch):
        self.p = place
        self.wide_out, self.tall_out = wide_out, tall_out
        self.acc, self.half_in, self.side_in = scratch[0:3], scratch[3:6], scratch[6:9]
        self.send, self.recv, self.local = scratch[9:12]
        self.rows = tall_out.shape[0]
        self.share = wide_out.shape[2] // 8

    @staticmethod
    def scratch(arrays):
        shapes = []
        for kind in ((4, 1), (2, 2), (2, 1)):
            for rows, width in arrays:
                shapes.append(pltpu.VMEM((kind[0], rows // kind[1], width), jnp.bfloat16))
        return shapes + [
            pltpu.SemaphoreType.DMA((SumsFlow.SENDS,)),
            pltpu.SemaphoreType.DMA((SumsFlow.RECVS,)),
            pltpu.SemaphoreType.DMA((SumsFlow.LOCALS,)),
        ]

    def halves(self, ref):
        half = ref.shape[0] // 2
        return ref.at[pl.ds(0, half)], ref.at[pl.ds(half, half)]

    def corner(self, which, k):
        src = self.halves(self.acc[which].at[3])[k - 1]
        slot = 4 * which + k - 1
        return remote(src, self.half_in[which].at[k - 1], self.send.at[slot], self.recv.at[slot], self.p.at(k))

    def side(self, which, k):
        slot = 4 * which + 1 + k
        return remote(
            self.acc[which].at[k], self.side_in[which].at[k - 1], self.send.at[slot], self.recv.at[slot], self.p.at(k)
        )

    def piece(self, to, i):
        rows = pl.ds(pl.multiple_of(to * self.rows, self.rows), self.rows)
        dst = self.wide_out.at[i, :, pl.ds(pl.multiple_of(self.p.col * self.share, self.share), self.share)]
        if i == 2:
            return self.acc[2].at[0, rows], dst
        return self.acc[0].at[0, rows, pl.ds(i * self.share, self.share)], dst

    def deal(self, step, i):
        to = (self.p.col + step) % 8
        src, dst = self.piece(to, i)
        return remote(
            src,
            dst,
            self.send.at[12 + 3 * step + i],
            self.recv.at[12 + 8 * (i // 2) + self.p.col],
            (self.p.dp, to // 4, to % 4),
        )

    def keep(self, i):
        src, dst = self.piece(self.p.col, i)
        return pltpu.make_async_copy(src, dst, self.local.at[i])

    def swap(self):
        return remote(
            self.acc[1].at[0],
            self.tall_out,
            self.send.at[36],
            self.recv.at[28],
            (self.p.col // 2, self.p.col % 2, self.p.dp),
        )

    def stay(self):
        return pltpu.make_async_copy(self.acc[1].at[0], self.tall_out, self.local.at[3])

    def at_home(self):
        return (self.p.col // 2 == self.p.dp) & (self.p.col % 2 == self.p.blk) & (self.p.z == self.p.dp)

    def corners(self, which):
        self.corner(which, 1).start()
        self.corner(which, 2).start()

    def sides(self, which):
        for k, other in ((2, 1), (1, 2)):
            self.corner(which, other).wait_recv()
            target = self.halves(self.acc[which].at[k])[other - 1]
            add_rows(target, [target, self.half_in[which].at[other - 1]], target.shape[0])
            self.side(which, k).start()

    def total(self, which):
        self.side(which, 1).wait_recv()
        self.side(which, 2).wait_recv()
        mine = self.acc[which].at[0]
        add_rows(mine, [mine, self.side_in[which].at[0], self.side_in[which].at[1]], mine.shape[0])

    def hand_out_tall(self):
        home = self.at_home()

        @pl.when(home)
        def _():
            self.stay().start()

        @pl.when(jnp.logical_not(home))
        def _():
            self.swap().start()

    def hand_out(self, weights):
        @pl.loop(1, 8)
        def _(step):
            for i in weights:
                self.deal(step, i).start()

        for i in weights:
            self.keep(i).start()

    def finish(self):
        home = self.at_home()

        @pl.when(home)
        def _():
            self.stay().wait()

        @pl.when(jnp.logical_not(home))
        def _():
            self.swap().wait()

        for i in range(3):
            self.keep(i).wait()

        @pl.loop(1, 8)
        def _(step):
            col = (self.p.col + step) % 8
            for which, landed in (
                (0, self.acc[0].at[0, pl.ds(0, self.rows)]),
                (1, self.acc[2].at[0, pl.ds(0, self.rows)]),
            ):
                remote(
                    landed,
                    landed,
                    self.send.at[0],
                    self.recv.at[12 + 8 * which + col],
                    self.p.at(0, 1 - self.p.blk),
                ).wait_recv()
            for i in range(3):
                self.deal(step, i).wait_send()

        for which in (1, 2, 0):
            for k in (1, 2):
                self.corner(which, k).wait_send()
                self.side(which, k).wait_send()


class DealFlow:
    def __init__(self, place, src, out, send, recv, local):
        self.p, self.src, self.out, self.send, self.recv, self.local = place, src, out, send, recv, local
        self.me = (place.dp * 2 + place.blk) * 4 + place.z

    def copy(self, step):
        to = (self.me + step) % 32
        return remote(
            self.src.at[to], self.out.at[self.me], self.send.at[step], self.recv.at[self.me], (to // 8, (to // 4) % 2, to % 4)
        )

    def keep(self):
        return pltpu.make_async_copy(self.src.at[self.me], self.out.at[self.me], self.local.at[0])

    def begin(self):
        self.keep().start()

        @pl.loop(1, 32)
        def _(step):
            self.copy(step).start()

    def finish(self):
        self.keep().wait()

        @pl.loop(1, 32)
        def _(step):
            landed = self.out.at[(self.me + step) % 32]
            remote(
                landed,
                landed,
                self.send.at[0],
                self.recv.at[(self.me + step) % 32],
                self.p.at(0, 1 - self.p.blk),
            ).wait_recv()
            self.copy(step).wait_send()

    @staticmethod
    def scratch():
        return [pltpu.SemaphoreType.DMA((32,)), pltpu.SemaphoreType.DMA((32,)), pltpu.SemaphoreType.DMA((1,))]

    def steps(self, length=18):
        return [self.begin] + [lambda: None] * (length - 2) + [self.finish]


def hbm_call(kernel, shapes, scratch, name, collective_id, args, in_vmem=(), out_vmem=()):
    return pl.pallas_call(
        kernel,
        out_shape=shapes,
        in_specs=[
            pl.BlockSpec(memory_space=pltpu.VMEM if i in in_vmem else pl.ANY) for i in range(len(args))
        ],
        out_specs=[
            pl.BlockSpec(memory_space=pltpu.VMEM if i in out_vmem else pl.ANY) for i in range(len(shapes))
        ],
        scratch_shapes=scratch,
        compiler_params=pltpu.CompilerParams(
            collective_id=collective_id, has_side_effects=True, vmem_limit_bytes=VMEM_BYTES
        ),
        name=name,
    )(*args)


def gather_sems():
    return [pltpu.SemaphoreType.DMA((GatherFlow.SENDS,)), pltpu.SemaphoreType.DMA((GatherFlow.RECVS,))]


def plane_sems(count):
    return gather_sems() + [pltpu.SemaphoreType.DMA((count,))]


def attention_call(
    tokens, small, cotangent, query_weight, key_weight, value_weight, output_weight, cosine, sine, experts
):
    tok_rows, width = tokens.shape
    own_rows = query_weight.shape[0]
    rows = 8 * tok_rows
    share = width // 8
    heads = share // HEAD_DIM
    block = 2 * tok_rows
    blocks = rows // block
    scale = 1.0 / math.sqrt(HEAD_DIM)
    bf16, f32 = jnp.bfloat16, jnp.float32
    line = ScatterFlow.scratch(tok_rows, width, bf16, False)

    def kernel(tok, sml, cot, wq, wk, wv, wo, cos, sin, *refs):
        outs, scratch = refs[:14], refs[14:]
        normed_out, unit_out, row_out, context_out, scale_out, log_out = outs[:6]
        attended, small_out, gathered_out, wide_out, tall_out, gains, place_out, head_out = outs[6:]
        held, wide_ref, tall_ref, normed, unit, qkv, context, part, sums, landed = scratch[:10]
        small_held, hits, normed_t, context_t, stores, send, recv = scratch[10:17]
        rest = list(scratch[17:])

        def take(count):
            taken = rest[:count]
            del rest[:count]
            return taken

        place = Place()
        entry_barrier(place, "all")
        flow = ScatterFlow(place, part, attended, take(len(line)), False)
        params = GatherFlow(place, sml, small_held, *take(2), True, True)
        tokens_in = GatherFlow(place, tok, held, *take(2), False)
        others = GatherFlow(place, cot, gathered_out, *take(2), True, others=True)
        plane = PlaneFlow(place, [(place.z, cot)], gathered_out, *take(3))
        weights = ColumnsFlow(place, (wq, wk, wv), wo, wide_ref, tall_ref, *take(3))
        params.begin()
        weights.begin()
        sums[...] = jnp.zeros_like(sums)
        for d in range(1, 4):
            params.along(d)
        plane.begin()
        for d in range(4):
            params.turn(d)
        weights.settle(3)
        weights.settle(0)
        plane.turns()
        weights.settle(1)
        tokens_in.begin()
        weights.turns(3)
        for d in range(4):
            params.corner(d)
        plane.corners()
        weights.settle(2)
        weights.turns(0)
        tokens_in.along(1)
        weights.turns(1)
        params.finish()
        for to in range(32):
            rows_here = small_held[to, own_rows : own_rows + 16, :own_rows].astype(f32)
            gains[:, to * own_rows : (to + 1) * own_rows] = rows_here[:4]
        tokens_in.along(2)
        weights.turns(2)
        first_expert = (place.dp * 4 + place.z) * experts

        @pl.loop(0, 32)
        def _(d):
            named = small_held[d, own_rows + 16 : own_rows + 32].astype(f32)[:TOPK]
            for e in range(experts):
                matches = jnp.where(named == (first_expert + e).astype(f32), 1.0, 0.0)
                hits[e, pl.ds(d, 1)] = jnp.sum(matches, axis=0, keepdims=True)

        earlier = lax.broadcasted_iota(jnp.int32, (tok_rows, tok_rows), 0)
        earlier = earlier < lax.broadcasted_iota(jnp.int32, (tok_rows, tok_rows), 1)
        earlier = earlier.astype(f32).astype(bf16)
        for e in range(experts):
            hit = hits[e]
            rank = inner(hit.astype(bf16), earlier)
            shift = lax.broadcasted_iota(jnp.int32, hit.shape, 0) % 2 * CAP
            slots = jnp.where(hit > 0.5, rank.astype(jnp.int32) + shift, -1)
            for d in range(32):
                lanes = slice(d % 2 * tok_rows, (d % 2 + 1) * tok_rows)
                place_out[d // 2, e : e + 1, lanes] = slots[d : d + 1]

        tokens_in.along(3)
        plane.finish()
        weights.finish()
        tokens_in.finish()
        others.begin()
        head_gain = gains[1:3, pl.ds(pl.multiple_of(place.col * share, share), share)]
        head_out[...] = head_gain

        @pl.loop(0, blocks)
        def _(i):
            at = pl.ds(pl.multiple_of(i * block, block), block)
            values = held[pl.ds(2 * i, 2)].reshape(block, width).astype(f32)
            mean = jnp.mean(values * values, axis=1, keepdims=True)
            low = (values * lax.rsqrt(mean + NORM_EPSILON) * gains[0:1]).astype(bf16)
            normed[at] = low
            linear = inner(low, wide_ref[...])
            unit[at] = linear[:, : 2 * share]
            qkv[at, 2 * share :] = linear[:, 2 * share :].astype(bf16)
            for n in range(2):
                part_lin = linear[:, n * share : (n + 1) * share]
                sums[n : n + 1, at] = jnp.sum(jnp.transpose(part_lin * part_lin), axis=0, keepdims=True)

        def exchange(step):
            to = (place.col + step) % 8
            return remote(
                sums, landed.at[place.col], send.at[step], recv.at[place.col], (place.dp, to // 4, to % 4)
            )

        @pl.loop(1, 8)
        def _(step):
            exchange(step).start()

        landed[place.col] = sums[...]

        @pl.loop(1, 8)
        def _(step):
            col = (place.col + step) % 8
            remote(sums, landed.at[col], send.at[0], recv.at[col], place.at(0, 1 - place.blk)).wait_recv()
            exchange(step).wait_send()

        total = landed[0]
        for col in range(1, 8):
            total = total + landed[col]
        scales = jnp.transpose(lax.rsqrt(total / width + NORM_EPSILON))
        scale_out[...] = scales

        @pl.loop(0, blocks)
        def _(i):
            at = pl.ds(pl.multiple_of(i * block, block), block)
            for n in range(2):
                for h in range(heads):
                    lanes = pl.ds(n * share + h * HEAD_DIM, HEAD_DIM)
                    mine = unit[at, lanes] * scale_out[at, n : n + 1]
                    unit[at, lanes] = mine
                    scaled = mine * head_gain[n : n + 1, h * HEAD_DIM : (h + 1) * HEAD_DIM]
                    turned = scaled * cos[at] + pltpu.roll(scaled, HEAD_DIM // 2, 1) * sin[at]
                    qkv[at, lanes] = turned.astype(bf16)

        out_copies = [
            pltpu.make_async_copy(src, dst, stores.at[n])
            for n, (src, dst) in enumerate(
                (
                    (unit, unit_out),
                    (qkv, row_out),
                    (wide_ref, wide_out),
                    (tall_ref, tall_out),
                    (small_held, small_out),
                )
            )
        ]
        for copy in out_copies:
            copy.start()
        for h in range(heads):
            for i in range(blocks):
                seen = (i + 1) * block
                queries = qkv[i * block : seen, h * HEAD_DIM : (h + 1) * HEAD_DIM]
                keys = qkv[:seen, share + h * HEAD_DIM : share + (h + 1) * HEAD_DIM]
                values = qkv[:seen, 2 * share + h * HEAD_DIM : 2 * share + (h + 1) * HEAD_DIM]
                scores = inner(queries, keys, 1, 1) * scale
                row = lax.broadcasted_iota(jnp.int32, scores.shape, 0) + i * block
                column = lax.broadcasted_iota(jnp.int32, scores.shape, 1)
                scores = jnp.where(column <= row, scores, MASKED)
                peak = jnp.max(scores, axis=1, keepdims=True)
                exponent = jnp.exp(scores - peak)
                sum_row = jnp.sum(exponent, axis=1, keepdims=True)
                low = (exponent / sum_row).astype(bf16)
                context[i * block : seen, h * HEAD_DIM : (h + 1) * HEAD_DIM] = inner(low, values).astype(bf16)
                log_out[i * block : seen, h : h + 1] = peak + jnp.log(sum_row)
            if h == 0:
                others.along(1)

        @pl.loop(0, blocks)
        def _(i):
            at = pl.ds(pl.multiple_of(i * block, block), block)
            rows_here = inner(context[at], tall_ref[...]).astype(bf16)
            part[pl.ds(2 * i, 2)] = rows_here.reshape(2, tok_rows, width)

        flow.begin()
        others.along(2)
        for i in range(blocks):
            at = slice(i * block, (i + 1) * block)
            normed_t[:, at] = jnp.transpose(normed[at])
            context_t[:, at] = jnp.transpose(context[at])
        last = [
            pltpu.make_async_copy(normed_t, normed_out, stores.at[5]),
            pltpu.make_async_copy(context_t, context_out, stores.at[6]),
        ]
        for copy in last:
            copy.start()
        flow.stage3(0)
        flow.stage3(1)
        flow.chain(0)
        others.along(3)
        others.turn(1)
        flow.stage3(2)
        flow.chain(1)
        flow.chain(2)
        others.turn(2)
        others.corner(1)
        flow.stage3(3)
        flow.final()
        others.turn(3)
        others.corner(2)
        others.corner(3)
        others.finish()
        for copy in out_copies + last:
            copy.wait()

    shapes = [
        jax.ShapeDtypeStruct((width, rows), bf16),
        jax.ShapeDtypeStruct((rows, 2 * share), f32),
        jax.ShapeDtypeStruct((rows, 3 * share), bf16),
        jax.ShapeDtypeStruct((share, rows), bf16),
        jax.ShapeDtypeStruct((rows, 8), f32),
        jax.ShapeDtypeStruct((rows, 8), f32),
        jax.ShapeDtypeStruct((tok_rows, width), f32),
        jax.ShapeDtypeStruct((32,) + small.shape, bf16),
        jax.ShapeDtypeStruct((32,) + cotangent.shape, bf16),
        jax.ShapeDtypeStruct((width, 3 * share), bf16),
        jax.ShapeDtypeStruct((share, width), bf16),
        jax.ShapeDtypeStruct((4, width), f32),
        jax.ShapeDtypeStruct((16, experts, 2 * tok_rows), jnp.int32),
        jax.ShapeDtypeStruct((2, share), f32),
    ]
    scratch = [
        pltpu.VMEM((8, tok_rows, width), bf16),
        pltpu.VMEM((width, 3 * share), bf16),
        pltpu.VMEM((share, width), bf16),
        pltpu.VMEM((rows, width), bf16),
        pltpu.VMEM((rows, 2 * share), f32),
        pltpu.VMEM((rows, 3 * share), bf16),
        pltpu.VMEM((rows, share), bf16),
        pltpu.VMEM((8, tok_rows, width), bf16),
        pltpu.VMEM((8, rows), f32),
        pltpu.VMEM((8, 8, rows), f32),
        pltpu.VMEM((32,) + small.shape, bf16),
        pltpu.VMEM((experts, 32, tok_rows), f32),
        pltpu.VMEM((width, rows), bf16),
        pltpu.VMEM((share, rows), bf16),
        pltpu.SemaphoreType.DMA((7,)),
        pltpu.SemaphoreType.DMA((8,)),
        pltpu.SemaphoreType.DMA((8,)),
    ]
    scratch += line + gather_sems() * 3 + plane_sems(1)
    scratch += [
        pltpu.SemaphoreType.DMA((ColumnsFlow.SENDS,)),
        pltpu.SemaphoreType.DMA((ColumnsFlow.RECVS,)),
        pltpu.SemaphoreType.DMA((ColumnsFlow.LOCALS,)),
    ]
    args = (tokens, small, cotangent, query_weight, key_weight, value_weight, output_weight, cosine, sine)
    return hbm_call(kernel, shapes, scratch, "attention", 5, args, (7, 8), (4, 5, 11, 12, 13))


def run_units(work, first, last):
    @pl.loop(first, last)
    def _(unit):
        work.run(unit)


def features_call(features, probs, places, cotangent_all, down_weight, per):
    experts, hidden, width = down_weight.shape
    slots = places.shape[0] * per

    def kernel(feature_ref, prob_ref, place_ref, cot, weight, feature_out, prob_out, rows, plain, *scratch):
        place = Place()
        entry_barrier(place, "planes")
        small = GatherFlow(place, prob_ref, prob_out, scratch[2], scratch[3], True)
        flow = GatherFlow(place, feature_ref, feature_out, scratch[0], scratch[1], True)
        work = PickWork(place_ref, cot, weight, rows, plain, scratch[4:])

        flows = (small, flow)

        def along(d):
            for each in flows:
                each.along(d)

        def turn(d):
            for each in flows:
                each.turn(d)

        def corner(d):
            for each in flows:
                each.corner(d)

        for each in flows:
            each.begin()
        work.begin()
        run_units(work, 0, 4)
        along(1)
        turn(0)
        run_units(work, 4, 9)
        along(2)
        corner(0)
        run_units(work, 9, 13)
        along(3)
        turn(1)
        run_units(work, 13, work.units)
        corner(1)
        turn(2)
        corner(2)
        turn(3)
        corner(3)
        for each in flows:
            each.finish()
        work.finish()

    shapes = [
        jax.ShapeDtypeStruct((32,) + features.shape, features.dtype),
        jax.ShapeDtypeStruct((32,) + probs.shape, probs.dtype),
        jax.ShapeDtypeStruct((experts, slots, width), features.dtype),
        jax.ShapeDtypeStruct((experts, slots, hidden), jnp.float32),
    ]
    scratch = gather_sems() * 2 + PickWork.scratch(cotangent_all, down_weight, per)
    return hbm_call(
        kernel, shapes, scratch, "features", 6, (features, probs, places, cotangent_all, down_weight), (2,)
    )


def experts_back_call(input_rows, row_grads, places, hidden, weight, tok_rows):
    width = input_rows.shape[2]
    pairs, experts, pair_rows = places.shape
    per = input_rows.shape[1] // pairs
    sums = ScatterFlow.scratch(tok_rows, width, input_rows.dtype, True)
    out_shape = jax.ShapeDtypeStruct((pairs, pair_rows, width), input_rows.dtype)
    dealt = jax.ShapeDtypeStruct((2 * pairs, 8, tok_rows), jnp.float32)
    put_scratch = PutWork.scratch(input_rows, per)

    def kernel(source, grad_ref, place_ref, hidden_ref, weight_ref, out, dealt_out, mixed, *scratch):
        place = Place()
        entry_barrier(place, "all")
        stage, deals = scratch[:2]
        rest = scratch[2 + len(put_scratch) + 3 :]
        deal = DealFlow(place, deals, dealt_out, *scratch[2 + len(put_scratch) :][:3])
        flow = MadeFlow(place, out, rest[: len(sums)], stage)
        put = PutWork(place, place_ref, source, grad_ref, flow, deals, scratch[2 : 2 + len(put_scratch)])
        work = OutputWork(place_ref, hidden_ref, weight_ref, mixed, rest[len(sums) :])
        put.load(3, 0, 0).start()
        work.begin()
        deals[...] = jnp.zeros_like(deals)
        put.column(3)
        put.column(2)
        for i in range(4):
            flow.stage1(i)
        put.column(1)
        put.column(0)
        deal.begin()
        flow.stage2(0)
        flow.stage2(1)
        run_units(work, 0, 8)
        flow.stage2(2)
        flow.stage2(3)
        run_units(work, 8, 16)
        flow.stage3(0)
        flow.stage3(1)
        flow.chain(0)
        run_units(work, 16, 20)
        flow.stage3(2)
        flow.chain(1)
        flow.chain(2)
        run_units(work, 20, work.units)
        flow.stage3(3)
        flow.final()
        work.finish()
        deal.finish()

    shapes = [jax.ShapeDtypeStruct((tok_rows, width), jnp.float32), dealt, out_shape]
    scratch = [
        pltpu.VMEM((2, 4, tok_rows, width), input_rows.dtype),
        pltpu.VMEM(dealt.shape, jnp.float32),
    ]
    scratch += put_scratch + DealFlow.scratch() + sums + OutputWork.scratch(hidden, weight, out_shape)
    return hbm_call(
        kernel, shapes, scratch, "experts_back", 3, (input_rows, row_grads, places, hidden, weight), (1, 2)
    )


def attention_back_call(
    grad, logit_grad, out_part, tokens, gain, feature_row, wide, tall, head_gains, cosine, sine, kept
):
    tok_rows, width = grad.shape
    rows = kept[0].shape[1]
    share = tall.shape[0]
    heads = share // HEAD_DIM
    own_rows = width // 32
    block = 2 * tok_rows
    blocks = rows // block
    band_rows = width // 4
    height = tok_rows // 2
    scale = 1.0 / math.sqrt(HEAD_DIM)
    bf16, f32 = jnp.bfloat16, jnp.float32
    line = ScatterFlow.scratch(tok_rows, width, bf16, False)
    mixed = ScatterFlow.scratch(height, width, bf16, True)
    sums = SumsFlow.scratch(((band_rows, 2 * share), (share // 4, width), (band_rows, share)))
    flow_scratch = line + mixed + mixed[-5:] + sums + DealFlow.scratch() + gather_sems() * 2
    flow_scratch += [pltpu.SemaphoreType.REGULAR]

    def kernel(*refs):
        grad_ref, logit_ref, part_ref, tok_in, gain_ref, feature_ref, wide_in, tall_in = refs[:8]
        head_gain, cos, sin, normed_in, unit_in, qkv_in, context_in, scale_ref, log_ref = refs[8:17]
        logit_out, first_out, second_out, normed_grad, wide_out, tall_out, gain_out = refs[17:24]
        scratch = refs[24:]
        grads, tok, wide_ref, tall_ref, normed, unit, qkv, context, context_grad = scratch[:9]
        grad_q, grad_k, grad_v, low_grads, dots, landed, deals, dealt, tall_grad = scratch[9:18]
        ins, send, recv = scratch[18:21]
        rest = list(scratch[21:])

        def take(count):
            taken = rest[:count]
            del rest[:count]
            return taken

        place = Place()
        entry_barrier(place, "all")
        line_scratch, mixed_scratch, more = take(len(line)), take(len(mixed)), take(5)
        weights = SumsFlow(place, wide_out, tall_out, take(len(sums)))
        deal = DealFlow(place, deals, dealt, *take(3))
        gather = GatherFlow(place, grad_ref, grads, *take(2), False)
        logits = GatherFlow(place, logit_ref, logit_out, *take(2), True)
        freed = take(1)[0]
        flow = ScatterFlow(place, grads, normed_grad, line_scratch, False)
        first = ScatterFlow(place, part_ref, first_out, mixed_scratch, True, (0, height))
        second = ScatterFlow(
            place, part_ref, second_out, mixed_scratch[:-5] + more, True, (height, height)
        )
        gather.begin()
        logits.begin()
        first.begin()
        sources = (tok_in, wide_in, tall_in, normed_in, unit_in, qkv_in, context_in)
        held = (tok, wide_ref, tall_ref, normed, unit, qkv, context)
        loads = [pltpu.make_async_copy(s, d, ins.at[n]) for n, (s, d) in enumerate(zip(sources, held))]
        for copy in loads:
            copy.start()
        deals[...] = jnp.zeros_like(deals)
        dots[...] = jnp.zeros_like(dots)
        first.stage1(0)
        first.stage1(1)
        gather.along(1)
        logits.along(1)
        logits.turn(0)
        first.stage1(2)
        first.stage1(3)
        first.stage2(0)
        gather.along(2)
        logits.along(2)
        logits.turn(1)
        first.stage2(1)
        first.stage2(2)
        gather.along(3)
        logits.along(3)
        logits.turn(2)
        logits.turn(3)
        first.stage3(0)
        first.stage2(3)
        first.stage3(1)
        first.chain(0)
        for d in range(4):
            logits.corner(d)
        gather.finish()
        for copy in loads:
            copy.wait()
        first.stage3(2)
        first.chain(1)
        first.stage3(3)
        tell_partners(place, freed)

        @pl.loop(0, blocks)
        def _(i):
            at = pl.ds(pl.multiple_of(i * block, block), block)
            values = grads[pl.ds(2 * i, 2)].reshape(block, width)
            context_grad[at] = inner(values, tall_ref[...], 1, 1).astype(bf16)

        wait_partners(place, freed)
        first.leave_all()
        second.begin((3, 2, 1))
        first.chain(2)

        @pl.loop(0, 4)
        def _(i):
            lanes = pl.ds(pl.multiple_of(i * band_rows, band_rows), band_rows)
            values = grads[:, :, lanes].reshape(rows, band_rows)
            tall_grad[:, lanes] = inner(context[...], values).astype(bf16)

        for k in range(4):
            at = pl.ds(pl.multiple_of(place.column(k) * own_rows, own_rows), own_rows)
            weights.acc[1][k] = tall_grad[at]
        weights.corners(1)
        first.final()
        second.begin((0,))

        def back_block(h, i):
            seen = (i + 1) * block
            here, lanes = slice(i * block, seen), slice(h * HEAD_DIM, (h + 1) * HEAD_DIM)
            queries = qkv[here, lanes]
            keys = qkv[:seen, share + h * HEAD_DIM : share + (h + 1) * HEAD_DIM]
            values = qkv[:seen, 2 * share + h * HEAD_DIM : 2 * share + (h + 1) * HEAD_DIM]
            outer = context_grad[here, lanes]
            scores = inner(queries, keys, 1, 1) * scale
            row = lax.broadcasted_iota(jnp.int32, scores.shape, 0) + i * block
            column = lax.broadcasted_iota(jnp.int32, scores.shape, 1)
            probs = jnp.where(column <= row, jnp.exp(scores - log_ref[here, h : h + 1]), 0.0)
            prob_dots = inner(outer, values, 1, 1)
            delta = jnp.sum(probs * prob_dots, axis=1, keepdims=True)
            score_grad = (probs * (prob_dots - delta)).astype(bf16)
            grad_q[here, lanes] = inner(score_grad, keys) * scale
            key_part = inner(score_grad, queries, 0, 0) * scale
            value_part = inner(probs.astype(bf16), outer, 0, 0)
            if i == blocks - 1:
                grad_k[:, lanes] = key_part
                grad_v[:, lanes] = value_part
            else:
                grad_k[:seen, lanes] += key_part
                grad_v[:seen, lanes] += value_part

        back_block(0, 3)
        back_block(0, 2)
        second.stage1(0)
        second.stage1(1)
        back_block(0, 1)
        back_block(0, 0)
        second.stage1(2)
        second.stage1(3)
        back_block(1, 3)
        back_block(1, 2)
        weights.sides(1)
        second.stage2(0)
        back_block(1, 1)
        back_block(1, 0)
        low_grads[:, 2 * share :] = grad_v[...].astype(bf16)

        def band_grad(which, k):
            band = pl.ds(pl.multiple_of(place.column(k) * band_rows, band_rows), band_rows)
            lanes = slice(2 * share, 3 * share) if which == 2 else slice(0, 2 * share)
            weights.acc[which][k] = inner(normed[band], low_grads[:, lanes]).astype(bf16)

        for k in (3, 2, 1, 0):
            band_grad(2, k)

        second.stage2(1)

        @pl.loop(0, blocks)
        def _(i):
            at = pl.ds(pl.multiple_of(i * block, block), block)
            for n, grad_n in enumerate((grad_q, grad_k)):
                total = jnp.zeros((block, 1), f32)
                for h in range(heads):
                    lanes = slice(h * HEAD_DIM, (h + 1) * HEAD_DIM)
                    turned = grad_n[at, lanes].astype(bf16).astype(f32)
                    back = turned * cos[at] - pltpu.roll(turned, HEAD_DIM // 2, 1) * sin[at]
                    mine = unit[at, n * share + h * HEAD_DIM : n * share + (h + 1) * HEAD_DIM]
                    for j in range(HEAD_DIM // own_rows):
                        to = place.col * 4 + h * (HEAD_DIM // own_rows) + j
                        columns = slice(j * own_rows, (j + 1) * own_rows)
                        deals[to, 1 + n : 2 + n, :own_rows] += jnp.sum(
                            (back * mine)[:, columns], axis=0, keepdims=True
                        )
                    weighted = back * head_gain[n : n + 1, lanes]
                    grad_n[at, lanes] = weighted
                    total += jnp.sum(weighted * mine, axis=1, keepdims=True)
                dots[n : n + 1, at] = jnp.transpose(jnp.broadcast_to(total, (block, 128)))[:1]

        def exchange(step):
            to = (place.col + step) % 8
            return remote(
                dots, landed.at[place.col], send.at[step], recv.at[place.col], (place.dp, to // 4, to % 4)
            )

        @pl.loop(1, 8)
        def _(step):
            exchange(step).start()

        landed[place.col] = dots[...]

        @pl.loop(1, 8)
        def _(step):
            col = (place.col + step) % 8
            remote(dots, landed.at[col], send.at[0], recv.at[col], place.at(0, 1 - place.blk)).wait_recv()
            exchange(step).wait_send()

        total_dots = landed[0]
        for col in range(1, 8):
            total_dots = total_dots + landed[col]
        columns = jnp.transpose(total_dots / width)
        for n, grad_n in enumerate((grad_q, grad_k)):
            mine = unit[:, n * share : (n + 1) * share]
            low = scale_ref[:, n : n + 1] * (grad_n[...] - mine * columns[:, n : n + 1])
            low_grads[:, n * share : (n + 1) * share] = low.astype(bf16)

        weights.corners(2)
        band_grad(0, 3)
        weights.corners(0)

        @pl.loop(0, blocks)
        def _(i):
            at = pl.ds(pl.multiple_of(i * block, block), block)
            values = inner(low_grads[at], wide_ref[...], 1, 1).astype(bf16)
            grads[pl.ds(2 * i, 2)] = values.reshape(2, tok_rows, width)

        flow.begin()
        weights.sides(2)
        band_grad(0, 2)
        band_grad(0, 1)
        flow.stage3(0)
        weights.sides(0)
        flow.stage3(1)
        band_grad(0, 0)
        second.stage2(2)
        flow.chain(0)
        weights.total(2)
        weights.hand_out((2,))
        second.stage2(3)
        flow.stage3(2)
        flow.chain(1)
        weights.total(0)
        weights.hand_out((0, 1))
        second.stage3(0)
        second.stage3(1)
        flow.chain(2)
        flow.stage3(3)
        second.chain(0)
        second.stage3(2)
        second.chain(1)
        second.chain(2)
        weights.total(1)
        weights.hand_out_tall()
        flow.final()

        values = tok[...].astype(f32)
        scaled = values * lax.rsqrt(jnp.mean(values * values, axis=1, keepdims=True) + NORM_EPSILON)
        attention_row = jnp.sum(scaled * flow.sum[...], axis=0, keepdims=True)
        for to in range(32):
            lanes = slice(to * own_rows, (to + 1) * own_rows)
            deals[to, 0:1, :own_rows] = attention_row[:, lanes]
            deals[to, 3:4, :own_rows] = feature_ref[:, lanes]
        deal.begin()
        second.stage3(3)
        second.final()
        logits.finish()
        weights.finish()
        deal.finish()
        total = dealt[0]
        for index in range(1, 32):
            total = total + dealt[index]
        gain_out[...] = total

    shapes = [
        jax.ShapeDtypeStruct((32,) + logit_grad.shape, logit_grad.dtype),
        jax.ShapeDtypeStruct((height, width), f32),
        jax.ShapeDtypeStruct((height, width), f32),
        jax.ShapeDtypeStruct((tok_rows, width), f32),
        jax.ShapeDtypeStruct((3, own_rows, width), bf16),
        jax.ShapeDtypeStruct((own_rows, width), bf16),
        jax.ShapeDtypeStruct((8, 128), f32),
    ]
    scratch = [
        pltpu.VMEM((8, tok_rows, width), bf16),
        pltpu.VMEM((tok_rows, width), bf16),
        pltpu.VMEM(wide.shape, bf16),
        pltpu.VMEM(tall.shape, bf16),
        pltpu.VMEM((width, rows), bf16),
        pltpu.VMEM((rows, 2 * share), f32),
        pltpu.VMEM((rows, 3 * share), bf16),
        pltpu.VMEM((share, rows), bf16),
        pltpu.VMEM((rows, share), bf16),
        pltpu.VMEM((rows, share), f32),
        pltpu.VMEM((rows, share), f32),
        pltpu.VMEM((rows, share), f32),
        pltpu.VMEM((rows, 3 * share), bf16),
        pltpu.VMEM((8, rows), f32),
        pltpu.VMEM((8, 8, rows), f32),
        pltpu.VMEM((32, 8, 128), f32),
        pltpu.VMEM((32, 8, 128), f32),
        pltpu.VMEM(tall.shape, bf16),
        pltpu.SemaphoreType.DMA((7,)),
        pltpu.SemaphoreType.DMA((8,)),
        pltpu.SemaphoreType.DMA((8,)),
    ]
    args = (grad, logit_grad, out_part, tokens, gain, feature_row, wide, tall, head_gains, cosine, sine)
    return hbm_call(
        kernel,
        shapes,
        scratch + flow_scratch,
        "attention_back",
        2,
        args + tuple(kept),
        (4, 5, 8, 9, 10, 15, 16),
        (6,),
    )


def turn_tables(count):
    half = HEAD_DIM // 2
    frequencies = np.exp(-math.log(ROPE_BASE) * 2.0 * np.arange(half) / HEAD_DIM).astype(np.float32)
    angles = np.arange(count, dtype=np.float32)[:, None] * frequencies[None, :]
    return np.cos(angles), np.sin(angles)


def product(left, right, sums, batches=((), ()), out=jnp.float32):
    return lax.dot_general(left, right, (sums, batches), preferred_element_type=out)


def body_fast(
    tokens,
    query_weight,
    key_weight,
    value_weight,
    output_weight,
    router_weight,
    attention_gain,
    query_gain,
    key_gain,
    feature_gain,
    gate_weight,
    up_weight,
    down_weight,
    routes,
    cotangent,
):
    tok_rows, model_width = tokens.shape
    column_size = 8
    devices = 32
    share = model_width // column_size
    heads_here = share // HEAD_DIM
    seq_rows = tok_rows * column_size
    experts_here = gate_weight.shape[0]
    own_rows = query_weight.shape[0]
    score_scale = 1.0 / math.sqrt(HEAD_DIM)
    column = lax.axis_index(BLK) * 4 + lax.axis_index(SP)
    f32, bf16 = jnp.float32, jnp.bfloat16

    gains = jnp.stack([attention_gain, query_gain, key_gain, feature_gain])
    small = jnp.concatenate(
        [
            jnp.pad(router_weight, ((0, 0), (0, 128 - EXPERTS))),
            jnp.pad(gains, ((0, 12), (0, 128 - own_rows))),
            jnp.pad(routes.T.astype(bf16), ((0, 16 - TOPK), (0, 0))),
        ],
        axis=0,
    )
    half_cos, half_sin = turn_tables(seq_rows)
    cosine = np.concatenate([half_cos, half_cos], axis=1)
    sine = np.concatenate([-half_sin, half_sin], axis=1)
    (
        *kept,
        attended,
        small_all,
        cotangent_all,
        wide_weight,
        tall_weight,
        gain_all,
        places,
        head_gains,
    ) = attention_call(
        tokens, small, cotangent, query_weight, key_weight, value_weight, output_weight, cosine, sine, experts_here
    )
    router_full = small_all[:, :own_rows, :EXPERTS].reshape(model_width, EXPERTS)
    gain_attention, gain_feature = gain_all[0], gain_all[3]

    tokens_f = tokens.astype(f32)
    residual = tokens_f + attended
    features_f, feature_pull = jax.vjp(norm_apply, residual, gain_feature)
    features = features_f.astype(bf16)
    logits = jnp.dot(features, router_full, preferred_element_type=f32)
    router_probs = jax.nn.softmax(logits, axis=-1)

    first_expert = (lax.axis_index(DP) * 4 + lax.axis_index(SP)) * experts_here
    pairs, pair_rows, per = devices // 2, 2 * tok_rows, 2 * CAP
    cotangent_all = cotangent_all.reshape(pairs, pair_rows, model_width)
    features_all, probs_all, grad_rows, plain_grads = features_call(
        features, router_probs.T, places, cotangent_all, down_weight, per
    )
    probs_here = lax.dynamic_slice_in_dim(probs_all, first_expert, experts_here, axis=1)
    features_all = features_all.reshape(pairs, pair_rows, model_width)
    expert_rows, row_probs = pick_rows(places, probs_here, features_all, per)
    weighted_hidden, gate_grad, up_grad, input_rows, row_grads = run_experts(
        expert_rows, plain_grads, row_probs, gate_weight, up_weight
    )
    input_grad, prob_parts, out_part = experts_back_call(
        input_rows, row_grads, places, weighted_hidden, down_weight, tok_rows
    )
    out_part = out_part.reshape(devices, tok_rows, model_width)

    prob_parts = prob_parts.reshape(4, 2, 4, 8, tok_rows)[:, :, :, :experts_here]
    prob_grad = jnp.sum(prob_parts, axis=1).reshape(EXPERTS, tok_rows).T
    logit_grad = (
        router_probs * (prob_grad - jnp.sum(prob_grad * router_probs, axis=-1, keepdims=True))
    ).astype(bf16)
    feature_grad = jnp.dot(logit_grad, router_full.T, preferred_element_type=f32) + input_grad
    residual_part, feature_gain_grad = feature_pull(feature_grad)
    residual_grad = cotangent.astype(f32) + residual_part
    attended_grad = residual_grad.astype(bf16)
    logit_all, first_half, second_half, normed_grad, wide_back, tall_back, gain_sums = attention_back_call(
        attended_grad,
        logit_grad.reshape(tok_rows // 2, 2 * EXPERTS),
        out_part,
        tokens,
        gain_attention[None],
        feature_gain_grad[None],
        wide_weight,
        tall_weight,
        head_gains,
        cosine,
        sine,
        kept,
    )
    own_index = (lax.axis_index(DP) * 2 + lax.axis_index(BLK)) * 4 + lax.axis_index(SP)
    own_features = lax.dynamic_slice_in_dim(
        features_all.reshape(devices * tok_rows, model_width), own_index * own_rows, own_rows, axis=1
    )
    router_grad = product(own_features, logit_all.reshape(devices * tok_rows, EXPERTS), ((0,), (0,)))

    _, attention_pull = jax.vjp(lambda values: norm_apply(values, gain_attention), tokens_f)
    input_gradient = residual_grad + attention_pull(normed_grad)[0]
    block_output = (residual + jnp.concatenate([first_half, second_half], axis=0)).astype(bf16)
    gate_grad_local, up_grad_local, down_grad_local = expert_weight_grads(
        expert_rows, grad_rows, weighted_hidden, gate_grad, up_grad
    )
    return (
        block_output,
        input_gradient,
        wide_back[0].astype(f32),
        wide_back[1].astype(f32),
        wide_back[2].astype(f32),
        tall_back.astype(f32),
        router_grad,
        gain_sums[0, :own_rows],
        gain_sums[1, :own_rows],
        gain_sums[2, :own_rows],
        gain_sums[3, :own_rows],
        gate_grad_local,
        up_grad_local,
        down_grad_local,
    )


def body(
    tokens,
    query_weight,
    key_weight,
    value_weight,
    output_weight,
    router_weight,
    attention_gain,
    query_gain,
    key_gain,
    feature_gain,
    gate_weight,
    up_weight,
    down_weight,
    routes,
    cotangent,
):
    sp_size = lax.axis_size(SP)
    blk_size = lax.axis_size(BLK)
    dp_size = lax.axis_size(DP)
    tok_rows = tokens.shape[0]
    model_width = tokens.shape[1]
    heads_here = HEADS // sp_size
    head_width = heads_here * HEAD_DIM
    experts_here = gate_weight.shape[0]
    capacity = CAP
    score_scale = 1.0 / math.sqrt(HEAD_DIM)
    (
        query_full,
        key_full,
        value_full,
        output_full,
        router_full,
        gain_attention,
        gain_query,
        gain_key,
        gain_feature,
    ) = (
        lax.all_gather(query_weight, AXES, axis=0, tiled=True),
        lax.all_gather(key_weight, AXES, axis=0, tiled=True),
        lax.all_gather(value_weight, AXES, axis=0, tiled=True),
        lax.all_gather(output_weight, AXES, axis=0, tiled=True),
        lax.all_gather(router_weight, AXES, axis=0, tiled=True),
        lax.all_gather(attention_gain, AXES, axis=0, tiled=True),
        lax.all_gather(query_gain, AXES, axis=0, tiled=True),
        lax.all_gather(key_gain, AXES, axis=0, tiled=True),
        lax.all_gather(feature_gain, AXES, axis=0, tiled=True),
    )
    gain_attention = gain_attention.astype(jnp.float32)
    gain_query = gain_query.astype(jnp.float32)
    gain_key = gain_key.astype(jnp.float32)
    gain_feature = gain_feature.astype(jnp.float32)
    tokens_f = tokens.astype(jnp.float32)
    normed_f, attention_pull = jax.vjp(norm_apply, tokens_f, gain_attention)
    normed = normed_f.astype(jnp.bfloat16)
    query_lin = jnp.dot(normed, query_full, preferred_element_type=jnp.float32)
    key_lin = jnp.dot(normed, key_full, preferred_element_type=jnp.float32)
    value_rows = jnp.dot(normed, value_full, preferred_element_type=jnp.float32).astype(
        jnp.bfloat16
    )
    seq_start = (lax.axis_index(BLK) * sp_size + lax.axis_index(SP)) * tok_rows
    cosine, sine = rope_tables(seq_start + jnp.arange(tok_rows, dtype=jnp.int32), HEAD_DIM)

    def rotated(linear, norm_gain):
        normalized = norm_apply(linear, norm_gain).reshape(
            tok_rows, model_width // HEAD_DIM, HEAD_DIM
        )
        return rotate(normalized, cosine, sine).reshape(tok_rows, model_width)

    query_rot, query_pull = jax.vjp(rotated, query_lin, gain_query)
    key_rot, key_pull = jax.vjp(rotated, key_lin, gain_key)
    query_heads, key_heads, value_heads = (
        lax.all_to_all(
            query_rot.astype(jnp.bfloat16).reshape(tok_rows, sp_size, head_width),
            SP,
            split_axis=1,
            concat_axis=0,
            tiled=True,
        ),
        lax.all_to_all(
            key_rot.astype(jnp.bfloat16).reshape(tok_rows, sp_size, head_width),
            SP,
            split_axis=1,
            concat_axis=0,
            tiled=True,
        ),
        lax.all_to_all(
            value_rows.reshape(tok_rows, sp_size, head_width),
            SP,
            split_axis=1,
            concat_axis=0,
            tiled=True,
        ),
    )
    head_rows = sp_size * tok_rows
    keys_all, values_all = (
        lax.all_gather(key_heads, BLK, axis=0, tiled=True),
        lax.all_gather(value_heads, BLK, axis=0, tiled=True),
    )
    key_rows = keys_all.shape[0]
    keys_all = keys_all.reshape(key_rows, heads_here, HEAD_DIM)
    values_all = values_all.reshape(key_rows, heads_here, HEAD_DIM)
    block_rows = math.gcd(512, head_rows)
    blocks = head_rows // block_rows
    query_base = lax.axis_index(BLK) * head_rows
    key_places = jnp.arange(key_rows, dtype=jnp.int32)
    query_blocks = query_heads.reshape(blocks, block_rows, heads_here, HEAD_DIM)
    block_starts = jnp.arange(blocks, dtype=jnp.int32) * block_rows

    def masked_scores(block_queries, block_start):
        scores = (
            jnp.einsum("qhd,khd->hqk", block_queries, keys_all, preferred_element_type=jnp.float32)
            * score_scale
        )
        query_places = query_base + block_start + jnp.arange(block_rows, dtype=jnp.int32)
        causal = key_places[None, :] <= query_places[:, None]
        return jnp.where(causal[None], scores, MASKED)

    def attend_block(block_input):
        block_queries, block_start = block_input
        scores = masked_scores(block_queries, block_start)
        row_peak = jnp.max(scores, axis=-1, keepdims=True)
        exponent = jnp.exp(scores - row_peak)
        row_total = jnp.sum(exponent, axis=-1, keepdims=True)
        attn_weights = (exponent / row_total).astype(jnp.bfloat16)
        context = jnp.einsum(
            "hqk,khd->qhd", attn_weights, values_all, preferred_element_type=jnp.float32
        )
        return (context.astype(jnp.bfloat16), (row_peak + jnp.log(row_total))[..., 0])

    context_blocks, logsum = lax.map(attend_block, (query_blocks, block_starts))
    context_rows = lax.all_to_all(
        context_blocks.reshape(head_rows, 1, head_width),
        SP,
        split_axis=0,
        concat_axis=1,
        tiled=True,
    ).reshape(tok_rows, model_width)
    attended = jnp.dot(context_rows, output_full, preferred_element_type=jnp.float32)
    residual = tokens_f + attended
    features_f, feature_pull = jax.vjp(norm_apply, residual, gain_feature)
    features = features_f.astype(jnp.bfloat16)
    logits = jnp.dot(features, router_full, preferred_element_type=jnp.float32)
    router_probs = jax.nn.softmax(logits, axis=-1)
    flat_experts, slot_rank = rank_slots(routes)
    slot_index = flat_experts * capacity + slot_rank
    token_of = jnp.arange(tok_rows * TOPK, dtype=jnp.int32) // TOPK
    slot_token = jnp.zeros((EXPERTS * capacity,), jnp.int32).at[slot_index].set(token_of)
    slot_used = jnp.zeros((EXPERTS * capacity,), jnp.bool_).at[slot_index].set(True)
    slot_rows = jnp.where(slot_used[:, None], features[slot_token], jnp.zeros((), jnp.bfloat16))

    def spread_halves(per_slot):
        grouped = per_slot.reshape(dp_size, 1, sp_size, experts_here, capacity, model_width)
        grouped = jnp.broadcast_to(
            grouped, (dp_size, blk_size, sp_size, experts_here, capacity, model_width)
        )
        return grouped.reshape(dp_size * blk_size * sp_size, experts_here, capacity, model_width)

    def join_halves(returned):
        grouped = returned.reshape(
            dp_size, blk_size, sp_size, experts_here, capacity, model_width
        ).astype(jnp.float32)
        return jnp.sum(grouped, axis=1).reshape(EXPERTS * capacity, model_width)

    send_rows = spread_halves(slot_rows)
    arrived = lax.all_to_all(
        send_rows, AXES, split_axis=0, concat_axis=0, tiled=True
    )
    gate_values = jnp.einsum(
        "secd,edf->secf", arrived, gate_weight, preferred_element_type=jnp.float32
    )
    up_values = jnp.einsum("secd,edf->secf", arrived, up_weight, preferred_element_type=jnp.float32)
    hidden = (jax.nn.silu(gate_values) * up_values).astype(jnp.bfloat16)
    part_out = jnp.einsum(
        "secf,efd->secd", hidden, down_weight, preferred_element_type=jnp.float32
    ).astype(jnp.bfloat16)
    returned = lax.all_to_all(
        part_out, AXES, split_axis=0, concat_axis=0, tiled=True
    )
    expert_out = join_halves(returned)
    route_rows = expert_out[slot_index].reshape(tok_rows, TOPK, model_width)
    route_probs = jnp.take_along_axis(router_probs, routes, axis=1)
    block_output = (residual + jnp.sum(route_probs[:, :, None] * route_rows, axis=1)).astype(
        jnp.bfloat16
    )
    out_grad = cotangent.astype(jnp.float32)
    route_grad = (
        (route_probs[:, :, None] * out_grad[:, None, :])
        .astype(jnp.bfloat16)
        .reshape(tok_rows * TOPK, model_width)
    )
    prob_route = jnp.sum(out_grad[:, None, :] * route_rows, axis=-1)
    expert_ids = jnp.arange(EXPERTS, dtype=jnp.int32)
    prob_grad = jnp.sum(
        jnp.where(routes[:, :, None] == expert_ids[None, None, :], prob_route[:, :, None], 0.0),
        axis=1,
    )
    logit_grad = (
        router_probs * (prob_grad - jnp.sum(prob_grad * router_probs, axis=-1, keepdims=True))
    ).astype(jnp.bfloat16)
    router_grad_full = jnp.dot(features.T, logit_grad, preferred_element_type=jnp.float32)
    gradient_slots = (
        jnp.zeros((EXPERTS * capacity, model_width), jnp.bfloat16).at[slot_index].set(route_grad)
    )
    gradient_send = spread_halves(gradient_slots)
    gradient_arrived, rows_arrived = (
        lax.all_to_all(gradient_send, AXES, split_axis=0, concat_axis=0, tiled=True),
        lax.all_to_all(send_rows, AXES, split_axis=0, concat_axis=0, tiled=True),
    )
    gate_values = jnp.einsum(
        "secd,edf->secf", rows_arrived, gate_weight, preferred_element_type=jnp.float32
    )
    up_values = jnp.einsum(
        "secd,edf->secf", rows_arrived, up_weight, preferred_element_type=jnp.float32
    )
    sigmoid_values = jax.nn.sigmoid(gate_values)
    silu_values = gate_values * sigmoid_values
    hidden = (silu_values * up_values).astype(jnp.bfloat16)
    hidden_grad = jnp.einsum(
        "secd,efd->secf", gradient_arrived, down_weight, preferred_element_type=jnp.float32
    ).astype(jnp.bfloat16)
    down_grad_local = jnp.einsum(
        "secf,secd->efd", hidden, gradient_arrived, preferred_element_type=jnp.float32
    )
    hidden_wide = hidden_grad.astype(jnp.float32)
    gate_grad = (
        hidden_wide * up_values * sigmoid_values * (1.0 + gate_values * (1.0 - sigmoid_values))
    ).astype(jnp.bfloat16)
    up_grad = (hidden_wide * silu_values).astype(jnp.bfloat16)
    gate_grad_local = jnp.einsum(
        "secd,secf->edf", rows_arrived, gate_grad, preferred_element_type=jnp.float32
    )
    up_grad_local = jnp.einsum(
        "secd,secf->edf", rows_arrived, up_grad, preferred_element_type=jnp.float32
    )
    input_parts = (
        jnp.einsum("secf,edf->secd", gate_grad, gate_weight, preferred_element_type=jnp.float32)
        + jnp.einsum("secf,edf->secd", up_grad, up_weight, preferred_element_type=jnp.float32)
    ).astype(jnp.bfloat16)
    returned_grads = lax.all_to_all(
        input_parts, AXES, split_axis=0, concat_axis=0, tiled=True
    )
    slot_input_grad = join_halves(returned_grads)
    expert_input_grad = slot_input_grad[slot_index].reshape(tok_rows, TOPK, model_width)
    feature_grad = jnp.dot(logit_grad, router_full.T, preferred_element_type=jnp.float32) + jnp.sum(
        expert_input_grad, axis=1
    )
    residual_part, feature_gain_grad = feature_pull(feature_grad)
    residual_grad = out_grad + residual_part
    attended_grad = residual_grad.astype(jnp.bfloat16)
    output_grad_full = jnp.dot(context_rows.T, attended_grad, preferred_element_type=jnp.float32)
    context_grad = jnp.dot(attended_grad, output_full.T, preferred_element_type=jnp.float32).astype(
        jnp.bfloat16
    )
    context_heads_grad = lax.all_to_all(
        context_grad.reshape(tok_rows, sp_size, head_width),
        SP,
        split_axis=1,
        concat_axis=0,
        tiled=True,
    )
    context_heads_grad = context_heads_grad.reshape(blocks, block_rows, heads_here, HEAD_DIM)

    def backward_block(carry, block_input):
        key_total, value_total = carry
        block_queries, block_grads, block_logsum, block_start = block_input
        scores = masked_scores(block_queries, block_start)
        attn_weights = jnp.exp(scores - block_logsum[..., None])
        prob_dots = jnp.einsum(
            "qhd,khd->hqk", block_grads, values_all, preferred_element_type=jnp.float32
        )
        row_delta = jnp.sum(attn_weights * prob_dots, axis=-1, keepdims=True)
        score_grad = (attn_weights * (prob_dots - row_delta)).astype(jnp.bfloat16)
        query_grad = (
            jnp.einsum("hqk,khd->qhd", score_grad, keys_all, preferred_element_type=jnp.float32)
            * score_scale
        )
        key_total = (
            key_total
            + jnp.einsum(
                "hqk,qhd->khd", score_grad, block_queries, preferred_element_type=jnp.float32
            )
            * score_scale
        )
        value_total = value_total + jnp.einsum(
            "hqk,qhd->khd",
            attn_weights.astype(jnp.bfloat16),
            block_grads,
            preferred_element_type=jnp.float32,
        )
        return ((key_total, value_total), query_grad.astype(jnp.bfloat16))

    zero_keys = jnp.zeros((key_rows, heads_here, HEAD_DIM), jnp.float32)
    (key_total, value_total), query_grads = lax.scan(
        backward_block,
        (zero_keys, zero_keys),
        (query_blocks, context_heads_grad, logsum, block_starts),
    )
    key_mine, value_mine = (
        lax.psum_scatter(key_total, BLK, scatter_dimension=0, tiled=True),
        lax.psum_scatter(value_total, BLK, scatter_dimension=0, tiled=True),
    )
    query_back, key_back, value_back = (
        lax.all_to_all(
            query_grads.reshape(head_rows, 1, head_width),
            SP,
            split_axis=0,
            concat_axis=1,
            tiled=True,
        ),
        lax.all_to_all(
            key_mine.astype(jnp.bfloat16).reshape(head_rows, 1, head_width),
            SP,
            split_axis=0,
            concat_axis=1,
            tiled=True,
        ),
        lax.all_to_all(
            value_mine.astype(jnp.bfloat16).reshape(head_rows, 1, head_width),
            SP,
            split_axis=0,
            concat_axis=1,
            tiled=True,
        ),
    )
    query_lin_grad, query_gain_grad = query_pull(
        query_back.reshape(tok_rows, model_width).astype(jnp.float32)
    )
    key_lin_grad, key_gain_grad = key_pull(
        key_back.reshape(tok_rows, model_width).astype(jnp.float32)
    )
    query_lin_low = query_lin_grad.astype(jnp.bfloat16)
    key_lin_low = key_lin_grad.astype(jnp.bfloat16)
    value_low = value_back.reshape(tok_rows, model_width)
    query_grad_full = jnp.dot(normed.T, query_lin_low, preferred_element_type=jnp.float32)
    key_grad_full = jnp.dot(normed.T, key_lin_low, preferred_element_type=jnp.float32)
    value_grad_full = jnp.dot(normed.T, value_low, preferred_element_type=jnp.float32)
    normed_grad = jnp.dot(query_lin_low, query_full.T, preferred_element_type=jnp.float32)
    normed_grad = normed_grad + jnp.dot(key_lin_low, key_full.T, preferred_element_type=jnp.float32)
    normed_grad = normed_grad + jnp.dot(value_low, value_full.T, preferred_element_type=jnp.float32)
    tokens_part, attention_gain_grad = attention_pull(normed_grad)
    input_gradient = residual_grad + tokens_part
    summed = (
        lax.psum_scatter(query_grad_full, AXES, scatter_dimension=0, tiled=True),
        lax.psum_scatter(key_grad_full, AXES, scatter_dimension=0, tiled=True),
        lax.psum_scatter(value_grad_full, AXES, scatter_dimension=0, tiled=True),
        lax.psum_scatter(output_grad_full, AXES, scatter_dimension=0, tiled=True),
        lax.psum_scatter(router_grad_full, AXES, scatter_dimension=0, tiled=True),
        lax.psum_scatter(attention_gain_grad, AXES, scatter_dimension=0, tiled=True),
        lax.psum_scatter(query_gain_grad, AXES, scatter_dimension=0, tiled=True),
        lax.psum_scatter(key_gain_grad, AXES, scatter_dimension=0, tiled=True),
        lax.psum_scatter(feature_gain_grad, AXES, scatter_dimension=0, tiled=True),
    )
    return (
        block_output,
        input_gradient,
        summed[0],
        summed[1],
        summed[2],
        summed[3],
        summed[4],
        summed[5],
        summed[6],
        summed[7],
        summed[8],
        gate_grad_local,
        up_grad_local,
        down_grad_local,
    )


def solution(mesh):
    in_specs = (
        P(AXES, None),
        P(AXES, None),
        P(AXES, None),
        P(AXES, None),
        P(AXES, None),
        P(AXES, None),
        P(AXES),
        P(AXES),
        P(AXES),
        P(AXES),
        P((DP, SP), None, BLK),
        P((DP, SP), None, BLK),
        P((DP, SP), BLK, None),
        P(AXES, None),
        P(AXES, None),
    )
    out_specs = (
        P(AXES, None),
        P(AXES, None),
        P(AXES, None),
        P(AXES, None),
        P(AXES, None),
        P(AXES, None),
        P(AXES, None),
        P(AXES),
        P(AXES),
        P(AXES),
        P(AXES),
        P((DP, SP), None, BLK),
        P((DP, SP), None, BLK),
        P((DP, SP), BLK, None),
    )
    fast = dict(mesh.shape) == {DP: 4, BLK: 2, SP: 4}
    return jax.shard_map(body_fast if fast else body, mesh=mesh, in_specs=in_specs, out_specs=out_specs, check_vma=False)
```
